32 devices in a mesh: dp: 8 (over z, core), sp: 4 (over y, x).
Axes of the slice: x: 2, y: 2, z: 4, core: 2. Of those that a mesh axis runs over, the one named last changes fastest.
Arguments:
- tokens_in: bfloat16 [16, 1024, 1024], P('dp', 'sp'), may hold values from -6 to 6
- expert_ids: int32 [8, 4, 512, 1], P('dp', 'sp'), may hold values from 0 to 7; in each aligned block of 512 rows (0 to 511, 512 to 1023, ..., all dimensions but the last counted through in order) at most 128 rows name the same one
- query_weight: bfloat16 [1024, 1024], replicated, may hold values from -0.1875 to 0.1875
- key_weight: bfloat16 [1024, 1024], replicated, may hold values from -0.1875 to 0.1875
- value_weight: bfloat16 [1024, 1024], replicated, may hold values from -0.1875 to 0.1875
- out_weight: bfloat16 [1024, 1024], replicated, may hold values from -3 to 3
- norm1_gain: float32 [1024], replicated, may hold values from 0.25 to 1.75
- norm1_shift: float32 [1024], replicated, may hold values from -3 to 3
- norm2_gain: float32 [1024], replicated, may hold values from 0.25 to 1.75
- norm2_shift: float32 [1024], replicated, may hold values from -3 to 3
- up_weight: bfloat16 [8, 4096, 1024], P('dp'), may hold values from -0.1875 to 0.1875
- down_weight: bfloat16 [8, 4096, 1024], P('dp'), may hold values from -0.09375 to 0.09375
- out_cotangent: bfloat16 [16, 1024, 1024], P('dp', 'sp'), may hold values from -6 to 6
- load_mean: float32 [8], replicated, may hold values from 0.5 to 2
Outputs:
- block_out: bfloat16 [16, 1024, 1024], P('dp', 'sp')
- tokens_grad: bfloat16 [16, 1024, 1024], P('dp', 'sp')
- query_grad: float32 [1024, 1024], replicated
- key_grad: float32 [1024, 1024], replicated
- value_grad: float32 [1024, 1024], replicated
- out_grad: float32 [1024, 1024], replicated
- norm1_gain_grad: float32 [1024], replicated
- norm1_shift_grad: float32 [1024], replicated
- norm2_gain_grad: float32 [1024], replicated
- norm2_shift_grad: float32 [1024], replicated
- up_grad: float32 [8, 4096, 1024], P('dp', 'sp')
- down_grad: float32 [8, 4096, 1024], P('dp', 'sp')
- load_next: float32 [8], replicated
The draws below stay inside these ranges and needn't reach their ends.
Inputs may be any that keep to these rules, and one draw needn't show every extreme that they name: `expert_ids`: among the 512 rows of one device no expert is named more than 128 times, and in some device's rows one expert is named exactly 128 times.
All inputs are finite; a program needn't handle non-finite values.
Results may differ from the reference program's by a relative error of at most 0.012.
Values may be sent and summed in bfloat16 or wider, within the bound.
A program may use at most 384 MiB of HBM per device.

```python
import math
import jax
import jax.numpy as jnp
import numpy as np
from jax import lax

D = 1024
HEADS = 16
HDIM = 64
FF = 4096
SEQS = 2
SHARD = 256
LEN = 1024
SEQ_ALL = 16
TOK = 512
EXPERTS = 8
CAP = 128
N_DP = 8
N_SP = 4


def level_of(rng, extent, split, smallest, top_value):
    level = 1.0
    for axis_at, blocks in split:
        draws = jax.random.uniform(jax.random.fold_in(jax.random.fold_in(rng, 6), axis_at), (blocks,), jnp.float32, smallest / len(split), top_value / len(split))
        level = level * jnp.repeat(jnp.exp(draws), extent[axis_at] // blocks).reshape((-1,) + (1,) * (len(extent) - 1 - axis_at))
    return level


def routed_block(own_key, own, number, rows, amount, top, bound, lean):
    ranking = jax.random.permutation(own_key, amount)
    heavy_load, ordinary = load_shares(amount, rows * top, bound, lean, True), load_shares(amount, rows * top, bound, lean, False)
    places = jnp.arange(amount)

    def named(tallies, rotation):
        used = int((tallies > 0).sum())
        fixed = max(1, used // 4)
        shifted = fixed + (places - fixed + rotation * (used - fixed)) % max(1, amount - fixed)
        return jnp.zeros((amount,), jnp.int32).at[ranking[jnp.where(places < fixed, places, shifted)]].set(jnp.asarray(tallies, jnp.int32))

    tallies = jnp.where(number % 4 == 0, named(heavy_load, number // 4), named(ordinary, number - number // 4 - 1))
    mixed = jax.random.permutation(jax.random.fold_in(own, 3), amount)
    donor, sink = mixed[0:amount // 2 * 2:2], mixed[1:amount // 2 * 2:2]
    slack = jnp.minimum(tallies[donor] - 1, bound - tallies[sink]) // 2
    slack = jnp.where((donor == ranking[0]) | (sink == ranking[0]) | (tallies[sink] == 0), 0, jnp.maximum(slack, 0))
    shifted = jax.random.randint(jax.random.fold_in(own, 4), (amount // 2,), 0, 1 << 20) % (slack + 1)
    tallies = tallies.at[donor].add(-shifted).at[sink].add(shifted)
    items = jnp.searchsorted(jnp.cumsum(tallies), jnp.arange(rows * top), side="right").astype(jnp.int32)
    table = items.reshape(top, rows).T
    table = table[jax.random.permutation(jax.random.fold_in(own, 1), rows)]
    rotation = jax.random.randint(jax.random.fold_in(own, 2), (rows, 1), 0, top)
    return jnp.take_along_axis(table, (jnp.arange(top)[None, :] + rotation) % top, axis=1)


def load_shares(amount, total, reach, lean, full):
    portions = [(1 << 20) // math.isqrt(grade ** lean) + 1 for grade in range(1, amount + 1)]
    largest = reach if full else min(reach, max(-(-total // amount), total * portions[0] // sum(portions)))
    least = 1 if total - largest >= amount - 1 else 0
    given, surplus = [largest] + [least] * (amount - 1), total - largest - least * (amount - 1)
    while surplus > 0:
        free = [i for i in range(1, amount) if given[i] < largest] or [i for i in range(1, amount) if given[i] < reach]
        mass, budget = sum([portions[i] for i in free]), surplus
        for i in free:
            extra = min(reach - given[i], max(1, budget * portions[i] // mass), surplus)
            given[i] = given[i] + extra
            surplus = surplus - extra
    return np.array(given)


def noise(key, extent, width, limit, pieces=(), kind=jnp.bfloat16):
    result = width * jax.random.normal(key, extent, jnp.float32)
    if pieces:
        result = result * level_of(key, extent, pieces, -0.22, 0.18)
    return jnp.clip(result, -limit, limit).astype(kind)


def setup_inputs(seed: int = 0) -> dict:
    keys = jax.random.split(jax.random.key(seed), 15)
    tokens_in = noise(keys[0], (SEQ_ALL, LEN, D), 1.0, 6.0, ((0, 8), (1, 4)))
    expert_ids_keys = jax.random.split(jax.random.fold_in(keys[1], 1), N_DP * N_SP * TOK // TOK)
    expert_ids_turns = jax.random.permutation(jax.random.fold_in(keys[1], 3), N_DP * N_SP * TOK // TOK)
    expert_ids = jax.vmap(lambda own, number: routed_block(jax.random.fold_in(keys[1], 2), own, number, TOK, EXPERTS, 1, CAP, 3))(expert_ids_keys, expert_ids_turns).reshape((N_DP, N_SP, TOK, 1))
    query_weight = noise(keys[2], (D, D), D ** -0.5, 0.1875)
    key_weight = noise(keys[3], (D, D), D ** -0.5, 0.1875)
    value_weight = noise(keys[4], (D, D), D ** -0.5, 0.1875)
    out_weight = noise(keys[5], (D, D), (max(D // 256, 1)) ** -0.5, 3.0)
    norm1_gain = jnp.clip(1.0 + 0.15 * jax.random.normal(keys[6], (D,), jnp.float32), 0.25, 1.75)
    norm1_shift = noise(keys[7], (D,), 0.3, 3.0, (), jnp.float32)
    norm2_gain = jnp.clip(1.0 + 0.15 * jax.random.normal(keys[8], (D,), jnp.float32), 0.25, 1.75)
    norm2_shift = noise(keys[9], (D,), 0.3, 3.0, (), jnp.float32)
    up_weight = noise(keys[10], (EXPERTS, FF, D), D ** -0.5, 0.1875, ((0, 8),))
    down_weight = noise(keys[11], (EXPERTS, FF, D), FF ** -0.5, 0.09375, ((0, 8),))
    out_cotangent = noise(keys[12], (SEQ_ALL, LEN, D), 1.0, 6.0, ((0, 8), (1, 4)))
    load_mean = jnp.clip(jnp.exp(jax.random.uniform(keys[13], (EXPERTS,), jnp.float32, math.log(0.5), math.log(2.0))), 0.5, 2.0)
    return dict(tokens_in=tokens_in, expert_ids=expert_ids, query_weight=query_weight, key_weight=key_weight, value_weight=value_weight, out_weight=out_weight, norm1_gain=norm1_gain, norm1_shift=norm1_shift, norm2_gain=norm2_gain, norm2_shift=norm2_shift, up_weight=up_weight, down_weight=down_weight, out_cotangent=out_cotangent, load_mean=load_mean)


NORM_EPSILON = 1e-05
EXACT_MATMUL = lax.Precision.HIGHEST
GELU_ROOT = 0.7978845608028654
CUBIC_TERM = 0.044715

@jax.custom_vjp
def reduced_copy(v):
    return lax.optimization_barrier(v.astype(jnp.bfloat16)).astype(jnp.float32)

@jax.custom_vjp
def reduced_backward(v):
    return v

def low_keep(v):
    return (reduced_copy(v), None)

def low_pass(kept, grad):
    return (grad,)

def back_keep(v):
    return (v, None)

def back_low(kept, grad):
    return (reduced_copy(grad),)
reduced_copy.defvjp(low_keep, low_pass)
reduced_backward.defvjp(back_keep, back_low)

def smooth(values):
    return 0.5 * values * (1.0 + jnp.tanh(GELU_ROOT * (values + CUBIC_TERM * values * values * values)))

def layer_norm(values, gain, shift):
    center = lax.optimization_barrier(jnp.mean(values, axis=-1, keepdims=True))
    offset = values - center
    spread = lax.optimization_barrier(jnp.mean(offset * offset, axis=-1, keepdims=True))
    return offset * lax.rsqrt(spread + NORM_EPSILON) * gain + shift

def reference(tokens_in, expert_ids, query_weight, key_weight, value_weight, out_weight, norm1_gain, norm1_shift, norm2_gain, norm2_shift, up_weight, down_weight, out_cotangent, load_mean):
    blocks = N_DP * N_SP
    routes = expert_ids.reshape(blocks, TOK).astype(jnp.int32)
    one_hot = (routes[:, :, None] == jnp.arange(EXPERTS, dtype=jnp.int32)[None, None, :]).astype(jnp.int32)
    running = jnp.cumsum(one_hot, axis=1) - 1
    slot_of = lax.optimization_barrier(jnp.sum(running * one_hot, axis=2))
    block_ids = jnp.arange(blocks, dtype=jnp.int32)[:, None]
    target = (routes * (blocks * CAP) + block_ids * CAP + slot_of).reshape(-1).astype(jnp.int32)
    counts = lax.optimization_barrier(jnp.sum(one_hot, axis=(0, 1))).astype(jnp.float32)
    positions = jnp.arange(LEN, dtype=jnp.int32)
    causal = positions[None, :] <= positions[:, None]
    score_scale = HDIM ** (-0.5)

    def to_blocks(values):
        return values.reshape(N_DP, SEQS, N_SP, SHARD, D).transpose(0, 2, 1, 3, 4).reshape(blocks * TOK, D)

    def from_blocks(values):
        return values.reshape(N_DP, N_SP, SEQS, SHARD, D).transpose(0, 2, 1, 3, 4).reshape(SEQ_ALL, LEN, D)

    def attend(triple):
        query_seq, key_seq, value_seq = triple
        query_h = query_seq.reshape(LEN, HEADS, HDIM)
        key_h = key_seq.reshape(LEN, HEADS, HDIM)
        value_h = value_seq.reshape(LEN, HEADS, HDIM)
        logits = jnp.einsum('qhd,khd->hqk', query_h, key_h, precision=EXACT_MATMUL) * score_scale
        logits = reduced_backward(logits)
        logits = jnp.where(causal[None], logits, -1e+30)
        row_max = lax.optimization_barrier(jnp.max(logits, axis=-1, keepdims=True))
        exp_terms = jnp.exp(logits - row_max)
        attn_prob = reduced_copy(exp_terms / lax.optimization_barrier(jnp.sum(exp_terms, axis=-1, keepdims=True)))
        return jnp.einsum('hqk,khd->qhd', attn_prob, value_h, precision=EXACT_MATMUL).reshape(LEN, D)

    def expert(expert_item):
        expert_rows, w_up, w_down = expert_item
        pre_act = reduced_backward(jnp.dot(expert_rows, w_up.T, precision=EXACT_MATMUL))
        hidden = reduced_copy(smooth(pre_act))
        return jnp.dot(hidden, w_down, precision=EXACT_MATMUL)

    def forward(token_inputs, query_projection, key_projection, value_projection, output_weight, gain_one, shift_one, gain_two, shift_two, w_up, w_down):
        first_normed = reduced_copy(layer_norm(token_inputs, gain_one, shift_one))
        query_states = reduced_backward(reduced_copy(jnp.einsum('zjr,rv->zjv', first_normed, query_projection, precision=EXACT_MATMUL)))
        key = reduced_backward(reduced_copy(jnp.einsum('zjr,rv->zjv', first_normed, key_projection, precision=EXACT_MATMUL)))
        value_states = reduced_backward(reduced_copy(jnp.einsum('zjr,rv->zjv', first_normed, value_projection, precision=EXACT_MATMUL)))
        attention_mixed = lax.map(jax.checkpoint(attend), (query_states, key, value_states))
        attention_mixed = reduced_backward(reduced_copy(attention_mixed))
        residual_stream = token_inputs + reduced_backward(jnp.einsum('zjr,rv->zjv', attention_mixed, output_weight, precision=EXACT_MATMUL))
        normed2 = reduced_backward(reduced_copy(layer_norm(residual_stream, gain_two, shift_two)))
        buffer = jnp.zeros((EXPERTS * blocks * CAP, D), jnp.float32).at[target].set(to_blocks(normed2))
        expert_out = lax.map(jax.checkpoint(expert), (buffer.reshape(EXPERTS, blocks * CAP, D), w_up, w_down))
        expert_out = reduced_backward(reduced_copy(expert_out.reshape(EXPERTS * blocks * CAP, D)))
        return residual_stream + from_blocks(expert_out[target])
    inputs = (tokens_in.astype(jnp.float32), query_weight.astype(jnp.float32), key_weight.astype(jnp.float32), value_weight.astype(jnp.float32), out_weight.astype(jnp.float32), norm1_gain, norm1_shift, norm2_gain, norm2_shift, up_weight.astype(jnp.float32), down_weight.astype(jnp.float32))
    block_out, pullback = jax.vjp(forward, *inputs)
    grads = pullback(out_cotangent.astype(jnp.float32))
    load_now = counts * EXPERTS / (blocks * TOK)
    load_next = 0.9 * load_mean + 0.1 * load_now
    return (block_out.astype(jnp.bfloat16), grads[0].astype(jnp.bfloat16), grads[1], grads[2], grads[3], grads[4], grads[5], grads[6], grads[7], grads[8], grads[9], grads[10], load_next)
```

```python
import functools

import jax
import jax.numpy as jnp
from jax import lax
from jax.experimental import pallas as pl
from jax.experimental.pallas import tpu as pltpu
from jax.sharding import PartitionSpec as P

HEADS = 16
MESH = pl.DeviceIdType.MESH
BLOCK = 256
LANES = 128
VMEM_BYTES = 60 * 2**20

NORM_EPSILON = 1e-05
GELU_ROOT = 0.7978845608028654
CUBIC_TERM = 0.044715

ROWS_BY_COLS = (((1,), (0,)), ((), ()))
ROWS_BY_ROWS = (((1,), (1,)), ((), ()))
COLS_BY_COLS = (((0,), (0,)), ((), ()))


def smooth(values):
    return (
        0.5
        * values
        * (1.0 + jnp.tanh(GELU_ROOT * (values + CUBIC_TERM * values * values * values)))
    )


def smooth_slope(values):
    inner = jnp.tanh(GELU_ROOT * (values + CUBIC_TERM * values * values * values))
    return 0.5 * (1.0 + inner) + 0.5 * values * (1.0 - inner * inner) * GELU_ROOT * (
        1.0 + 3.0 * CUBIC_TERM * values * values
    )


def norm_forward(values, gain, shift):
    center = jnp.mean(values, axis=-1, keepdims=True)
    offset = values - center
    rstd = lax.rsqrt(jnp.mean(offset * offset, axis=-1, keepdims=True) + NORM_EPSILON)
    unit = offset * rstd
    return (unit * gain + shift, unit, rstd)


def norm_backward(grad, unit, rstd, gain):
    scaled = grad * gain
    inner = (
        scaled
        - jnp.mean(scaled, axis=-1, keepdims=True)
        - unit * jnp.mean(scaled * unit, axis=-1, keepdims=True)
    )
    return (inner * rstd, jnp.sum(grad * unit, axis=0), jnp.sum(grad, axis=0))


def mxu(left, right, dims=ROWS_BY_COLS):
    return lax.dot_general(left, right, dims, preferred_element_type=jnp.float32)


def span(index, size):
    return pl.ds(pl.multiple_of(index * size, size), size)


def greet(peers):
    barrier = pltpu.get_barrier_semaphore()
    for peer in peers:
        pl.semaphore_signal(barrier, inc=1, device_id=peer, device_id_type=MESH)
    pl.semaphore_wait(barrier, len(peers))


def send(source, target, send_sem, recv_sem, peer):
    return pltpu.make_async_remote_copy(
        src_ref=source,
        dst_ref=target,
        send_sem=send_sem,
        recv_sem=recv_sem,
        device_id=peer,
        device_id_type=MESH,
    )


def attend_forward(
    ways,
    head_dim,
    x_ref,
    wq_ref,
    wk_ref,
    wv_ref,
    gain_ref,
    shift_ref,
    normed_ref,
    q_ref,
    k_ref,
    v_ref,
    log_ref,
    mixed_ref,
    x_all,
    mixed_f,
    mixed_h,
    log_s,
    x_send,
    x_recv,
    m_send,
    m_recv,
):
    seqs, shard, _ = x_ref.shape
    seq_len, width = q_ref.shape[1:]
    heads = width // head_dim
    me = lax.axis_index("sp")
    peer = [lax.rem(me + d, ways) for d in range(ways)]
    origin = [lax.rem(me + ways - d, ways) for d in range(ways)]
    greet([{"sp": peer[d]} for d in range(1, ways)])

    def x_copy(s, d):
        return send(
            x_ref.at[s],
            x_all.at[s, span(me, shard)],
            x_send.at[s, d],
            x_recv.at[s, d],
            {"sp": peer[d]},
        )

    def mixed_copy(s, d):
        return send(
            mixed_h.at[s, span(peer[d], shard)],
            mixed_ref.at[s, :, span(me, width)],
            m_send.at[s, d],
            m_recv.at[s, d],
            {"sp": peer[d]},
        )

    lane = lax.broadcasted_iota(jnp.int32, (1, width), 1) // head_dim
    log_lane = lax.broadcasted_iota(jnp.int32, (1, LANES), 1)
    visible = lax.broadcasted_iota(jnp.int32, (BLOCK, BLOCK), 1) <= lax.broadcasted_iota(
        jnp.int32, (BLOCK, BLOCK), 0
    )
    scale = head_dim ** (-0.5)

    def project(s, rows, values):
        normed, _, _ = norm_forward(values.astype(jnp.float32), gain_ref[...], shift_ref[...])
        normed = normed.astype(jnp.bfloat16)
        normed_ref[s, rows, :] = normed
        q_ref[s, rows, :] = mxu(normed, wq_ref[...]).astype(jnp.bfloat16)
        k_ref[s, rows, :] = mxu(normed, wk_ref[...]).astype(jnp.bfloat16)
        v_ref[s, rows, :] = mxu(normed, wv_ref[...]).astype(jnp.bfloat16)

    for d in range(1, ways):
        x_copy(0, d).start()
    for s in range(seqs):
        project(s, span(me, shard), x_ref[s])
        for d in range(1, ways):
            x_copy(s, d).wait_recv()
            if d == ways - 1 and s + 1 < seqs:
                for later in range(1, ways):
                    x_copy(s + 1, later).start()
            rows = span(origin[d], shard)
            project(s, rows, x_all[s, rows, :])
        mixed_f[...] = jnp.zeros_like(mixed_f)
        log_s[...] = jnp.zeros_like(log_s)

        def one_head(h, carry):
            mine = (lane == h).astype(jnp.float32)
            for at in range(0, seq_len, BLOCK):
                rows = slice(at, at + BLOCK)
                query = (q_ref[s, rows, :].astype(jnp.float32) * (mine * scale)).astype(
                    jnp.bfloat16
                )
                near = mxu(query, k_ref[s, rows, :], ROWS_BY_ROWS)
                near = jnp.where(visible, near, -1e30)
                top = jnp.max(near, axis=1, keepdims=True)
                if at:
                    far = mxu(query, k_ref[s, :at, :], ROWS_BY_ROWS)
                    top = jnp.maximum(top, jnp.max(far, axis=1, keepdims=True))
                near = jnp.exp(near - top)
                total = jnp.sum(near, axis=1, keepdims=True)
                if at:
                    far = jnp.exp(far - top)
                    total += jnp.sum(far, axis=1, keepdims=True)
                inverse = 1.0 / total
                out = mxu((near * inverse).astype(jnp.bfloat16), v_ref[s, rows, :])
                if at:
                    out += mxu((far * inverse).astype(jnp.bfloat16), v_ref[s, :at, :])
                mixed_f[rows, :] += out * mine
                log_s[rows, :] = jnp.where(log_lane == h, top + jnp.log(total), log_s[rows, :])
            return carry

        lax.fori_loop(0, heads, one_head, 0)
        log_ref[s] = jnp.transpose(log_s[...])[: log_ref.shape[1], :]
        mixed_h[s] = mixed_f[...].astype(jnp.bfloat16)
        for d in range(1, ways):
            mixed_copy(s, d).start()
        mixed_ref[s, :, span(me, width)] = mixed_h[s, span(me, shard), :]
    for s in range(seqs):
        for d in range(1, ways):
            x_copy(s, d).wait_send()
            mixed_copy(s, d).wait()


def attend_backward(
    ways,
    head_dim,
    dmixed_ref,
    q_ref,
    k_ref,
    v_ref,
    log_ref,
    dq_ref,
    dk_ref,
    dv_ref,
    dq_tok,
    dk_tok,
    dv_tok,
    dmixed_h,
    dq_f,
    dk_f,
    dv_f,
    m_send,
    m_recv,
    g_send,
    g_recv,
):
    seqs, shard, _ = dmixed_ref.shape
    seq_len, width = q_ref.shape[1:]
    heads = width // head_dim
    me = lax.axis_index("sp")
    peer = [lax.rem(me + d, ways) for d in range(ways)]
    greet([{"sp": peer[d]} for d in range(1, ways)])

    def dmixed_copy(s, d):
        return send(
            dmixed_ref.at[s, :, span(peer[d], width)],
            dmixed_h.at[s, span(me, shard)],
            m_send.at[s, d],
            m_recv.at[s, d],
            {"sp": peer[d]},
        )

    pairs = ((dq_ref, dq_tok), (dk_ref, dk_tok), (dv_ref, dv_tok))

    def grad_copy(i, s, d):
        source, target = pairs[i]
        return send(
            source.at[s, span(peer[d], shard)],
            target.at[s, :, span(me, width)],
            g_send.at[i, s, d],
            g_recv.at[i, s, d],
            {"sp": peer[d]},
        )

    for s in range(seqs):
        for d in range(1, ways):
            dmixed_copy(s, d).start()
    lane = lax.broadcasted_iota(jnp.int32, (1, width), 1) // head_dim
    visible = lax.broadcasted_iota(jnp.int32, (BLOCK, BLOCK), 0) <= lax.broadcasted_iota(
        jnp.int32, (BLOCK, BLOCK), 1
    )
    scale = head_dim ** (-0.5)
    for s in range(seqs):
        dmixed_h[s, span(me, shard), :] = dmixed_ref[s, :, span(me, width)]
        for d in range(1, ways):
            dmixed_copy(s, d).wait_recv()
        dq_f[...] = jnp.zeros_like(dq_f)
        dk_f[...] = jnp.zeros_like(dk_f)
        dv_f[...] = jnp.zeros_like(dv_f)

        def one_head(h, carry):
            mine = (lane == h).astype(jnp.float32)
            for at in range(0, seq_len, BLOCK):
                rows = slice(at, at + BLOCK)
                query = (q_ref[s, rows, :].astype(jnp.float32) * (mine * scale)).astype(
                    jnp.bfloat16
                )
                dout = (dmixed_h[s, rows, :].astype(jnp.float32) * mine).astype(jnp.bfloat16)
                log_row = log_ref[s, pl.ds(h, 1), rows]
                parts = [(rows, True)] + ([(slice(0, at), False)] if at else [])
                kept = []
                delta = jnp.zeros((1, BLOCK), jnp.float32)
                for keys, diagonal in parts:
                    prob = jnp.exp(mxu(k_ref[s, keys, :], query, ROWS_BY_ROWS) - log_row)
                    if diagonal:
                        prob = jnp.where(visible, prob, 0.0)
                    dprob = mxu(v_ref[s, keys, :], dout, ROWS_BY_ROWS)
                    delta += jnp.sum(prob * dprob, axis=0, keepdims=True)
                    kept.append((keys, prob, dprob))
                dquery = jnp.zeros((BLOCK, width), jnp.float32)
                for keys, prob, dprob in kept:
                    dv_f[keys, :] += mxu(prob.astype(jnp.bfloat16), dout)
                    dlogit = (prob * (dprob - delta)).astype(jnp.bfloat16)
                    dk_f[keys, :] += mxu(dlogit, query)
                    dquery += mxu(dlogit, k_ref[s, keys, :], COLS_BY_COLS)
                dq_f[rows, :] += dquery * (mine * scale)
            return carry

        lax.fori_loop(0, heads, one_head, 0)
        for i, total in enumerate((dq_f, dk_f, dv_f)):
            source, target = pairs[i]
            source[s] = total[...].astype(jnp.bfloat16)
            for d in range(1, ways):
                grad_copy(i, s, d).start()
            target[s, :, span(me, width)] = source[s, span(me, shard), :]
    for s in range(seqs):
        for d in range(1, ways):
            dmixed_copy(s, d).wait_send()
            for i in range(3):
                grad_copy(i, s, d).wait()


def reduce_everywhere(
    ways,
    columns,
    part_ref,
    small_ref,
    out_ref,
    small_out,
    core_land,
    core_sum,
    column_land,
    piece,
    small_land,
    small_sum,
    core_send,
    core_recv,
    column_send,
    column_recv,
    spread_send,
    spread_recv,
    ring_send,
    ring_recv,
    cross_send,
    cross_recv,
    small_send,
    small_recv,
    local_sem,
):
    rows = part_ref.shape[2]
    width = part_ref.shape[3]
    me = lax.axis_index("sp")
    dp = lax.axis_index("dp")
    core = lax.rem(dp, 2)
    column = dp // 2
    twin = {"dp": dp + 1 - 2 * core}
    column_peer = [lax.rem(column + d, columns) for d in range(columns)]
    sp_peer = [lax.rem(me + d, ways) for d in range(ways)]
    sp_origin = [lax.rem(me + ways - d, ways) for d in range(ways)]
    column_id = [{"dp": 2 * column_peer[d] + core} for d in range(columns)]
    sp_id = [{"sp": sp_peer[d]} for d in range(ways)]
    greet([twin] + column_id[1:] + sp_id[1:])

    first = send(part_ref.at[1 - core], core_land, core_send, core_recv, twin)
    first.start()
    small_first = send(small_ref, small_land.at[0], small_send.at[0], small_recv.at[0], twin)
    small_first.start()
    small_first.wait()
    small_sum[0] = small_ref[...] + small_land[0]

    def small_column(d):
        return send(
            small_sum.at[0],
            small_land.at[d],
            small_send.at[d],
            small_recv.at[d],
            column_id[d],
        )

    def small_ring(d):
        at = columns + d
        return send(
            small_sum.at[1],
            small_land.at[at],
            small_send.at[at],
            small_recv.at[at],
            sp_id[d],
        )

    for d in range(1, columns):
        small_column(d).start()
    first.wait()
    core_sum[...] = (
        part_ref[core].astype(jnp.float32) + core_land[...].astype(jnp.float32)
    ).astype(jnp.bfloat16)

    def column_copy(d):
        return send(
            core_sum.at[column_peer[d]],
            column_land.at[d],
            column_send.at[d],
            column_recv.at[d],
            column_id[d],
        )

    for d in range(1, columns):
        column_copy(d).start()
    for d in range(1, columns):
        small_column(d).wait()
    total = small_sum[0]
    for d in range(1, columns):
        total += small_land[d]
    small_sum[1] = total
    for d in range(1, ways):
        small_ring(d).start()
    total = core_sum[column].astype(jnp.float32)
    for d in range(1, columns):
        column_copy(d).wait()
        total += column_land[d].astype(jnp.float32)
    piece[...] = total.astype(jnp.bfloat16)

    def block(at_core, at_column, at_sp, count=1):
        first_row = pl.multiple_of((at_core * columns + at_column) * rows, rows)
        return out_ref.at[pl.ds(first_row, count * rows), span(at_sp, width)]

    def spread_copy(d):
        return send(
            piece,
            block(core, column, me),
            spread_send.at[d],
            spread_recv.at[d],
            column_id[d],
        )

    for d in range(1, columns):
        spread_copy(d).start()
    own = pltpu.make_async_copy(piece, block(core, column, me), local_sem)
    own.start()
    for d in range(1, ways):
        small_ring(d).wait()
    total = small_sum[1]
    for d in range(1, ways):
        total += small_land[columns + d]
    small_out[...] = total
    own.wait()
    for d in range(1, columns):
        spread_copy(d).wait()

    def ring_copy(d):
        half = block(core, 0, me, columns)
        return send(half, half, ring_send.at[d], ring_recv.at[d], sp_id[d])

    def cross_copy(d):
        half = block(core, 0, sp_origin[d], columns)
        return send(half, half, cross_send.at[d], cross_recv.at[d], twin)

    for d in range(1, ways):
        ring_copy(d).start()
    cross_copy(0).start()
    for d in range(1, ways):
        ring_copy(d).wait_recv()
        cross_copy(d).start()
    for d in range(1, ways):
        ring_copy(d).wait_send()
    for d in range(ways):
        cross_copy(d).wait()


def vmem(count):
    return [pl.BlockSpec(memory_space=pltpu.VMEM)] * count


def params(collective_id):
    return pltpu.CompilerParams(
        collective_id=collective_id, has_side_effects=True, vmem_limit_bytes=VMEM_BYTES
    )


def dma(*shape):
    return pltpu.SemaphoreType.DMA(shape)


def local(
    tokens_in,
    expert_ids,
    query_weight,
    key_weight,
    value_weight,
    out_weight,
    norm1_gain,
    norm1_shift,
    norm2_gain,
    norm2_shift,
    up_weight,
    down_weight,
    out_cotangent,
    load_mean,
):
    seq_count, shard_len, model_width = tokens_in.shape
    row_count = seq_count * shard_len
    head_dim = model_width // HEADS
    dp_ways = lax.axis_size("dp")
    sp_ways = lax.axis_size("sp")
    sp_at = lax.axis_index("sp")
    seq_len = shard_len * sp_ways
    experts = load_mean.shape[0]
    slot_count = 2 * row_count // experts
    local_experts = up_weight.shape[0]
    ff_width = up_weight.shape[1]
    width = model_width // sp_ways
    bf16 = jnp.bfloat16
    f32 = jnp.float32

    def shape(*sizes, dtype=bf16):
        return jax.ShapeDtypeStruct(sizes, dtype)

    routes = expert_ids.reshape(row_count)
    one_hot = (routes[:, None] == jnp.arange(experts, dtype=jnp.int32)[None, :]).astype(jnp.int32)
    running = jnp.cumsum(one_hot, axis=0) - 1
    slot_of = jnp.sum(running * one_hot, axis=1)
    target = routes * slot_count + slot_of
    placer = (jnp.arange(experts * slot_count, dtype=jnp.int32)[:, None] == target[None, :]).astype(
        bf16
    )
    cot_b = out_cotangent.reshape(row_count, model_width)
    cot_send = jnp.dot(placer, cot_b, preferred_element_type=f32).astype(bf16)
    cot_send = cot_send.reshape(experts, slot_count, model_width)
    arrived = lax.all_to_all(cot_send, "dp", split_axis=0, concat_axis=0, tiled=True)

    def columns_of(weight):
        return lax.dynamic_slice_in_dim(weight, sp_at * width, width, axis=1)

    normed_all, query_h, key_h, value_h, log_total, mixed_b = pl.pallas_call(
        functools.partial(attend_forward, sp_ways, head_dim),
        out_shape=[
            shape(seq_count, seq_len, model_width),
            shape(seq_count, seq_len, width),
            shape(seq_count, seq_len, width),
            shape(seq_count, seq_len, width),
            shape(seq_count, 8, seq_len, dtype=f32),
            shape(seq_count, shard_len, model_width),
        ],
        in_specs=vmem(6),
        out_specs=vmem(6),
        scratch_shapes=[
            pltpu.VMEM((seq_count, seq_len, model_width), bf16),
            pltpu.VMEM((seq_len, width), f32),
            pltpu.VMEM((seq_count, seq_len, width), bf16),
            pltpu.VMEM((seq_len, LANES), f32),
            dma(seq_count, sp_ways),
            dma(seq_count, sp_ways),
            dma(seq_count, sp_ways),
            dma(seq_count, sp_ways),
        ],
        compiler_params=params(0),
    )(
        tokens_in,
        columns_of(query_weight),
        columns_of(key_weight),
        columns_of(value_weight),
        norm1_gain.reshape(1, model_width),
        norm1_shift.reshape(1, model_width),
    )
    mixed_b = mixed_b.reshape(row_count, model_width)
    inputs = tokens_in.reshape(row_count, model_width).astype(f32)
    attn_out = jnp.dot(mixed_b, out_weight, preferred_element_type=f32)
    residual_stream = inputs + attn_out
    normed2, unit2, rstd2 = norm_forward(residual_stream, norm2_gain, norm2_shift)
    normed2_b = normed2.astype(bf16)
    outgoing = jnp.dot(placer, normed2_b, preferred_element_type=f32).astype(bf16)
    outgoing = outgoing.reshape(experts, slot_count, model_width)
    received = lax.all_to_all(outgoing, "dp", split_axis=0, concat_axis=0, tiled=True)
    parts = received.reshape(-1, local_experts, slot_count, model_width)
    pre_act = jnp.einsum("sxcd,xfd->sxcf", parts, up_weight, preferred_element_type=f32)
    hidden_b = smooth(pre_act).astype(bf16)
    arrived_p = arrived.reshape(-1, local_experts, slot_count, model_width)
    dhidden = jnp.einsum("sxcd,xfd->sxcf", arrived_p, down_weight, preferred_element_type=f32)
    dpre_b = (dhidden * smooth_slope(pre_act)).astype(bf16)
    dnormed_send = jnp.einsum("sxcf,xfd->sxcd", dpre_b, up_weight, preferred_element_type=f32)
    dnormed_send = dnormed_send.astype(bf16).reshape(-1, slot_count, model_width)
    dnormed_back = lax.all_to_all(dnormed_send, "dp", split_axis=0, concat_axis=0, tiled=True)
    expert_out = jnp.einsum("sxcf,xfd->sxcd", hidden_b, down_weight, preferred_element_type=f32)
    expert_out = expert_out.astype(bf16).reshape(received.shape)
    returned = lax.all_to_all(expert_out, "dp", split_axis=0, concat_axis=0, tiled=True)
    expert_rows = jnp.einsum(
        "er,ed->rd",
        placer,
        returned.reshape(experts * slot_count, model_width),
        preferred_element_type=f32,
    )
    block_out = (residual_stream + expert_rows).astype(bf16)
    block_out = block_out.reshape(seq_count, shard_len, model_width)
    up_full = jnp.einsum("sxcf,sxcd->xfd", dpre_b, parts, preferred_element_type=f32)
    down_full = jnp.einsum("sxcf,sxcd->xfd", hidden_b, arrived_p, preferred_element_type=f32)
    up_grad, down_grad = (
        lax.psum_scatter(grad.astype(bf16), "sp", scatter_dimension=1, tiled=True).astype(f32)
        for grad in (up_full, down_full)
    )
    dnormed2 = jnp.einsum(
        "er,ed->rd",
        placer,
        dnormed_back.reshape(experts * slot_count, model_width),
        preferred_element_type=f32,
    )
    dresid_norm, gain_two_grad, shift_two_grad = norm_backward(dnormed2, unit2, rstd2, norm2_gain)
    dresid = cot_b.astype(f32) + dresid_norm
    dattn_b = dresid.astype(bf16)
    dmixed_b = jnp.einsum("re,de->rd", dattn_b, out_weight, preferred_element_type=f32)
    dmixed_b = dmixed_b.astype(bf16).reshape(seq_count, shard_len, model_width)
    out_grad = jnp.einsum("rd,re->de", mixed_b, dattn_b, preferred_element_type=f32).astype(bf16)
    out_part = lax.psum_scatter(out_grad, "sp", scatter_dimension=1, tiled=True)
    grads = pl.pallas_call(
        functools.partial(attend_backward, sp_ways, head_dim),
        out_shape=[shape(seq_count, seq_len, width)] * 3
        + [shape(seq_count, shard_len, model_width)] * 3,
        in_specs=vmem(5),
        out_specs=vmem(6),
        scratch_shapes=[
            pltpu.VMEM((seq_count, seq_len, width), bf16),
            pltpu.VMEM((seq_len, width), f32),
            pltpu.VMEM((seq_len, width), f32),
            pltpu.VMEM((seq_len, width), f32),
            dma(seq_count, sp_ways),
            dma(seq_count, sp_ways),
            dma(3, seq_count, sp_ways),
            dma(3, seq_count, sp_ways),
        ],
        compiler_params=params(1),
    )(dmixed_b, query_h, key_h, value_h, log_total)
    head_grads, token_grads = grads[:3], grads[3:]
    weight_parts = [
        jnp.einsum("skd,ske->de", normed_all, grad, preferred_element_type=f32).astype(bf16)
        for grad in head_grads
    ]
    dnormed1 = sum(
        jnp.einsum(
            "re,de->rd",
            grad.reshape(row_count, model_width),
            weight,
            preferred_element_type=f32,
        )
        for grad, weight in zip(token_grads, (query_weight, key_weight, value_weight))
    )
    _, unit1, rstd1 = norm_forward(inputs, norm1_gain, norm1_shift)
    dinput_norm, gain_one_grad, shift_one_grad = norm_backward(dnormed1, unit1, rstd1, norm1_gain)
    tokens_grad = (dresid + dinput_norm).astype(bf16)
    tokens_grad = tokens_grad.reshape(seq_count, shard_len, model_width)
    counts = jnp.sum(one_hot, axis=0).astype(f32)
    counts = jnp.pad(counts, (0, model_width - experts))
    small = jnp.stack(
        [gain_one_grad, shift_one_grad, gain_two_grad, shift_two_grad, counts]
        + [jnp.zeros((model_width,), f32)] * 3
    )
    columns = dp_ways // 2
    piece_rows = 4 * model_width // dp_ways
    packed = jnp.concatenate(weight_parts + [out_part], axis=0)
    packed = packed.reshape(2, columns, piece_rows, width)
    gathered, small_sum = pl.pallas_call(
        functools.partial(reduce_everywhere, sp_ways, columns),
        out_shape=[
            shape(4 * model_width, model_width),
            shape(8, model_width, dtype=f32),
        ],
        in_specs=vmem(2),
        out_specs=[pl.BlockSpec(memory_space=pl.ANY), pl.BlockSpec(memory_space=pltpu.VMEM)],
        scratch_shapes=[
            pltpu.VMEM((columns, piece_rows, width), bf16),
            pltpu.VMEM((columns, piece_rows, width), bf16),
            pltpu.VMEM((columns, piece_rows, width), bf16),
            pltpu.VMEM((piece_rows, width), bf16),
            pltpu.VMEM((columns + sp_ways, 8, model_width), f32),
            pltpu.VMEM((2, 8, model_width), f32),
            pltpu.SemaphoreType.DMA,
            pltpu.SemaphoreType.DMA,
            dma(columns),
            dma(columns),
            dma(columns),
            dma(columns),
            dma(sp_ways),
            dma(sp_ways),
            dma(sp_ways),
            dma(sp_ways),
            dma(columns + sp_ways),
            dma(columns + sp_ways),
            pltpu.SemaphoreType.DMA,
        ],
        compiler_params=params(2),
    )(packed, small)
    query_grad, key_grad, value_grad, out_grad = (
        gathered[i * model_width : (i + 1) * model_width].astype(f32) for i in range(4)
    )
    load_now = small_sum[4, :experts] * experts / (row_count * dp_ways * sp_ways)
    load_next = 0.9 * load_mean + 0.1 * load_now
    return (
        block_out,
        tokens_grad,
        query_grad,
        key_grad,
        value_grad,
        out_grad,
        small_sum[0],
        small_sum[1],
        small_sum[2],
        small_sum[3],
        up_grad,
        down_grad,
        load_next,
    )


def solution(mesh):
    return jax.shard_map(
        local,
        mesh=mesh,
        in_specs=(
            P("dp", "sp", None),
            P("dp", "sp", None, None),
            P(),
            P(),
            P(),
            P(),
            P(),
            P(),
            P(),
            P(),
            P("dp", None, None),
            P("dp", None, None),
            P("dp", "sp", None),
            P(),
        ),
        out_specs=(
            P("dp", "sp", None),
            P("dp", "sp", None),
            P(),
            P(),
            P(),
            P(),
            P(),
            P(),
            P(),
            P(),
            P("dp", "sp", None),
            P("dp", "sp", None),
            P(),
        ),
        check_vma=False,
    )
```

```python
import functools

import jax
import jax.numpy as jnp
from jax import lax
from jax.experimental import pallas as pl
from jax.experimental.pallas import tpu as pltpu
from jax.sharding import PartitionSpec as P

HEADS = 16
MESH = pl.DeviceIdType.MESH
BLOCK = 256
LANES = 128
STEP = 512
ALONG_X = [(0, 1), (1, 0), (2, 3), (3, 2)]
ALONG_Y = [(0, 2), (2, 0), (1, 3), (3, 1)]
VMEM_BYTES = 60 * 2**20

NORM_EPSILON = 1e-05
GELU_ROOT = 0.7978845608028654
CUBIC_TERM = 0.044715

ROWS_BY_COLS = (((1,), (0,)), ((), ()))
ROWS_BY_ROWS = (((1,), (1,)), ((), ()))
COLS_BY_COLS = (((0,), (0,)), ((), ()))


def smooth(values):
    return (
        0.5
        * values
        * (1.0 + jnp.tanh(GELU_ROOT * (values + CUBIC_TERM * values * values * values)))
    )


def smooth_slope(values):
    inner = jnp.tanh(GELU_ROOT * (values + CUBIC_TERM * values * values * values))
    return 0.5 * (1.0 + inner) + 0.5 * values * (1.0 - inner * inner) * GELU_ROOT * (
        1.0 + 3.0 * CUBIC_TERM * values * values
    )


def norm_forward(values, gain, shift):
    center = jnp.mean(values, axis=-1, keepdims=True)
    offset = values - center
    rstd = lax.rsqrt(jnp.mean(offset * offset, axis=-1, keepdims=True) + NORM_EPSILON)
    unit = offset * rstd
    return (unit * gain + shift, unit, rstd)


def norm_backward(grad, unit, rstd, gain):
    scaled = grad * gain
    inner = (
        scaled
        - jnp.mean(scaled, axis=-1, keepdims=True)
        - unit * jnp.mean(scaled * unit, axis=-1, keepdims=True)
    )
    return (inner * rstd, jnp.sum(grad * unit, axis=0), jnp.sum(grad, axis=0))


def mxu(left, right, dims=ROWS_BY_COLS):
    return lax.dot_general(left, right, dims, preferred_element_type=jnp.float32)


def span(index, size):
    return pl.ds(pl.multiple_of(index * size, size), size)


def greet(peers):
    barrier = pltpu.get_barrier_semaphore()
    for peer in peers:
        pl.semaphore_signal(barrier, inc=1, device_id=peer, device_id_type=MESH)
    pl.semaphore_wait(barrier, len(peers))


def send(source, target, send_sem, recv_sem, peer):
    return pltpu.make_async_remote_copy(
        src_ref=source,
        dst_ref=target,
        send_sem=send_sem,
        recv_sem=recv_sem,
        device_id=peer,
        device_id_type=MESH,
    )


def exchange(others, source, target, send_sem, recv_sem):
    me = lax.axis_index("dp")
    return [
        send(
            source.at[flip(me, d)],
            target.at[me],
            send_sem.at[d],
            recv_sem.at[d],
            {"dp": flip(me, d)},
        )
        for d in range(1, others)
    ]


def flip(index, bits):
    bit = 1
    while bit <= bits:
        if bits & bit:
            index = index + bit - 2 * bit * lax.rem(index // bit, 2)
        bit *= 2
    return index


def attend_forward(
    ways,
    others,
    head_dim,
    cot_ref,
    x_ref,
    wq_ref,
    wk_ref,
    wv_ref,
    gain_ref,
    shift_ref,
    normed_ref,
    q_ref,
    k_ref,
    v_ref,
    log_ref,
    mixed_ref,
    arrived_ref,
    x_all,
    mixed_f,
    mixed_h,
    log_s,
    x_send,
    x_recv,
    m_send,
    m_recv,
    c_send,
    c_recv,
    local_sem,
):
    seqs, shard, _ = x_ref.shape
    seq_len, width = q_ref.shape[1:]
    heads = width // head_dim
    me = lax.axis_index("sp")
    peer = [lax.rem(me + d, ways) for d in range(ways)]
    origin = [lax.rem(me + ways - d, ways) for d in range(ways)]
    greet(
        [{"sp": peer[d]} for d in range(1, ways)]
        + [{"dp": flip(lax.axis_index("dp"), d)} for d in range(1, others)]
    )
    background = exchange(others, cot_ref, arrived_ref, c_send, c_recv)
    own = pltpu.make_async_copy(
        cot_ref.at[lax.axis_index("dp")], arrived_ref.at[lax.axis_index("dp")], local_sem
    )

    def x_copy(s, d):
        return send(
            x_ref.at[s],
            x_all.at[s, span(me, shard)],
            x_send.at[s, d],
            x_recv.at[s, d],
            {"sp": peer[d]},
        )

    def mixed_copy(s, d):
        return send(
            mixed_h.at[s, span(peer[d], shard)],
            mixed_ref.at[s, :, span(me, width)],
            m_send.at[s, d],
            m_recv.at[s, d],
            {"sp": peer[d]},
        )

    lane = lax.broadcasted_iota(jnp.int32, (1, width), 1) // head_dim
    log_lane = lax.broadcasted_iota(jnp.int32, (1, LANES), 1)
    visible = lax.broadcasted_iota(jnp.int32, (BLOCK, BLOCK), 1) <= lax.broadcasted_iota(
        jnp.int32, (BLOCK, BLOCK), 0
    )
    scale = head_dim ** (-0.5)

    def project(s, rows, values):
        normed, _, _ = norm_forward(values.astype(jnp.float32), gain_ref[...], shift_ref[...])
        normed = normed.astype(jnp.bfloat16)
        normed_ref[s, rows, :] = normed
        q_ref[s, rows, :] = mxu(normed, wq_ref[...]).astype(jnp.bfloat16)
        k_ref[s, rows, :] = mxu(normed, wk_ref[...]).astype(jnp.bfloat16)
        v_ref[s, rows, :] = mxu(normed, wv_ref[...]).astype(jnp.bfloat16)

    for d in range(1, ways):
        x_copy(0, d).start()
    own.start()
    for copy in background:
        copy.start()
    for s in range(seqs):
        project(s, span(me, shard), x_ref[s])
        for d in range(1, ways):
            x_copy(s, d).wait_recv()
            if d == ways - 1 and s + 1 < seqs:
                for later in range(1, ways):
                    x_copy(s + 1, later).start()
            rows = span(origin[d], shard)
            project(s, rows, x_all[s, rows, :])
        mixed_f[...] = jnp.zeros_like(mixed_f)
        log_s[...] = jnp.zeros_like(log_s)

        def one_head(h, carry):
            mine = (lane == h).astype(jnp.float32)
            for at in range(0, seq_len, BLOCK):
                rows = slice(at, at + BLOCK)
                query = (q_ref[s, rows, :].astype(jnp.float32) * (mine * scale)).astype(
                    jnp.bfloat16
                )
                near = mxu(query, k_ref[s, rows, :], ROWS_BY_ROWS)
                near = jnp.where(visible, near, -1e30)
                top = jnp.max(near, axis=1, keepdims=True)
                if at:
                    far = mxu(query, k_ref[s, :at, :], ROWS_BY_ROWS)
                    top = jnp.maximum(top, jnp.max(far, axis=1, keepdims=True))
                near = jnp.exp(near - top)
                total = jnp.sum(near, axis=1, keepdims=True)
                if at:
                    far = jnp.exp(far - top)
                    total += jnp.sum(far, axis=1, keepdims=True)
                inverse = 1.0 / total
                out = mxu((near * inverse).astype(jnp.bfloat16), v_ref[s, rows, :])
                if at:
                    out += mxu((far * inverse).astype(jnp.bfloat16), v_ref[s, :at, :])
                mixed_f[rows, :] += out * mine
                log_s[rows, :] = jnp.where(log_lane == h, top + jnp.log(total), log_s[rows, :])
            return carry

        lax.fori_loop(0, heads, one_head, 0)
        log_ref[s] = jnp.transpose(log_s[...])[: log_ref.shape[1], :]
        mixed_h[s] = mixed_f[...].astype(jnp.bfloat16)
        for d in range(1, ways):
            mixed_copy(s, d).start()
        mixed_ref[s, :, span(me, width)] = mixed_h[s, span(me, shard), :]
    for s in range(seqs):
        for d in range(1, ways):
            x_copy(s, d).wait_send()
            mixed_copy(s, d).wait()
    own.wait()
    for copy in background:
        copy.wait()


def attend_backward(
    ways,
    others,
    head_dim,
    result_ref,
    dmixed_ref,
    q_ref,
    k_ref,
    v_ref,
    log_ref,
    dq_ref,
    dk_ref,
    dv_ref,
    dq_tok,
    dk_tok,
    dv_tok,
    returned_ref,
    dmixed_h,
    dq_f,
    dk_f,
    dv_f,
    m_send,
    m_recv,
    g_send,
    g_recv,
    c_send,
    c_recv,
    local_sem,
):
    seqs, shard, _ = dmixed_ref.shape
    seq_len, width = q_ref.shape[1:]
    heads = width // head_dim
    me = lax.axis_index("sp")
    peer = [lax.rem(me + d, ways) for d in range(ways)]
    greet(
        [{"sp": peer[d]} for d in range(1, ways)]
        + [{"dp": flip(lax.axis_index("dp"), d)} for d in range(1, others)]
    )
    background = exchange(others, result_ref, returned_ref, c_send, c_recv)
    own = pltpu.make_async_copy(
        result_ref.at[lax.axis_index("dp")], returned_ref.at[lax.axis_index("dp")], local_sem
    )

    def dmixed_copy(s, d):
        return send(
            dmixed_ref.at[s, :, span(peer[d], width)],
            dmixed_h.at[s, span(me, shard)],
            m_send.at[s, d],
            m_recv.at[s, d],
            {"sp": peer[d]},
        )

    pairs = ((dq_ref, dq_tok), (dk_ref, dk_tok), (dv_ref, dv_tok))

    def grad_copy(i, s, d):
        source, target = pairs[i]
        return send(
            source.at[s, span(peer[d], shard)],
            target.at[s, :, span(me, width)],
            g_send.at[i, s, d],
            g_recv.at[i, s, d],
            {"sp": peer[d]},
        )

    for s in range(seqs):
        for d in range(1, ways):
            dmixed_copy(s, d).start()
    own.start()
    for copy in background:
        copy.start()
    lane = lax.broadcasted_iota(jnp.int32, (1, width), 1) // head_dim
    visible = lax.broadcasted_iota(jnp.int32, (BLOCK, BLOCK), 0) <= lax.broadcasted_iota(
        jnp.int32, (BLOCK, BLOCK), 1
    )
    scale = head_dim ** (-0.5)
    for s in range(seqs):
        dmixed_h[s, span(me, shard), :] = dmixed_ref[s, :, span(me, width)]
        for d in range(1, ways):
            dmixed_copy(s, d).wait_recv()
        dq_f[...] = jnp.zeros_like(dq_f)
        dk_f[...] = jnp.zeros_like(dk_f)
        dv_f[...] = jnp.zeros_like(dv_f)

        def one_head(h, carry):
            mine = (lane == h).astype(jnp.float32)
            for at in range(0, seq_len, BLOCK):
                rows = slice(at, at + BLOCK)
                query = (q_ref[s, rows, :].astype(jnp.float32) * (mine * scale)).astype(
                    jnp.bfloat16
                )
                dout = (dmixed_h[s, rows, :].astype(jnp.float32) * mine).astype(jnp.bfloat16)
                log_row = log_ref[s, pl.ds(h, 1), rows]
                parts = [(rows, True)] + ([(slice(0, at), False)] if at else [])
                kept = []
                delta = jnp.zeros((1, BLOCK), jnp.float32)
                for keys, diagonal in parts:
                    prob = jnp.exp(mxu(k_ref[s, keys, :], query, ROWS_BY_ROWS) - log_row)
                    if diagonal:
                        prob = jnp.where(visible, prob, 0.0)
                    dprob = mxu(v_ref[s, keys, :], dout, ROWS_BY_ROWS)
                    delta += jnp.sum(prob * dprob, axis=0, keepdims=True)
                    kept.append((keys, prob, dprob))
                dquery = jnp.zeros((BLOCK, width), jnp.float32)
                for keys, prob, dprob in kept:
                    dv_f[keys, :] += mxu(prob.astype(jnp.bfloat16), dout)
                    dlogit = (prob * (dprob - delta)).astype(jnp.bfloat16)
                    dk_f[keys, :] += mxu(dlogit, query)
                    dquery += mxu(dlogit, k_ref[s, keys, :], COLS_BY_COLS)
                dq_f[rows, :] += dquery * (mine * scale)
            return carry

        lax.fori_loop(0, heads, one_head, 0)
        for i, total in enumerate((dq_f, dk_f, dv_f)):
            source, target = pairs[i]
            source[s] = total[...].astype(jnp.bfloat16)
            for d in range(1, ways):
                grad_copy(i, s, d).start()
            target[s, :, span(me, width)] = source[s, span(me, shard), :]
    for s in range(seqs):
        for d in range(1, ways):
            dmixed_copy(s, d).wait_send()
            for i in range(3):
                grad_copy(i, s, d).wait()
    own.wait()
    for copy in background:
        copy.wait()


def run_experts(
    others,
    ways,
    outgoing_ref,
    arrived_ref,
    up_ref,
    down_ref,
    back_ref,
    result_ref,
    up_part,
    down_part,
    *rest,
):
    if ways == 4:
        land_x, land_y, *rest = rest
    (
        received,
        up_v,
        down_v,
        hidden,
        slope_v,
        total,
        dnormed,
        w_sem,
        o_sem,
        a_send,
        a_recv,
        b_send,
        b_recv,
        *rest,
    ) = rest
    slots, width = received.shape[1:]
    ff = up_v.shape[0]
    me = lax.axis_index("dp")
    sp = lax.axis_index("sp")
    chip = me // 2
    load_down = pltpu.make_async_copy(down_ref, down_v, w_sem.at[0])
    load_up = pltpu.make_async_copy(up_ref, up_v, w_sem.at[1])
    load_down.start()
    load_up.start()
    peers = [{"dp": flip(me, d)} for d in range(1, others)]
    if ways == 4:
        peers += [{"sp": flip(sp, 1)}, {"sp": flip(sp, 2)}]
    greet(peers)
    inward = exchange(others, outgoing_ref, received, a_send, a_recv)
    outward = exchange(others, dnormed, back_ref, b_send, b_recv)
    for copy in reversed(inward):
        copy.start()
    received[me] = outgoing_ref[me]

    rows = others * slots
    load_down.wait()

    def cot_step(i, carry):
        at = span(i, STEP)
        cot = arrived_ref[...].reshape(rows, width)
        slope_v[:, at] = mxu(cot, down_v[at, :], ROWS_BY_ROWS).astype(jnp.bfloat16)
        return carry

    lax.fori_loop(0, ff // STEP, cot_step, 0)
    load_up.wait()
    for group in range(others // 2):
        near = flip(chip, group)
        for d in (2 * group, 2 * group + 1):
            if d:
                inward[d - 1].wait_recv()
        slab = span(near, 2 * slots)
        total[...] = jnp.zeros_like(total)

        def up_step(i, carry):
            at = span(i, STEP)
            tokens = received[pl.ds(2 * near, 2)].reshape(2 * slots, width)
            pre = mxu(tokens, up_v[at, :], ROWS_BY_ROWS)
            square = pre * pre
            inner = jnp.tanh(GELU_ROOT * pre * (1.0 + CUBIC_TERM * square))
            half = 0.5 * (1.0 + inner)
            hidden[slab, at] = (pre * half).astype(jnp.bfloat16)
            slope = half + (0.5 * GELU_ROOT) * pre * (1.0 - inner * inner) * (
                1.0 + (3.0 * CUBIC_TERM) * square
            )
            dpre = (slope_v[slab, at].astype(jnp.float32) * slope).astype(jnp.bfloat16)
            slope_v[slab, at] = dpre
            total[...] += mxu(dpre, up_v[at, :])
            return carry

        lax.fori_loop(0, ff // STEP, up_step, 0)
        dnormed[pl.ds(2 * near, 2)] = total[...].reshape(2, slots, width).astype(jnp.bfloat16)
        for d in (2 * group, 2 * group + 1):
            if d:
                outward[d - 1].start()
            else:
                back_ref[me] = dnormed[me]

    quarter = ff // 4

    def grad_shard(target, left, right_ref, shard):
        def grad_step(i, carry):
            at = pl.ds(pl.multiple_of(shard * quarter + i * STEP, STEP), STEP)
            right = right_ref[...].reshape(rows, width)
            target[at, :] = mxu(left[:, at], right, COLS_BY_COLS).astype(jnp.bfloat16)
            return carry

        lax.fori_loop(0, quarter // STEP, grad_step, 0)

    side = []
    if ways == 4:
        x_send, x_recv, y_send, y_recv = rest
        x_at, y_at = lax.rem(sp, 2), sp // 2
        half = width // 2

        def to_x(shard, slot, i):
            return send(
                up_v.at[span(shard, quarter), 0:half],
                land_x.at[slot],
                x_send.at[i],
                x_recv.at[i],
                {"sp": flip(sp, 1)},
            )

        def to_y(shard, slot, i):
            return send(
                up_v.at[span(shard, quarter), half:width],
                land_y.at[slot],
                y_send.at[i],
                y_recv.at[i],
                {"sp": flip(sp, 2)},
            )

        side = [
            to_x(flip(sp, 3), 1 - y_at, 0),
            to_y(flip(sp, 3), 1 - x_at, 0),
            to_x(flip(sp, 1), y_at, 1),
            to_y(flip(sp, 2), x_at, 1),
        ]
        grad_shard(up_v, hidden, arrived_ref, flip(sp, 3))
        side[0].start()
        side[1].start()
        grad_shard(up_v, hidden, arrived_ref, flip(sp, 1))
        side[2].start()
        grad_shard(up_v, hidden, arrived_ref, flip(sp, 2))
        side[3].start()
        grad_shard(up_v, hidden, arrived_ref, sp)
    else:
        for shard in range(4):
            grad_shard(up_v, hidden, arrived_ref, shard)
    store_down = pltpu.make_async_copy(up_v, down_part, o_sem.at[0])
    store_down.start()

    def out_step(i, carry):
        slab = span(i, 2 * slots)
        result_ref[pl.ds(2 * i, 2)] = (
            mxu(hidden[slab, :], down_v[...]).reshape(2, slots, width).astype(jnp.bfloat16)
        )
        return carry

    lax.fori_loop(0, others // 2, out_step, 0)
    for shard in range(4):
        grad_shard(down_v, slope_v, received, shard)
    store_up = pltpu.make_async_copy(down_v, up_part, o_sem.at[1])
    store_up.start()
    for copy in inward:
        copy.wait_send()
    for copy in outward + side:
        copy.wait()
    store_down.wait()
    store_up.wait()


def reduce_everywhere(
    ways,
    columns,
    part_ref,
    small_ref,
    out_ref,
    small_out,
    core_land,
    core_sum,
    column_land,
    piece,
    small_land,
    small_sum,
    core_send,
    core_recv,
    column_send,
    column_recv,
    spread_send,
    spread_recv,
    ring_send,
    ring_recv,
    cross_send,
    cross_recv,
    small_send,
    small_recv,
    local_sem,
):
    rows = part_ref.shape[2]
    width = part_ref.shape[3]
    me = lax.axis_index("sp")
    dp = lax.axis_index("dp")
    core = lax.rem(dp, 2)
    column = dp // 2
    twin = {"dp": dp + 1 - 2 * core}
    column_peer = [lax.rem(column + d, columns) for d in range(columns)]
    sp_peer = [lax.rem(me + d, ways) for d in range(ways)]
    sp_origin = [lax.rem(me + ways - d, ways) for d in range(ways)]
    column_id = [{"dp": 2 * column_peer[d] + core} for d in range(columns)]
    sp_id = [{"sp": sp_peer[d]} for d in range(ways)]
    greet([twin] + column_id[1:] + sp_id[1:])

    first = send(part_ref.at[1 - core], core_land, core_send, core_recv, twin)
    first.start()
    small_first = send(small_ref, small_land.at[0], small_send.at[0], small_recv.at[0], twin)
    small_first.start()
    small_first.wait()
    small_sum[0] = small_ref[...] + small_land[0]

    def small_column(d):
        return send(
            small_sum.at[0],
            small_land.at[d],
            small_send.at[d],
            small_recv.at[d],
            column_id[d],
        )

    def small_ring(d):
        at = columns + d
        return send(
            small_sum.at[1],
            small_land.at[at],
            small_send.at[at],
            small_recv.at[at],
            sp_id[d],
        )

    for d in range(1, columns):
        small_column(d).start()
    first.wait()
    core_sum[...] = (
        part_ref[core].astype(jnp.float32) + core_land[...].astype(jnp.float32)
    ).astype(jnp.bfloat16)

    def column_copy(d):
        return send(
            core_sum.at[column_peer[d]],
            column_land.at[d],
            column_send.at[d],
            column_recv.at[d],
            column_id[d],
        )

    for d in range(1, columns):
        column_copy(d).start()
    for d in range(1, columns):
        small_column(d).wait()
    total = small_sum[0]
    for d in range(1, columns):
        total += small_land[d]
    small_sum[1] = total
    for d in range(1, ways):
        small_ring(d).start()
    total = core_sum[column].astype(jnp.float32)
    for d in range(1, columns):
        column_copy(d).wait()
        total += column_land[d].astype(jnp.float32)
    piece[...] = total.astype(jnp.bfloat16)

    def block(at_core, at_column, at_sp, count=1):
        first_row = pl.multiple_of((at_core * columns + at_column) * rows, rows)
        return out_ref.at[pl.ds(first_row, count * rows), span(at_sp, width)]

    def spread_copy(d):
        return send(
            piece,
            block(core, column, me),
            spread_send.at[d],
            spread_recv.at[d],
            column_id[d],
        )

    for d in range(1, columns):
        spread_copy(d).start()
    own = pltpu.make_async_copy(piece, block(core, column, me), local_sem)
    own.start()
    for d in range(1, ways):
        small_ring(d).wait()
    total = small_sum[1]
    for d in range(1, ways):
        total += small_land[columns + d]
    small_out[...] = total
    own.wait()
    for d in range(1, columns):
        spread_copy(d).wait()

    def ring_copy(d):
        half = block(core, 0, me, columns)
        return send(half, half, ring_send.at[d], ring_recv.at[d], sp_id[d])

    def cross_copy(d):
        half = block(core, 0, sp_origin[d], columns)
        return send(half, half, cross_send.at[d], cross_recv.at[d], twin)

    for d in range(1, ways):
        ring_copy(d).start()
    cross_copy(0).start()
    for d in range(1, ways):
        ring_copy(d).wait_recv()
        cross_copy(d).start()
    for d in range(1, ways):
        ring_copy(d).wait_send()
    for d in range(ways):
        cross_copy(d).wait()


def scatter_halves(x_half, y_half, x_land, y_land, sp_at):
    x_at, y_at = sp_at % 2, sp_at // 2
    pick = lax.dynamic_index_in_dim
    f32 = jnp.float32

    def both(half, land, at, where):
        return pick(half, where, 0, False).astype(f32) + pick(land, at, 0, False).astype(f32)

    x_out = both(x_half, x_land, 1 - y_at, sp_at + 2 - 4 * y_at).astype(jnp.bfloat16)
    y_out = both(y_half, y_land, 1 - x_at, sp_at + 1 - 2 * x_at).astype(jnp.bfloat16)
    x_in = lax.ppermute(x_out, "sp", ALONG_Y)
    y_in = lax.ppermute(y_out, "sp", ALONG_X)
    return jnp.concatenate(
        [
            both(x_half, x_land, y_at, sp_at) + x_in.astype(f32),
            both(y_half, y_land, x_at, sp_at) + y_in.astype(f32),
        ],
        axis=1,
    )


def first_stage(x_half, y_half, sp_at):
    x_at, y_at = sp_at % 2, sp_at // 2
    shape = (2, 2) + x_half.shape[1:]
    x_out = lax.dynamic_index_in_dim(x_half.reshape(shape), 1 - x_at, 1, False)
    y_out = lax.dynamic_index_in_dim(y_half.reshape(shape), 1 - y_at, 0, False)
    return lax.ppermute(x_out, "sp", ALONG_X), lax.ppermute(y_out, "sp", ALONG_Y)


def vmem(count):
    return [pl.BlockSpec(memory_space=pltpu.VMEM)] * count


def params(collective_id):
    return pltpu.CompilerParams(
        collective_id=collective_id, has_side_effects=True, vmem_limit_bytes=VMEM_BYTES
    )


def dma(*shape):
    return pltpu.SemaphoreType.DMA(shape)


def local(
    tokens_in,
    expert_ids,
    query_weight,
    key_weight,
    value_weight,
    out_weight,
    norm1_gain,
    norm1_shift,
    norm2_gain,
    norm2_shift,
    up_weight,
    down_weight,
    out_cotangent,
    load_mean,
):
    seq_count, shard_len, model_width = tokens_in.shape
    row_count = seq_count * shard_len
    head_dim = model_width // HEADS
    dp_ways = lax.axis_size("dp")
    sp_ways = lax.axis_size("sp")
    sp_at = lax.axis_index("sp")
    seq_len = shard_len * sp_ways
    experts = load_mean.shape[0]
    slot_count = 2 * row_count // experts
    local_experts = up_weight.shape[0]
    ff_width = up_weight.shape[1]
    width = model_width // sp_ways
    bf16 = jnp.bfloat16
    f32 = jnp.float32

    def shape(*sizes, dtype=bf16):
        return jax.ShapeDtypeStruct(sizes, dtype)

    routes = expert_ids.reshape(row_count)
    one_hot = (routes[:, None] == jnp.arange(experts, dtype=jnp.int32)[None, :]).astype(jnp.int32)
    running = jnp.cumsum(one_hot, axis=0) - 1
    slot_of = jnp.sum(running * one_hot, axis=1)
    target = routes * slot_count + slot_of
    placer = (jnp.arange(experts * slot_count, dtype=jnp.int32)[:, None] == target[None, :]).astype(
        bf16
    )
    cot_b = out_cotangent.reshape(row_count, model_width)
    cot_send = jnp.dot(placer, cot_b, preferred_element_type=f32).astype(bf16)
    cot_send = cot_send.reshape(experts, slot_count, model_width)

    def columns_of(weight):
        return lax.dynamic_slice_in_dim(weight, sp_at * width, width, axis=1)

    routed = shape(experts, slot_count, model_width)
    hbm = [pl.BlockSpec(memory_space=pl.ANY)]
    normed_all, query_h, key_h, value_h, log_total, mixed_b, arrived = pl.pallas_call(
        functools.partial(attend_forward, sp_ways, dp_ways, head_dim),
        out_shape=[
            shape(seq_count, seq_len, model_width),
            shape(seq_count, seq_len, width),
            shape(seq_count, seq_len, width),
            shape(seq_count, seq_len, width),
            shape(seq_count, 8, seq_len, dtype=f32),
            shape(seq_count, shard_len, model_width),
            routed,
        ],
        in_specs=hbm + vmem(6),
        out_specs=vmem(6) + hbm,
        scratch_shapes=[
            pltpu.VMEM((seq_count, seq_len, model_width), bf16),
            pltpu.VMEM((seq_len, width), f32),
            pltpu.VMEM((seq_count, seq_len, width), bf16),
            pltpu.VMEM((seq_len, LANES), f32),
            dma(seq_count, sp_ways),
            dma(seq_count, sp_ways),
            dma(seq_count, sp_ways),
            dma(seq_count, sp_ways),
            dma(dp_ways),
            dma(dp_ways),
            pltpu.SemaphoreType.DMA,
        ],
        compiler_params=params(0),
    )(
        cot_send,
        tokens_in,
        columns_of(query_weight),
        columns_of(key_weight),
        columns_of(value_weight),
        norm1_gain.reshape(1, model_width),
        norm1_shift.reshape(1, model_width),
    )
    mixed_b = mixed_b.reshape(row_count, model_width)
    inputs = tokens_in.reshape(row_count, model_width).astype(f32)
    attn_out = jnp.dot(mixed_b, out_weight, preferred_element_type=f32)
    residual_stream = inputs + attn_out
    normed2, unit2, rstd2 = norm_forward(residual_stream, norm2_gain, norm2_shift)
    normed2_b = normed2.astype(bf16)
    outgoing = jnp.dot(placer, normed2_b, preferred_element_type=f32).astype(bf16)
    outgoing = outgoing.reshape(experts, slot_count, model_width)
    landing = [shape(2, ff_width // 4, model_width // 2)] * 2 if sp_ways == 4 else []
    side_sems = [dma(2)] * 4 if sp_ways == 4 else []
    dnormed_back, expert_out, up_part, down_part, *landed = pl.pallas_call(
        functools.partial(run_experts, dp_ways, sp_ways),
        out_shape=[routed, routed, shape(ff_width, model_width), shape(ff_width, model_width)]
        + landing,
        in_specs=vmem(2) + hbm * 2,
        out_specs=vmem(2) + hbm * (2 + len(landing)),
        scratch_shapes=[
            pltpu.VMEM((experts, slot_count, model_width), bf16),
            pltpu.VMEM((ff_width, model_width), bf16),
            pltpu.VMEM((ff_width, model_width), bf16),
            pltpu.VMEM((experts * slot_count, ff_width), bf16),
            pltpu.VMEM((experts * slot_count, ff_width), bf16),
            pltpu.VMEM((2 * slot_count, model_width), f32),
            pltpu.VMEM((experts, slot_count, model_width), bf16),
            dma(2),
            dma(2),
            dma(dp_ways),
            dma(dp_ways),
            dma(dp_ways),
            dma(dp_ways),
        ]
        + side_sems,
        compiler_params=params(3),
    )(outgoing, arrived, up_weight[0], down_weight[0])
    if sp_ways == 4:

        def halves(part):
            part = part.reshape(4, ff_width // 4, model_width)
            return part[:, :, : model_width // 2], part[:, :, model_width // 2 :]

        down_grad = scatter_halves(*halves(down_part), *landed, sp_at)[None]
        landed = first_stage(*halves(up_part), sp_at)
        up_grad = scatter_halves(*halves(up_part), *landed, sp_at)[None]
    else:
        up_grad, down_grad = (
            lax.psum_scatter(part, "sp", scatter_dimension=0, tiled=True).astype(f32)[None]
            for part in (up_part, down_part)
        )
    dnormed2 = jnp.einsum(
        "er,ed->rd",
        placer,
        dnormed_back.reshape(experts * slot_count, model_width),
        preferred_element_type=f32,
    )
    dresid_norm, gain_two_grad, shift_two_grad = norm_backward(dnormed2, unit2, rstd2, norm2_gain)
    dresid = cot_b.astype(f32) + dresid_norm
    dattn_b = dresid.astype(bf16)
    dmixed_b = jnp.einsum("re,de->rd", dattn_b, out_weight, preferred_element_type=f32)
    dmixed_b = dmixed_b.astype(bf16).reshape(seq_count, shard_len, model_width)
    out_grad = jnp.einsum("rd,re->de", mixed_b, dattn_b, preferred_element_type=f32).astype(bf16)
    out_part = lax.psum_scatter(out_grad, "sp", scatter_dimension=1, tiled=True)
    grads = pl.pallas_call(
        functools.partial(attend_backward, sp_ways, dp_ways, head_dim),
        out_shape=[shape(seq_count, seq_len, width)] * 3
        + [shape(seq_count, shard_len, model_width)] * 3
        + [routed],
        in_specs=hbm + vmem(5),
        out_specs=vmem(6) + hbm,
        scratch_shapes=[
            pltpu.VMEM((seq_count, seq_len, width), bf16),
            pltpu.VMEM((seq_len, width), f32),
            pltpu.VMEM((seq_len, width), f32),
            pltpu.VMEM((seq_len, width), f32),
            dma(seq_count, sp_ways),
            dma(seq_count, sp_ways),
            dma(3, seq_count, sp_ways),
            dma(3, seq_count, sp_ways),
            dma(dp_ways),
            dma(dp_ways),
            pltpu.SemaphoreType.DMA,
        ],
        compiler_params=params(1),
    )(expert_out, dmixed_b, query_h, key_h, value_h, log_total)
    head_grads, token_grads, returned = grads[:3], grads[3:6], grads[6]
    expert_rows = jnp.einsum(
        "er,ed->rd",
        placer,
        returned.reshape(experts * slot_count, model_width),
        preferred_element_type=f32,
    )
    block_out = (residual_stream + expert_rows).astype(bf16)
    block_out = block_out.reshape(seq_count, shard_len, model_width)
    weight_parts = [
        jnp.einsum("skd,ske->de", normed_all, grad, preferred_element_type=f32).astype(bf16)
        for grad in head_grads
    ]
    dnormed1 = sum(
        jnp.einsum(
            "re,de->rd",
            grad.reshape(row_count, model_width),
            weight,
            preferred_element_type=f32,
        )
        for grad, weight in zip(token_grads, (query_weight, key_weight, value_weight))
    )
    _, unit1, rstd1 = norm_forward(inputs, norm1_gain, norm1_shift)
    dinput_norm, gain_one_grad, shift_one_grad = norm_backward(dnormed1, unit1, rstd1, norm1_gain)
    tokens_grad = (dresid + dinput_norm).astype(bf16)
    tokens_grad = tokens_grad.reshape(seq_count, shard_len, model_width)
    counts = jnp.sum(one_hot, axis=0).astype(f32)
    counts = jnp.pad(counts, (0, model_width - experts))
    small = jnp.stack(
        [gain_one_grad, shift_one_grad, gain_two_grad, shift_two_grad, counts]
        + [jnp.zeros((model_width,), f32)] * 3
    )
    columns = dp_ways // 2
    piece_rows = 4 * model_width // dp_ways
    packed = jnp.concatenate(weight_parts + [out_part], axis=0)
    packed = packed.reshape(2, columns, piece_rows, width)
    gathered, small_sum = pl.pallas_call(
        functools.partial(reduce_everywhere, sp_ways, columns),
        out_shape=[
            shape(4 * model_width, model_width),
            shape(8, model_width, dtype=f32),
        ],
        in_specs=vmem(2),
        out_specs=[pl.BlockSpec(memory_space=pl.ANY), pl.BlockSpec(memory_space=pltpu.VMEM)],
        scratch_shapes=[
            pltpu.VMEM((columns, piece_rows, width), bf16),
            pltpu.VMEM((columns, piece_rows, width), bf16),
            pltpu.VMEM((columns, piece_rows, width), bf16),
            pltpu.VMEM((piece_rows, width), bf16),
            pltpu.VMEM((columns + sp_ways, 8, model_width), f32),
            pltpu.VMEM((2, 8, model_width), f32),
            pltpu.SemaphoreType.DMA,
            pltpu.SemaphoreType.DMA,
            dma(columns),
            dma(columns),
            dma(columns),
            dma(columns),
            dma(sp_ways),
            dma(sp_ways),
            dma(sp_ways),
            dma(sp_ways),
            dma(columns + sp_ways),
            dma(columns + sp_ways),
            pltpu.SemaphoreType.DMA,
        ],
        compiler_params=params(2),
    )(packed, small)
    query_grad, key_grad, value_grad, out_grad = (
        gathered[i * model_width : (i + 1) * model_width].astype(f32) for i in range(4)
    )
    load_now = small_sum[4, :experts] * experts / (row_count * dp_ways * sp_ways)
    load_next = 0.9 * load_mean + 0.1 * load_now
    return (
        block_out,
        tokens_grad,
        query_grad,
        key_grad,
        value_grad,
        out_grad,
        small_sum[0],
        small_sum[1],
        small_sum[2],
        small_sum[3],
        up_grad,
        down_grad,
        load_next,
    )


def solution(mesh):
    return jax.shard_map(
        local,
        mesh=mesh,
        in_specs=(
            P("dp", "sp", None),
            P("dp", "sp", None, None),
            P(),
            P(),
            P(),
            P(),
            P(),
            P(),
            P(),
            P(),
            P("dp", None, None),
            P("dp", None, None),
            P("dp", "sp", None),
            P(),
        ),
        out_specs=(
            P("dp", "sp", None),
            P("dp", "sp", None),
            P(),
            P(),
            P(),
            P(),
            P(),
            P(),
            P(),
            P(),
            P("dp", "sp", None),
            P("dp", "sp", None),
            P(),
        ),
        check_vma=False,
    )
```

```python
import functools

import jax
import jax.numpy as jnp
from jax import lax
from jax.experimental import pallas as pl
from jax.experimental.pallas import tpu as pltpu
from jax.sharding import PartitionSpec as P

HEADS = 16
MESH = pl.DeviceIdType.MESH
BLOCK = 256
LANES = 128
STEP = 512
VMEM_BYTES = 60 * 2**20

NORM_EPSILON = 1e-05
GELU_ROOT = 0.7978845608028654
CUBIC_TERM = 0.044715

ROWS_BY_COLS = (((1,), (0,)), ((), ()))
ROWS_BY_ROWS = (((1,), (1,)), ((), ()))
COLS_BY_COLS = (((0,), (0,)), ((), ()))


def smooth(values):
    return (
        0.5
        * values
        * (1.0 + jnp.tanh(GELU_ROOT * (values + CUBIC_TERM * values * values * values)))
    )


def smooth_slope(values):
    inner = jnp.tanh(GELU_ROOT * (values + CUBIC_TERM * values * values * values))
    return 0.5 * (1.0 + inner) + 0.5 * values * (1.0 - inner * inner) * GELU_ROOT * (
        1.0 + 3.0 * CUBIC_TERM * values * values
    )


def norm_forward(values, gain, shift):
    center = jnp.mean(values, axis=-1, keepdims=True)
    offset = values - center
    rstd = lax.rsqrt(jnp.mean(offset * offset, axis=-1, keepdims=True) + NORM_EPSILON)
    unit = offset * rstd
    return (unit * gain + shift, unit, rstd)


def norm_backward(grad, unit, rstd, gain):
    scaled = grad * gain
    inner = (
        scaled
        - jnp.mean(scaled, axis=-1, keepdims=True)
        - unit * jnp.mean(scaled * unit, axis=-1, keepdims=True)
    )
    return (inner * rstd, jnp.sum(grad * unit, axis=0), jnp.sum(grad, axis=0))


def mxu(left, right, dims=ROWS_BY_COLS):
    return lax.dot_general(left, right, dims, preferred_element_type=jnp.float32)


def span(index, size):
    return pl.ds(pl.multiple_of(index * size, size), size)


def greet(peers):
    barrier = pltpu.get_barrier_semaphore()
    for peer in peers:
        pl.semaphore_signal(barrier, inc=1, device_id=peer, device_id_type=MESH)
    pl.semaphore_wait(barrier, len(peers))


def send(source, target, send_sem, recv_sem, peer):
    return pltpu.make_async_remote_copy(
        src_ref=source,
        dst_ref=target,
        send_sem=send_sem,
        recv_sem=recv_sem,
        device_id=peer,
        device_id_type=MESH,
    )


def exchange(others, source, target, send_sem, recv_sem):
    me = lax.axis_index("dp")
    return [
        send(
            source.at[flip(me, d)],
            target.at[me],
            send_sem.at[d],
            recv_sem.at[d],
            {"dp": flip(me, d)},
        )
        for d in range(1, others)
    ]


def flip(index, bits):
    bit = 1
    while bit <= bits:
        if bits & bit:
            index = index + bit - 2 * bit * lax.rem(index // bit, 2)
        bit *= 2
    return index


def attend_forward(
    ways,
    others,
    head_dim,
    cot_ref,
    x_ref,
    wq_ref,
    wk_ref,
    wv_ref,
    gain_ref,
    shift_ref,
    normed_ref,
    q_ref,
    k_ref,
    v_ref,
    log_ref,
    mixed_ref,
    arrived_ref,
    x_all,
    mixed_f,
    mixed_h,
    log_s,
    x_send,
    x_recv,
    m_send,
    m_recv,
    c_send,
    c_recv,
    local_sem,
):
    seqs, shard, _ = x_ref.shape
    seq_len, width = q_ref.shape[1:]
    heads = width // head_dim
    me = lax.axis_index("sp")
    peer = [lax.rem(me + d, ways) for d in range(ways)]
    origin = [lax.rem(me + ways - d, ways) for d in range(ways)]
    greet(
        [{"sp": peer[d]} for d in range(1, ways)]
        + [{"dp": flip(lax.axis_index("dp"), d)} for d in range(1, others)]
    )
    background = exchange(others, cot_ref, arrived_ref, c_send, c_recv)
    own = pltpu.make_async_copy(
        cot_ref.at[lax.axis_index("dp")], arrived_ref.at[lax.axis_index("dp")], local_sem
    )

    def x_copy(s, d):
        return send(
            x_ref.at[s],
            x_all.at[s, span(me, shard)],
            x_send.at[s, d],
            x_recv.at[s, d],
            {"sp": peer[d]},
        )

    def mixed_copy(s, d):
        return send(
            mixed_h.at[s, span(peer[d], shard)],
            mixed_ref.at[s, :, span(me, width)],
            m_send.at[s, d],
            m_recv.at[s, d],
            {"sp": peer[d]},
        )

    lane = lax.broadcasted_iota(jnp.int32, (1, width), 1) // head_dim
    log_lane = lax.broadcasted_iota(jnp.int32, (1, LANES), 1)
    visible = lax.broadcasted_iota(jnp.int32, (BLOCK, BLOCK), 1) <= lax.broadcasted_iota(
        jnp.int32, (BLOCK, BLOCK), 0
    )
    scale = head_dim ** (-0.5)

    def project(s, rows, values):
        normed, _, _ = norm_forward(values.astype(jnp.float32), gain_ref[...], shift_ref[...])
        normed = normed.astype(jnp.bfloat16)
        normed_ref[s, rows, :] = normed
        q_ref[s, rows, :] = mxu(normed, wq_ref[...]).astype(jnp.bfloat16)
        k_ref[s, rows, :] = mxu(normed, wk_ref[...]).astype(jnp.bfloat16)
        v_ref[s, rows, :] = mxu(normed, wv_ref[...]).astype(jnp.bfloat16)

    for d in range(1, ways):
        x_copy(0, d).start()
    own.start()
    for copy in background:
        copy.start()
    for s in range(seqs):
        project(s, span(me, shard), x_ref[s])
        for d in range(1, ways):
            x_copy(s, d).wait_recv()
            if d == ways - 1 and s + 1 < seqs:
                for later in range(1, ways):
                    x_copy(s + 1, later).start()
            rows = span(origin[d], shard)
            project(s, rows, x_all[s, rows, :])
        mixed_f[...] = jnp.zeros_like(mixed_f)
        log_s[...] = jnp.zeros_like(log_s)

        def one_head(h, carry):
            mine = (lane == h).astype(jnp.float32)
            for at in range(0, seq_len, BLOCK):
                rows = slice(at, at + BLOCK)
                query = (q_ref[s, rows, :].astype(jnp.float32) * (mine * scale)).astype(
                    jnp.bfloat16
                )
                near = mxu(query, k_ref[s, rows, :], ROWS_BY_ROWS)
                near = jnp.where(visible, near, -1e30)
                top = jnp.max(near, axis=1, keepdims=True)
                if at:
                    far = mxu(query, k_ref[s, :at, :], ROWS_BY_ROWS)
                    top = jnp.maximum(top, jnp.max(far, axis=1, keepdims=True))
                near = jnp.exp(near - top)
                total = jnp.sum(near, axis=1, keepdims=True)
                if at:
                    far = jnp.exp(far - top)
                    total += jnp.sum(far, axis=1, keepdims=True)
                inverse = 1.0 / total
                out = mxu((near * inverse).astype(jnp.bfloat16), v_ref[s, rows, :])
                if at:
                    out += mxu((far * inverse).astype(jnp.bfloat16), v_ref[s, :at, :])
                mixed_f[rows, :] += out * mine
                log_s[rows, :] = jnp.where(log_lane == h, top + jnp.log(total), log_s[rows, :])
            return carry

        lax.fori_loop(0, heads, one_head, 0)
        log_ref[s] = jnp.transpose(log_s[...])[: log_ref.shape[1], :]
        mixed_h[s] = mixed_f[...].astype(jnp.bfloat16)
        for d in range(1, ways):
            mixed_copy(s, d).start()
        mixed_ref[s, :, span(me, width)] = mixed_h[s, span(me, shard), :]
    for s in range(seqs):
        for d in range(1, ways):
            x_copy(s, d).wait_send()
            mixed_copy(s, d).wait()
    own.wait()
    for copy in background:
        copy.wait()


def attend_backward(
    ways,
    others,
    head_dim,
    result_ref,
    up_part,
    down_part,
    dmixed_ref,
    q_ref,
    k_ref,
    v_ref,
    log_ref,
    dq_ref,
    dk_ref,
    dv_ref,
    dq_tok,
    dk_tok,
    dv_tok,
    returned_ref,
    up_land,
    down_land,
    dmixed_h,
    dq_f,
    dk_f,
    dv_f,
    m_send,
    m_recv,
    g_send,
    g_recv,
    c_send,
    c_recv,
    s_send,
    s_recv,
    local_sem,
):
    seqs, shard, _ = dmixed_ref.shape
    seq_len, width = q_ref.shape[1:]
    heads = width // head_dim
    me = lax.axis_index("sp")
    peer = [lax.rem(me + d, ways) for d in range(ways)]
    greet(
        [{"sp": peer[d]} for d in range(1, ways)]
        + [{"dp": flip(lax.axis_index("dp"), d)} for d in range(1, others)]
    )
    background = exchange(others, result_ref, returned_ref, c_send, c_recv)
    shards = shards_of(me, ways)
    size = up_land.shape[1]
    background += [
        send(
            part.at[i * size : (i + 1) * size],
            land.at[i - 1],
            s_send.at[j, i],
            s_recv.at[j, i],
            {"sp": shards[i]},
        )
        for j, (part, land) in enumerate(((up_part, up_land), (down_part, down_land)))
        for i in range(1, len(shards))
    ]
    own = pltpu.make_async_copy(
        result_ref.at[lax.axis_index("dp")], returned_ref.at[lax.axis_index("dp")], local_sem
    )

    def dmixed_copy(s, d):
        return send(
            dmixed_ref.at[s, :, span(peer[d], width)],
            dmixed_h.at[s, span(me, shard)],
            m_send.at[s, d],
            m_recv.at[s, d],
            {"sp": peer[d]},
        )

    pairs = ((dq_ref, dq_tok), (dk_ref, dk_tok), (dv_ref, dv_tok))

    def grad_copy(i, s, d):
        source, target = pairs[i]
        return send(
            source.at[s, span(peer[d], shard)],
            target.at[s, :, span(me, width)],
            g_send.at[i, s, d],
            g_recv.at[i, s, d],
            {"sp": peer[d]},
        )

    for s in range(seqs):
        for d in range(1, ways):
            dmixed_copy(s, d).start()
    own.start()
    for copy in background:
        copy.start()
    lane = lax.broadcasted_iota(jnp.int32, (1, width), 1) // head_dim
    visible = lax.broadcasted_iota(jnp.int32, (BLOCK, BLOCK), 0) <= lax.broadcasted_iota(
        jnp.int32, (BLOCK, BLOCK), 1
    )
    scale = head_dim ** (-0.5)
    for s in range(seqs):
        dmixed_h[s, span(me, shard), :] = dmixed_ref[s, :, span(me, width)]
        for d in range(1, ways):
            dmixed_copy(s, d).wait_recv()
        dq_f[...] = jnp.zeros_like(dq_f)
        dk_f[...] = jnp.zeros_like(dk_f)
        dv_f[...] = jnp.zeros_like(dv_f)

        def one_head(h, carry):
            mine = (lane == h).astype(jnp.float32)
            for at in range(0, seq_len, BLOCK):
                rows = slice(at, at + BLOCK)
                query = (q_ref[s, rows, :].astype(jnp.float32) * (mine * scale)).astype(
                    jnp.bfloat16
                )
                dout = (dmixed_h[s, rows, :].astype(jnp.float32) * mine).astype(jnp.bfloat16)
                log_row = log_ref[s, pl.ds(h, 1), rows]
                parts = [(rows, True)] + ([(slice(0, at), False)] if at else [])
                kept = []
                delta = jnp.zeros((1, BLOCK), jnp.float32)
                for keys, diagonal in parts:
                    prob = jnp.exp(mxu(k_ref[s, keys, :], query, ROWS_BY_ROWS) - log_row)
                    if diagonal:
                        prob = jnp.where(visible, prob, 0.0)
                    dprob = mxu(v_ref[s, keys, :], dout, ROWS_BY_ROWS)
                    delta += jnp.sum(prob * dprob, axis=0, keepdims=True)
                    kept.append((keys, prob, dprob))
                dquery = jnp.zeros((BLOCK, width), jnp.float32)
                for keys, prob, dprob in kept:
                    dv_f[keys, :] += mxu(prob.astype(jnp.bfloat16), dout)
                    dlogit = (prob * (dprob - delta)).astype(jnp.bfloat16)
                    dk_f[keys, :] += mxu(dlogit, query)
                    dquery += mxu(dlogit, k_ref[s, keys, :], COLS_BY_COLS)
                dq_f[rows, :] += dquery * (mine * scale)
            return carry

        lax.fori_loop(0, heads, one_head, 0)
        for i, total in enumerate((dq_f, dk_f, dv_f)):
            source, target = pairs[i]
            source[s] = total[...].astype(jnp.bfloat16)
            for d in range(1, ways):
                grad_copy(i, s, d).start()
            target[s, :, span(me, width)] = source[s, span(me, shard), :]
    for s in range(seqs):
        for d in range(1, ways):
            dmixed_copy(s, d).wait_send()
            for i in range(3):
                grad_copy(i, s, d).wait()
    own.wait()
    for copy in background:
        copy.wait()


def pair_of(sp):
    core = lax.rem(lax.axis_index("dp"), 2)
    along_x, along_y = flip(sp, 1), flip(sp, 2)
    return along_x + core * (along_y - along_x)


def shards_of(sp, ways):
    shards = [sp, flip(pair_of(sp), 3)]
    bit = 4
    while bit < ways:
        shards += [flip(shard, bit) for shard in shards]
        bit *= 2
    return shards


def run_experts(
    others,
    ways,
    outgoing_ref,
    cot_ref,
    up_ref,
    down_ref,
    back_ref,
    result_ref,
    up_part,
    down_part,
    received,
    arrived,
    up_v,
    down_v,
    hidden,
    slope_v,
    total,
    dn_own,
    dn_pair,
    dn_land,
    dnormed,
    out_pair,
    out_land,
    w_sem,
    o_sem,
    c_sem,
    a_send,
    a_recv,
    b_send,
    b_recv,
    f_send,
    f_recv,
    p_send,
    p_recv,
):
    slots, width = received.shape[2:]
    rows = others * slots
    ff = up_v.shape[0]
    groups = others // 2
    me = lax.axis_index("dp")
    sp = lax.axis_index("sp")
    chip = me // 2
    pair = {"sp": pair_of(sp)}
    shards = shards_of(sp, ways)
    size = ff // len(shards)
    loads = [
        pltpu.make_async_copy(
            source.at[span(shard, size)], target.at[i * size : (i + 1) * size], w_sem.at[j, i]
        )
        for j, (source, target) in enumerate(((down_ref, down_v), (up_ref, up_v)))
        for i, shard in enumerate(shards)
    ]
    own_cot = pltpu.make_async_copy(cot_ref, arrived.at[0], c_sem)
    own_cot.start()
    for copy in loads:
        copy.start()
    greet([{"dp": flip(me, d)} for d in range(1, others)] + [pair])
    inward = exchange(others, outgoing_ref, received.at[0], a_send, a_recv)
    outward = exchange(others, dnormed, back_ref, b_send, b_recv)
    near = [flip(chip, group) for group in range(groups)]
    chips = [pl.ds(2 * near[group], 2) for group in range(groups)]
    forward = [
        send(
            received.at[0, chips[group]],
            received.at[1, chips[group]],
            f_send.at[group],
            f_recv.at[group],
            pair,
        )
        for group in range(groups)
    ]
    cot_copy = send(cot_ref, arrived.at[1], f_send.at[groups], f_recv.at[groups], pair)
    dn_copy = [
        send(
            dn_pair.at[chips[group]],
            dn_land.at[chips[group]],
            p_send.at[group],
            p_recv.at[group],
            pair,
        )
        for group in range(groups)
    ]
    out_copy = send(out_pair, out_land, p_send.at[groups], p_recv.at[groups], pair)

    for copy in inward:
        copy.start()
    received[0, me] = outgoing_ref[me]
    cot_copy.start()

    def slab_of(half, group):
        return pl.ds(pl.multiple_of(half * rows + near[group] * (2 * slots), 2 * slots), 2 * slots)

    def cot_half(half):
        def cot_step(i, carry):
            at = span(i, STEP)
            cot = arrived[half].reshape(rows, width)
            slope_v[half * rows : (half + 1) * rows, at] = mxu(
                cot, down_v[at, :], ROWS_BY_ROWS
            ).astype(jnp.bfloat16)
            return carry

        lax.fori_loop(0, ff // STEP, cot_step, 0)

    def up_half(half, group):
        slab = slab_of(half, group)
        total[...] = jnp.zeros_like(total)

        def up_step(i, carry):
            at = span(i, STEP)
            tokens = received[half, chips[group]].reshape(2 * slots, width)
            pre = mxu(tokens, up_v[at, :], ROWS_BY_ROWS)
            square = pre * pre
            inner = jnp.tanh(GELU_ROOT * pre * (1.0 + CUBIC_TERM * square))
            gate = 0.5 * (1.0 + inner)
            hidden[slab, at] = (pre * gate).astype(jnp.bfloat16)
            slope = gate + (0.5 * GELU_ROOT) * pre * (1.0 - inner * inner) * (
                1.0 + (3.0 * CUBIC_TERM) * square
            )
            dpre = (slope_v[slab, at].astype(jnp.float32) * slope).astype(jnp.bfloat16)
            slope_v[slab, at] = dpre
            total[...] += mxu(dpre, up_v[at, :])
            return carry

        lax.fori_loop(0, ff // STEP, up_step, 0)
        shaped = total[...].reshape(2, slots, width)
        if half:
            dn_pair[chips[group]] = shaped.astype(jnp.bfloat16)
            dn_copy[group].start()
        else:
            dn_own[chips[group]] = shaped

    def pass_on(group):
        for d in (2 * group, 2 * group + 1):
            if d:
                inward[d - 1].wait_recv()
        forward[group].start()

    def finish(group):
        dn_copy[group].wait_recv()
        at = chips[group]
        dnormed[at] = (dn_own[at] + dn_land[at].astype(jnp.float32)).astype(jnp.bfloat16)
        for d in (2 * group, 2 * group + 1):
            if d:
                outward[d - 1].start()
            else:
                back_ref[me] = dnormed[me]

    pass_on(0)
    own_cot.wait()
    for copy in loads[: len(shards)]:
        copy.wait()
    cot_half(0)
    for copy in loads[len(shards) :]:
        copy.wait()
    up_half(0, 0)
    cot_copy.wait_recv()
    cot_half(1)
    forward[0].wait_recv()
    up_half(1, 0)
    early = groups // 2
    for group in range(1, early):
        pass_on(group)
        up_half(0, group)
        forward[group].wait_recv()
        up_half(1, group)
    for group in range(early):
        finish(group)
    for group in range(early, groups):
        pass_on(group)
        up_half(0, group)
        if group > early:
            forward[group - 1].wait_recv()
            up_half(1, group - 1)
    forward[groups - 1].wait_recv()
    up_half(1, groups - 1)
    for group in range(early, groups):
        finish(group)

    def out_half(half):
        def out_step(i, carry):
            slab = pl.ds(pl.multiple_of(half * rows + i * (2 * slots), 2 * slots), 2 * slots)
            out = mxu(hidden[slab, :], down_v[...]).reshape(2, slots, width)
            at = pl.ds(2 * i, 2)
            if half:
                out_pair[at] = out.astype(jnp.bfloat16)
            else:
                result_ref[at] = (out + out_land[at].astype(jnp.float32)).astype(jnp.bfloat16)
            return carry

        lax.fori_loop(0, groups, out_step, 0)

    def grad(target, left, right_ref):
        def grad_step(i, carry):
            at = span(i, STEP)
            right = right_ref[...].reshape(2 * rows, width)
            target[at, :] = mxu(left[:, at], right, COLS_BY_COLS).astype(jnp.bfloat16)
            return carry

        lax.fori_loop(0, ff // STEP, grad_step, 0)

    out_half(1)
    out_copy.start()
    grad(up_v, slope_v, received)
    store_up = pltpu.make_async_copy(up_v, up_part, o_sem.at[0])
    store_up.start()
    out_copy.wait_recv()
    out_half(0)
    grad(down_v, hidden, arrived)
    store_down = pltpu.make_async_copy(down_v, down_part, o_sem.at[1])
    store_down.start()
    for copy in inward + forward + [cot_copy] + dn_copy + [out_copy]:
        copy.wait_send()
    for copy in outward:
        copy.wait()
    store_up.wait()
    store_down.wait()


def reduce_everywhere(
    ways,
    columns,
    part_ref,
    small_ref,
    out_ref,
    small_out,
    core_land,
    core_sum,
    column_land,
    piece,
    small_land,
    small_sum,
    core_send,
    core_recv,
    column_send,
    column_recv,
    spread_send,
    spread_recv,
    ring_send,
    ring_recv,
    cross_send,
    cross_recv,
    small_send,
    small_recv,
    local_sem,
):
    rows = part_ref.shape[2]
    width = part_ref.shape[3]
    me = lax.axis_index("sp")
    dp = lax.axis_index("dp")
    core = lax.rem(dp, 2)
    column = dp // 2
    twin = {"dp": dp + 1 - 2 * core}
    column_peer = [lax.rem(column + d, columns) for d in range(columns)]
    sp_peer = [lax.rem(me + d, ways) for d in range(ways)]
    sp_origin = [lax.rem(me + ways - d, ways) for d in range(ways)]
    column_id = [{"dp": 2 * column_peer[d] + core} for d in range(columns)]
    sp_id = [{"sp": sp_peer[d]} for d in range(ways)]
    greet([twin] + column_id[1:] + sp_id[1:])

    first = send(part_ref.at[1 - core], core_land, core_send, core_recv, twin)
    first.start()
    small_first = send(small_ref, small_land.at[0], small_send.at[0], small_recv.at[0], twin)
    small_first.start()
    small_first.wait()
    small_sum[0] = small_ref[...] + small_land[0]

    def small_column(d):
        return send(
            small_sum.at[0],
            small_land.at[d],
            small_send.at[d],
            small_recv.at[d],
            column_id[d],
        )

    def small_ring(d):
        at = columns + d
        return send(
            small_sum.at[1],
            small_land.at[at],
            small_send.at[at],
            small_recv.at[at],
            sp_id[d],
        )

    for d in range(1, columns):
        small_column(d).start()
    first.wait()
    core_sum[...] = (
        part_ref[core].astype(jnp.float32) + core_land[...].astype(jnp.float32)
    ).astype(jnp.bfloat16)

    def column_copy(d):
        return send(
            core_sum.at[column_peer[d]],
            column_land.at[d],
            column_send.at[d],
            column_recv.at[d],
            column_id[d],
        )

    for d in range(1, columns):
        column_copy(d).start()
    for d in range(1, columns):
        small_column(d).wait()
    total = small_sum[0]
    for d in range(1, columns):
        total += small_land[d]
    small_sum[1] = total
    for d in range(1, ways):
        small_ring(d).start()
    total = core_sum[column].astype(jnp.float32)
    for d in range(1, columns):
        column_copy(d).wait()
        total += column_land[d].astype(jnp.float32)
    piece[...] = total.astype(jnp.bfloat16)

    def block(at_core, at_column, at_sp, count=1):
        first_row = pl.multiple_of((at_core * columns + at_column) * rows, rows)
        return out_ref.at[pl.ds(first_row, count * rows), span(at_sp, width)]

    def spread_copy(d):
        return send(
            piece,
            block(core, column, me),
            spread_send.at[d],
            spread_recv.at[d],
            column_id[d],
        )

    for d in range(1, columns):
        spread_copy(d).start()
    own = pltpu.make_async_copy(piece, block(core, column, me), local_sem)
    own.start()
    for d in range(1, ways):
        small_ring(d).wait()
    total = small_sum[1]
    for d in range(1, ways):
        total += small_land[columns + d]
    small_out[...] = total
    own.wait()
    for d in range(1, columns):
        spread_copy(d).wait()

    def ring_copy(d):
        half = block(core, 0, me, columns)
        return send(half, half, ring_send.at[d], ring_recv.at[d], sp_id[d])

    def cross_copy(d):
        half = block(core, 0, sp_origin[d], columns)
        return send(half, half, cross_send.at[d], cross_recv.at[d], twin)

    for d in range(1, ways):
        ring_copy(d).start()
    cross_copy(0).start()
    for d in range(1, ways):
        ring_copy(d).wait_recv()
        cross_copy(d).start()
    for d in range(1, ways):
        ring_copy(d).wait_send()
    for d in range(ways):
        cross_copy(d).wait()


def vmem(count):
    return [pl.BlockSpec(memory_space=pltpu.VMEM)] * count


def params(collective_id):
    return pltpu.CompilerParams(
        collective_id=collective_id, has_side_effects=True, vmem_limit_bytes=VMEM_BYTES
    )


def dma(*shape):
    return pltpu.SemaphoreType.DMA(shape)


def local(
    tokens_in,
    expert_ids,
    query_weight,
    key_weight,
    value_weight,
    out_weight,
    norm1_gain,
    norm1_shift,
    norm2_gain,
    norm2_shift,
    up_weight,
    down_weight,
    out_cotangent,
    load_mean,
):
    seq_count, shard_len, model_width = tokens_in.shape
    row_count = seq_count * shard_len
    head_dim = model_width // HEADS
    dp_ways = lax.axis_size("dp")
    sp_ways = lax.axis_size("sp")
    sp_at = lax.axis_index("sp")
    seq_len = shard_len * sp_ways
    experts = load_mean.shape[0]
    slot_count = 2 * row_count // experts
    local_experts = up_weight.shape[0]
    ff_width = up_weight.shape[1]
    width = model_width // sp_ways
    bf16 = jnp.bfloat16
    f32 = jnp.float32

    def shape(*sizes, dtype=bf16):
        return jax.ShapeDtypeStruct(sizes, dtype)

    routes = expert_ids.reshape(row_count)
    one_hot = (routes[:, None] == jnp.arange(experts, dtype=jnp.int32)[None, :]).astype(jnp.int32)
    running = jnp.cumsum(one_hot, axis=0) - 1
    slot_of = jnp.sum(running * one_hot, axis=1)
    target = routes * slot_count + slot_of
    placer = (jnp.arange(experts * slot_count, dtype=jnp.int32)[:, None] == target[None, :]).astype(
        bf16
    )
    cot_b = out_cotangent.reshape(row_count, model_width)
    cot_send = jnp.dot(placer, cot_b, preferred_element_type=f32).astype(bf16)
    cot_send = cot_send.reshape(experts, slot_count, model_width)

    def columns_of(weight):
        return lax.dynamic_slice_in_dim(weight, sp_at * width, width, axis=1)

    routed = shape(experts, slot_count, model_width)
    hbm = [pl.BlockSpec(memory_space=pl.ANY)]
    normed_all, query_h, key_h, value_h, log_total, mixed_b, arrived = pl.pallas_call(
        functools.partial(attend_forward, sp_ways, dp_ways, head_dim),
        out_shape=[
            shape(seq_count, seq_len, model_width),
            shape(seq_count, seq_len, width),
            shape(seq_count, seq_len, width),
            shape(seq_count, seq_len, width),
            shape(seq_count, 8, seq_len, dtype=f32),
            shape(seq_count, shard_len, model_width),
            routed,
        ],
        in_specs=hbm + vmem(6),
        out_specs=vmem(6) + hbm,
        scratch_shapes=[
            pltpu.VMEM((seq_count, seq_len, model_width), bf16),
            pltpu.VMEM((seq_len, width), f32),
            pltpu.VMEM((seq_count, seq_len, width), bf16),
            pltpu.VMEM((seq_len, LANES), f32),
            dma(seq_count, sp_ways),
            dma(seq_count, sp_ways),
            dma(seq_count, sp_ways),
            dma(seq_count, sp_ways),
            dma(dp_ways),
            dma(dp_ways),
            pltpu.SemaphoreType.DMA,
        ],
        compiler_params=params(0),
    )(
        cot_send,
        tokens_in,
        columns_of(query_weight),
        columns_of(key_weight),
        columns_of(value_weight),
        norm1_gain.reshape(1, model_width),
        norm1_shift.reshape(1, model_width),
    )
    mixed_b = mixed_b.reshape(row_count, model_width)
    inputs = tokens_in.reshape(row_count, model_width).astype(f32)
    attn_out = jnp.dot(mixed_b, out_weight, preferred_element_type=f32)
    residual_stream = inputs + attn_out
    normed2, unit2, rstd2 = norm_forward(residual_stream, norm2_gain, norm2_shift)
    normed2_b = normed2.astype(bf16)
    outgoing = jnp.dot(placer, normed2_b, preferred_element_type=f32).astype(bf16)
    outgoing = outgoing.reshape(experts, slot_count, model_width)
    ff_own = ff_width // 2
    part = shape(ff_own, model_width)
    dnormed_back, expert_out, up_part, down_part = pl.pallas_call(
        functools.partial(run_experts, dp_ways, sp_ways),
        out_shape=[routed, routed, part, part],
        in_specs=vmem(1) + hbm * 3,
        out_specs=vmem(2) + hbm * 2,
        scratch_shapes=[
            pltpu.VMEM((2,) + routed.shape, bf16),
            pltpu.VMEM((2,) + routed.shape, bf16),
            pltpu.VMEM((ff_own, model_width), bf16),
            pltpu.VMEM((ff_own, model_width), bf16),
            pltpu.VMEM((2 * experts * slot_count, ff_own), bf16),
            pltpu.VMEM((2 * experts * slot_count, ff_own), bf16),
            pltpu.VMEM((2 * slot_count, model_width), f32),
            pltpu.VMEM(routed.shape, f32),
            pltpu.VMEM(routed.shape, bf16),
            pltpu.VMEM(routed.shape, bf16),
            pltpu.VMEM(routed.shape, bf16),
            pltpu.VMEM(routed.shape, bf16),
            pltpu.VMEM(routed.shape, bf16),
            dma(2, sp_ways // 2),
            dma(2),
            pltpu.SemaphoreType.DMA,
            dma(dp_ways),
            dma(dp_ways),
            dma(dp_ways),
            dma(dp_ways),
            dma(dp_ways // 2 + 1),
            dma(dp_ways // 2 + 1),
            dma(dp_ways // 2 + 1),
            dma(dp_ways // 2 + 1),
        ],
        compiler_params=params(3),
    )(outgoing, arrived, up_weight[0], down_weight[0])
    dnormed2 = jnp.einsum(
        "er,ed->rd",
        placer,
        dnormed_back.reshape(experts * slot_count, model_width),
        preferred_element_type=f32,
    )
    dresid_norm, gain_two_grad, shift_two_grad = norm_backward(dnormed2, unit2, rstd2, norm2_gain)
    dresid = cot_b.astype(f32) + dresid_norm
    dattn_b = dresid.astype(bf16)
    dmixed_b = jnp.einsum("re,de->rd", dattn_b, out_weight, preferred_element_type=f32)
    dmixed_b = dmixed_b.astype(bf16).reshape(seq_count, shard_len, model_width)
    out_grad = jnp.einsum("rd,re->de", mixed_b, dattn_b, preferred_element_type=f32).astype(bf16)
    out_part = lax.psum_scatter(out_grad, "sp", scatter_dimension=1, tiled=True)
    landing = shape(sp_ways // 2 - 1, ff_width // sp_ways, model_width)
    grads = pl.pallas_call(
        functools.partial(attend_backward, sp_ways, dp_ways, head_dim),
        out_shape=[shape(seq_count, seq_len, width)] * 3
        + [shape(seq_count, shard_len, model_width)] * 3
        + [routed, landing, landing],
        in_specs=hbm * 3 + vmem(5),
        out_specs=vmem(6) + hbm * 3,
        scratch_shapes=[
            pltpu.VMEM((seq_count, seq_len, width), bf16),
            pltpu.VMEM((seq_len, width), f32),
            pltpu.VMEM((seq_len, width), f32),
            pltpu.VMEM((seq_len, width), f32),
            dma(seq_count, sp_ways),
            dma(seq_count, sp_ways),
            dma(3, seq_count, sp_ways),
            dma(3, seq_count, sp_ways),
            dma(dp_ways),
            dma(dp_ways),
            dma(2, sp_ways // 2),
            dma(2, sp_ways // 2),
            pltpu.SemaphoreType.DMA,
        ],
        compiler_params=params(1),
    )(expert_out, up_part, down_part, dmixed_b, query_h, key_h, value_h, log_total)
    head_grads, token_grads, returned, *landed = grads[:3], grads[3:6], *grads[6:]
    up_grad, down_grad = (
        part[: ff_width // sp_ways].astype(f32)[None] + jnp.sum(land.astype(f32), axis=0)[None]
        for part, land in zip((up_part, down_part), landed)
    )
    expert_rows = jnp.einsum(
        "er,ed->rd",
        placer,
        returned.reshape(experts * slot_count, model_width),
        preferred_element_type=f32,
    )
    block_out = (residual_stream + expert_rows).astype(bf16)
    block_out = block_out.reshape(seq_count, shard_len, model_width)
    weight_parts = [
        jnp.einsum("skd,ske->de", normed_all, grad, preferred_element_type=f32).astype(bf16)
        for grad in head_grads
    ]
    dnormed1 = sum(
        jnp.einsum(
            "re,de->rd",
            grad.reshape(row_count, model_width),
            weight,
            preferred_element_type=f32,
        )
        for grad, weight in zip(token_grads, (query_weight, key_weight, value_weight))
    )
    _, unit1, rstd1 = norm_forward(inputs, norm1_gain, norm1_shift)
    dinput_norm, gain_one_grad, shift_one_grad = norm_backward(dnormed1, unit1, rstd1, norm1_gain)
    tokens_grad = (dresid + dinput_norm).astype(bf16)
    tokens_grad = tokens_grad.reshape(seq_count, shard_len, model_width)
    counts = jnp.sum(one_hot, axis=0).astype(f32)
    counts = jnp.pad(counts, (0, model_width - experts))
    small = jnp.stack(
        [gain_one_grad, shift_one_grad, gain_two_grad, shift_two_grad, counts]
        + [jnp.zeros((model_width,), f32)] * 3
    )
    columns = dp_ways // 2
    piece_rows = 4 * model_width // dp_ways
    packed = jnp.concatenate(weight_parts + [out_part], axis=0)
    packed = packed.reshape(2, columns, piece_rows, width)
    gathered, small_sum = pl.pallas_call(
        functools.partial(reduce_everywhere, sp_ways, columns),
        out_shape=[
            shape(4 * model_width, model_width),
            shape(8, model_width, dtype=f32),
        ],
        in_specs=vmem(2),
        out_specs=[pl.BlockSpec(memory_space=pl.ANY), pl.BlockSpec(memory_space=pltpu.VMEM)],
        scratch_shapes=[
            pltpu.VMEM((columns, piece_rows, width), bf16),
            pltpu.VMEM((columns, piece_rows, width), bf16),
            pltpu.VMEM((columns, piece_rows, width), bf16),
            pltpu.VMEM((piece_rows, width), bf16),
            pltpu.VMEM((columns + sp_ways, 8, model_width), f32),
            pltpu.VMEM((2, 8, model_width), f32),
            pltpu.SemaphoreType.DMA,
            pltpu.SemaphoreType.DMA,
            dma(columns),
            dma(columns),
            dma(columns),
            dma(columns),
            dma(sp_ways),
            dma(sp_ways),
            dma(sp_ways),
            dma(sp_ways),
            dma(columns + sp_ways),
            dma(columns + sp_ways),
            pltpu.SemaphoreType.DMA,
        ],
        compiler_params=params(2),
    )(packed, small)
    query_grad, key_grad, value_grad, out_grad = (
        gathered[i * model_width : (i + 1) * model_width].astype(f32) for i in range(4)
    )
    load_now = small_sum[4, :experts] * experts / (row_count * dp_ways * sp_ways)
    load_next = 0.9 * load_mean + 0.1 * load_now
    return (
        block_out,
        tokens_grad,
        query_grad,
        key_grad,
        value_grad,
        out_grad,
        small_sum[0],
        small_sum[1],
        small_sum[2],
        small_sum[3],
        up_grad,
        down_grad,
        load_next,
    )


def solution(mesh):
    return jax.shard_map(
        local,
        mesh=mesh,
        in_specs=(
            P("dp", "sp", None),
            P("dp", "sp", None, None),
            P(),
            P(),
            P(),
            P(),
            P(),
            P(),
            P(),
            P(),
            P("dp", None, None),
            P("dp", None, None),
            P("dp", "sp", None),
            P(),
        ),
        out_specs=(
            P("dp", "sp", None),
            P("dp", "sp", None),
            P(),
            P(),
            P(),
            P(),
            P(),
            P(),
            P(),
            P(),
            P("dp", "sp", None),
            P("dp", "sp", None),
            P(),
        ),
        check_vma=False,
    )
```

```python
import functools

import jax
import jax.numpy as jnp
from jax import lax
from jax.experimental import pallas as pl
from jax.experimental.pallas import tpu as pltpu
from jax.sharding import PartitionSpec as P

HEADS = 16
MESH = pl.DeviceIdType.MESH
BLOCK = 256
LANES = 128
STEP = 512
VMEM_BYTES = 60 * 2**20

NORM_EPSILON = 1e-05
GELU_ROOT = 0.7978845608028654
CUBIC_TERM = 0.044715

ROWS_BY_COLS = (((1,), (0,)), ((), ()))
ROWS_BY_ROWS = (((1,), (1,)), ((), ()))
COLS_BY_COLS = (((0,), (0,)), ((), ()))


def smooth(values):
    return (
        0.5
        * values
        * (1.0 + jnp.tanh(GELU_ROOT * (values + CUBIC_TERM * values * values * values)))
    )


def smooth_slope(values):
    inner = jnp.tanh(GELU_ROOT * (values + CUBIC_TERM * values * values * values))
    return 0.5 * (1.0 + inner) + 0.5 * values * (1.0 - inner * inner) * GELU_ROOT * (
        1.0 + 3.0 * CUBIC_TERM * values * values
    )


def norm_forward(values, gain, shift):
    center = jnp.mean(values, axis=-1, keepdims=True)
    offset = values - center
    rstd = lax.rsqrt(jnp.mean(offset * offset, axis=-1, keepdims=True) + NORM_EPSILON)
    unit = offset * rstd
    return (unit * gain + shift, unit, rstd)


def norm_backward(grad, unit, rstd, gain):
    scaled = grad * gain
    inner = (
        scaled
        - jnp.mean(scaled, axis=-1, keepdims=True)
        - unit * jnp.mean(scaled * unit, axis=-1, keepdims=True)
    )
    return (inner * rstd, jnp.sum(grad * unit, axis=0), jnp.sum(grad, axis=0))


def mxu(left, right, dims=ROWS_BY_COLS):
    return lax.dot_general(left, right, dims, preferred_element_type=jnp.float32)


def span(index, size):
    return pl.ds(pl.multiple_of(index * size, size), size)


def greet(peers):
    barrier = pltpu.get_barrier_semaphore()
    for peer in peers:
        pl.semaphore_signal(barrier, inc=1, device_id=peer, device_id_type=MESH)
    pl.semaphore_wait(barrier, len(peers))


def send(source, target, send_sem, recv_sem, peer):
    return pltpu.make_async_remote_copy(
        src_ref=source,
        dst_ref=target,
        send_sem=send_sem,
        recv_sem=recv_sem,
        device_id=peer,
        device_id_type=MESH,
    )


def exchange(others, source, target, send_sem, recv_sem):
    me = lax.axis_index("dp")
    return [
        send(
            source.at[flip(me, d)],
            target.at[me],
            send_sem.at[d],
            recv_sem.at[d],
            {"dp": flip(me, d)},
        )
        for d in range(1, others)
    ]


def flip(index, bits):
    bit = 1
    while bit <= bits:
        if bits & bit:
            index = index + bit - 2 * bit * lax.rem(index // bit, 2)
        bit *= 2
    return index


def attend_forward(
    ways,
    others,
    head_dim,
    cot_ref,
    x_ref,
    wq_ref,
    wk_ref,
    wv_ref,
    gain_ref,
    shift_ref,
    normed_ref,
    q_ref,
    k_ref,
    v_ref,
    log_ref,
    mixed_ref,
    arrived_ref,
    x_all,
    mixed_f,
    mixed_h,
    log_s,
    x_send,
    x_recv,
    m_send,
    m_recv,
    c_send,
    c_recv,
    local_sem,
):
    seqs, shard, _ = x_ref.shape
    seq_len, width = q_ref.shape[1:]
    heads = width // head_dim
    me = lax.axis_index("sp")
    peer = [lax.rem(me + d, ways) for d in range(ways)]
    origin = [lax.rem(me + ways - d, ways) for d in range(ways)]
    greet(
        [{"sp": peer[d]} for d in range(1, ways)]
        + [{"dp": flip(lax.axis_index("dp"), d)} for d in range(1, others)]
    )
    background = exchange(others, cot_ref, arrived_ref, c_send, c_recv)
    own = pltpu.make_async_copy(
        cot_ref.at[lax.axis_index("dp")], arrived_ref.at[lax.axis_index("dp")], local_sem
    )

    def x_copy(s, d):
        return send(
            x_ref.at[s],
            x_all.at[s, span(me, shard)],
            x_send.at[s, d],
            x_recv.at[s, d],
            {"sp": peer[d]},
        )

    def mixed_copy(s, d):
        return send(
            mixed_h.at[s, span(peer[d], shard)],
            mixed_ref.at[s, :, span(me, width)],
            m_send.at[s, d],
            m_recv.at[s, d],
            {"sp": peer[d]},
        )

    lane = lax.broadcasted_iota(jnp.int32, (1, width), 1) // head_dim
    log_lane = lax.broadcasted_iota(jnp.int32, (1, LANES), 1)
    visible = lax.broadcasted_iota(jnp.int32, (BLOCK, BLOCK), 1) <= lax.broadcasted_iota(
        jnp.int32, (BLOCK, BLOCK), 0
    )
    scale = head_dim ** (-0.5)

    def project(s, rows, values):
        normed, _, _ = norm_forward(values.astype(jnp.float32), gain_ref[...], shift_ref[...])
        normed = normed.astype(jnp.bfloat16)
        normed_ref[s, rows, :] = normed
        q_ref[s, rows, :] = mxu(normed, wq_ref[...]).astype(jnp.bfloat16)
        k_ref[s, rows, :] = mxu(normed, wk_ref[...]).astype(jnp.bfloat16)
        v_ref[s, rows, :] = mxu(normed, wv_ref[...]).astype(jnp.bfloat16)

    for d in range(1, ways):
        x_copy(0, d).start()
    own.start()
    for copy in background:
        copy.start()
    for s in range(seqs):
        project(s, span(me, shard), x_ref[s])
        for d in range(1, ways):
            x_copy(s, d).wait_recv()
            if d == ways - 1 and s + 1 < seqs:
                for later in range(1, ways):
                    x_copy(s + 1, later).start()
            rows = span(origin[d], shard)
            project(s, rows, x_all[s, rows, :])
        mixed_f[...] = jnp.zeros_like(mixed_f)
        log_s[...] = jnp.zeros_like(log_s)

        def one_head(h, carry):
            mine = (lane == h).astype(jnp.float32)
            for at in range(0, seq_len, BLOCK):
                rows = slice(at, at + BLOCK)
                query = (q_ref[s, rows, :].astype(jnp.float32) * (mine * scale)).astype(
                    jnp.bfloat16
                )
                near = mxu(query, k_ref[s, rows, :], ROWS_BY_ROWS)
                near = jnp.where(visible, near, -1e30)
                top = jnp.max(near, axis=1, keepdims=True)
                if at:
                    far = mxu(query, k_ref[s, :at, :], ROWS_BY_ROWS)
                    top = jnp.maximum(top, jnp.max(far, axis=1, keepdims=True))
                near = jnp.exp(near - top)
                total = jnp.sum(near, axis=1, keepdims=True)
                if at:
                    far = jnp.exp(far - top)
                    total += jnp.sum(far, axis=1, keepdims=True)
                inverse = 1.0 / total
                out = mxu((near * inverse).astype(jnp.bfloat16), v_ref[s, rows, :])
                if at:
                    out += mxu((far * inverse).astype(jnp.bfloat16), v_ref[s, :at, :])
                mixed_f[rows, :] += out * mine
                log_s[rows, :] = jnp.where(log_lane == h, top + jnp.log(total), log_s[rows, :])
            return carry

        lax.fori_loop(0, heads, one_head, 0)
        log_ref[s] = jnp.transpose(log_s[...])[: log_ref.shape[1], :]
        mixed_h[s] = mixed_f[...].astype(jnp.bfloat16)
        for d in range(1, ways):
            mixed_copy(s, d).start()
        mixed_ref[s, :, span(me, width)] = mixed_h[s, span(me, shard), :]
    for s in range(seqs):
        for d in range(1, ways):
            x_copy(s, d).wait_send()
            mixed_copy(s, d).wait()
    own.wait()
    for copy in background:
        copy.wait()


def pair_of(sp):
    core = lax.rem(lax.axis_index("dp"), 2)
    along_x, along_y = flip(sp, 1), flip(sp, 2)
    return along_x + core * (along_y - along_x)


def shards_of(sp, ways):
    shards = [sp, flip(pair_of(sp), 3)]
    bit = 4
    while bit < ways:
        shards += [flip(shard, bit) for shard in shards]
        bit *= 2
    return shards


def run_experts(
    others,
    ways,
    outgoing_ref,
    cot_ref,
    up_ref,
    down_ref,
    back_ref,
    result_ref,
    up_part,
    down_part,
    received,
    arrived,
    up_v,
    down_v,
    hidden,
    slope_v,
    total,
    dn_own,
    dn_pair,
    dn_land,
    dnormed,
    out_pair,
    out_land,
    w_sem,
    o_sem,
    c_sem,
    a_send,
    a_recv,
    b_send,
    b_recv,
    f_send,
    f_recv,
    p_send,
    p_recv,
):
    slots, width = received.shape[2:]
    rows = others * slots
    ff = up_v.shape[0]
    groups = others // 2
    me = lax.axis_index("dp")
    sp = lax.axis_index("sp")
    chip = me // 2
    pair = {"sp": pair_of(sp)}
    shards = shards_of(sp, ways)
    size = ff // len(shards)
    loads = [
        pltpu.make_async_copy(
            source.at[span(shard, size)], target.at[i * size : (i + 1) * size], w_sem.at[j, i]
        )
        for j, (source, target) in enumerate(((down_ref, down_v), (up_ref, up_v)))
        for i, shard in enumerate(shards)
    ]
    own_cot = pltpu.make_async_copy(cot_ref, arrived.at[0], c_sem)
    own_cot.start()
    for copy in loads:
        copy.start()
    greet([{"dp": flip(me, d)} for d in range(1, others)] + [pair])
    inward = exchange(others, outgoing_ref, received.at[0], a_send, a_recv)
    outward = exchange(others, dnormed, back_ref, b_send, b_recv)
    near = [flip(chip, group) for group in range(groups)]
    chips = [pl.ds(2 * near[group], 2) for group in range(groups)]
    forward = [
        send(
            received.at[0, chips[group]],
            received.at[1, chips[group]],
            f_send.at[group],
            f_recv.at[group],
            pair,
        )
        for group in range(groups)
    ]
    cot_copy = send(cot_ref, arrived.at[1], f_send.at[groups], f_recv.at[groups], pair)
    dn_copy = [
        send(
            dn_pair.at[chips[group]],
            dn_land.at[chips[group]],
            p_send.at[group],
            p_recv.at[group],
            pair,
        )
        for group in range(groups)
    ]
    out_copy = send(out_pair, out_land, p_send.at[groups], p_recv.at[groups], pair)

    for copy in inward:
        copy.start()
    received[0, me] = outgoing_ref[me]
    cot_copy.start()

    def slab_of(half, group):
        return pl.ds(pl.multiple_of(half * rows + near[group] * (2 * slots), 2 * slots), 2 * slots)

    def cot_half(half):
        def cot_step(i, carry):
            at = span(i, STEP)
            cot = arrived[half].reshape(rows, width)
            slope_v[half * rows : (half + 1) * rows, at] = mxu(
                cot, down_v[at, :], ROWS_BY_ROWS
            ).astype(jnp.bfloat16)
            return carry

        lax.fori_loop(0, ff // STEP, cot_step, 0)

    def up_half(half, group):
        slab = slab_of(half, group)
        total[...] = jnp.zeros_like(total)

        def up_step(i, carry):
            at = span(i, STEP)
            tokens = received[half, chips[group]].reshape(2 * slots, width)
            pre = mxu(tokens, up_v[at, :], ROWS_BY_ROWS)
            square = pre * pre
            inner = jnp.tanh(GELU_ROOT * pre * (1.0 + CUBIC_TERM * square))
            gate = 0.5 * (1.0 + inner)
            hidden[slab, at] = (pre * gate).astype(jnp.bfloat16)
            slope = gate + (0.5 * GELU_ROOT) * pre * (1.0 - inner * inner) * (
                1.0 + (3.0 * CUBIC_TERM) * square
            )
            dpre = (slope_v[slab, at].astype(jnp.float32) * slope).astype(jnp.bfloat16)
            slope_v[slab, at] = dpre
            total[...] += mxu(dpre, up_v[at, :])
            return carry

        lax.fori_loop(0, ff // STEP, up_step, 0)
        shaped = total[...].reshape(2, slots, width)
        if half:
            dn_pair[chips[group]] = shaped.astype(jnp.bfloat16)
            dn_copy[group].start()
        else:
            dn_own[chips[group]] = shaped

    def pass_on(group):
        for d in (2 * group, 2 * group + 1):
            if d:
                inward[d - 1].wait_recv()
        forward[group].start()

    def finish(group):
        dn_copy[group].wait_recv()
        at = chips[group]
        dnormed[at] = (dn_own[at] + dn_land[at].astype(jnp.float32)).astype(jnp.bfloat16)
        for d in (2 * group, 2 * group + 1):
            if d:
                outward[d - 1].start()
            else:
                back_ref[me] = dnormed[me]

    pass_on(0)
    own_cot.wait()
    for copy in loads[: len(shards)]:
        copy.wait()
    cot_half(0)
    for copy in loads[len(shards) :]:
        copy.wait()
    up_half(0, 0)
    cot_copy.wait_recv()
    cot_half(1)
    forward[0].wait_recv()
    up_half(1, 0)
    early = groups // 2
    for group in range(1, early):
        pass_on(group)
        up_half(0, group)
        forward[group].wait_recv()
        up_half(1, group)
    for group in range(early):
        finish(group)
    for group in range(early, groups):
        pass_on(group)
        up_half(0, group)
        if group > early:
            forward[group - 1].wait_recv()
            up_half(1, group - 1)
    forward[groups - 1].wait_recv()
    up_half(1, groups - 1)
    for group in range(early, groups):
        finish(group)

    def out_half(half):
        def out_step(i, carry):
            slab = pl.ds(pl.multiple_of(half * rows + i * (2 * slots), 2 * slots), 2 * slots)
            out = mxu(hidden[slab, :], down_v[...]).reshape(2, slots, width)
            at = pl.ds(2 * i, 2)
            if half:
                out_pair[at] = out.astype(jnp.bfloat16)
            else:
                result_ref[at] = (out + out_land[at].astype(jnp.float32)).astype(jnp.bfloat16)
            return carry

        lax.fori_loop(0, groups, out_step, 0)

    def grad(target, left, right_ref):
        def grad_step(i, carry):
            at = span(i, STEP)
            right = right_ref[...].reshape(2 * rows, width)
            target[at, :] = mxu(left[:, at], right, COLS_BY_COLS).astype(jnp.bfloat16)
            return carry

        lax.fori_loop(0, ff // STEP, grad_step, 0)

    out_half(1)
    out_copy.start()
    grad(up_v, slope_v, received)
    store_up = pltpu.make_async_copy(up_v, up_part, o_sem.at[0])
    store_up.start()
    out_copy.wait_recv()
    out_half(0)
    grad(down_v, hidden, arrived)
    store_down = pltpu.make_async_copy(down_v, down_part, o_sem.at[1])
    store_down.start()
    for copy in inward + forward + [cot_copy] + dn_copy + [out_copy]:
        copy.wait_send()
    for copy in outward:
        copy.wait()
    store_up.wait()
    store_down.wait()


class Reduction:
    def __init__(self, ways, columns, part, out, scratch):
        (
            self.core_land,
            self.core_sum,
            self.column_land,
            self.piece,
            core_send,
            core_recv,
            column_send,
            column_recv,
            spread_send,
            spread_recv,
            ring_send,
            ring_recv,
            cross_send,
            cross_recv,
            own_sem,
        ) = scratch
        me = lax.axis_index("sp")
        dp = lax.axis_index("dp")
        core = lax.rem(dp, 2)
        column = dp // 2
        twin = {"dp": dp + 1 - 2 * core}
        self.ways, self.columns, self.part = ways, columns, part
        self.core, self.column = core, column
        rows, width = self.piece.shape
        self.rows = rows

        def beside(d):
            return {"dp": 2 * lax.rem(column + d, columns) + core}

        def block(at_core, at_column, at_sp, count):
            first = pl.multiple_of((at_core * columns + at_column) * rows, rows)
            return out.at[pl.ds(first, count * rows), span(at_sp, width)]

        self.core_copy = send(
            part.at[span(1 - core, columns * rows)], self.core_land, core_send, core_recv, twin
        )
        self.column_copy = [
            send(
                self.core_sum.at[span(lax.rem(column + d, columns), rows)],
                self.column_land.at[d - 1],
                column_send.at[d],
                column_recv.at[d],
                beside(d),
            )
            for d in range(1, columns)
        ]
        spot = block(core, column, me, 1)
        self.own = pltpu.make_async_copy(self.piece, spot, own_sem)
        self.spread_copy = [
            send(self.piece, spot, spread_send.at[d], spread_recv.at[d], beside(d))
            for d in range(1, columns)
        ]
        half = [block(core, 0, lax.rem(me + ways - d, ways), columns) for d in range(ways)]
        self.ring_copy = [
            send(
                half[0],
                half[0],
                ring_send.at[d],
                ring_recv.at[d],
                {"sp": lax.rem(me + d, ways)},
            )
            for d in range(1, ways)
        ]
        self.cross_copy = [
            send(half[d], half[d], cross_send.at[d], cross_recv.at[d], twin) for d in range(ways)
        ]

    def add_core(self):
        self.core_copy.wait()
        self.core_sum[...] = (
            self.part[span(self.core, self.columns * self.rows), :].astype(jnp.float32)
            + self.core_land[...].astype(jnp.float32)
        ).astype(jnp.bfloat16)
        for copy in self.column_copy:
            copy.start()

    def add_column(self):
        total = self.core_sum[span(self.column, self.rows), :].astype(jnp.float32)
        for d, copy in enumerate(self.column_copy):
            copy.wait()
            total += self.column_land[d].astype(jnp.float32)
        return total

    def spread(self):
        self.own.start()
        for copy in self.spread_copy:
            copy.start()

    def ring(self):
        self.own.wait()
        for copy in self.spread_copy:
            copy.wait()
        for copy in self.ring_copy:
            copy.start()
        self.cross_copy[0].start()

    def cross(self):
        for ring, cross in zip(self.ring_copy, self.cross_copy[1:]):
            ring.wait_recv()
            cross.start()

    def finish(self):
        for copy in self.ring_copy:
            copy.wait_send()
        for copy in self.cross_copy:
            copy.wait()


def backward(
    ways,
    others,
    head_dim,
    result_ref,
    up_part,
    down_part,
    normed_ref,
    wq_ref,
    wk_ref,
    wv_ref,
    dmixed_ref,
    mixed_ref,
    dattn_ref,
    q_ref,
    k_ref,
    v_ref,
    log_ref,
    x_ref,
    dresid_ref,
    gain_ref,
    small_ref,
    out_qkv,
    out_o,
    returned_ref,
    up_land,
    down_land,
    tokens_ref,
    small_out,
    dmixed_h,
    dq_f,
    dk_f,
    dv_f,
    grads_h,
    grads_tok,
    normed_v,
    weights_v,
    part_o,
    part_w,
    o_land,
    small_own,
    small_land,
    small_sum,
    m_send,
    m_recv,
    g_send,
    g_recv,
    c_send,
    c_recv,
    s_send,
    s_recv,
    o_send,
    o_recv,
    small_send,
    small_recv,
    load_sem,
    *scratch,
):
    seqs, shard, model = dmixed_ref.shape
    seq_len, width = q_ref.shape[1:]
    heads = width // head_dim
    columns = others // 2
    me = lax.axis_index("sp")
    dp = lax.axis_index("dp")
    core = lax.rem(dp, 2)
    peer = [lax.rem(me + d, ways) for d in range(ways)]
    loads = [
        pltpu.make_async_copy(source, target, load_sem.at[i])
        for i, (source, target) in enumerate(
            [(normed_ref, normed_v)]
            + [(source, weights_v.at[i]) for i, source in enumerate((wq_ref, wk_ref, wv_ref))]
            + [(result_ref.at[dp], returned_ref.at[dp])]
        )
    ]
    for copy in loads:
        copy.start()
    greet(
        [{"sp": peer[d]} for d in range(1, ways)]
        + [{"dp": flip(dp, d)} for d in range(1, others)]
    )

    def dmixed_copy(s, d):
        return send(
            dmixed_ref.at[s, :, span(peer[d], width)],
            dmixed_h.at[s, span(me, shard)],
            m_send.at[s, d],
            m_recv.at[s, d],
            {"sp": peer[d]},
        )

    def grad_copy(s, d):
        return send(
            grads_h.at[s, span(peer[d], shard)],
            grads_tok.at[s, :, span(me, 3 * width)],
            g_send.at[s, d],
            g_recv.at[s, d],
            {"sp": peer[d]},
        )

    for s in range(seqs):
        for d in range(1, ways):
            dmixed_copy(s, d).start()
    routed_back = exchange(others, result_ref, returned_ref, c_send, c_recv)
    for copy in routed_back[: others // 2 - 1]:
        copy.start()
    shards = shards_of(me, ways)
    size = up_land.shape[1]
    scatter = [
        send(
            part.at[i * size : (i + 1) * size],
            land.at[i - 1],
            s_send.at[j, i],
            s_recv.at[j, i],
            {"sp": shards[i]},
        )
        for j, (part, land) in enumerate(((up_part, up_land), (down_part, down_land)))
        for i in range(1, len(shards))
    ]
    sum_o = Reduction(ways, columns, part_o, out_o, scratch[:15])
    sum_w = Reduction(ways, columns, part_w, out_qkv, scratch[15:])

    def out_step(i, carry):
        at = span(i, BLOCK)
        left = mixed_ref[:, :, at].reshape(seqs * shard, BLOCK)
        part_o[at, :] = mxu(left, dattn_ref[...], COLS_BY_COLS).astype(jnp.bfloat16)
        return carry

    lax.fori_loop(0, model // BLOCK, out_step, 0)
    sum_o.core_copy.start()

    lane = lax.broadcasted_iota(jnp.int32, (1, width), 1) // head_dim
    visible = lax.broadcasted_iota(jnp.int32, (BLOCK, BLOCK), 0) <= lax.broadcasted_iota(
        jnp.int32, (BLOCK, BLOCK), 1
    )
    scale = head_dim ** (-0.5)
    for s in range(seqs):
        dmixed_h[s, span(me, shard), :] = dmixed_ref[s, :, span(me, width)]
        for d in range(1, ways):
            dmixed_copy(s, d).wait_recv()
        if s == 0:
            sum_o.add_core()
            for copy in scatter:
                copy.start()
        dq_f[...] = jnp.zeros_like(dq_f)
        dk_f[...] = jnp.zeros_like(dk_f)
        dv_f[...] = jnp.zeros_like(dv_f)

        def one_head(h, carry):
            mine = (lane == h).astype(jnp.float32)
            for at in range(0, seq_len, BLOCK):
                rows = slice(at, at + BLOCK)
                query = (q_ref[s, rows, :].astype(jnp.float32) * (mine * scale)).astype(
                    jnp.bfloat16
                )
                dout = (dmixed_h[s, rows, :].astype(jnp.float32) * mine).astype(jnp.bfloat16)
                log_row = log_ref[s, pl.ds(h, 1), rows]
                parts = [(rows, True)] + ([(slice(0, at), False)] if at else [])
                kept = []
                delta = jnp.zeros((1, BLOCK), jnp.float32)
                for keys, diagonal in parts:
                    prob = jnp.exp(mxu(k_ref[s, keys, :], query, ROWS_BY_ROWS) - log_row)
                    if diagonal:
                        prob = jnp.where(visible, prob, 0.0)
                    dprob = mxu(v_ref[s, keys, :], dout, ROWS_BY_ROWS)
                    delta += jnp.sum(prob * dprob, axis=0, keepdims=True)
                    kept.append((keys, prob, dprob))
                dquery = jnp.zeros((BLOCK, width), jnp.float32)
                for keys, prob, dprob in kept:
                    dv_f[keys, :] += mxu(prob.astype(jnp.bfloat16), dout)
                    dlogit = (prob * (dprob - delta)).astype(jnp.bfloat16)
                    dk_f[keys, :] += mxu(dlogit, query)
                    dquery += mxu(dlogit, k_ref[s, keys, :], COLS_BY_COLS)
                dq_f[rows, :] += dquery * (mine * scale)
            return carry

        lax.fori_loop(0, heads, one_head, 0)
        for i, total in enumerate((dq_f, dk_f, dv_f)):
            grads_h[s, :, i * width : (i + 1) * width] = total[...].astype(jnp.bfloat16)
        for d in range(1, ways):
            grad_copy(s, d).start()
        grads_tok[s, :, span(me, 3 * width)] = grads_h[s, span(me, shard), :]

    loads[0].wait()

    def weight_step(i, carry):
        at = span(i, BLOCK)
        grad = mxu(normed_v[0, :, at], grads_h[0], COLS_BY_COLS)
        for s in range(1, seqs):
            grad += mxu(normed_v[s, :, at], grads_h[s], COLS_BY_COLS)
        for j in range(3):
            rows = pl.ds(pl.multiple_of(j * model + i * BLOCK, BLOCK), BLOCK)
            part_w[rows, :] = grad[:, j * width : (j + 1) * width].astype(jnp.bfloat16)
        return carry

    lax.fori_loop(0, model // BLOCK, weight_step, 0)
    sum_w.core_copy.start()

    o_land[0] = sum_o.add_column().astype(jnp.bfloat16)
    o_copy = [
        send(
            o_land.at[0, :, span(peer[d], width)],
            o_land.at[d, :, 0:width],
            o_send.at[d],
            o_recv.at[d],
            {"sp": peer[d]},
        )
        for d in range(1, ways)
    ]
    for copy in o_copy:
        copy.start()
    sum_w.add_core()
    total = o_land[0, :, span(me, width)].astype(jnp.float32)
    for d, copy in enumerate(o_copy):
        copy.wait()
        total += o_land[d + 1, :, 0:width].astype(jnp.float32)
    sum_o.piece[...] = total.astype(jnp.bfloat16)
    sum_o.spread()
    sum_w.piece[...] = sum_w.add_column().astype(jnp.bfloat16)
    sum_w.spread()
    for copy in routed_back[others // 2 - 1 :]:
        copy.start()
    small_own[...] = small_ref[...]

    def norm_grad(s):
        for d in range(1, ways):
            grad_copy(s, d).wait()
        dnormed = jnp.zeros((shard, model), jnp.float32)
        for j in range(ways):
            for i in range(3):
                at = (3 * j + i) * width
                dnormed += mxu(
                    grads_tok[s, :, at : at + width],
                    weights_v[i, :, j * width : (j + 1) * width],
                    ROWS_BY_ROWS,
                )
        values = x_ref[s].astype(jnp.float32)
        gain = gain_ref[...]
        _, unit, rstd = norm_forward(values, gain, jnp.zeros_like(gain))
        dinput, gain_grad, shift_grad = norm_backward(dnormed, unit, rstd, gain)
        tokens_ref[s] = (dresid_ref[s] + dinput).astype(jnp.bfloat16)
        small_own[0:1, :] += gain_grad.reshape(1, model)
        small_own[1:2, :] += shift_grad.reshape(1, model)

    for copy in loads[1:4]:
        copy.wait()
    for s in range(seqs - 1):
        norm_grad(s)
    sum_o.ring()
    sum_w.ring()
    norm_grad(seqs - 1)

    steps = [[{"dp": dp + 1 - 2 * core}]]
    steps.append([{"dp": 2 * lax.rem(dp // 2 + d, columns) + core} for d in range(1, columns)])
    steps.append([{"sp": peer[d]} for d in range(1, ways)])
    slot = 0
    source = small_own
    for number, peers in enumerate(steps):
        copies = [
            send(
                source,
                small_land.at[slot + i],
                small_send.at[slot + i],
                small_recv.at[slot + i],
                device,
            )
            for i, device in enumerate(peers)
        ]
        for copy in copies:
            copy.start()
        if number == 0:
            sum_o.cross()
        total = source[...]
        for i, copy in enumerate(copies):
            copy.wait()
            total += small_land[slot + i]
        slot += len(peers)
        if number == len(steps) - 1:
            small_out[...] = total
        else:
            small_sum[number] = total
            source = small_sum.at[number]
    sum_w.cross()
    for s in range(seqs):
        for d in range(1, ways):
            dmixed_copy(s, d).wait_send()
    for copy in routed_back + scatter:
        copy.wait()
    loads[4].wait()
    sum_o.finish()
    sum_w.finish()


def vmem(count):
    return [pl.BlockSpec(memory_space=pltpu.VMEM)] * count


def params(collective_id):
    return pltpu.CompilerParams(
        collective_id=collective_id, has_side_effects=True, vmem_limit_bytes=VMEM_BYTES
    )


def dma(*shape):
    return pltpu.SemaphoreType.DMA(shape)


def local(
    tokens_in,
    expert_ids,
    query_weight,
    key_weight,
    value_weight,
    out_weight,
    norm1_gain,
    norm1_shift,
    norm2_gain,
    norm2_shift,
    up_weight,
    down_weight,
    out_cotangent,
    load_mean,
):
    seq_count, shard_len, model_width = tokens_in.shape
    row_count = seq_count * shard_len
    head_dim = model_width // HEADS
    dp_ways = lax.axis_size("dp")
    sp_ways = lax.axis_size("sp")
    sp_at = lax.axis_index("sp")
    seq_len = shard_len * sp_ways
    experts = load_mean.shape[0]
    slot_count = 2 * row_count // experts
    local_experts = up_weight.shape[0]
    ff_width = up_weight.shape[1]
    width = model_width // sp_ways
    bf16 = jnp.bfloat16
    f32 = jnp.float32

    def shape(*sizes, dtype=bf16):
        return jax.ShapeDtypeStruct(sizes, dtype)

    routes = expert_ids.reshape(row_count)
    one_hot = (routes[:, None] == jnp.arange(experts, dtype=jnp.int32)[None, :]).astype(jnp.int32)
    running = jnp.cumsum(one_hot, axis=0) - 1
    slot_of = jnp.sum(running * one_hot, axis=1)
    target = routes * slot_count + slot_of
    placer = (jnp.arange(experts * slot_count, dtype=jnp.int32)[:, None] == target[None, :]).astype(
        bf16
    )
    cot_b = out_cotangent.reshape(row_count, model_width)
    cot_send = jnp.dot(placer, cot_b, preferred_element_type=f32).astype(bf16)
    cot_send = cot_send.reshape(experts, slot_count, model_width)

    def columns_of(weight):
        return lax.dynamic_slice_in_dim(weight, sp_at * width, width, axis=1)

    routed = shape(experts, slot_count, model_width)
    hbm = [pl.BlockSpec(memory_space=pl.ANY)]
    normed_all, query_h, key_h, value_h, log_total, mixed_b, arrived = pl.pallas_call(
        functools.partial(attend_forward, sp_ways, dp_ways, head_dim),
        out_shape=[
            shape(seq_count, seq_len, model_width),
            shape(seq_count, seq_len, width),
            shape(seq_count, seq_len, width),
            shape(seq_count, seq_len, width),
            shape(seq_count, 8, seq_len, dtype=f32),
            shape(seq_count, shard_len, model_width),
            routed,
        ],
        in_specs=hbm + vmem(6),
        out_specs=vmem(6) + hbm,
        scratch_shapes=[
            pltpu.VMEM((seq_count, seq_len, model_width), bf16),
            pltpu.VMEM((seq_len, width), f32),
            pltpu.VMEM((seq_count, seq_len, width), bf16),
            pltpu.VMEM((seq_len, LANES), f32),
            dma(seq_count, sp_ways),
            dma(seq_count, sp_ways),
            dma(seq_count, sp_ways),
            dma(seq_count, sp_ways),
            dma(dp_ways),
            dma(dp_ways),
            pltpu.SemaphoreType.DMA,
        ],
        compiler_params=params(0),
    )(
        cot_send,
        tokens_in,
        columns_of(query_weight),
        columns_of(key_weight),
        columns_of(value_weight),
        norm1_gain.reshape(1, model_width),
        norm1_shift.reshape(1, model_width),
    )
    mixed_b = mixed_b.reshape(row_count, model_width)
    inputs = tokens_in.reshape(row_count, model_width).astype(f32)
    attn_out = jnp.dot(mixed_b, out_weight, preferred_element_type=f32)
    residual_stream = inputs + attn_out
    normed2, unit2, rstd2 = norm_forward(residual_stream, norm2_gain, norm2_shift)
    normed2_b = normed2.astype(bf16)
    outgoing = jnp.dot(placer, normed2_b, preferred_element_type=f32).astype(bf16)
    outgoing = outgoing.reshape(experts, slot_count, model_width)
    ff_own = ff_width // 2
    part = shape(ff_own, model_width)
    dnormed_back, expert_out, up_part, down_part = pl.pallas_call(
        functools.partial(run_experts, dp_ways, sp_ways),
        out_shape=[routed, routed, part, part],
        in_specs=vmem(1) + hbm * 3,
        out_specs=vmem(2) + hbm * 2,
        scratch_shapes=[
            pltpu.VMEM((2,) + routed.shape, bf16),
            pltpu.VMEM((2,) + routed.shape, bf16),
            pltpu.VMEM((ff_own, model_width), bf16),
            pltpu.VMEM((ff_own, model_width), bf16),
            pltpu.VMEM((2 * experts * slot_count, ff_own), bf16),
            pltpu.VMEM((2 * experts * slot_count, ff_own), bf16),
            pltpu.VMEM((2 * slot_count, model_width), f32),
            pltpu.VMEM(routed.shape, f32),
            pltpu.VMEM(routed.shape, bf16),
            pltpu.VMEM(routed.shape, bf16),
            pltpu.VMEM(routed.shape, bf16),
            pltpu.VMEM(routed.shape, bf16),
            pltpu.VMEM(routed.shape, bf16),
            dma(2, sp_ways // 2),
            dma(2),
            pltpu.SemaphoreType.DMA,
            dma(dp_ways),
            dma(dp_ways),
            dma(dp_ways),
            dma(dp_ways),
            dma(dp_ways // 2 + 1),
            dma(dp_ways // 2 + 1),
            dma(dp_ways // 2 + 1),
            dma(dp_ways // 2 + 1),
        ],
        compiler_params=params(3),
    )(outgoing, arrived, up_weight[0], down_weight[0])
    dnormed2 = jnp.einsum(
        "er,ed->rd",
        placer,
        dnormed_back.reshape(experts * slot_count, model_width),
        preferred_element_type=f32,
    )
    dresid_norm, gain_two_grad, shift_two_grad = norm_backward(dnormed2, unit2, rstd2, norm2_gain)
    dresid = cot_b.astype(f32) + dresid_norm
    dattn_b = dresid.astype(bf16)
    dmixed_b = jnp.einsum("re,de->rd", dattn_b, out_weight, preferred_element_type=f32)
    counts = jnp.sum(one_hot, axis=0).astype(f32)
    counts = jnp.pad(counts, (0, model_width - experts))
    zeros = jnp.zeros((model_width,), f32)
    small = jnp.stack([zeros, zeros, gain_two_grad, shift_two_grad, counts, zeros, zeros, zeros])
    columns = dp_ways // 2
    rows_o, rows_w = model_width // dp_ways, 3 * model_width // dp_ways
    landing = shape(sp_ways // 2 - 1, ff_width // sp_ways, model_width)
    token_shape = (seq_count, shard_len, model_width)

    def reduction(rows, part_width):
        return [
            pltpu.VMEM((columns * rows, part_width), bf16),
            pltpu.VMEM((columns * rows, part_width), bf16),
            pltpu.VMEM((columns - 1, rows, part_width), bf16),
            pltpu.VMEM((rows, width), bf16),
            pltpu.SemaphoreType.DMA,
            pltpu.SemaphoreType.DMA,
            dma(columns),
            dma(columns),
            dma(columns),
            dma(columns),
            dma(sp_ways),
            dma(sp_ways),
            dma(sp_ways),
            dma(sp_ways),
            pltpu.SemaphoreType.DMA,
        ]

    small_slots = 1 + (columns - 1) + (sp_ways - 1)
    out_qkv, out_o, returned, up_land, down_land, tokens_grad, small_sum = pl.pallas_call(
        functools.partial(backward, sp_ways, dp_ways, head_dim),
        out_shape=[
            shape(3 * model_width, model_width),
            shape(model_width, model_width),
            routed,
            landing,
            landing,
            shape(*token_shape),
            shape(8, model_width, dtype=f32),
        ],
        in_specs=hbm * 7 + vmem(11),
        out_specs=hbm * 5 + vmem(2),
        scratch_shapes=[
            pltpu.VMEM((seq_count, seq_len, width), bf16),
            pltpu.VMEM((seq_len, width), f32),
            pltpu.VMEM((seq_len, width), f32),
            pltpu.VMEM((seq_len, width), f32),
            pltpu.VMEM((seq_count, seq_len, 3 * width), bf16),
            pltpu.VMEM((seq_count, shard_len, 3 * model_width), bf16),
            pltpu.VMEM((seq_count, seq_len, model_width), bf16),
            pltpu.VMEM((3, model_width, model_width), bf16),
            pltpu.VMEM((model_width, model_width), bf16),
            pltpu.VMEM((3 * model_width, width), bf16),
            pltpu.VMEM((sp_ways, rows_o, model_width), bf16),
            pltpu.VMEM((8, model_width), f32),
            pltpu.VMEM((small_slots, 8, model_width), f32),
            pltpu.VMEM((2, 8, model_width), f32),
            dma(seq_count, sp_ways),
            dma(seq_count, sp_ways),
            dma(seq_count, sp_ways),
            dma(seq_count, sp_ways),
            dma(dp_ways),
            dma(dp_ways),
            dma(2, sp_ways // 2),
            dma(2, sp_ways // 2),
            dma(sp_ways),
            dma(sp_ways),
            dma(small_slots),
            dma(small_slots),
            dma(5),
        ]
        + reduction(rows_o, model_width)
        + reduction(rows_w, width),
        compiler_params=params(1),
    )(
        expert_out,
        up_part,
        down_part,
        normed_all,
        query_weight,
        key_weight,
        value_weight,
        dmixed_b.astype(bf16).reshape(token_shape),
        mixed_b.reshape(token_shape),
        dattn_b,
        query_h,
        key_h,
        value_h,
        log_total,
        tokens_in,
        dresid.reshape(token_shape),
        norm1_gain.reshape(1, model_width),
        small,
    )
    up_grad, down_grad = (
        (part[: ff_width // sp_ways].astype(f32) + jnp.sum(land.astype(f32), axis=0))[None]
        for part, land in ((up_part, up_land), (down_part, down_land))
    )
    expert_rows = jnp.einsum(
        "er,ed->rd",
        placer,
        returned.reshape(experts * slot_count, model_width),
        preferred_element_type=f32,
    )
    block_out = (residual_stream + expert_rows).astype(bf16)
    block_out = block_out.reshape(token_shape)
    query_grad, key_grad, value_grad = (
        out_qkv[i * model_width : (i + 1) * model_width].astype(f32) for i in range(3)
    )
    out_grad = out_o.astype(f32)
    load_now = small_sum[4, :experts] * experts / (row_count * dp_ways * sp_ways)
    load_next = 0.9 * load_mean + 0.1 * load_now
    return (
        block_out,
        tokens_grad,
        query_grad,
        key_grad,
        value_grad,
        out_grad,
        small_sum[0],
        small_sum[1],
        small_sum[2],
        small_sum[3],
        up_grad,
        down_grad,
        load_next,
    )


def solution(mesh):
    return jax.shard_map(
        local,
        mesh=mesh,
        in_specs=(
            P("dp", "sp", None),
            P("dp", "sp", None, None),
            P(),
            P(),
            P(),
            P(),
            P(),
            P(),
            P(),
            P(),
            P("dp", None, None),
            P("dp", None, None),
            P("dp", "sp", None),
            P(),
        ),
        out_specs=(
            P("dp", "sp", None),
            P("dp", "sp", None),
            P(),
            P(),
            P(),
            P(),
            P(),
            P(),
            P(),
            P(),
            P("dp", "sp", None),
            P("dp", "sp", None),
            P(),
        ),
        check_vma=False,
    )
```

```python
import functools

import jax
import jax.numpy as jnp
from jax import lax
from jax.experimental import pallas as pl
from jax.experimental.pallas import tpu as pltpu
from jax.sharding import PartitionSpec as P

HEADS = 16
MESH = pl.DeviceIdType.MESH
BLOCK = 256
LANES = 128
STEP = 512
VMEM_BYTES = 60 * 2**20

NORM_EPSILON = 1e-05
GELU_ROOT = 0.7978845608028654
CUBIC_TERM = 0.044715

ROWS_BY_COLS = (((1,), (0,)), ((), ()))
ROWS_BY_ROWS = (((1,), (1,)), ((), ()))
COLS_BY_COLS = (((0,), (0,)), ((), ()))


def smooth(values):
    return (
        0.5
        * values
        * (1.0 + jnp.tanh(GELU_ROOT * (values + CUBIC_TERM * values * values * values)))
    )


def smooth_slope(values):
    inner = jnp.tanh(GELU_ROOT * (values + CUBIC_TERM * values * values * values))
    return 0.5 * (1.0 + inner) + 0.5 * values * (1.0 - inner * inner) * GELU_ROOT * (
        1.0 + 3.0 * CUBIC_TERM * values * values
    )


def norm_forward(values, gain, shift):
    center = jnp.mean(values, axis=-1, keepdims=True)
    offset = values - center
    rstd = lax.rsqrt(jnp.mean(offset * offset, axis=-1, keepdims=True) + NORM_EPSILON)
    unit = offset * rstd
    return (unit * gain + shift, unit, rstd)


def norm_backward(grad, unit, rstd, gain):
    scaled = grad * gain
    inner = (
        scaled
        - jnp.mean(scaled, axis=-1, keepdims=True)
        - unit * jnp.mean(scaled * unit, axis=-1, keepdims=True)
    )
    return (inner * rstd, jnp.sum(grad * unit, axis=0), jnp.sum(grad, axis=0))


def mxu(left, right, dims=ROWS_BY_COLS):
    return lax.dot_general(left, right, dims, preferred_element_type=jnp.float32)


def span(index, size):
    return pl.ds(pl.multiple_of(index * size, size), size)


def greet(peers):
    barrier = pltpu.get_barrier_semaphore()
    for peer in peers:
        pl.semaphore_signal(barrier, inc=1, device_id=peer, device_id_type=MESH)
    pl.semaphore_wait(barrier, len(peers))


def send(source, target, send_sem, recv_sem, peer):
    return pltpu.make_async_remote_copy(
        src_ref=source,
        dst_ref=target,
        send_sem=send_sem,
        recv_sem=recv_sem,
        device_id=peer,
        device_id_type=MESH,
    )


def exchange(others, source, target, send_sem, recv_sem):
    me = lax.axis_index("dp")
    return [
        send(
            source.at[flip(me, d)],
            target.at[me],
            send_sem.at[d],
            recv_sem.at[d],
            {"dp": flip(me, d)},
        )
        for d in range(1, others)
    ]


def flip(index, bits):
    bit = 1
    while bit <= bits:
        if bits & bit:
            index = index + bit - 2 * bit * lax.rem(index // bit, 2)
        bit *= 2
    return index


def attend_forward(
    ways,
    others,
    head_dim,
    cot_ref,
    x_ref,
    wq_ref,
    wk_ref,
    wv_ref,
    gain_ref,
    shift_ref,
    normed_ref,
    q_ref,
    k_ref,
    v_ref,
    log_ref,
    mixed_ref,
    arrived_ref,
    x_all,
    mixed_f,
    mixed_h,
    log_s,
    x_send,
    x_recv,
    m_send,
    m_recv,
    c_send,
    c_recv,
    local_sem,
):
    seqs, shard, _ = x_ref.shape
    seq_len, width = q_ref.shape[1:]
    heads = width // head_dim
    me = lax.axis_index("sp")
    peer = [lax.rem(me + d, ways) for d in range(ways)]
    origin = [lax.rem(me + ways - d, ways) for d in range(ways)]
    greet(
        [{"sp": peer[d]} for d in range(1, ways)]
        + [{"dp": flip(lax.axis_index("dp"), d)} for d in range(1, others)]
    )
    background = exchange(others, cot_ref, arrived_ref, c_send, c_recv)
    own = pltpu.make_async_copy(
        cot_ref.at[lax.axis_index("dp")], arrived_ref.at[lax.axis_index("dp")], local_sem
    )

    def x_copy(s, d):
        return send(
            x_ref.at[s],
            x_all.at[s, span(me, shard)],
            x_send.at[s, d],
            x_recv.at[s, d],
            {"sp": peer[d]},
        )

    def mixed_copy(s, d):
        return send(
            mixed_h.at[s, span(peer[d], shard)],
            mixed_ref.at[s, :, span(me, width)],
            m_send.at[s, d],
            m_recv.at[s, d],
            {"sp": peer[d]},
        )

    lane = lax.broadcasted_iota(jnp.int32, (1, width), 1) // head_dim
    log_lane = lax.broadcasted_iota(jnp.int32, (1, LANES), 1)
    visible = lax.broadcasted_iota(jnp.int32, (BLOCK, BLOCK), 1) <= lax.broadcasted_iota(
        jnp.int32, (BLOCK, BLOCK), 0
    )
    scale = head_dim ** (-0.5)

    def project(s, rows, values):
        normed, _, _ = norm_forward(values.astype(jnp.float32), gain_ref[...], shift_ref[...])
        normed = normed.astype(jnp.bfloat16)
        normed_ref[s, rows, :] = normed
        q_ref[s, rows, :] = mxu(normed, wq_ref[...]).astype(jnp.bfloat16)
        k_ref[s, rows, :] = mxu(normed, wk_ref[...]).astype(jnp.bfloat16)
        v_ref[s, rows, :] = mxu(normed, wv_ref[...]).astype(jnp.bfloat16)

    for d in range(1, ways):
        x_copy(0, d).start()
    own.start()
    for copy in background:
        copy.start()
    for s in range(seqs):
        project(s, span(me, shard), x_ref[s])
        for d in range(1, ways):
            x_copy(s, d).wait_recv()
            if d == ways - 1 and s + 1 < seqs:
                for later in range(1, ways):
                    x_copy(s + 1, later).start()
            rows = span(origin[d], shard)
            project(s, rows, x_all[s, rows, :])
        mixed_f[...] = jnp.zeros_like(mixed_f)
        log_s[...] = jnp.zeros_like(log_s)

        def one_head(h, carry):
            mine = (lane == h).astype(jnp.float32)
            for at in range(0, seq_len, BLOCK):
                rows = slice(at, at + BLOCK)
                query = (q_ref[s, rows, :].astype(jnp.float32) * (mine * scale)).astype(
                    jnp.bfloat16
                )
                near = mxu(query, k_ref[s, rows, :], ROWS_BY_ROWS)
                near = jnp.where(visible, near, -1e30)
                top = jnp.max(near, axis=1, keepdims=True)
                if at:
                    far = mxu(query, k_ref[s, :at, :], ROWS_BY_ROWS)
                    top = jnp.maximum(top, jnp.max(far, axis=1, keepdims=True))
                near = jnp.exp(near - top)
                total = jnp.sum(near, axis=1, keepdims=True)
                if at:
                    far = jnp.exp(far - top)
                    total += jnp.sum(far, axis=1, keepdims=True)
                inverse = 1.0 / total
                out = mxu((near * inverse).astype(jnp.bfloat16), v_ref[s, rows, :])
                if at:
                    out += mxu((far * inverse).astype(jnp.bfloat16), v_ref[s, :at, :])
                mixed_f[rows, :] += out * mine
                log_s[rows, :] = jnp.where(log_lane == h, top + jnp.log(total), log_s[rows, :])
            return carry

        lax.fori_loop(0, heads, one_head, 0)
        log_ref[s] = jnp.transpose(log_s[...])[: log_ref.shape[1], :]
        mixed_h[s] = mixed_f[...].astype(jnp.bfloat16)
        for d in range(1, ways):
            mixed_copy(s, d).start()
        mixed_ref[s, :, span(me, width)] = mixed_h[s, span(me, shard), :]
    for s in range(seqs):
        for d in range(1, ways):
            x_copy(s, d).wait_send()
            mixed_copy(s, d).wait()
    own.wait()
    for copy in background:
        copy.wait()


def pair_of(sp):
    core = lax.rem(lax.axis_index("dp"), 2)
    along_x, along_y = flip(sp, 1), flip(sp, 2)
    return along_x + core * (along_y - along_x)


def shards_of(sp, ways):
    shards = [sp, flip(pair_of(sp), 3)]
    bit = 4
    while bit < ways:
        shards += [flip(shard, bit) for shard in shards]
        bit *= 2
    return shards


def run_experts(
    others,
    ways,
    outgoing_ref,
    cot_ref,
    up_ref,
    down_ref,
    back_ref,
    result_ref,
    up_part,
    down_part,
    up_land,
    received,
    arrived,
    up_v,
    down_v,
    hidden,
    slope_v,
    total,
    dn_own,
    dn_pair,
    dn_land,
    dnormed,
    out_pair,
    out_land,
    w_sem,
    o_sem,
    c_sem,
    a_send,
    a_recv,
    b_send,
    b_recv,
    f_send,
    f_recv,
    p_send,
    p_recv,
    s_send,
    s_recv,
):
    slots, width = received.shape[1:]
    rows = others * slots
    ff = up_v.shape[0]
    groups = others // 2
    me = lax.axis_index("dp")
    sp = lax.axis_index("sp")
    chip = me // 2
    pair = {"sp": pair_of(sp)}
    shards = shards_of(sp, ways)
    size = ff // len(shards)
    loads = [
        pltpu.make_async_copy(
            source.at[span(shard, size)], target.at[i * size : (i + 1) * size], w_sem.at[j, i]
        )
        for j, (source, target) in enumerate(((down_ref, down_v), (up_ref, up_v)))
        for i, shard in enumerate(shards)
    ]
    own_cot = pltpu.make_async_copy(cot_ref, arrived.at[0], c_sem)
    own_cot.start()
    for copy in loads:
        copy.start()
    greet(
        [{"dp": flip(me, d)} for d in range(1, others)]
        + [pair]
        + [{"sp": shard} for shard in shards[1:]]
    )
    inward = exchange(others, outgoing_ref, received.at[0:others], a_send, a_recv)
    outward = exchange(others, dnormed, back_ref, b_send, b_recv)
    near = [flip(chip, group) for group in range(groups)]
    chips = [pl.ds(2 * near[group], 2) for group in range(groups)]
    forward = [
        send(
            received.at[chips[group]],
            received.at[pl.ds(others + 2 * near[group], 2)],
            f_send.at[group],
            f_recv.at[group],
            pair,
        )
        for group in range(groups)
    ]
    cot_copy = send(cot_ref, arrived.at[1], f_send.at[groups], f_recv.at[groups], pair)
    dn_copy = [
        send(
            dn_pair.at[chips[group]],
            dn_land.at[chips[group]],
            p_send.at[group],
            p_recv.at[group],
            pair,
        )
        for group in range(groups)
    ]
    out_copy = send(out_pair, out_land, p_send.at[groups], p_recv.at[groups], pair)

    early = range(groups // 2)
    middle = range(groups // 2, 3 * groups // 4)
    late = range(3 * groups // 4, groups)
    for copy in inward[: 2 * late[0] - 1]:
        copy.start()
    received[me] = outgoing_ref[me]
    cot_copy.start()

    def slab_of(half, group):
        return pl.ds(pl.multiple_of(half * rows + near[group] * (2 * slots), 2 * slots), 2 * slots)

    def cot_half(half):
        def cot_step(i, carry):
            at = span(i, STEP)
            cot = arrived[half].reshape(rows, width)
            slope_v[half * rows : (half + 1) * rows, at] = mxu(
                cot, down_v[at, :], ROWS_BY_ROWS
            ).astype(jnp.bfloat16)
            return carry

        lax.fori_loop(0, ff // STEP, cot_step, 0)

    def up_half(half, group):
        slab = slab_of(half, group)
        total[...] = jnp.zeros_like(total)

        def up_step(i, carry):
            at = span(i, STEP)
            tokens = received[pl.ds(half * others + 2 * near[group], 2)].reshape(2 * slots, width)
            pre = mxu(tokens, up_v[at, :], ROWS_BY_ROWS)
            square = pre * pre
            inner = jnp.tanh(GELU_ROOT * pre * (1.0 + CUBIC_TERM * square))
            gate = 0.5 * (1.0 + inner)
            hidden[slab, at] = (pre * gate).astype(jnp.bfloat16)
            slope = gate + (0.5 * GELU_ROOT) * pre * (1.0 - inner * inner) * (
                1.0 + (3.0 * CUBIC_TERM) * square
            )
            dpre = (slope_v[slab, at].astype(jnp.float32) * slope).astype(jnp.bfloat16)
            slope_v[slab, at] = dpre
            total[...] += mxu(dpre, up_v[at, :])
            return carry

        lax.fori_loop(0, ff // STEP, up_step, 0)
        shaped = total[...].reshape(2, slots, width)
        if half:
            dn_pair[chips[group]] = shaped.astype(jnp.bfloat16)
            dn_copy[group].start()
        else:
            dn_own[chips[group]] = shaped

    def pass_on(group):
        for d in (2 * group, 2 * group + 1):
            if d:
                inward[d - 1].wait_recv()
        forward[group].start()

    def finish(group):
        dn_copy[group].wait_recv()
        at = chips[group]
        dnormed[at] = (dn_own[at] + dn_land[at].astype(jnp.float32)).astype(jnp.bfloat16)
        for d in (2 * group, 2 * group + 1):
            if d:
                outward[d - 1].start()
            else:
                back_ref[me] = dnormed[me]

    def up_pair(group):
        forward[group].wait_recv()
        up_half(1, group)

    pass_on(0)
    own_cot.wait()
    for copy in loads[: len(shards)]:
        copy.wait()
    cot_half(0)
    for copy in loads[len(shards) :]:
        copy.wait()
    up_half(0, 0)
    for group in early[1:]:
        pass_on(group)
    for copy in inward[2 * middle[0] - 1 : 2 * late[0] - 1]:
        copy.wait_send()
    for copy in inward[2 * late[0] - 1 :]:
        copy.start()
    cot_copy.wait_recv()
    cot_half(1)
    for group in middle:
        pass_on(group)
    up_pair(0)
    for group in early[1:]:
        up_half(0, group)
        up_pair(group)
    for group in middle:
        up_half(0, group)
    for group in early:
        finish(group)
    for group in middle:
        up_pair(group)
    for group in late:
        pass_on(group)
        up_half(0, group)
    for group in middle:
        finish(group)
    for group in late:
        up_pair(group)

    def out_half(half):
        def out_step(i, carry):
            slab = pl.ds(pl.multiple_of(half * rows + i * (2 * slots), 2 * slots), 2 * slots)
            out = mxu(hidden[slab, :], down_v[...]).reshape(2, slots, width)
            at = pl.ds(2 * i, 2)
            if half:
                out_pair[at] = out.astype(jnp.bfloat16)
            else:
                result_ref[at] = (out + out_land[at].astype(jnp.float32)).astype(jnp.bfloat16)
            return carry

        lax.fori_loop(0, groups, out_step, 0)

    def grad(target, left, right_ref, block=0):
        def grad_step(i, carry):
            at = span(i, STEP)
            right = right_ref[...].reshape(2 * rows, width)
            out = mxu(left[:, at], right, COLS_BY_COLS).astype(jnp.bfloat16)
            if block:
                target[span(i, STEP // block)] = out.reshape(STEP // block, block, width)
            else:
                target[at, :] = out
            return carry

        lax.fori_loop(0, ff // STEP, grad_step, 0)

    out_half(1)
    out_copy.start()
    for group in late:
        finish(group)
    grad(up_v, slope_v, received.at[0 : 2 * others])
    store_up = pltpu.make_async_copy(up_v.at[0:size], up_part, o_sem.at[0])
    store_up.start()
    scatter = [
        send(
            up_v.at[i * size : (i + 1) * size],
            up_land.at[i - 1],
            s_send.at[i],
            s_recv.at[i],
            {"sp": shards[i]},
        )
        for i in range(1, len(shards))
    ]
    for copy in scatter:
        copy.start()
    for copy in forward:
        copy.wait_send()
    grad(received, hidden, arrived, slots)
    down_g = received.at[0 : ff // slots]
    store_down = pltpu.make_async_copy(down_g, down_part, o_sem.at[1])
    store_down.start()
    out_copy.wait_recv()
    out_half(0)
    for copy in inward[: 2 * middle[0] - 1] + inward[2 * late[0] - 1 :]:
        copy.wait_send()
    for copy in [cot_copy] + dn_copy + [out_copy]:
        copy.wait_send()
    for copy in outward + scatter:
        copy.wait()
    store_up.wait()
    store_down.wait()


class Reduction:
    def __init__(self, ways, columns, part, out, scratch):
        (
            self.core_land,
            self.core_sum,
            self.column_land,
            self.piece,
            core_send,
            core_recv,
            column_send,
            column_recv,
            spread_send,
            spread_recv,
            ring_send,
            ring_recv,
            cross_send,
            cross_recv,
            own_sem,
        ) = scratch
        me = lax.axis_index("sp")
        dp = lax.axis_index("dp")
        core = lax.rem(dp, 2)
        column = dp // 2
        twin = {"dp": dp + 1 - 2 * core}
        self.ways, self.columns, self.part = ways, columns, part
        self.core, self.column = core, column
        rows, width = self.piece.shape
        self.rows = rows

        def beside(d):
            return {"dp": 2 * lax.rem(column + d, columns) + core}

        def block(at_core, at_column, at_sp, count):
            first = pl.multiple_of((at_core * columns + at_column) * rows, rows)
            return out.at[pl.ds(first, count * rows), span(at_sp, width)]

        self.core_copy = send(
            part.at[span(1 - core, columns * rows)], self.core_land, core_send, core_recv, twin
        )
        self.column_copy = [
            send(
                self.core_sum.at[span(lax.rem(column + d, columns), rows)],
                self.column_land.at[d - 1],
                column_send.at[d],
                column_recv.at[d],
                beside(d),
            )
            for d in range(1, columns)
        ]
        spot = block(core, column, me, 1)
        self.own = pltpu.make_async_copy(self.piece, spot, own_sem)
        self.spread_copy = [
            send(self.piece, spot, spread_send.at[d], spread_recv.at[d], beside(d))
            for d in range(1, columns)
        ]
        half = [block(core, 0, lax.rem(me + ways - d, ways), columns) for d in range(ways)]
        self.ring_copy = [
            send(
                half[0],
                half[0],
                ring_send.at[d],
                ring_recv.at[d],
                {"sp": lax.rem(me + d, ways)},
            )
            for d in range(1, ways)
        ]
        self.cross_copy = [
            send(half[d], half[d], cross_send.at[d], cross_recv.at[d], twin) for d in range(ways)
        ]

    def add_core(self):
        self.core_copy.wait()
        self.core_sum[...] = (
            self.part[span(self.core, self.columns * self.rows), :].astype(jnp.float32)
            + self.core_land[...].astype(jnp.float32)
        ).astype(jnp.bfloat16)
        for copy in self.column_copy:
            copy.start()

    def add_column(self):
        total = self.core_sum[span(self.column, self.rows), :].astype(jnp.float32)
        for d, copy in enumerate(self.column_copy):
            copy.wait()
            total += self.column_land[d].astype(jnp.float32)
        return total

    def spread(self):
        self.own.start()
        for copy in self.spread_copy:
            copy.start()

    def ring(self):
        self.own.wait()
        for copy in self.spread_copy:
            copy.wait()
        for copy in self.ring_copy:
            copy.start()
        self.cross_copy[0].start()

    def cross(self):
        for ring, cross in zip(self.ring_copy, self.cross_copy[1:]):
            ring.wait_recv()
            cross.start()

    def finish(self):
        for copy in self.ring_copy:
            copy.wait_send()
        for copy in self.cross_copy:
            copy.wait()


def backward(
    ways,
    others,
    head_dim,
    result_ref,
    down_part,
    normed_ref,
    wq_ref,
    wk_ref,
    wv_ref,
    dmixed_ref,
    mixed_ref,
    dattn_ref,
    q_ref,
    k_ref,
    v_ref,
    log_ref,
    x_ref,
    dresid_ref,
    gain_ref,
    small_ref,
    out_qkv,
    out_o,
    returned_ref,
    down_land,
    tokens_ref,
    small_out,
    dmixed_h,
    dq_f,
    dk_f,
    dv_f,
    grads_h,
    grads_tok,
    normed_v,
    weights_v,
    part_o,
    part_w,
    o_land,
    small_own,
    small_land,
    small_sum,
    m_send,
    m_recv,
    g_send,
    g_recv,
    c_send,
    c_recv,
    s_send,
    s_recv,
    o_send,
    o_recv,
    small_send,
    small_recv,
    load_sem,
    *scratch,
):
    seqs, shard, model = dmixed_ref.shape
    seq_len, width = q_ref.shape[1:]
    heads = width // head_dim
    columns = others // 2
    me = lax.axis_index("sp")
    dp = lax.axis_index("dp")
    core = lax.rem(dp, 2)
    peer = [lax.rem(me + d, ways) for d in range(ways)]
    loads = [
        pltpu.make_async_copy(source, target, load_sem.at[i])
        for i, (source, target) in enumerate(
            [(normed_ref, normed_v)]
            + [(source, weights_v.at[i]) for i, source in enumerate((wq_ref, wk_ref, wv_ref))]
            + [(result_ref.at[dp], returned_ref.at[dp])]
        )
    ]
    for copy in loads:
        copy.start()
    greet(
        [{"sp": peer[d]} for d in range(1, ways)]
        + [{"dp": flip(dp, d)} for d in range(1, others)]
    )

    def dmixed_copy(s, d):
        return send(
            dmixed_ref.at[s, :, span(peer[d], width)],
            dmixed_h.at[s, span(me, shard)],
            m_send.at[s, d],
            m_recv.at[s, d],
            {"sp": peer[d]},
        )

    def grad_copy(s, d):
        return send(
            grads_h.at[s, span(peer[d], shard)],
            grads_tok.at[s, :, span(me, 3 * width)],
            g_send.at[s, d],
            g_recv.at[s, d],
            {"sp": peer[d]},
        )

    for s in range(seqs):
        for d in range(1, ways):
            dmixed_copy(s, d).start()
    routed_back = exchange(others, result_ref, returned_ref, c_send, c_recv)
    for copy in routed_back[: others // 2 - 1]:
        copy.start()
    shards = shards_of(me, ways)
    size = down_part.shape[0] // len(shards)
    scatter = [
        send(
            down_part.at[i * size : (i + 1) * size],
            down_land.at[i - 1],
            s_send.at[i],
            s_recv.at[i],
            {"sp": shards[i]},
        )
        for i in range(1, len(shards))
    ]
    sum_o = Reduction(ways, columns, part_o, out_o, scratch[:15])
    sum_w = Reduction(ways, columns, part_w, out_qkv, scratch[15:])

    def out_step(i, carry):
        at = span(i, BLOCK)
        left = mixed_ref[:, :, at].reshape(seqs * shard, BLOCK)
        part_o[at, :] = mxu(left, dattn_ref[...], COLS_BY_COLS).astype(jnp.bfloat16)
        return carry

    lax.fori_loop(0, model // BLOCK, out_step, 0)
    sum_o.core_copy.start()

    lane = lax.broadcasted_iota(jnp.int32, (1, width), 1) // head_dim
    visible = lax.broadcasted_iota(jnp.int32, (BLOCK, BLOCK), 0) <= lax.broadcasted_iota(
        jnp.int32, (BLOCK, BLOCK), 1
    )
    scale = head_dim ** (-0.5)
    for s in range(seqs):
        dmixed_h[s, span(me, shard), :] = dmixed_ref[s, :, span(me, width)]
        for d in range(1, ways):
            dmixed_copy(s, d).wait_recv()
        if s == 0:
            sum_o.add_core()
            for copy in scatter:
                copy.start()
        dq_f[...] = jnp.zeros_like(dq_f)
        dk_f[...] = jnp.zeros_like(dk_f)
        dv_f[...] = jnp.zeros_like(dv_f)

        def one_head(h, carry):
            mine = (lane == h).astype(jnp.float32)
            for at in range(0, seq_len, BLOCK):
                rows = slice(at, at + BLOCK)
                query = (q_ref[s, rows, :].astype(jnp.float32) * (mine * scale)).astype(
                    jnp.bfloat16
                )
                dout = (dmixed_h[s, rows, :].astype(jnp.float32) * mine).astype(jnp.bfloat16)
                log_row = log_ref[s, pl.ds(h, 1), rows]
                parts = [(rows, True)] + ([(slice(0, at), False)] if at else [])
                kept = []
                delta = jnp.zeros((1, BLOCK), jnp.float32)
                for keys, diagonal in parts:
                    prob = jnp.exp(mxu(k_ref[s, keys, :], query, ROWS_BY_ROWS) - log_row)
                    if diagonal:
                        prob = jnp.where(visible, prob, 0.0)
                    dprob = mxu(v_ref[s, keys, :], dout, ROWS_BY_ROWS)
                    delta += jnp.sum(prob * dprob, axis=0, keepdims=True)
                    kept.append((keys, prob, dprob))
                dquery = jnp.zeros((BLOCK, width), jnp.float32)
                for keys, prob, dprob in kept:
                    dv_f[keys, :] += mxu(prob.astype(jnp.bfloat16), dout)
                    dlogit = (prob * (dprob - delta)).astype(jnp.bfloat16)
                    dk_f[keys, :] += mxu(dlogit, query)
                    dquery += mxu(dlogit, k_ref[s, keys, :], COLS_BY_COLS)
                dq_f[rows, :] += dquery * (mine * scale)
            return carry

        lax.fori_loop(0, heads, one_head, 0)
        for i, total in enumerate((dq_f, dk_f, dv_f)):
            grads_h[s, :, i * width : (i + 1) * width] = total[...].astype(jnp.bfloat16)
        for d in range(1, ways):
            grad_copy(s, d).start()
        grads_tok[s, :, span(me, 3 * width)] = grads_h[s, span(me, shard), :]

    loads[0].wait()

    def weight_step(i, carry):
        at = span(i, BLOCK)
        grad = mxu(normed_v[0, :, at], grads_h[0], COLS_BY_COLS)
        for s in range(1, seqs):
            grad += mxu(normed_v[s, :, at], grads_h[s], COLS_BY_COLS)
        for j in range(3):
            rows = pl.ds(pl.multiple_of(j * model + i * BLOCK, BLOCK), BLOCK)
            part_w[rows, :] = grad[:, j * width : (j + 1) * width].astype(jnp.bfloat16)
        return carry

    lax.fori_loop(0, model // BLOCK, weight_step, 0)
    sum_w.core_copy.start()

    o_land[0] = sum_o.add_column().astype(jnp.bfloat16)
    o_copy = [
        send(
            o_land.at[0, :, span(peer[d], width)],
            o_land.at[d, :, 0:width],
            o_send.at[d],
            o_recv.at[d],
            {"sp": peer[d]},
        )
        for d in range(1, ways)
    ]
    for copy in o_copy:
        copy.start()
    sum_w.add_core()
    total = o_land[0, :, span(me, width)].astype(jnp.float32)
    for d, copy in enumerate(o_copy):
        copy.wait()
        total += o_land[d + 1, :, 0:width].astype(jnp.float32)
    sum_o.piece[...] = total.astype(jnp.bfloat16)
    sum_o.spread()
    sum_w.piece[...] = sum_w.add_column().astype(jnp.bfloat16)
    sum_w.spread()
    for copy in routed_back[others // 2 - 1 :]:
        copy.start()
    small_own[...] = small_ref[...]

    def norm_grad(s):
        for d in range(1, ways):
            grad_copy(s, d).wait()
        dnormed = jnp.zeros((shard, model), jnp.float32)
        for j in range(ways):
            for i in range(3):
                at = (3 * j + i) * width
                dnormed += mxu(
                    grads_tok[s, :, at : at + width],
                    weights_v[i, :, j * width : (j + 1) * width],
                    ROWS_BY_ROWS,
                )
        values = x_ref[s].astype(jnp.float32)
        gain = gain_ref[...]
        _, unit, rstd = norm_forward(values, gain, jnp.zeros_like(gain))
        dinput, gain_grad, shift_grad = norm_backward(dnormed, unit, rstd, gain)
        tokens_ref[s] = (dresid_ref[s] + dinput).astype(jnp.bfloat16)
        small_own[0:1, :] += gain_grad.reshape(1, model)
        small_own[1:2, :] += shift_grad.reshape(1, model)

    for copy in loads[1:4]:
        copy.wait()
    for s in range(seqs - 1):
        norm_grad(s)
    sum_o.ring()
    sum_w.ring()
    norm_grad(seqs - 1)

    steps = [[{"dp": dp + 1 - 2 * core}]]
    steps.append([{"dp": 2 * lax.rem(dp // 2 + d, columns) + core} for d in range(1, columns)])
    steps.append([{"sp": peer[d]} for d in range(1, ways)])
    slot = 0
    source = small_own
    for number, peers in enumerate(steps):
        copies = [
            send(
                source,
                small_land.at[slot + i],
                small_send.at[slot + i],
                small_recv.at[slot + i],
                device,
            )
            for i, device in enumerate(peers)
        ]
        for copy in copies:
            copy.start()
        if number == 0:
            sum_o.cross()
        total = source[...]
        for i, copy in enumerate(copies):
            copy.wait()
            total += small_land[slot + i]
        slot += len(peers)
        if number == len(steps) - 1:
            small_out[...] = total
        else:
            small_sum[number] = total
            source = small_sum.at[number]
    sum_w.cross()
    for s in range(seqs):
        for d in range(1, ways):
            dmixed_copy(s, d).wait_send()
    for copy in routed_back + scatter:
        copy.wait()
    loads[4].wait()
    sum_o.finish()
    sum_w.finish()


def vmem(count):
    return [pl.BlockSpec(memory_space=pltpu.VMEM)] * count


def params(collective_id):
    return pltpu.CompilerParams(
        collective_id=collective_id, has_side_effects=True, vmem_limit_bytes=VMEM_BYTES
    )


def dma(*shape):
    return pltpu.SemaphoreType.DMA(shape)


def local(
    tokens_in,
    expert_ids,
    query_weight,
    key_weight,
    value_weight,
    out_weight,
    norm1_gain,
    norm1_shift,
    norm2_gain,
    norm2_shift,
    up_weight,
    down_weight,
    out_cotangent,
    load_mean,
):
    seq_count, shard_len, model_width = tokens_in.shape
    row_count = seq_count * shard_len
    head_dim = model_width // HEADS
    dp_ways = lax.axis_size("dp")
    sp_ways = lax.axis_size("sp")
    sp_at = lax.axis_index("sp")
    seq_len = shard_len * sp_ways
    experts = load_mean.shape[0]
    slot_count = 2 * row_count // experts
    local_experts = up_weight.shape[0]
    ff_width = up_weight.shape[1]
    width = model_width // sp_ways
    bf16 = jnp.bfloat16
    f32 = jnp.float32

    def shape(*sizes, dtype=bf16):
        return jax.ShapeDtypeStruct(sizes, dtype)

    routes = expert_ids.reshape(row_count)
    one_hot = (routes[:, None] == jnp.arange(experts, dtype=jnp.int32)[None, :]).astype(jnp.int32)
    running = jnp.cumsum(one_hot, axis=0) - 1
    slot_of = jnp.sum(running * one_hot, axis=1)
    target = routes * slot_count + slot_of
    placer = (jnp.arange(experts * slot_count, dtype=jnp.int32)[:, None] == target[None, :]).astype(
        bf16
    )
    cot_b = out_cotangent.reshape(row_count, model_width)
    cot_send = jnp.dot(placer, cot_b, preferred_element_type=f32).astype(bf16)
    cot_send = cot_send.reshape(experts, slot_count, model_width)

    def columns_of(weight):
        return lax.dynamic_slice_in_dim(weight, sp_at * width, width, axis=1)

    routed = shape(experts, slot_count, model_width)
    hbm = [pl.BlockSpec(memory_space=pl.ANY)]
    normed_all, query_h, key_h, value_h, log_total, mixed_b, arrived = pl.pallas_call(
        functools.partial(attend_forward, sp_ways, dp_ways, head_dim),
        out_shape=[
            shape(seq_count, seq_len, model_width),
            shape(seq_count, seq_len, width),
            shape(seq_count, seq_len, width),
            shape(seq_count, seq_len, width),
            shape(seq_count, 8, seq_len, dtype=f32),
            shape(seq_count, shard_len, model_width),
            routed,
        ],
        in_specs=hbm + vmem(6),
        out_specs=vmem(6) + hbm,
        scratch_shapes=[
            pltpu.VMEM((seq_count, seq_len, model_width), bf16),
            pltpu.VMEM((seq_len, width), f32),
            pltpu.VMEM((seq_count, seq_len, width), bf16),
            pltpu.VMEM((seq_len, LANES), f32),
            dma(seq_count, sp_ways),
            dma(seq_count, sp_ways),
            dma(seq_count, sp_ways),
            dma(seq_count, sp_ways),
            dma(dp_ways),
            dma(dp_ways),
            pltpu.SemaphoreType.DMA,
        ],
        compiler_params=params(0),
    )(
        cot_send,
        tokens_in,
        columns_of(query_weight),
        columns_of(key_weight),
        columns_of(value_weight),
        norm1_gain.reshape(1, model_width),
        norm1_shift.reshape(1, model_width),
    )
    mixed_b = mixed_b.reshape(row_count, model_width)
    inputs = tokens_in.reshape(row_count, model_width).astype(f32)
    attn_out = jnp.dot(mixed_b, out_weight, preferred_element_type=f32)
    residual_stream = inputs + attn_out
    normed2, unit2, rstd2 = norm_forward(residual_stream, norm2_gain, norm2_shift)
    normed2_b = normed2.astype(bf16)
    outgoing = jnp.dot(placer, normed2_b, preferred_element_type=f32).astype(bf16)
    outgoing = outgoing.reshape(experts, slot_count, model_width)
    ff_own = ff_width // 2
    received_blocks = max(2 * experts, ff_own // slot_count)
    part = shape(ff_own // slot_count, slot_count, model_width)
    landing = shape(sp_ways // 2 - 1, ff_width // sp_ways, model_width)
    down_landing = shape(sp_ways // 2 - 1, part.shape[0] * 2 // sp_ways, slot_count, model_width)
    own_part = shape(ff_width // sp_ways, model_width)
    dnormed_back, expert_out, up_part, down_part, up_land = pl.pallas_call(
        functools.partial(run_experts, dp_ways, sp_ways),
        out_shape=[routed, routed, own_part, part, landing],
        in_specs=vmem(1) + hbm * 3,
        out_specs=vmem(2) + hbm * 3,
        scratch_shapes=[
            pltpu.VMEM((received_blocks, slot_count, model_width), bf16),
            pltpu.VMEM((2,) + routed.shape, bf16),
            pltpu.VMEM((ff_own, model_width), bf16),
            pltpu.VMEM((ff_own, model_width), bf16),
            pltpu.VMEM((2 * experts * slot_count, ff_own), bf16),
            pltpu.VMEM((2 * experts * slot_count, ff_own), bf16),
            pltpu.VMEM((2 * slot_count, model_width), f32),
            pltpu.VMEM(routed.shape, f32),
            pltpu.VMEM(routed.shape, bf16),
            pltpu.VMEM(routed.shape, bf16),
            pltpu.VMEM(routed.shape, bf16),
            pltpu.VMEM(routed.shape, bf16),
            pltpu.VMEM(routed.shape, bf16),
            dma(2, sp_ways // 2),
            dma(2),
            pltpu.SemaphoreType.DMA,
            dma(dp_ways),
            dma(dp_ways),
            dma(dp_ways),
            dma(dp_ways),
            dma(dp_ways // 2 + 1),
            dma(dp_ways // 2 + 1),
            dma(dp_ways // 2 + 1),
            dma(dp_ways // 2 + 1),
            dma(sp_ways // 2),
            dma(sp_ways // 2),
        ],
        compiler_params=params(3),
    )(outgoing, arrived, up_weight[0], down_weight[0])
    dnormed2 = jnp.einsum(
        "er,ed->rd",
        placer,
        dnormed_back.reshape(experts * slot_count, model_width),
        preferred_element_type=f32,
    )
    dresid_norm, gain_two_grad, shift_two_grad = norm_backward(dnormed2, unit2, rstd2, norm2_gain)
    dresid = cot_b.astype(f32) + dresid_norm
    dattn_b = dresid.astype(bf16)
    dmixed_b = jnp.einsum("re,de->rd", dattn_b, out_weight, preferred_element_type=f32)
    counts = jnp.sum(one_hot, axis=0).astype(f32)
    counts = jnp.pad(counts, (0, model_width - experts))
    zeros = jnp.zeros((model_width,), f32)
    small = jnp.stack([zeros, zeros, gain_two_grad, shift_two_grad, counts, zeros, zeros, zeros])
    columns = dp_ways // 2
    rows_o, rows_w = model_width // dp_ways, 3 * model_width // dp_ways
    token_shape = (seq_count, shard_len, model_width)

    def reduction(rows, part_width):
        return [
            pltpu.VMEM((columns * rows, part_width), bf16),
            pltpu.VMEM((columns * rows, part_width), bf16),
            pltpu.VMEM((columns - 1, rows, part_width), bf16),
            pltpu.VMEM((rows, width), bf16),
            pltpu.SemaphoreType.DMA,
            pltpu.SemaphoreType.DMA,
            dma(columns),
            dma(columns),
            dma(columns),
            dma(columns),
            dma(sp_ways),
            dma(sp_ways),
            dma(sp_ways),
            dma(sp_ways),
            pltpu.SemaphoreType.DMA,
        ]

    small_slots = 1 + (columns - 1) + (sp_ways - 1)
    out_qkv, out_o, returned, down_land, tokens_grad, small_sum = pl.pallas_call(
        functools.partial(backward, sp_ways, dp_ways, head_dim),
        out_shape=[
            shape(3 * model_width, model_width),
            shape(model_width, model_width),
            routed,
            down_landing,
            shape(*token_shape),
            shape(8, model_width, dtype=f32),
        ],
        in_specs=hbm * 6 + vmem(11),
        out_specs=hbm * 4 + vmem(2),
        scratch_shapes=[
            pltpu.VMEM((seq_count, seq_len, width), bf16),
            pltpu.VMEM((seq_len, width), f32),
            pltpu.VMEM((seq_len, width), f32),
            pltpu.VMEM((seq_len, width), f32),
            pltpu.VMEM((seq_count, seq_len, 3 * width), bf16),
            pltpu.VMEM((seq_count, shard_len, 3 * model_width), bf16),
            pltpu.VMEM((seq_count, seq_len, model_width), bf16),
            pltpu.VMEM((3, model_width, model_width), bf16),
            pltpu.VMEM((model_width, model_width), bf16),
            pltpu.VMEM((3 * model_width, width), bf16),
            pltpu.VMEM((sp_ways, rows_o, model_width), bf16),
            pltpu.VMEM((8, model_width), f32),
            pltpu.VMEM((small_slots, 8, model_width), f32),
            pltpu.VMEM((2, 8, model_width), f32),
            dma(seq_count, sp_ways),
            dma(seq_count, sp_ways),
            dma(seq_count, sp_ways),
            dma(seq_count, sp_ways),
            dma(dp_ways),
            dma(dp_ways),
            dma(sp_ways // 2),
            dma(sp_ways // 2),
            dma(sp_ways),
            dma(sp_ways),
            dma(small_slots),
            dma(small_slots),
            dma(5),
        ]
        + reduction(rows_o, model_width)
        + reduction(rows_w, width),
        compiler_params=params(1),
    )(
        expert_out,
        down_part,
        normed_all,
        query_weight,
        key_weight,
        value_weight,
        dmixed_b.astype(bf16).reshape(token_shape),
        mixed_b.reshape(token_shape),
        dattn_b,
        query_h,
        key_h,
        value_h,
        log_total,
        tokens_in,
        dresid.reshape(token_shape),
        norm1_gain.reshape(1, model_width),
        small,
    )
    down_part = down_part.reshape(ff_own, model_width)[: ff_width // sp_ways]
    up_grad, down_grad = (
        (part.astype(f32) + jnp.sum(land.reshape(landing.shape).astype(f32), axis=0))[None]
        for part, land in ((up_part, up_land), (down_part, down_land))
    )
    expert_rows = jnp.einsum(
        "er,ed->rd",
        placer,
        returned.reshape(experts * slot_count, model_width),
        preferred_element_type=f32,
    )
    block_out = (residual_stream + expert_rows).astype(bf16)
    block_out = block_out.reshape(token_shape)
    query_grad, key_grad, value_grad = (
        out_qkv[i * model_width : (i + 1) * model_width].astype(f32) for i in range(3)
    )
    out_grad = out_o.astype(f32)
    load_now = small_sum[4, :experts] * experts / (row_count * dp_ways * sp_ways)
    load_next = 0.9 * load_mean + 0.1 * load_now
    return (
        block_out,
        tokens_grad,
        query_grad,
        key_grad,
        value_grad,
        out_grad,
        small_sum[0],
        small_sum[1],
        small_sum[2],
        small_sum[3],
        up_grad,
        down_grad,
        load_next,
    )


def solution(mesh):
    return jax.shard_map(
        local,
        mesh=mesh,
        in_specs=(
            P("dp", "sp", None),
            P("dp", "sp", None, None),
            P(),
            P(),
            P(),
            P(),
            P(),
            P(),
            P(),
            P(),
            P("dp", None, None),
            P("dp", None, None),
            P("dp", "sp", None),
            P(),
        ),
        out_specs=(
            P("dp", "sp", None),
            P("dp", "sp", None),
            P(),
            P(),
            P(),
            P(),
            P(),
            P(),
            P(),
            P(),
            P("dp", "sp", None),
            P("dp", "sp", None),
            P(),
        ),
        check_vma=False,
    )
```

```python
import functools

import jax
import jax.numpy as jnp
from jax import lax
from jax.experimental import pallas as pl
from jax.experimental.pallas import tpu as pltpu
from jax.sharding import PartitionSpec as P

HEADS = 16
MESH = pl.DeviceIdType.MESH
BLOCK = 256
LANES = 128
STEP = 512
VMEM_BYTES = 60 * 2**20

NORM_EPSILON = 1e-05
GELU_ROOT = 0.7978845608028654
CUBIC_TERM = 0.044715

ROWS_BY_COLS = (((1,), (0,)), ((), ()))
ROWS_BY_ROWS = (((1,), (1,)), ((), ()))
COLS_BY_COLS = (((0,), (0,)), ((), ()))


def smooth(values):
    return (
        0.5
        * values
        * (1.0 + jnp.tanh(GELU_ROOT * (values + CUBIC_TERM * values * values * values)))
    )


def smooth_slope(values):
    inner = jnp.tanh(GELU_ROOT * (values + CUBIC_TERM * values * values * values))
    return 0.5 * (1.0 + inner) + 0.5 * values * (1.0 - inner * inner) * GELU_ROOT * (
        1.0 + 3.0 * CUBIC_TERM * values * values
    )


def norm_forward(values, gain, shift):
    center = jnp.mean(values, axis=-1, keepdims=True)
    offset = values - center
    rstd = lax.rsqrt(jnp.mean(offset * offset, axis=-1, keepdims=True) + NORM_EPSILON)
    unit = offset * rstd
    return (unit * gain + shift, unit, rstd)


def norm_backward(grad, unit, rstd, gain):
    scaled = grad * gain
    inner = (
        scaled
        - jnp.mean(scaled, axis=-1, keepdims=True)
        - unit * jnp.mean(scaled * unit, axis=-1, keepdims=True)
    )
    return (inner * rstd, jnp.sum(grad * unit, axis=0), jnp.sum(grad, axis=0))


def mxu(left, right, dims=ROWS_BY_COLS):
    return lax.dot_general(left, right, dims, preferred_element_type=jnp.float32)


def span(index, size):
    return pl.ds(pl.multiple_of(index * size, size), size)


def greet(peers):
    barrier = pltpu.get_barrier_semaphore()
    for peer in peers:
        pl.semaphore_signal(barrier, inc=1, device_id=peer, device_id_type=MESH)
    pl.semaphore_wait(barrier, len(peers))


def send(source, target, send_sem, recv_sem, peer):
    return pltpu.make_async_remote_copy(
        src_ref=source,
        dst_ref=target,
        send_sem=send_sem,
        recv_sem=recv_sem,
        device_id=peer,
        device_id_type=MESH,
    )


def exchange(others, source, target, send_sem, recv_sem):
    me = lax.axis_index("dp")
    return [
        send(
            source.at[flip(me, d)],
            target.at[me],
            send_sem.at[d],
            recv_sem.at[d],
            {"dp": flip(me, d)},
        )
        for d in range(1, others)
    ]


def flip(index, bits):
    bit = 1
    while bit <= bits:
        if bits & bit:
            index = index + bit - 2 * bit * lax.rem(index // bit, 2)
        bit *= 2
    return index


def attend_forward(
    ways,
    others,
    head_dim,
    cot_ref,
    x_ref,
    wq_ref,
    wk_ref,
    wv_ref,
    gain_ref,
    shift_ref,
    normed_ref,
    q_ref,
    k_ref,
    v_ref,
    log_ref,
    mixed_ref,
    arrived_ref,
    x_all,
    mixed_f,
    mixed_h,
    log_s,
    x_send,
    x_recv,
    m_send,
    m_recv,
    c_send,
    c_recv,
    local_sem,
):
    seqs, shard, _ = x_ref.shape
    seq_len, width = q_ref.shape[1:]
    heads = width // head_dim
    me = lax.axis_index("sp")
    peer = [lax.rem(me + d, ways) for d in range(ways)]
    origin = [lax.rem(me + ways - d, ways) for d in range(ways)]
    greet(
        [{"sp": peer[d]} for d in range(1, ways)]
        + [{"dp": flip(lax.axis_index("dp"), d)} for d in range(1, others)]
    )
    background = exchange(others, cot_ref, arrived_ref, c_send, c_recv)
    own = pltpu.make_async_copy(
        cot_ref.at[lax.axis_index("dp")], arrived_ref.at[lax.axis_index("dp")], local_sem
    )

    def x_copy(s, d):
        return send(
            x_ref.at[s],
            x_all.at[s, span(me, shard)],
            x_send.at[s, d],
            x_recv.at[s, d],
            {"sp": peer[d]},
        )

    def mixed_copy(s, d):
        return send(
            mixed_h.at[s, span(peer[d], shard)],
            mixed_ref.at[s, :, span(me, width)],
            m_send.at[s, d],
            m_recv.at[s, d],
            {"sp": peer[d]},
        )

    lane = lax.broadcasted_iota(jnp.int32, (1, width), 1) // head_dim
    log_lane = lax.broadcasted_iota(jnp.int32, (1, LANES), 1)
    visible = lax.broadcasted_iota(jnp.int32, (BLOCK, BLOCK), 1) <= lax.broadcasted_iota(
        jnp.int32, (BLOCK, BLOCK), 0
    )
    scale = head_dim ** (-0.5)

    def project(s, rows, values):
        normed, _, _ = norm_forward(values.astype(jnp.float32), gain_ref[...], shift_ref[...])
        normed = normed.astype(jnp.bfloat16)
        normed_ref[s, rows, :] = normed
        q_ref[s, rows, :] = mxu(normed, wq_ref[...]).astype(jnp.bfloat16)
        k_ref[s, rows, :] = mxu(normed, wk_ref[...]).astype(jnp.bfloat16)
        v_ref[s, rows, :] = mxu(normed, wv_ref[...]).astype(jnp.bfloat16)

    for d in range(1, ways):
        x_copy(0, d).start()
    own.start()
    for copy in background:
        copy.start()
    for s in range(seqs):
        project(s, span(me, shard), x_ref[s])
        for d in range(1, ways):
            x_copy(s, d).wait_recv()
            if d == ways - 1 and s + 1 < seqs:
                for later in range(1, ways):
                    x_copy(s + 1, later).start()
            rows = span(origin[d], shard)
            project(s, rows, x_all[s, rows, :])
        mixed_f[...] = jnp.zeros_like(mixed_f)
        log_s[...] = jnp.zeros_like(log_s)

        def one_head(h, carry):
            mine = (lane == h).astype(jnp.float32)
            for at in range(0, seq_len, BLOCK):
                rows = slice(at, at + BLOCK)
                query = (q_ref[s, rows, :].astype(jnp.float32) * (mine * scale)).astype(
                    jnp.bfloat16
                )
                near = mxu(query, k_ref[s, rows, :], ROWS_BY_ROWS)
                near = jnp.where(visible, near, -1e30)
                top = jnp.max(near, axis=1, keepdims=True)
                if at:
                    far = mxu(query, k_ref[s, :at, :], ROWS_BY_ROWS)
                    top = jnp.maximum(top, jnp.max(far, axis=1, keepdims=True))
                near = jnp.exp(near - top)
                total = jnp.sum(near, axis=1, keepdims=True)
                if at:
                    far = jnp.exp(far - top)
                    total += jnp.sum(far, axis=1, keepdims=True)
                inverse = 1.0 / total
                out = mxu((near * inverse).astype(jnp.bfloat16), v_ref[s, rows, :])
                if at:
                    out += mxu((far * inverse).astype(jnp.bfloat16), v_ref[s, :at, :])
                mixed_f[rows, :] += out * mine
                log_s[rows, :] = jnp.where(log_lane == h, top + jnp.log(total), log_s[rows, :])
            return carry

        lax.fori_loop(0, heads, one_head, 0)
        log_ref[s] = jnp.transpose(log_s[...])[: log_ref.shape[1], :]
        mixed_h[s] = mixed_f[...].astype(jnp.bfloat16)
        for d in range(1, ways):
            mixed_copy(s, d).start()
        mixed_ref[s, :, span(me, width)] = mixed_h[s, span(me, shard), :]
    for s in range(seqs):
        for d in range(1, ways):
            x_copy(s, d).wait_send()
            mixed_copy(s, d).wait()
    own.wait()
    for copy in background:
        copy.wait()


def pair_of(sp):
    core = lax.rem(lax.axis_index("dp"), 2)
    along_x, along_y = flip(sp, 1), flip(sp, 2)
    return along_x + core * (along_y - along_x)


def shards_of(sp, ways):
    shards = [sp, flip(pair_of(sp), 3)]
    bit = 4
    while bit < ways:
        shards += [flip(shard, bit) for shard in shards]
        bit *= 2
    return shards


def run_experts(
    others,
    ways,
    outgoing_ref,
    cot_ref,
    up_ref,
    down_ref,
    back_ref,
    result_ref,
    up_part,
    down_part,
    up_land,
    received,
    arrived,
    up_v,
    down_v,
    hidden,
    slope_v,
    total,
    dn_own,
    dn_pair,
    dn_land,
    dnormed,
    out_pair,
    out_land,
    w_sem,
    o_sem,
    c_sem,
    a_send,
    a_recv,
    b_send,
    b_recv,
    f_send,
    f_recv,
    p_send,
    p_recv,
    s_send,
    s_recv,
):
    slots, width = received.shape[1:]
    rows = others * slots
    ff = up_v.shape[0]
    groups = others // 2
    me = lax.axis_index("dp")
    sp = lax.axis_index("sp")
    chip = me // 2
    pair = {"sp": pair_of(sp)}
    shards = shards_of(sp, ways)
    size = ff // len(shards)
    loads = [
        pltpu.make_async_copy(
            source.at[span(shard, size)], target.at[i * size : (i + 1) * size], w_sem.at[j, i]
        )
        for j, (source, target) in enumerate(((down_ref, down_v), (up_ref, up_v)))
        for i, shard in enumerate(shards)
    ]
    own_cot = pltpu.make_async_copy(cot_ref, arrived.at[0], c_sem)
    own_cot.start()
    for copy in loads:
        copy.start()
    greet(
        [{"dp": flip(me, d)} for d in range(1, others)]
        + [pair]
        + [{"sp": shard} for shard in shards[1:]]
    )
    inward = exchange(others, outgoing_ref, received.at[0:others], a_send, a_recv)
    outward = exchange(others, dnormed, back_ref, b_send, b_recv)
    near = [flip(chip, group) for group in range(groups)]
    chips = [pl.ds(2 * near[group], 2) for group in range(groups)]
    forward = [
        send(
            received.at[chips[group]],
            received.at[pl.ds(others + 2 * near[group], 2)],
            f_send.at[group],
            f_recv.at[group],
            pair,
        )
        for group in range(groups)
    ]
    cot_copy = send(cot_ref, arrived.at[1], f_send.at[groups], f_recv.at[groups], pair)
    dn_copy = [
        send(
            dn_pair.at[chips[group]],
            dn_land.at[chips[group]],
            p_send.at[group],
            p_recv.at[group],
            pair,
        )
        for group in range(groups)
    ]
    out_copy = send(out_pair, out_land, p_send.at[groups], p_recv.at[groups], pair)

    early = range(groups // 2)
    middle = range(groups // 2, 3 * groups // 4)
    late = range(3 * groups // 4, groups)
    for copy in inward[: 2 * late[0] - 1]:
        copy.start()
    received[me] = outgoing_ref[me]
    cot_copy.start()

    def slab_of(half, group):
        return pl.ds(pl.multiple_of(half * rows + near[group] * (2 * slots), 2 * slots), 2 * slots)

    def cot_half(half):
        def cot_step(i, carry):
            at = span(i, STEP)
            cot = arrived[half].reshape(rows, width)
            slope_v[half * rows : (half + 1) * rows, at] = mxu(
                cot, down_v[at, :], ROWS_BY_ROWS
            ).astype(jnp.bfloat16)
            return carry

        lax.fori_loop(0, ff // STEP, cot_step, 0)

    def up_half(half, group):
        slab = slab_of(half, group)
        total[...] = jnp.zeros_like(total)

        def up_step(i, carry):
            at = span(i, STEP)
            tokens = received[pl.ds(half * others + 2 * near[group], 2)].reshape(2 * slots, width)
            pre = mxu(tokens, up_v[at, :], ROWS_BY_ROWS)
            square = pre * pre
            inner = jnp.tanh(GELU_ROOT * pre * (1.0 + CUBIC_TERM * square))
            gate = 0.5 * (1.0 + inner)
            hidden[slab, at] = (pre * gate).astype(jnp.bfloat16)
            slope = gate + (0.5 * GELU_ROOT) * pre * (1.0 - inner * inner) * (
                1.0 + (3.0 * CUBIC_TERM) * square
            )
            dpre = (slope_v[slab, at].astype(jnp.float32) * slope).astype(jnp.bfloat16)
            slope_v[slab, at] = dpre
            total[...] += mxu(dpre, up_v[at, :])
            return carry

        lax.fori_loop(0, ff // STEP, up_step, 0)
        shaped = total[...].reshape(2, slots, width)
        if half:
            dn_pair[chips[group]] = shaped.astype(jnp.bfloat16)
            dn_copy[group].start()
        else:
            dn_own[chips[group]] = shaped

    def pass_on(group):
        for d in (2 * group, 2 * group + 1):
            if d:
                inward[d - 1].wait_recv()
        forward[group].start()

    def finish(group):
        dn_copy[group].wait_recv()
        at = chips[group]
        dnormed[at] = (dn_own[at] + dn_land[at].astype(jnp.float32)).astype(jnp.bfloat16)
        for d in (2 * group, 2 * group + 1):
            if d:
                outward[d - 1].start()
            else:
                back_ref[me] = dnormed[me]

    def up_pair(group):
        forward[group].wait_recv()
        up_half(1, group)

    pass_on(0)
    own_cot.wait()
    for copy in loads[: len(shards)]:
        copy.wait()
    cot_half(0)
    for copy in loads[len(shards) :]:
        copy.wait()
    up_half(0, 0)
    for group in early[1:]:
        pass_on(group)
    for copy in inward[2 * middle[0] - 1 : 2 * late[0] - 1]:
        copy.wait_send()
    for copy in inward[2 * late[0] - 1 :]:
        copy.start()
    cot_copy.wait_recv()
    cot_half(1)
    for group in middle:
        pass_on(group)
    up_pair(0)
    for group in early[1:]:
        up_half(0, group)
        up_pair(group)
    for group in middle:
        up_half(0, group)
    for group in early:
        finish(group)
    for group in middle:
        up_pair(group)
    for group in late:
        pass_on(group)
        up_half(0, group)
    for group in middle:
        finish(group)
    for group in late:
        up_pair(group)

    def out_half(half):
        def out_step(i, carry):
            slab = pl.ds(pl.multiple_of(half * rows + i * (2 * slots), 2 * slots), 2 * slots)
            out = mxu(hidden[slab, :], down_v[...]).reshape(2, slots, width)
            at = pl.ds(2 * i, 2)
            if half:
                out_pair[at] = out.astype(jnp.bfloat16)
            else:
                result_ref[at] = (out + out_land[at].astype(jnp.float32)).astype(jnp.bfloat16)
            return carry

        lax.fori_loop(0, groups, out_step, 0)

    def grad(target, left, right_ref, block=0):
        def grad_step(i, carry):
            at = span(i, STEP)
            right = right_ref[...].reshape(2 * rows, width)
            out = mxu(left[:, at], right, COLS_BY_COLS).astype(jnp.bfloat16)
            if block:
                target[span(i, STEP // block)] = out.reshape(STEP // block, block, width)
            else:
                target[at, :] = out
            return carry

        lax.fori_loop(0, ff // STEP, grad_step, 0)

    out_half(1)
    out_copy.start()
    for group in late:
        finish(group)
    grad(up_v, slope_v, received.at[0 : 2 * others])
    store_up = pltpu.make_async_copy(up_v.at[0:size], up_part, o_sem.at[0])
    store_up.start()
    scatter = [
        send(
            up_v.at[i * size : (i + 1) * size],
            up_land.at[i - 1],
            s_send.at[i],
            s_recv.at[i],
            {"sp": shards[i]},
        )
        for i in range(1, len(shards))
    ]
    for copy in scatter:
        copy.start()
    for copy in forward:
        copy.wait_send()
    grad(received, hidden, arrived, slots)
    down_g = received.at[0 : ff // slots]
    store_down = pltpu.make_async_copy(down_g, down_part, o_sem.at[1])
    store_down.start()
    out_copy.wait_recv()
    out_half(0)
    for copy in inward[: 2 * middle[0] - 1] + inward[2 * late[0] - 1 :]:
        copy.wait_send()
    for copy in [cot_copy] + dn_copy + [out_copy]:
        copy.wait_send()
    for copy in outward + scatter:
        copy.wait()
    store_up.wait()
    store_down.wait()


class Reduction:
    def __init__(self, ways, columns, part, out, scratch):
        (
            self.core_land,
            self.core_sum,
            self.column_land,
            self.piece,
            core_send,
            core_recv,
            column_send,
            column_recv,
            spread_send,
            spread_recv,
            ring_send,
            ring_recv,
            cross_send,
            cross_recv,
            own_sem,
        ) = scratch
        me = lax.axis_index("sp")
        dp = lax.axis_index("dp")
        core = lax.rem(dp, 2)
        column = dp // 2
        twin = {"dp": dp + 1 - 2 * core}
        self.ways, self.columns, self.part = ways, columns, part
        self.core, self.column = core, column
        rows, width = self.piece.shape
        self.rows = rows

        def beside(d):
            return {"dp": 2 * lax.rem(column + d, columns) + core}

        def block(at_core, at_column, at_sp, count):
            first = pl.multiple_of((at_core * columns + at_column) * rows, rows)
            return out.at[pl.ds(first, count * rows), span(at_sp, width)]

        self.core_copy = send(
            part.at[span(1 - core, columns * rows)], self.core_land, core_send, core_recv, twin
        )
        self.column_copy = [
            send(
                self.core_sum.at[span(lax.rem(column + d, columns), rows)],
                self.column_land.at[d - 1],
                column_send.at[d],
                column_recv.at[d],
                beside(d),
            )
            for d in range(1, columns)
        ]
        spot = block(core, column, me, 1)
        self.own = pltpu.make_async_copy(self.piece, spot, own_sem)
        self.spread_copy = [
            send(self.piece, spot, spread_send.at[d], spread_recv.at[d], beside(d))
            for d in range(1, columns)
        ]
        origin = [flip(me, d) for d in range(ways)]
        half = [block(core, 0, at, columns) for at in origin]
        self.relays = []
        direct = range(1, ways)
        if ways == 4:
            direct = (1, 2)
            count = columns * rows // 2
            for i, (d, to) in enumerate(((1, 2), (2, 1))):
                first = pl.multiple_of(core * columns * rows + i * count, count)
                piece = out.at[pl.ds(first, count), span(origin[d], width)]
                self.relays.append(
                    send(piece, piece, ring_send.at[i], ring_recv.at[i], {"sp": origin[to]})
                )
            ring_send, ring_recv = ring_send.at[1:ways], ring_recv.at[1:ways]
        self.ring_copy = [
            send(half[0], half[0], ring_send.at[d], ring_recv.at[d], {"sp": origin[d]})
            for d in direct
        ]
        self.cross_copy = [
            send(half[d], half[d], cross_send.at[d], cross_recv.at[d], twin) for d in range(ways)
        ]

    def add_core(self):
        self.core_copy.wait()
        self.core_sum[...] = (
            self.part[span(self.core, self.columns * self.rows), :].astype(jnp.float32)
            + self.core_land[...].astype(jnp.float32)
        ).astype(jnp.bfloat16)
        for copy in self.column_copy:
            copy.start()

    def add_column(self):
        total = self.core_sum[span(self.column, self.rows), :].astype(jnp.float32)
        for d, copy in enumerate(self.column_copy):
            copy.wait()
            total += self.column_land[d].astype(jnp.float32)
        return total

    def spread(self):
        self.own.start()
        for copy in self.spread_copy:
            copy.start()

    def ring(self):
        self.own.wait()
        for copy in self.spread_copy:
            copy.wait()
        for copy in self.ring_copy:
            copy.start()
        self.cross_copy[0].start()

    def relay(self):
        for ring, cross in zip(self.ring_copy, self.cross_copy[1:]):
            ring.wait_recv()
            cross.start()
        for relay in self.relays:
            relay.start()

    def cross(self):
        for relay in self.relays:
            relay.wait_recv()
        if self.relays:
            self.cross_copy[3].start()

    def finish(self):
        for copy in self.ring_copy + self.relays:
            copy.wait_send()
        for copy in self.cross_copy:
            copy.wait()


def backward(
    ways,
    others,
    head_dim,
    back_ref,
    placer_ref,
    cot_ref,
    residual_ref,
    wo_ref,
    mixed_ref,
    q_ref,
    k_ref,
    v_ref,
    normed_ref,
    wq_ref,
    wk_ref,
    wv_ref,
    x_ref,
    result_ref,
    down_part,
    log_ref,
    gain1_ref,
    gain2_ref,
    counts_ref,
    out_q,
    out_k,
    out_v,
    out_o,
    down_land,
    block_ref,
    tokens_ref,
    small_out,
    back_v,
    placer_v,
    cot_v,
    residual_v,
    wo_v,
    mixed_v,
    q_v,
    k_v,
    v_v,
    normed_v,
    wq_v,
    wk_v,
    wv_v,
    x_v,
    returned,
    dresid,
    dattn,
    dmixed,
    dmixed_h,
    dq_f,
    dk_f,
    dv_f,
    grads_h,
    grads_tok,
    part_o,
    parts_w,
    o_land,
    small_own,
    small_land,
    small_sum,
    m_send,
    m_recv,
    g_send,
    g_recv,
    c_send,
    c_recv,
    s_send,
    s_recv,
    o_send,
    o_recv,
    small_send,
    small_recv,
    load_sem,
    *scratch,
):
    seqs, shard, model = x_v.shape
    seq_len, width = q_v.shape[1:]
    heads = width // head_dim
    columns = others // 2
    me = lax.axis_index("sp")
    dp = lax.axis_index("dp")
    core = lax.rem(dp, 2)
    peer = [lax.rem(me + d, ways) for d in range(ways)]
    barrier = pltpu.get_barrier_semaphore()
    neighbours = [{"sp": peer[d]} for d in range(1, ways)]
    neighbours += [{"dp": flip(dp, d)} for d in range(1, others)]
    for device in neighbours:
        pl.semaphore_signal(barrier, inc=1, device_id=device, device_id_type=MESH)
    sources = (
        (back_ref, back_v),
        (placer_ref, placer_v),
        (residual_ref, residual_v),
        (cot_ref, cot_v),
        (wo_ref, wo_v),
        (mixed_ref, mixed_v),
        (q_ref, q_v),
        (k_ref, k_v),
        (v_ref, v_v),
        (normed_ref, normed_v),
        (wq_ref, wq_v),
        (wk_ref, wk_v),
        (wv_ref, wv_v),
        (x_ref, x_v),
        (result_ref.at[dp], returned.at[dp]),
    )
    loads = [
        pltpu.make_async_copy(source, target, load_sem.at[i])
        for i, (source, target) in enumerate(sources)
    ]
    for copy in loads:
        copy.start()

    def dmixed_copy(s, d):
        return send(
            dmixed.at[s, :, span(peer[d], width)],
            dmixed_h.at[s, span(me, shard)],
            m_send.at[s, d],
            m_recv.at[s, d],
            {"sp": peer[d]},
        )

    def grad_copy(s, d):
        return send(
            grads_h.at[s, span(peer[d], shard)],
            grads_tok.at[s, :, span(me, 3 * width)],
            g_send.at[s, d],
            g_recv.at[s, d],
            {"sp": peer[d]},
        )

    small_own[...] = jnp.zeros_like(small_own)
    small_own[4:5, :] = counts_ref[...]
    for s in range(seqs):
        if s == 0:
            for copy in loads[:4]:
                copy.wait()
        rows = slice(s * shard, (s + 1) * shard)
        dnormed = mxu(placer_v[:, rows], back_v[...].reshape(-1, model), COLS_BY_COLS)
        gain = gain2_ref[...]
        _, unit, rstd = norm_forward(residual_v[rows, :], gain, jnp.zeros_like(gain))
        dinput, gain_grad, shift_grad = norm_backward(dnormed, unit, rstd, gain)
        total = cot_v[rows, :].astype(jnp.float32) + dinput
        dresid[s] = total
        dattn[rows, :] = total.astype(jnp.bfloat16)
        small_own[2:3, :] += gain_grad.reshape(1, model)
        small_own[3:4, :] += shift_grad.reshape(1, model)
        if s == 0:
            loads[4].wait()
        dmixed[s] = mxu(dattn[rows, :], wo_v[...], ROWS_BY_ROWS).astype(jnp.bfloat16)
        if s == 0:
            pl.semaphore_wait(barrier, len(neighbours))
        for d in range(1, ways):
            dmixed_copy(s, d).start()
    routed_back = exchange(others, result_ref, returned, c_send, c_recv)
    for copy in routed_back[: others // 2 - 1]:
        copy.start()
    shards = shards_of(me, ways)
    size = down_part.shape[0] // len(shards)
    scatter = [
        send(
            down_part.at[i * size : (i + 1) * size],
            down_land.at[i - 1],
            s_send.at[i],
            s_recv.at[i],
            {"sp": shards[i]},
        )
        for i in range(1, len(shards))
    ]
    sum_o = Reduction(ways, columns, part_o, out_o, scratch[:15])
    sums_w = [
        Reduction(ways, columns, parts_w.at[i], out, scratch[15 * (i + 1) : 15 * (i + 2)])
        for i, out in enumerate((out_q, out_k, out_v))
    ]
    sum_q, sum_k, sum_v = sums_w

    loads[5].wait()

    def out_step(i, carry):
        at = span(i, BLOCK)
        left = mixed_v[:, :, at].reshape(seqs * shard, BLOCK)
        part_o[at, :] = mxu(left, dattn[...], COLS_BY_COLS).astype(jnp.bfloat16)
        return carry

    lax.fori_loop(0, model // BLOCK, out_step, 0)
    sum_o.core_copy.start()
    for copy in loads[6:9]:
        copy.wait()

    lane = lax.broadcasted_iota(jnp.int32, (1, width), 1) // head_dim
    visible = lax.broadcasted_iota(jnp.int32, (BLOCK, BLOCK), 0) <= lax.broadcasted_iota(
        jnp.int32, (BLOCK, BLOCK), 1
    )
    scale = head_dim ** (-0.5)
    for s in range(seqs):
        dmixed_h[s, span(me, shard), :] = dmixed[s, :, span(me, width)]
        for d in range(1, ways):
            dmixed_copy(s, d).wait_recv()
        if s == 0:
            sum_o.add_core()
            for copy in scatter:
                copy.start()
        dq_f[...] = jnp.zeros_like(dq_f)
        dk_f[...] = jnp.zeros_like(dk_f)
        dv_f[...] = jnp.zeros_like(dv_f)

        def one_head(h, carry):
            mine = (lane == h).astype(jnp.float32)
            for at in range(0, seq_len, BLOCK):
                rows = slice(at, at + BLOCK)
                query = (q_v[s, rows, :].astype(jnp.float32) * (mine * scale)).astype(
                    jnp.bfloat16
                )
                dout = (dmixed_h[s, rows, :].astype(jnp.float32) * mine).astype(jnp.bfloat16)
                log_row = log_ref[s, pl.ds(h, 1), rows]
                parts = [(rows, True)] + ([(slice(0, at), False)] if at else [])
                kept = []
                delta = jnp.zeros((1, BLOCK), jnp.float32)
                for keys, diagonal in parts:
                    prob = jnp.exp(mxu(k_v[s, keys, :], query, ROWS_BY_ROWS) - log_row)
                    if diagonal:
                        prob = jnp.where(visible, prob, 0.0)
                    dprob = mxu(v_v[s, keys, :], dout, ROWS_BY_ROWS)
                    delta += jnp.sum(prob * dprob, axis=0, keepdims=True)
                    kept.append((keys, prob, dprob))
                dquery = jnp.zeros((BLOCK, width), jnp.float32)
                for keys, prob, dprob in kept:
                    dv_f[keys, :] += mxu(prob.astype(jnp.bfloat16), dout)
                    dlogit = (prob * (dprob - delta)).astype(jnp.bfloat16)
                    dk_f[keys, :] += mxu(dlogit, query)
                    dquery += mxu(dlogit, k_v[s, keys, :], COLS_BY_COLS)
                dq_f[rows, :] += dquery * (mine * scale)
            return carry

        lax.fori_loop(0, heads, one_head, 0)
        for i, total in enumerate((dq_f, dk_f, dv_f)):
            grads_h[s, :, i * width : (i + 1) * width] = total[...].astype(jnp.bfloat16)
        for d in range(1, ways):
            grad_copy(s, d).start()
        grads_tok[s, :, span(me, 3 * width)] = grads_h[s, span(me, shard), :]

    loads[9].wait()

    def weight_step(i, carry):
        at = span(i, BLOCK)
        grad = mxu(normed_v[0, :, at], grads_h[0], COLS_BY_COLS)
        for s in range(1, seqs):
            grad += mxu(normed_v[s, :, at], grads_h[s], COLS_BY_COLS)
        for j in range(3):
            parts_w[j, at, :] = grad[:, j * width : (j + 1) * width].astype(jnp.bfloat16)
        return carry

    lax.fori_loop(0, model // BLOCK, weight_step, 0)
    for total in (sum_v, sum_k, sum_q):
        total.core_copy.start()

    o_land[0] = sum_o.add_column().astype(jnp.bfloat16)
    o_copy = [
        send(
            o_land.at[0, :, span(peer[d], width)],
            o_land.at[d, :, 0:width],
            o_send.at[d],
            o_recv.at[d],
            {"sp": peer[d]},
        )
        for d in range(1, ways)
    ]
    for copy in o_copy:
        copy.start()
    for total in (sum_v, sum_k, sum_q):
        total.add_core()
    total = o_land[0, :, span(me, width)].astype(jnp.float32)
    for d, copy in enumerate(o_copy):
        copy.wait()
        total += o_land[d + 1, :, 0:width].astype(jnp.float32)
    sum_o.piece[...] = total.astype(jnp.bfloat16)
    sum_o.spread()
    sum_v.piece[...] = sum_v.add_column().astype(jnp.bfloat16)
    sum_v.spread()
    sum_k.piece[...] = sum_k.add_column().astype(jnp.bfloat16)
    sum_k.spread()
    sum_o.ring()
    sum_q.piece[...] = sum_q.add_column().astype(jnp.bfloat16)
    sum_q.spread()
    for copy in routed_back[others // 2 - 1 :]:
        copy.start()
    sum_v.ring()
    sum_o.relay()

    def norm_grad(s):
        for d in range(1, ways):
            grad_copy(s, d).wait()
        dnormed = jnp.zeros((shard, model), jnp.float32)
        for j in range(ways):
            for i, weight in enumerate((wq_v, wk_v, wv_v)):
                at = (3 * j + i) * width
                dnormed += mxu(
                    grads_tok[s, :, at : at + width],
                    weight[:, j * width : (j + 1) * width],
                    ROWS_BY_ROWS,
                )
        gain = gain1_ref[...]
        _, unit, rstd = norm_forward(x_v[s].astype(jnp.float32), gain, jnp.zeros_like(gain))
        dinput, gain_grad, shift_grad = norm_backward(dnormed, unit, rstd, gain)
        tokens_ref[s] = (dresid[s] + dinput).astype(jnp.bfloat16)
        small_own[0:1, :] += gain_grad.reshape(1, model)
        small_own[1:2, :] += shift_grad.reshape(1, model)

    for copy in loads[10:14]:
        copy.wait()
    for s in range(seqs - 1):
        norm_grad(s)
    sum_k.ring()
    sum_v.relay()
    sum_q.ring()
    sum_k.relay()
    sum_o.cross()
    norm_grad(seqs - 1)
    sum_v.cross()

    steps = [[{"dp": dp + 1 - 2 * core}]]
    steps.append([{"dp": 2 * lax.rem(dp // 2 + d, columns) + core} for d in range(1, columns)])
    steps.append([{"sp": peer[d]} for d in range(1, ways)])
    slot = 0
    source = small_own
    for number, peers in enumerate(steps):
        copies = [
            send(
                source,
                small_land.at[slot + i],
                small_send.at[slot + i],
                small_recv.at[slot + i],
                device,
            )
            for i, device in enumerate(peers)
        ]
        for copy in copies:
            copy.start()
        if number == 0:
            sum_q.relay()
        elif number == 1:
            sum_k.cross()
        total = source[...]
        for i, copy in enumerate(copies):
            copy.wait()
            total += small_land[slot + i]
        slot += len(peers)
        if number == len(steps) - 1:
            small_out[...] = total
        else:
            small_sum[number] = total
            source = small_sum.at[number]

    loads[14].wait()
    for copy in routed_back:
        copy.wait()
    for s in range(seqs):
        rows = slice(s * shard, (s + 1) * shard)
        out = mxu(placer_v[:, rows], returned[...].reshape(-1, model), COLS_BY_COLS)
        block_ref[s] = (residual_v[rows, :] + out).astype(jnp.bfloat16)
    sum_q.cross()
    for s in range(seqs):
        for d in range(1, ways):
            dmixed_copy(s, d).wait_send()
    for copy in scatter:
        copy.wait()
    for total in [sum_o] + sums_w:
        total.finish()


def vmem(count):
    return [pl.BlockSpec(memory_space=pltpu.VMEM)] * count


def params(collective_id):
    return pltpu.CompilerParams(
        collective_id=collective_id, has_side_effects=True, vmem_limit_bytes=VMEM_BYTES
    )


def dma(*shape):
    return pltpu.SemaphoreType.DMA(shape)


def local(
    tokens_in,
    expert_ids,
    query_weight,
    key_weight,
    value_weight,
    out_weight,
    norm1_gain,
    norm1_shift,
    norm2_gain,
    norm2_shift,
    up_weight,
    down_weight,
    out_cotangent,
    load_mean,
):
    seq_count, shard_len, model_width = tokens_in.shape
    row_count = seq_count * shard_len
    head_dim = model_width // HEADS
    dp_ways = lax.axis_size("dp")
    sp_ways = lax.axis_size("sp")
    sp_at = lax.axis_index("sp")
    seq_len = shard_len * sp_ways
    experts = load_mean.shape[0]
    slot_count = 2 * row_count // experts
    local_experts = up_weight.shape[0]
    ff_width = up_weight.shape[1]
    width = model_width // sp_ways
    bf16 = jnp.bfloat16
    f32 = jnp.float32

    def shape(*sizes, dtype=bf16):
        return jax.ShapeDtypeStruct(sizes, dtype)

    routes = expert_ids.reshape(row_count)
    one_hot = (routes[:, None] == jnp.arange(experts, dtype=jnp.int32)[None, :]).astype(jnp.int32)
    running = jnp.cumsum(one_hot, axis=0) - 1
    slot_of = jnp.sum(running * one_hot, axis=1)
    target = routes * slot_count + slot_of
    placer = (jnp.arange(experts * slot_count, dtype=jnp.int32)[:, None] == target[None, :]).astype(
        bf16
    )
    cot_b = out_cotangent.reshape(row_count, model_width)
    cot_send = jnp.dot(placer, cot_b, preferred_element_type=f32).astype(bf16)
    cot_send = cot_send.reshape(experts, slot_count, model_width)

    def columns_of(weight):
        return lax.dynamic_slice_in_dim(weight, sp_at * width, width, axis=1)

    routed = shape(experts, slot_count, model_width)
    hbm = [pl.BlockSpec(memory_space=pl.ANY)]
    normed_all, query_h, key_h, value_h, log_total, mixed_b, arrived = pl.pallas_call(
        functools.partial(attend_forward, sp_ways, dp_ways, head_dim),
        out_shape=[
            shape(seq_count, seq_len, model_width),
            shape(seq_count, seq_len, width),
            shape(seq_count, seq_len, width),
            shape(seq_count, seq_len, width),
            shape(seq_count, 8, seq_len, dtype=f32),
            shape(seq_count, shard_len, model_width),
            routed,
        ],
        in_specs=hbm + vmem(6),
        out_specs=vmem(6) + hbm,
        scratch_shapes=[
            pltpu.VMEM((seq_count, seq_len, model_width), bf16),
            pltpu.VMEM((seq_len, width), f32),
            pltpu.VMEM((seq_count, seq_len, width), bf16),
            pltpu.VMEM((seq_len, LANES), f32),
            dma(seq_count, sp_ways),
            dma(seq_count, sp_ways),
            dma(seq_count, sp_ways),
            dma(seq_count, sp_ways),
            dma(dp_ways),
            dma(dp_ways),
            pltpu.SemaphoreType.DMA,
        ],
        compiler_params=params(0),
    )(
        cot_send,
        tokens_in,
        columns_of(query_weight),
        columns_of(key_weight),
        columns_of(value_weight),
        norm1_gain.reshape(1, model_width),
        norm1_shift.reshape(1, model_width),
    )
    mixed_b = mixed_b.reshape(row_count, model_width)
    inputs = tokens_in.reshape(row_count, model_width).astype(f32)
    attn_out = jnp.dot(mixed_b, out_weight, preferred_element_type=f32)
    residual_stream = inputs + attn_out
    normed2, _, _ = norm_forward(residual_stream, norm2_gain, norm2_shift)
    normed2_b = normed2.astype(bf16)
    outgoing = jnp.dot(placer, normed2_b, preferred_element_type=f32).astype(bf16)
    outgoing = outgoing.reshape(experts, slot_count, model_width)
    ff_own = ff_width // 2
    received_blocks = max(2 * experts, ff_own // slot_count)
    part = shape(ff_own // slot_count, slot_count, model_width)
    landing = shape(sp_ways // 2 - 1, ff_width // sp_ways, model_width)
    down_landing = shape(sp_ways // 2 - 1, part.shape[0] * 2 // sp_ways, slot_count, model_width)
    own_part = shape(ff_width // sp_ways, model_width)
    dnormed_back, expert_out, up_part, down_part, up_land = pl.pallas_call(
        functools.partial(run_experts, dp_ways, sp_ways),
        out_shape=[routed, routed, own_part, part, landing],
        in_specs=vmem(1) + hbm * 3,
        out_specs=vmem(2) + hbm * 3,
        scratch_shapes=[
            pltpu.VMEM((received_blocks, slot_count, model_width), bf16),
            pltpu.VMEM((2,) + routed.shape, bf16),
            pltpu.VMEM((ff_own, model_width), bf16),
            pltpu.VMEM((ff_own, model_width), bf16),
            pltpu.VMEM((2 * experts * slot_count, ff_own), bf16),
            pltpu.VMEM((2 * experts * slot_count, ff_own), bf16),
            pltpu.VMEM((2 * slot_count, model_width), f32),
            pltpu.VMEM(routed.shape, f32),
            pltpu.VMEM(routed.shape, bf16),
            pltpu.VMEM(routed.shape, bf16),
            pltpu.VMEM(routed.shape, bf16),
            pltpu.VMEM(routed.shape, bf16),
            pltpu.VMEM(routed.shape, bf16),
            dma(2, sp_ways // 2),
            dma(2),
            pltpu.SemaphoreType.DMA,
            dma(dp_ways),
            dma(dp_ways),
            dma(dp_ways),
            dma(dp_ways),
            dma(dp_ways // 2 + 1),
            dma(dp_ways // 2 + 1),
            dma(dp_ways // 2 + 1),
            dma(dp_ways // 2 + 1),
            dma(sp_ways // 2),
            dma(sp_ways // 2),
        ],
        compiler_params=params(3),
    )(outgoing, arrived, up_weight[0], down_weight[0])
    counts = jnp.sum(one_hot, axis=0).astype(f32)
    counts = jnp.pad(counts, (0, model_width - experts)).reshape(1, model_width)
    columns = dp_ways // 2
    rows = model_width // dp_ways
    token_shape = (seq_count, shard_len, model_width)

    def reduction(part_width):
        return [
            pltpu.VMEM((columns * rows, part_width), bf16),
            pltpu.VMEM((columns * rows, part_width), bf16),
            pltpu.VMEM((columns - 1, rows, part_width), bf16),
            pltpu.VMEM((rows, width), bf16),
            pltpu.SemaphoreType.DMA,
            pltpu.SemaphoreType.DMA,
            dma(columns),
            dma(columns),
            dma(columns),
            dma(columns),
            dma(sp_ways),
            dma(sp_ways),
            dma(sp_ways),
            dma(sp_ways),
            pltpu.SemaphoreType.DMA,
        ]

    small_slots = 1 + (columns - 1) + (sp_ways - 1)
    whole = shape(model_width, model_width)
    tokens = pltpu.VMEM(token_shape, bf16)
    by_head = pltpu.VMEM((seq_count, seq_len, width), bf16)
    square = pltpu.VMEM((model_width, model_width), bf16)
    flat = (row_count, model_width)
    *weight_grads, down_land, block_out, tokens_grad, small_sum = pl.pallas_call(
        functools.partial(backward, sp_ways, dp_ways, head_dim),
        out_shape=[whole] * 4
        + [
            down_landing,
            shape(*token_shape),
            shape(*token_shape),
            shape(8, model_width, dtype=f32),
        ],
        in_specs=hbm * 16 + vmem(4),
        out_specs=hbm * 5 + vmem(3),
        scratch_shapes=[
            pltpu.VMEM(routed.shape, bf16),
            pltpu.VMEM(placer.shape, bf16),
            pltpu.VMEM(flat, bf16),
            pltpu.VMEM(flat, f32),
            square,
            tokens,
            by_head,
            by_head,
            by_head,
            pltpu.VMEM((seq_count, seq_len, model_width), bf16),
            square,
            square,
            square,
            tokens,
            pltpu.VMEM(routed.shape, bf16),
            pltpu.VMEM(token_shape, f32),
            pltpu.VMEM(flat, bf16),
            tokens,
            by_head,
            pltpu.VMEM((seq_len, width), f32),
            pltpu.VMEM((seq_len, width), f32),
            pltpu.VMEM((seq_len, width), f32),
            pltpu.VMEM((seq_count, seq_len, 3 * width), bf16),
            pltpu.VMEM((seq_count, shard_len, 3 * model_width), bf16),
            square,
            pltpu.VMEM((3, model_width, width), bf16),
            pltpu.VMEM((sp_ways, rows, model_width), bf16),
            pltpu.VMEM((8, model_width), f32),
            pltpu.VMEM((small_slots, 8, model_width), f32),
            pltpu.VMEM((2, 8, model_width), f32),
            dma(seq_count, sp_ways),
            dma(seq_count, sp_ways),
            dma(seq_count, sp_ways),
            dma(seq_count, sp_ways),
            dma(dp_ways),
            dma(dp_ways),
            dma(sp_ways // 2),
            dma(sp_ways // 2),
            dma(sp_ways),
            dma(sp_ways),
            dma(small_slots),
            dma(small_slots),
            dma(15),
        ]
        + reduction(model_width)
        + reduction(width) * 3,
        compiler_params=params(1),
    )(
        dnormed_back,
        placer,
        cot_b,
        residual_stream,
        out_weight,
        mixed_b.reshape(token_shape),
        query_h,
        key_h,
        value_h,
        normed_all,
        query_weight,
        key_weight,
        value_weight,
        tokens_in,
        expert_out,
        down_part,
        log_total,
        norm1_gain.reshape(1, model_width),
        norm2_gain.reshape(1, model_width),
        counts,
    )
    down_part = down_part.reshape(ff_own, model_width)[: ff_width // sp_ways]
    up_grad, down_grad = (
        (part.astype(f32) + jnp.sum(land.reshape(landing.shape).astype(f32), axis=0))[None]
        for part, land in ((up_part, up_land), (down_part, down_land))
    )
    query_grad, key_grad, value_grad, out_grad = (grad.astype(f32) for grad in weight_grads)
    load_now = small_sum[4, :experts] * experts / (row_count * dp_ways * sp_ways)
    load_next = 0.9 * load_mean + 0.1 * load_now
    return (
        block_out,
        tokens_grad,
        query_grad,
        key_grad,
        value_grad,
        out_grad,
        small_sum[0],
        small_sum[1],
        small_sum[2],
        small_sum[3],
        up_grad,
        down_grad,
        load_next,
    )


def solution(mesh):
    return jax.shard_map(
        local,
        mesh=mesh,
        in_specs=(
            P("dp", "sp", None),
            P("dp", "sp", None, None),
            P(),
            P(),
            P(),
            P(),
            P(),
            P(),
            P(),
            P(),
            P("dp", None, None),
            P("dp", None, None),
            P("dp", "sp", None),
            P(),
        ),
        out_specs=(
            P("dp", "sp", None),
            P("dp", "sp", None),
            P(),
            P(),
            P(),
            P(),
            P(),
            P(),
            P(),
            P(),
            P("dp", "sp", None),
            P("dp", "sp", None),
            P(),
        ),
        check_vma=False,
    )
```

```python
import functools

import jax
import jax.numpy as jnp
from jax import lax
from jax.experimental import pallas as pl
from jax.experimental.pallas import tpu as pltpu
from jax.sharding import PartitionSpec as P

HEADS = 16
MESH = pl.DeviceIdType.MESH
BLOCK = 256
LANES = 128
STEP = 1024
VMEM_BYTES = 60 * 2**20

NORM_EPSILON = 1e-05
GELU_ROOT = 0.7978845608028654
CUBIC_TERM = 0.044715

ROWS_BY_COLS = (((1,), (0,)), ((), ()))
ROWS_BY_ROWS = (((1,), (1,)), ((), ()))
COLS_BY_COLS = (((0,), (0,)), ((), ()))


def smooth(values):
    return (
        0.5
        * values
        * (1.0 + jnp.tanh(GELU_ROOT * (values + CUBIC_TERM * values * values * values)))
    )


def smooth_slope(values):
    inner = jnp.tanh(GELU_ROOT * (values + CUBIC_TERM * values * values * values))
    return 0.5 * (1.0 + inner) + 0.5 * values * (1.0 - inner * inner) * GELU_ROOT * (
        1.0 + 3.0 * CUBIC_TERM * values * values
    )


def norm_forward(values, gain, shift):
    center = jnp.mean(values, axis=-1, keepdims=True)
    offset = values - center
    rstd = lax.rsqrt(jnp.mean(offset * offset, axis=-1, keepdims=True) + NORM_EPSILON)
    unit = offset * rstd
    return (unit * gain + shift, unit, rstd)


def norm_backward(grad, unit, rstd, gain):
    scaled = grad * gain
    inner = (
        scaled
        - jnp.mean(scaled, axis=-1, keepdims=True)
        - unit * jnp.mean(scaled * unit, axis=-1, keepdims=True)
    )
    return (inner * rstd, jnp.sum(grad * unit, axis=0), jnp.sum(grad, axis=0))


def mxu(left, right, dims=ROWS_BY_COLS):
    return lax.dot_general(left, right, dims, preferred_element_type=jnp.float32)


def span(index, size):
    return pl.ds(pl.multiple_of(index * size, size), size)


def greet(peers):
    barrier = pltpu.get_barrier_semaphore()
    for peer in peers:
        pl.semaphore_signal(barrier, inc=1, device_id=peer, device_id_type=MESH)
    pl.semaphore_wait(barrier, len(peers))


def send(source, target, send_sem, recv_sem, peer):
    return pltpu.make_async_remote_copy(
        src_ref=source,
        dst_ref=target,
        send_sem=send_sem,
        recv_sem=recv_sem,
        device_id=peer,
        device_id_type=MESH,
    )


def exchange(others, source, target, send_sem, recv_sem):
    me = lax.axis_index("dp")
    return [
        send(
            source.at[flip(me, d)],
            target.at[me],
            send_sem.at[d],
            recv_sem.at[d],
            {"dp": flip(me, d)},
        )
        for d in range(1, others)
    ]


def flip(index, bits):
    bit = 1
    while bit <= bits:
        if bits & bit:
            index = index + bit - 2 * bit * lax.rem(index // bit, 2)
        bit *= 2
    return index


def attend_forward(
    ways,
    others,
    head_dim,
    cot_ref,
    x_ref,
    wq_ref,
    wk_ref,
    wv_ref,
    gain_ref,
    shift_ref,
    normed_ref,
    q_ref,
    k_ref,
    v_ref,
    log_ref,
    mixed_ref,
    arrived_ref,
    x_all,
    mixed_f,
    mixed_h,
    log_s,
    x_send,
    x_recv,
    m_send,
    m_recv,
    c_send,
    c_recv,
    local_sem,
):
    seqs, shard, _ = x_ref.shape
    seq_len, width = q_ref.shape[1:]
    heads = width // head_dim
    me = lax.axis_index("sp")
    peer = [lax.rem(me + d, ways) for d in range(ways)]
    origin = [lax.rem(me + ways - d, ways) for d in range(ways)]
    greet(
        [{"sp": peer[d]} for d in range(1, ways)]
        + [{"dp": flip(lax.axis_index("dp"), d)} for d in range(1, others)]
    )
    background = exchange(others, cot_ref, arrived_ref, c_send, c_recv)
    own = pltpu.make_async_copy(
        cot_ref.at[lax.axis_index("dp")], arrived_ref.at[lax.axis_index("dp")], local_sem
    )

    def x_copy(s, d):
        return send(
            x_ref.at[s],
            x_all.at[s, span(me, shard)],
            x_send.at[s, d],
            x_recv.at[s, d],
            {"sp": peer[d]},
        )

    def mixed_copy(s, d):
        return send(
            mixed_h.at[s, span(peer[d], shard)],
            mixed_ref.at[s, :, span(me, width)],
            m_send.at[s, d],
            m_recv.at[s, d],
            {"sp": peer[d]},
        )

    lane = lax.broadcasted_iota(jnp.int32, (1, width), 1) // head_dim
    log_lane = lax.broadcasted_iota(jnp.int32, (1, LANES), 1)
    visible = lax.broadcasted_iota(jnp.int32, (BLOCK, BLOCK), 1) <= lax.broadcasted_iota(
        jnp.int32, (BLOCK, BLOCK), 0
    )
    scale = head_dim ** (-0.5)

    def project(s, rows, values):
        normed, _, _ = norm_forward(values.astype(jnp.float32), gain_ref[...], shift_ref[...])
        normed = normed.astype(jnp.bfloat16)
        normed_ref[s, rows, :] = normed
        q_ref[s, rows, :] = mxu(normed, wq_ref[...]).astype(jnp.bfloat16)
        k_ref[s, rows, :] = mxu(normed, wk_ref[...]).astype(jnp.bfloat16)
        v_ref[s, rows, :] = mxu(normed, wv_ref[...]).astype(jnp.bfloat16)

    for d in range(1, ways):
        x_copy(0, d).start()
    own.start()
    for copy in background:
        copy.start()
    for s in range(seqs):
        project(s, span(me, shard), x_ref[s])
        for d in range(1, ways):
            x_copy(s, d).wait_recv()
            if d == ways - 1 and s + 1 < seqs:
                for later in range(1, ways):
                    x_copy(s + 1, later).start()
            rows = span(origin[d], shard)
            project(s, rows, x_all[s, rows, :])
        mixed_f[...] = jnp.zeros_like(mixed_f)
        log_s[...] = jnp.zeros_like(log_s)

        def one_head(h, carry):
            mine = (lane == h).astype(jnp.float32)
            for at in range(0, seq_len, BLOCK):
                rows = slice(at, at + BLOCK)
                query = (q_ref[s, rows, :].astype(jnp.float32) * (mine * scale)).astype(
                    jnp.bfloat16
                )
                near = mxu(query, k_ref[s, rows, :], ROWS_BY_ROWS)
                near = jnp.where(visible, near, -1e30)
                top = jnp.max(near, axis=1, keepdims=True)
                if at:
                    far = mxu(query, k_ref[s, :at, :], ROWS_BY_ROWS)
                    top = jnp.maximum(top, jnp.max(far, axis=1, keepdims=True))
                near = jnp.exp(near - top)
                total = jnp.sum(near, axis=1, keepdims=True)
                if at:
                    far = jnp.exp(far - top)
                    total += jnp.sum(far, axis=1, keepdims=True)
                inverse = 1.0 / total
                out = mxu((near * inverse).astype(jnp.bfloat16), v_ref[s, rows, :])
                if at:
                    out += mxu((far * inverse).astype(jnp.bfloat16), v_ref[s, :at, :])
                mixed_f[rows, :] += out * mine
                log_s[rows, :] = jnp.where(log_lane == h, top + jnp.log(total), log_s[rows, :])
            return carry

        lax.fori_loop(0, heads, one_head, 0)
        log_ref[s] = jnp.transpose(log_s[...])[: log_ref.shape[1], :]
        mixed_h[s] = mixed_f[...].astype(jnp.bfloat16)
        for d in range(1, ways):
            mixed_copy(s, d).start()
        mixed_ref[s, :, span(me, width)] = mixed_h[s, span(me, shard), :]
    for s in range(seqs):
        for d in range(1, ways):
            x_copy(s, d).wait_send()
            mixed_copy(s, d).wait()
    own.wait()
    for copy in background:
        copy.wait()


def pair_of(sp):
    core = lax.rem(lax.axis_index("dp"), 2)
    along_x, along_y = flip(sp, 1), flip(sp, 2)
    return along_x + core * (along_y - along_x)


def shards_of(sp, ways):
    shards = [sp, flip(pair_of(sp), 3)]
    bit = 4
    while bit < ways:
        shards += [flip(shard, bit) for shard in shards]
        bit *= 2
    return shards


def run_experts(
    others,
    ways,
    outgoing_ref,
    cot_ref,
    up_ref,
    down_ref,
    back_ref,
    result_ref,
    up_own,
    up_rest,
    down_own,
    down_rest,
    received,
    arrived,
    up_v,
    down_v,
    hidden,
    slope_v,
    total,
    dn_own,
    dn_pair,
    dn_land,
    dnormed,
    out_pair,
    out_land,
    w_sem,
    o_sem,
    c_sem,
    a_send,
    a_recv,
    b_send,
    b_recv,
    f_send,
    f_recv,
    p_send,
    p_recv,
    e_send,
    e_recv,
):
    slots, width = received.shape[1:]
    rows = others * slots
    ff = up_v.shape[0]
    groups = others // 2
    me = lax.axis_index("dp")
    sp = lax.axis_index("sp")
    chip = me // 2
    pair = {"sp": pair_of(sp)}
    shards = shards_of(sp, ways)
    size = ff // len(shards)
    loads = [
        pltpu.make_async_copy(
            source.at[span(shard, size)], target.at[i * size : (i + 1) * size], w_sem.at[j, i]
        )
        for j, (source, target) in enumerate(((down_ref, down_v), (up_ref, up_v)))
        for i, shard in enumerate(shards)
    ]
    own_cot = pltpu.make_async_copy(cot_ref, arrived.at[0], c_sem)
    own_cot.start()
    for copy in loads:
        copy.start()
    greet([{"dp": flip(me, d)} for d in range(1, others)] + [pair])
    inward = exchange(others, outgoing_ref, received.at[0:others], a_send, a_recv)
    outward = exchange(others, dnormed, back_ref, b_send, b_recv)
    near = [flip(chip, group) for group in range(groups)]
    chips = [pl.ds(2 * near[group], 2) for group in range(groups)]
    forward = [
        send(
            received.at[chips[group]],
            received.at[pl.ds(others + 2 * near[group], 2)],
            f_send.at[group],
            f_recv.at[group],
            pair,
        )
        for group in range(groups)
    ]
    cot_copy = send(cot_ref, arrived.at[1], f_send.at[groups], f_recv.at[groups], pair)
    dn_copy = [
        send(
            dn_pair.at[chips[group]],
            dn_land.at[chips[group]],
            p_send.at[group],
            p_recv.at[group],
            pair,
        )
        for group in range(groups)
    ]
    out_copy = [
        send(
            out_pair.at[chips[group]],
            out_land.at[chips[group]],
            e_send.at[group],
            e_recv.at[group],
            pair,
        )
        for group in range(groups)
    ]

    early = range(groups // 2)
    middle = range(groups // 2, 3 * groups // 4)
    late = range(3 * groups // 4, groups)
    for copy in inward[: 2 * late[0] - 1]:
        copy.start()
    received[me] = outgoing_ref[me]
    cot_copy.start()

    def slab_of(half, group):
        return pl.ds(pl.multiple_of(half * rows + near[group] * (2 * slots), 2 * slots), 2 * slots)

    def cot_half(half):
        def cot_step(i, carry):
            at = span(i, STEP)
            cot = arrived[half].reshape(rows, width)
            slope_v[half * rows : (half + 1) * rows, at] = mxu(
                cot, down_v[at, :], ROWS_BY_ROWS
            ).astype(jnp.bfloat16)
            return carry

        lax.fori_loop(0, ff // STEP, cot_step, 0)

    def up_half(half, group):
        slab = slab_of(half, group)
        total[...] = jnp.zeros_like(total)

        def up_step(i, carry):
            at = span(i, STEP)
            tokens = received[pl.ds(half * others + 2 * near[group], 2)].reshape(2 * slots, width)
            pre = mxu(tokens, up_v[at, :], ROWS_BY_ROWS)
            square = pre * pre
            inner = jnp.tanh(GELU_ROOT * pre * (1.0 + CUBIC_TERM * square))
            gate = 0.5 * (1.0 + inner)
            hidden[slab, at] = (pre * gate).astype(jnp.bfloat16)
            slope = gate + (0.5 * GELU_ROOT) * pre * (1.0 - inner * inner) * (
                1.0 + (3.0 * CUBIC_TERM) * square
            )
            dpre = (slope_v[slab, at].astype(jnp.float32) * slope).astype(jnp.bfloat16)
            slope_v[slab, at] = dpre
            total[...] += mxu(dpre, up_v[at, :])
            return carry

        lax.fori_loop(0, ff // STEP, up_step, 0)
        shaped = total[...].reshape(2, slots, width)
        if half:
            dn_pair[chips[group]] = shaped.astype(jnp.bfloat16)
            dn_copy[group].start()
        else:
            dn_own[chips[group]] = shaped

    def out_half(half, group):
        at = chips[group]
        out = mxu(hidden[slab_of(half, group), :], down_v[...]).reshape(2, slots, width)
        if half:
            out_pair[at] = out.astype(jnp.bfloat16)
            out_copy[group].start()
        else:
            out_copy[group].wait_recv()
            result_ref[at] = (out + out_land[at].astype(jnp.float32)).astype(jnp.bfloat16)

    def pass_on(group):
        for d in (2 * group, 2 * group + 1):
            if d:
                inward[d - 1].wait_recv()
        forward[group].start()

    def finish(group):
        dn_copy[group].wait_recv()
        at = chips[group]
        dnormed[at] = (dn_own[at] + dn_land[at].astype(jnp.float32)).astype(jnp.bfloat16)
        for d in (2 * group, 2 * group + 1):
            if d:
                outward[d - 1].start()
            else:
                back_ref[me] = dnormed[me]

    def up_pair(group):
        forward[group].wait_recv()
        up_half(1, group)

    pass_on(0)
    own_cot.wait()
    for copy in loads[: len(shards)]:
        copy.wait()
    cot_half(0)
    for copy in loads[len(shards) :]:
        copy.wait()
    up_half(0, 0)
    for group in early[1:]:
        pass_on(group)
    for copy in inward[2 * middle[0] - 1 : 2 * late[0] - 1]:
        copy.wait_send()
    for copy in inward[2 * late[0] - 1 :]:
        copy.start()
    cot_copy.wait_recv()
    cot_half(1)
    for group in middle:
        pass_on(group)
    up_pair(0)
    for group in early[1:]:
        up_half(0, group)
        up_pair(group)
    for group in middle:
        up_half(0, group)
    for group in early:
        finish(group)
    for group in middle:
        up_pair(group)
    for group in early:
        out_half(1, group)
    for group in late:
        pass_on(group)
        up_half(0, group)
    for group in middle:
        finish(group)
    for group in late:
        up_pair(group)
    for group in [*middle, *late]:
        out_half(1, group)
    for group in late:
        finish(group)

    def grad(target, left, right_ref, block=0):
        def grad_step(i, carry):
            at = span(i, STEP)
            right = right_ref[...].reshape(2 * rows, width)
            out = mxu(left[:, at], right, COLS_BY_COLS).astype(jnp.bfloat16)
            if block:
                target[span(i, STEP // block)] = out.reshape(STEP // block, block, width)
            else:
                target[at, :] = out
            return carry

        lax.fori_loop(0, ff // STEP, grad_step, 0)

    grad(up_v, slope_v, received.at[0 : 2 * others])
    for copy in forward:
        copy.wait_send()
    grad(received, hidden, arrived, slots)
    first, every = size // slots, ff // slots
    stores = [
        pltpu.make_async_copy(source, target, o_sem.at[i])
        for i, (source, target) in enumerate(
            (
                (up_v.at[0:size], up_own),
                (up_v.at[size:ff], up_rest),
                (received.at[0:first], down_own),
                (received.at[first:every], down_rest),
            )
        )
    ]
    for copy in stores:
        copy.start()
    for group in range(groups):
        out_half(0, group)
    for copy in inward[: 2 * middle[0] - 1] + inward[2 * late[0] - 1 :]:
        copy.wait_send()
    for copy in [cot_copy] + dn_copy + out_copy:
        copy.wait_send()
    for copy in outward:
        copy.wait()
    for copy in stores:
        copy.wait()


class Reduction:
    def __init__(self, ways, columns, part, out, scratch):
        (
            self.core_land,
            self.core_sum,
            self.column_land,
            self.piece,
            core_send,
            core_recv,
            column_send,
            column_recv,
            spread_send,
            spread_recv,
            ring_send,
            ring_recv,
            cross_send,
            cross_recv,
            own_sem,
        ) = scratch
        me = lax.axis_index("sp")
        dp = lax.axis_index("dp")
        core = lax.rem(dp, 2)
        column = dp // 2
        twin = {"dp": dp + 1 - 2 * core}
        self.ways, self.columns, self.part = ways, columns, part
        self.core, self.column = core, column
        rows, width = self.piece.shape
        self.rows = rows

        def beside(d):
            return {"dp": 2 * lax.rem(column + d, columns) + core}

        def block(at_core, at_column, at_sp, count):
            first = pl.multiple_of((at_core * columns + at_column) * rows, rows)
            return out.at[pl.ds(first, count * rows), span(at_sp, width)]

        self.core_copy = send(
            part.at[span(1 - core, columns * rows)], self.core_land, core_send, core_recv, twin
        )
        self.column_copy = [
            send(
                self.core_sum.at[span(lax.rem(column + d, columns), rows)],
                self.column_land.at[d - 1],
                column_send.at[d],
                column_recv.at[d],
                beside(d),
            )
            for d in range(1, columns)
        ]
        spot = block(core, column, me, 1)
        self.own = pltpu.make_async_copy(self.piece, spot, own_sem)
        self.spread_copy = [
            send(self.piece, spot, spread_send.at[d], spread_recv.at[d], beside(d))
            for d in range(1, columns)
        ]
        origin = [flip(me, d) for d in range(ways)]
        half = [block(core, 0, at, columns) for at in origin]
        self.relays = []
        direct = range(1, ways)
        if ways == 4:
            direct = (1, 2)
            count = columns * rows // 2
            for i, (d, to) in enumerate(((1, 2), (2, 1))):
                first = pl.multiple_of(core * columns * rows + i * count, count)
                piece = out.at[pl.ds(first, count), span(origin[d], width)]
                self.relays.append(
                    send(piece, piece, ring_send.at[i], ring_recv.at[i], {"sp": origin[to]})
                )
            ring_send, ring_recv = ring_send.at[1:ways], ring_recv.at[1:ways]
        self.ring_copy = [
            send(half[0], half[0], ring_send.at[d], ring_recv.at[d], {"sp": origin[d]})
            for d in direct
        ]
        self.cross_copy = [
            send(half[d], half[d], cross_send.at[d], cross_recv.at[d], twin) for d in range(ways)
        ]

    def add_core(self):
        self.core_copy.wait()
        self.core_sum[...] = (
            self.part[span(self.core, self.columns * self.rows), :].astype(jnp.float32)
            + self.core_land[...].astype(jnp.float32)
        ).astype(jnp.bfloat16)
        for copy in self.column_copy:
            copy.start()

    def add_column(self):
        total = self.core_sum[span(self.column, self.rows), :].astype(jnp.float32)
        for d, copy in enumerate(self.column_copy):
            copy.wait()
            total += self.column_land[d].astype(jnp.float32)
        return total

    def spread(self):
        self.own.start()
        for copy in self.spread_copy:
            copy.start()

    def ring(self):
        self.own.wait()
        for copy in self.spread_copy:
            copy.wait()
        for copy in self.ring_copy:
            copy.start()
        self.cross_copy[0].start()

    def relay(self):
        for ring, cross in zip(self.ring_copy, self.cross_copy[1:]):
            ring.wait_recv()
            cross.start()
        for relay in self.relays:
            relay.start()

    def cross(self):
        for relay in self.relays:
            relay.wait_recv()
        if self.relays:
            self.cross_copy[3].start()

    def finish(self):
        for copy in self.ring_copy + self.relays:
            copy.wait_send()
        for copy in self.cross_copy:
            copy.wait()


def backward(
    ways,
    others,
    head_dim,
    back_ref,
    placer_ref,
    cot_ref,
    residual_ref,
    wo_ref,
    mixed_ref,
    q_ref,
    k_ref,
    v_ref,
    normed_ref,
    wq_ref,
    wk_ref,
    wv_ref,
    x_ref,
    result_ref,
    up_rest,
    down_rest,
    log_ref,
    gain1_ref,
    gain2_ref,
    counts_ref,
    out_q,
    out_k,
    out_v,
    out_o,
    up_land,
    down_land,
    block_ref,
    tokens_ref,
    small_out,
    back_v,
    placer_v,
    cot_v,
    residual_v,
    wo_v,
    mixed_v,
    q_v,
    k_v,
    v_v,
    normed_v,
    wq_v,
    wk_v,
    wv_v,
    x_v,
    returned,
    dresid,
    dattn,
    dmixed,
    dmixed_h,
    dq_f,
    dk_f,
    dv_f,
    grads_h,
    grads_tok,
    part_o,
    parts_w,
    o_land,
    small_own,
    small_land,
    small_sum,
    m_send,
    m_recv,
    g_send,
    g_recv,
    c_send,
    c_recv,
    s_send,
    s_recv,
    o_send,
    o_recv,
    small_send,
    small_recv,
    load_sem,
    *scratch,
):
    seqs, shard, model = x_v.shape
    seq_len, width = q_v.shape[1:]
    heads = width // head_dim
    columns = others // 2
    me = lax.axis_index("sp")
    dp = lax.axis_index("dp")
    core = lax.rem(dp, 2)
    peer = [lax.rem(me + d, ways) for d in range(ways)]
    barrier = pltpu.get_barrier_semaphore()
    neighbours = [{"sp": peer[d]} for d in range(1, ways)]
    neighbours += [{"dp": flip(dp, d)} for d in range(1, others)]
    for device in neighbours:
        pl.semaphore_signal(barrier, inc=1, device_id=device, device_id_type=MESH)
    sources = (
        (back_ref, back_v),
        (placer_ref, placer_v),
        (residual_ref, residual_v),
        (cot_ref, cot_v),
        (wo_ref, wo_v),
        (mixed_ref, mixed_v),
        (q_ref, q_v),
        (k_ref, k_v),
        (v_ref, v_v),
        (normed_ref, normed_v),
        (wq_ref, wq_v),
        (wk_ref, wk_v),
        (wv_ref, wv_v),
        (x_ref, x_v),
        (result_ref.at[dp], returned.at[dp]),
    )
    loads = [
        pltpu.make_async_copy(source, target, load_sem.at[i])
        for i, (source, target) in enumerate(sources)
    ]
    for copy in loads:
        copy.start()

    def dmixed_copy(s, d):
        return send(
            dmixed.at[s, :, span(peer[d], width)],
            dmixed_h.at[s, span(me, shard)],
            m_send.at[s, d],
            m_recv.at[s, d],
            {"sp": peer[d]},
        )

    def grad_copy(s, d):
        return send(
            grads_h.at[s, span(peer[d], shard)],
            grads_tok.at[s, :, span(me, 3 * width)],
            g_send.at[s, d],
            g_recv.at[s, d],
            {"sp": peer[d]},
        )

    small_own[...] = jnp.zeros_like(small_own)
    small_own[4:5, :] = counts_ref[...]
    for s in range(seqs):
        if s == 0:
            for copy in loads[:4]:
                copy.wait()
        rows = slice(s * shard, (s + 1) * shard)
        dnormed = mxu(placer_v[:, rows], back_v[...].reshape(-1, model), COLS_BY_COLS)
        gain = gain2_ref[...]
        _, unit, rstd = norm_forward(residual_v[rows, :], gain, jnp.zeros_like(gain))
        dinput, gain_grad, shift_grad = norm_backward(dnormed, unit, rstd, gain)
        total = cot_v[rows, :].astype(jnp.float32) + dinput
        dresid[s] = total
        dattn[rows, :] = total.astype(jnp.bfloat16)
        small_own[2:3, :] += gain_grad.reshape(1, model)
        small_own[3:4, :] += shift_grad.reshape(1, model)
        if s == 0:
            loads[4].wait()
        dmixed[s] = mxu(dattn[rows, :], wo_v[...], ROWS_BY_ROWS).astype(jnp.bfloat16)
        if s == 0:
            pl.semaphore_wait(barrier, len(neighbours))
        for d in range(1, ways):
            dmixed_copy(s, d).start()
    routed_back = exchange(others, result_ref, returned, c_send, c_recv)
    for copy in routed_back:
        copy.start()
    shards = shards_of(me, ways)
    scatter = []
    for j, (rest, land) in enumerate(((up_rest, up_land), (down_rest, down_land))):
        size = land.shape[1]
        scatter += [
            send(
                rest.at[(i - 1) * size : i * size],
                land.at[i - 1],
                s_send.at[j, i],
                s_recv.at[j, i],
                {"sp": shards[i]},
            )
            for i in range(1, len(shards))
        ]
    sum_o = Reduction(ways, columns, part_o, out_o, scratch[:15])
    sums_w = [
        Reduction(ways, columns, parts_w.at[i], out, scratch[15 * (i + 1) : 15 * (i + 2)])
        for i, out in enumerate((out_q, out_k, out_v))
    ]
    sum_q, sum_k, sum_v = sums_w

    loads[5].wait()

    def out_step(i, carry):
        at = span(i, BLOCK)
        left = mixed_v[:, :, at].reshape(seqs * shard, BLOCK)
        part_o[at, :] = mxu(left, dattn[...], COLS_BY_COLS).astype(jnp.bfloat16)
        return carry

    lax.fori_loop(0, model // BLOCK, out_step, 0)
    sum_o.core_copy.start()
    for copy in loads[6:9]:
        copy.wait()

    lane = lax.broadcasted_iota(jnp.int32, (1, width), 1) // head_dim
    visible = lax.broadcasted_iota(jnp.int32, (BLOCK, BLOCK), 0) <= lax.broadcasted_iota(
        jnp.int32, (BLOCK, BLOCK), 1
    )
    scale = head_dim ** (-0.5)
    for s in range(seqs):
        dmixed_h[s, span(me, shard), :] = dmixed[s, :, span(me, width)]
        for d in range(1, ways):
            dmixed_copy(s, d).wait_recv()
        if s == 0:
            sum_o.add_core()
            for copy in scatter:
                copy.start()
        dq_f[...] = jnp.zeros_like(dq_f)
        dk_f[...] = jnp.zeros_like(dk_f)
        dv_f[...] = jnp.zeros_like(dv_f)

        def one_head(h, carry):
            mine = (lane == h).astype(jnp.float32)
            for at in range(0, seq_len, BLOCK):
                rows = slice(at, at + BLOCK)
                query = (q_v[s, rows, :].astype(jnp.float32) * (mine * scale)).astype(
                    jnp.bfloat16
                )
                dout = (dmixed_h[s, rows, :].astype(jnp.float32) * mine).astype(jnp.bfloat16)
                log_row = log_ref[s, pl.ds(h, 1), rows]
                parts = [(rows, True)] + ([(slice(0, at), False)] if at else [])
                kept = []
                delta = jnp.zeros((1, BLOCK), jnp.float32)
                for keys, diagonal in parts:
                    prob = jnp.exp(mxu(k_v[s, keys, :], query, ROWS_BY_ROWS) - log_row)
                    if diagonal:
                        prob = jnp.where(visible, prob, 0.0)
                    dprob = mxu(v_v[s, keys, :], dout, ROWS_BY_ROWS)
                    delta += jnp.sum(prob * dprob, axis=0, keepdims=True)
                    kept.append((keys, prob, dprob))
                dquery = jnp.zeros((BLOCK, width), jnp.float32)
                for keys, prob, dprob in kept:
                    dv_f[keys, :] += mxu(prob.astype(jnp.bfloat16), dout)
                    dlogit = (prob * (dprob - delta)).astype(jnp.bfloat16)
                    dk_f[keys, :] += mxu(dlogit, query)
                    dquery += mxu(dlogit, k_v[s, keys, :], COLS_BY_COLS)
                dq_f[rows, :] += dquery * (mine * scale)
            return carry

        lax.fori_loop(0, heads, one_head, 0)
        for i, total in enumerate((dq_f, dk_f, dv_f)):
            grads_h[s, :, i * width : (i + 1) * width] = total[...].astype(jnp.bfloat16)
        for d in range(1, ways):
            grad_copy(s, d).start()
        grads_tok[s, :, span(me, 3 * width)] = grads_h[s, span(me, shard), :]

    loads[9].wait()

    def weight_step(i, carry):
        at = span(i, BLOCK)
        grad = mxu(normed_v[0, :, at], grads_h[0], COLS_BY_COLS)
        for s in range(1, seqs):
            grad += mxu(normed_v[s, :, at], grads_h[s], COLS_BY_COLS)
        for j in range(3):
            parts_w[j, at, :] = grad[:, j * width : (j + 1) * width].astype(jnp.bfloat16)
        return carry

    lax.fori_loop(0, model // BLOCK, weight_step, 0)
    for total in (sum_v, sum_k, sum_q):
        total.core_copy.start()

    o_land[0] = sum_o.add_column().astype(jnp.bfloat16)
    o_copy = [
        send(
            o_land.at[0, :, span(peer[d], width)],
            o_land.at[d, :, 0:width],
            o_send.at[d],
            o_recv.at[d],
            {"sp": peer[d]},
        )
        for d in range(1, ways)
    ]
    for copy in o_copy:
        copy.start()
    for total in (sum_v, sum_k, sum_q):
        total.add_core()
    total = o_land[0, :, span(me, width)].astype(jnp.float32)
    for d, copy in enumerate(o_copy):
        copy.wait()
        total += o_land[d + 1, :, 0:width].astype(jnp.float32)
    sum_o.piece[...] = total.astype(jnp.bfloat16)
    sum_o.spread()
    sum_v.piece[...] = sum_v.add_column().astype(jnp.bfloat16)
    sum_v.spread()
    sum_k.piece[...] = sum_k.add_column().astype(jnp.bfloat16)
    sum_k.spread()
    sum_o.ring()
    sum_q.piece[...] = sum_q.add_column().astype(jnp.bfloat16)
    sum_q.spread()
    sum_v.ring()
    sum_o.relay()

    def norm_grad(s):
        for d in range(1, ways):
            grad_copy(s, d).wait()
        dnormed = jnp.zeros((shard, model), jnp.float32)
        for j in range(ways):
            for i, weight in enumerate((wq_v, wk_v, wv_v)):
                at = (3 * j + i) * width
                dnormed += mxu(
                    grads_tok[s, :, at : at + width],
                    weight[:, j * width : (j + 1) * width],
                    ROWS_BY_ROWS,
                )
        gain = gain1_ref[...]
        _, unit, rstd = norm_forward(x_v[s].astype(jnp.float32), gain, jnp.zeros_like(gain))
        dinput, gain_grad, shift_grad = norm_backward(dnormed, unit, rstd, gain)
        tokens_ref[s] = (dresid[s] + dinput).astype(jnp.bfloat16)
        small_own[0:1, :] += gain_grad.reshape(1, model)
        small_own[1:2, :] += shift_grad.reshape(1, model)

    for copy in loads[10:14]:
        copy.wait()
    for s in range(seqs - 1):
        norm_grad(s)
    sum_k.ring()
    sum_v.relay()
    sum_q.ring()
    sum_k.relay()
    sum_o.cross()
    norm_grad(seqs - 1)
    sum_v.cross()

    steps = [[{"dp": dp + 1 - 2 * core}]]
    steps.append([{"dp": 2 * lax.rem(dp // 2 + d, columns) + core} for d in range(1, columns)])
    steps.append([{"sp": peer[d]} for d in range(1, ways)])
    slot = 0
    source = small_own
    for number, peers in enumerate(steps):
        copies = [
            send(
                source,
                small_land.at[slot + i],
                small_send.at[slot + i],
                small_recv.at[slot + i],
                device,
            )
            for i, device in enumerate(peers)
        ]
        for copy in copies:
            copy.start()
        if number == 0:
            sum_q.relay()
        elif number == 1:
            sum_k.cross()
        total = source[...]
        for i, copy in enumerate(copies):
            copy.wait()
            total += small_land[slot + i]
        slot += len(peers)
        if number == len(steps) - 1:
            small_out[...] = total
        else:
            small_sum[number] = total
            source = small_sum.at[number]

    loads[14].wait()
    for copy in routed_back:
        copy.wait()
    for s in range(seqs):
        rows = slice(s * shard, (s + 1) * shard)
        out = mxu(placer_v[:, rows], returned[...].reshape(-1, model), COLS_BY_COLS)
        block_ref[s] = (residual_v[rows, :] + out).astype(jnp.bfloat16)
    sum_q.cross()
    for s in range(seqs):
        for d in range(1, ways):
            dmixed_copy(s, d).wait_send()
    for copy in scatter:
        copy.wait()
    for total in [sum_o] + sums_w:
        total.finish()


def vmem(count):
    return [pl.BlockSpec(memory_space=pltpu.VMEM)] * count


def params(collective_id):
    return pltpu.CompilerParams(
        collective_id=collective_id, has_side_effects=True, vmem_limit_bytes=VMEM_BYTES
    )


def dma(*shape):
    return pltpu.SemaphoreType.DMA(shape)


def local(
    tokens_in,
    expert_ids,
    query_weight,
    key_weight,
    value_weight,
    out_weight,
    norm1_gain,
    norm1_shift,
    norm2_gain,
    norm2_shift,
    up_weight,
    down_weight,
    out_cotangent,
    load_mean,
):
    seq_count, shard_len, model_width = tokens_in.shape
    row_count = seq_count * shard_len
    head_dim = model_width // HEADS
    dp_ways = lax.axis_size("dp")
    sp_ways = lax.axis_size("sp")
    sp_at = lax.axis_index("sp")
    seq_len = shard_len * sp_ways
    experts = load_mean.shape[0]
    slot_count = 2 * row_count // experts
    local_experts = up_weight.shape[0]
    ff_width = up_weight.shape[1]
    width = model_width // sp_ways
    bf16 = jnp.bfloat16
    f32 = jnp.float32

    def shape(*sizes, dtype=bf16):
        return jax.ShapeDtypeStruct(sizes, dtype)

    routes = expert_ids.reshape(row_count)
    one_hot = (routes[:, None] == jnp.arange(experts, dtype=jnp.int32)[None, :]).astype(jnp.int32)
    running = jnp.cumsum(one_hot, axis=0) - 1
    slot_of = jnp.sum(running * one_hot, axis=1)
    target = routes * slot_count + slot_of
    placer = (jnp.arange(experts * slot_count, dtype=jnp.int32)[:, None] == target[None, :]).astype(
        bf16
    )
    cot_b = out_cotangent.reshape(row_count, model_width)
    cot_send = jnp.dot(placer, cot_b, preferred_element_type=f32).astype(bf16)
    cot_send = cot_send.reshape(experts, slot_count, model_width)

    def columns_of(weight):
        return lax.dynamic_slice_in_dim(weight, sp_at * width, width, axis=1)

    routed = shape(experts, slot_count, model_width)
    hbm = [pl.BlockSpec(memory_space=pl.ANY)]
    normed_all, query_h, key_h, value_h, log_total, mixed_b, arrived = pl.pallas_call(
        functools.partial(attend_forward, sp_ways, dp_ways, head_dim),
        out_shape=[
            shape(seq_count, seq_len, model_width),
            shape(seq_count, seq_len, width),
            shape(seq_count, seq_len, width),
            shape(seq_count, seq_len, width),
            shape(seq_count, 8, seq_len, dtype=f32),
            shape(seq_count, shard_len, model_width),
            routed,
        ],
        in_specs=hbm + vmem(6),
        out_specs=vmem(6) + hbm,
        scratch_shapes=[
            pltpu.VMEM((seq_count, seq_len, model_width), bf16),
            pltpu.VMEM((seq_len, width), f32),
            pltpu.VMEM((seq_count, seq_len, width), bf16),
            pltpu.VMEM((seq_len, LANES), f32),
            dma(seq_count, sp_ways),
            dma(seq_count, sp_ways),
            dma(seq_count, sp_ways),
            dma(seq_count, sp_ways),
            dma(dp_ways),
            dma(dp_ways),
            pltpu.SemaphoreType.DMA,
        ],
        compiler_params=params(0),
    )(
        cot_send,
        tokens_in,
        columns_of(query_weight),
        columns_of(key_weight),
        columns_of(value_weight),
        norm1_gain.reshape(1, model_width),
        norm1_shift.reshape(1, model_width),
    )
    mixed_b = mixed_b.reshape(row_count, model_width)
    inputs = tokens_in.reshape(row_count, model_width).astype(f32)
    attn_out = jnp.dot(mixed_b, out_weight, preferred_element_type=f32)
    residual_stream = inputs + attn_out
    normed2, _, _ = norm_forward(residual_stream, norm2_gain, norm2_shift)
    normed2_b = normed2.astype(bf16)
    outgoing = jnp.dot(placer, normed2_b, preferred_element_type=f32).astype(bf16)
    outgoing = outgoing.reshape(experts, slot_count, model_width)
    ff_own = ff_width // 2
    received_blocks = max(2 * experts, ff_own // slot_count)
    shard_size = ff_width // sp_ways
    rest = sp_ways // 2 - 1
    blocks = shard_size // slot_count
    dnormed_back, expert_out, up_own, up_rest, down_own, down_rest = pl.pallas_call(
        functools.partial(run_experts, dp_ways, sp_ways),
        out_shape=[
            routed,
            routed,
            shape(shard_size, model_width),
            shape(rest * shard_size, model_width),
            shape(blocks, slot_count, model_width),
            shape(rest * blocks, slot_count, model_width),
        ],
        in_specs=vmem(1) + hbm * 3,
        out_specs=vmem(2) + hbm * 4,
        scratch_shapes=[
            pltpu.VMEM((received_blocks, slot_count, model_width), bf16),
            pltpu.VMEM((2,) + routed.shape, bf16),
            pltpu.VMEM((ff_own, model_width), bf16),
            pltpu.VMEM((ff_own, model_width), bf16),
            pltpu.VMEM((2 * experts * slot_count, ff_own), bf16),
            pltpu.VMEM((2 * experts * slot_count, ff_own), bf16),
            pltpu.VMEM((2 * slot_count, model_width), f32),
            pltpu.VMEM(routed.shape, f32),
            pltpu.VMEM(routed.shape, bf16),
            pltpu.VMEM(routed.shape, bf16),
            pltpu.VMEM(routed.shape, bf16),
            pltpu.VMEM(routed.shape, bf16),
            pltpu.VMEM(routed.shape, bf16),
            dma(2, sp_ways // 2),
            dma(4),
            pltpu.SemaphoreType.DMA,
            dma(dp_ways),
            dma(dp_ways),
            dma(dp_ways),
            dma(dp_ways),
            dma(dp_ways // 2 + 1),
            dma(dp_ways // 2 + 1),
            dma(dp_ways // 2 + 1),
            dma(dp_ways // 2 + 1),
            dma(dp_ways // 2),
            dma(dp_ways // 2),
        ],
        compiler_params=params(3),
    )(outgoing, arrived, up_weight[0], down_weight[0])
    counts = jnp.sum(one_hot, axis=0).astype(f32)
    counts = jnp.pad(counts, (0, model_width - experts)).reshape(1, model_width)
    columns = dp_ways // 2
    rows = model_width // dp_ways
    token_shape = (seq_count, shard_len, model_width)

    def reduction(part_width):
        return [
            pltpu.VMEM((columns * rows, part_width), bf16),
            pltpu.VMEM((columns * rows, part_width), bf16),
            pltpu.VMEM((columns - 1, rows, part_width), bf16),
            pltpu.VMEM((rows, width), bf16),
            pltpu.SemaphoreType.DMA,
            pltpu.SemaphoreType.DMA,
            dma(columns),
            dma(columns),
            dma(columns),
            dma(columns),
            dma(sp_ways),
            dma(sp_ways),
            dma(sp_ways),
            dma(sp_ways),
            pltpu.SemaphoreType.DMA,
        ]

    small_slots = 1 + (columns - 1) + (sp_ways - 1)
    whole = shape(model_width, model_width)
    tokens = pltpu.VMEM(token_shape, bf16)
    by_head = pltpu.VMEM((seq_count, seq_len, width), bf16)
    square = pltpu.VMEM((model_width, model_width), bf16)
    flat = (row_count, model_width)
    *weight_grads, up_land, down_land, block_out, tokens_grad, small_sum = pl.pallas_call(
        functools.partial(backward, sp_ways, dp_ways, head_dim),
        out_shape=[whole] * 4
        + [
            shape(rest, shard_size, model_width),
            shape(rest, blocks, slot_count, model_width),
            shape(*token_shape),
            shape(*token_shape),
            shape(8, model_width, dtype=f32),
        ],
        in_specs=hbm * 17 + vmem(4),
        out_specs=hbm * 6 + vmem(3),
        scratch_shapes=[
            pltpu.VMEM(routed.shape, bf16),
            pltpu.VMEM(placer.shape, bf16),
            pltpu.VMEM(flat, bf16),
            pltpu.VMEM(flat, f32),
            square,
            tokens,
            by_head,
            by_head,
            by_head,
            pltpu.VMEM((seq_count, seq_len, model_width), bf16),
            square,
            square,
            square,
            tokens,
            pltpu.VMEM(routed.shape, bf16),
            pltpu.VMEM(token_shape, f32),
            pltpu.VMEM(flat, bf16),
            tokens,
            by_head,
            pltpu.VMEM((seq_len, width), f32),
            pltpu.VMEM((seq_len, width), f32),
            pltpu.VMEM((seq_len, width), f32),
            pltpu.VMEM((seq_count, seq_len, 3 * width), bf16),
            pltpu.VMEM((seq_count, shard_len, 3 * model_width), bf16),
            square,
            pltpu.VMEM((3, model_width, width), bf16),
            pltpu.VMEM((sp_ways, rows, model_width), bf16),
            pltpu.VMEM((8, model_width), f32),
            pltpu.VMEM((small_slots, 8, model_width), f32),
            pltpu.VMEM((2, 8, model_width), f32),
            dma(seq_count, sp_ways),
            dma(seq_count, sp_ways),
            dma(seq_count, sp_ways),
            dma(seq_count, sp_ways),
            dma(dp_ways),
            dma(dp_ways),
            dma(2, sp_ways // 2),
            dma(2, sp_ways // 2),
            dma(sp_ways),
            dma(sp_ways),
            dma(small_slots),
            dma(small_slots),
            dma(15),
        ]
        + reduction(model_width)
        + reduction(width) * 3,
        compiler_params=params(1),
    )(
        dnormed_back,
        placer,
        cot_b,
        residual_stream,
        out_weight,
        mixed_b.reshape(token_shape),
        query_h,
        key_h,
        value_h,
        normed_all,
        query_weight,
        key_weight,
        value_weight,
        tokens_in,
        expert_out,
        up_rest,
        down_rest,
        log_total,
        norm1_gain.reshape(1, model_width),
        norm2_gain.reshape(1, model_width),
        counts,
    )
    shard_shape = (shard_size, model_width)
    up_grad, down_grad = (
        sum((land[i].reshape(shard_shape).astype(f32) for i in range(rest)), own.astype(f32))[None]
        for own, land in ((up_own, up_land), (down_own.reshape(shard_shape), down_land))
    )
    query_grad, key_grad, value_grad, out_grad = (grad.astype(f32) for grad in weight_grads)
    load_now = small_sum[4, :experts] * experts / (row_count * dp_ways * sp_ways)
    load_next = 0.9 * load_mean + 0.1 * load_now
    return (
        block_out,
        tokens_grad,
        query_grad,
        key_grad,
        value_grad,
        out_grad,
        small_sum[0],
        small_sum[1],
        small_sum[2],
        small_sum[3],
        up_grad,
        down_grad,
        load_next,
    )


def solution(mesh):
    return jax.shard_map(
        local,
        mesh=mesh,
        in_specs=(
            P("dp", "sp", None),
            P("dp", "sp", None, None),
            P(),
            P(),
            P(),
            P(),
            P(),
            P(),
            P(),
            P(),
            P("dp", None, None),
            P("dp", None, None),
            P("dp", "sp", None),
            P(),
        ),
        out_specs=(
            P("dp", "sp", None),
            P("dp", "sp", None),
            P(),
            P(),
            P(),
            P(),
            P(),
            P(),
            P(),
            P(),
            P("dp", "sp", None),
            P("dp", "sp", None),
            P(),
        ),
        check_vma=False,
    )
```

```python
import functools

import jax
import jax.numpy as jnp
from jax import lax
from jax.experimental import pallas as pl
from jax.experimental.pallas import tpu as pltpu
from jax.sharding import PartitionSpec as P

HEADS = 16
MESH = pl.DeviceIdType.MESH
BLOCK = 256
LANES = 128
STEP = 1024
VMEM_BYTES = 60 * 2**20

NORM_EPSILON = 1e-05
GELU_ROOT = 0.7978845608028654
CUBIC_TERM = 0.044715

ROWS_BY_COLS = (((1,), (0,)), ((), ()))
ROWS_BY_ROWS = (((1,), (1,)), ((), ()))
COLS_BY_COLS = (((0,), (0,)), ((), ()))


def smooth(values):
    return (
        0.5
        * values
        * (1.0 + jnp.tanh(GELU_ROOT * (values + CUBIC_TERM * values * values * values)))
    )


def smooth_slope(values):
    inner = jnp.tanh(GELU_ROOT * (values + CUBIC_TERM * values * values * values))
    return 0.5 * (1.0 + inner) + 0.5 * values * (1.0 - inner * inner) * GELU_ROOT * (
        1.0 + 3.0 * CUBIC_TERM * values * values
    )


def norm_forward(values, gain, shift):
    center = jnp.mean(values, axis=-1, keepdims=True)
    offset = values - center
    rstd = lax.rsqrt(jnp.mean(offset * offset, axis=-1, keepdims=True) + NORM_EPSILON)
    unit = offset * rstd
    return (unit * gain + shift, unit, rstd)


def norm_backward(grad, unit, rstd, gain):
    scaled = grad * gain
    inner = (
        scaled
        - jnp.mean(scaled, axis=-1, keepdims=True)
        - unit * jnp.mean(scaled * unit, axis=-1, keepdims=True)
    )
    return (inner * rstd, jnp.sum(grad * unit, axis=0), jnp.sum(grad, axis=0))


def mxu(left, right, dims=ROWS_BY_COLS):
    return lax.dot_general(left, right, dims, preferred_element_type=jnp.float32)


def span(index, size):
    return pl.ds(pl.multiple_of(index * size, size), size)


def greet(peers):
    barrier = pltpu.get_barrier_semaphore()
    for peer in peers:
        pl.semaphore_signal(barrier, inc=1, device_id=peer, device_id_type=MESH)
    pl.semaphore_wait(barrier, len(peers))


def send(source, target, send_sem, recv_sem, peer):
    return pltpu.make_async_remote_copy(
        src_ref=source,
        dst_ref=target,
        send_sem=send_sem,
        recv_sem=recv_sem,
        device_id=peer,
        device_id_type=MESH,
    )


def exchange(others, source, target, send_sem, recv_sem):
    me = lax.axis_index("dp")
    return [
        send(
            source.at[flip(me, d)],
            target.at[me],
            send_sem.at[d],
            recv_sem.at[d],
            {"dp": flip(me, d)},
        )
        for d in range(1, others)
    ]


def flip(index, bits):
    bit = 1
    while bit <= bits:
        if bits & bit:
            index = index + bit - 2 * bit * lax.rem(index // bit, 2)
        bit *= 2
    return index


def forward(
    ways,
    others,
    head_dim,
    x_ref,
    cot_ref,
    wq_ref,
    wk_ref,
    wv_ref,
    wo_ref,
    ids_ref,
    gain1_ref,
    shift1_ref,
    gain2_ref,
    shift2_ref,
    normed_ref,
    q_ref,
    k_ref,
    v_ref,
    mixed_ref,
    arrived_ref,
    placer_ref,
    residual_ref,
    log_ref,
    outgoing_ref,
    counts_ref,
    x_all,
    cot_v,
    cot_out,
    wq_v,
    wk_v,
    wv_v,
    wo_v,
    placer_v,
    normed_v,
    q_v,
    k_v,
    v_v,
    mixed_f,
    mixed_h,
    mixed_tok,
    log_s,
    residual_v,
    normed2,
    x_send,
    x_recv,
    m_send,
    m_recv,
    c_send,
    c_recv,
    load_sem,
    x_sem,
    store_sem,
    own_sem,
):
    seqs, seq_len, model = x_all.shape
    shard = seq_len // ways
    width = q_v.shape[2]
    heads = width // head_dim
    slots = cot_out.shape[1]
    me = lax.axis_index("sp")
    dp = lax.axis_index("dp")
    peer = [flip(me, d) for d in range(ways)]
    near = (1, 2) if ways == 4 else tuple(range(1, ways))
    far = tuple(range(1 + len(near), ways))
    barrier = pltpu.get_barrier_semaphore()
    neighbours = [{"sp": peer[d]} for d in range(1, ways)]
    neighbours += [{"dp": flip(dp, d)} for d in range(1, others)]
    for device in neighbours:
        pl.semaphore_signal(barrier, inc=1, device_id=device, device_id_type=MESH)
    own_columns = span(me, width)
    loads = [
        pltpu.make_async_copy(source, target, load_sem.at[i])
        for i, (source, target) in enumerate(
            (
                (cot_ref, cot_v),
                (wq_ref.at[:, own_columns], wq_v),
                (wk_ref.at[:, own_columns], wk_v),
                (wv_ref.at[:, own_columns], wv_v),
                (wo_ref, wo_v),
            )
        )
    ]
    own_x = [
        pltpu.make_async_copy(x_ref.at[s], x_all.at[s, span(me, shard)], x_sem.at[s])
        for s in range(seqs)
    ]
    for copy in own_x + loads:
        copy.start()

    def x_copy(s, d):
        return send(
            x_ref.at[s],
            x_all.at[s, span(me, shard)],
            x_send.at[s, d],
            x_recv.at[s, d],
            {"sp": peer[d]},
        )

    def x_relays(s):
        if not far:
            return []
        size = shard // 2
        pieces = [
            x_all.at[s, pl.ds(pl.multiple_of(peer[1] * shard, size), size)],
            x_all.at[s, pl.ds(pl.multiple_of(peer[2] * shard + size, size), size)],
        ]
        return [
            send(piece, piece, x_send.at[s, at], x_recv.at[s, at], {"sp": peer[to]})
            for piece, at, to in zip(pieces, (0, 3), (2, 1))
        ]

    def mixed_copy(s, d):
        return send(
            mixed_h.at[s, span(peer[d], shard)],
            mixed_tok.at[s, :, own_columns],
            m_send.at[s, d],
            m_recv.at[s, d],
            {"sp": peer[d]},
        )

    tokens = seqs * shard
    ids = ids_ref[...]
    named = lax.broadcasted_iota(jnp.int32, (LANES, tokens), 0) == ids
    named = jnp.where(named, 1.0, 0.0)
    upper = lax.broadcasted_iota(jnp.int32, (tokens, tokens), 0) <= lax.broadcasted_iota(
        jnp.int32, (tokens, tokens), 1
    )
    running = mxu(named.astype(jnp.bfloat16), jnp.where(upper, 1.0, 0.0).astype(jnp.bfloat16))
    slot = jnp.sum(named * (running - 1.0), axis=0, keepdims=True).astype(jnp.int32)
    places = lax.broadcasted_iota(jnp.int32, placer_v.shape, 0) == ids * slots + slot
    placer_v[...] = jnp.where(places, 1.0, 0.0).astype(jnp.bfloat16)
    ones = jnp.ones((8, tokens), jnp.float32)
    counts_ref[...] = mxu(ones, named, ROWS_BY_ROWS)
    pl.semaphore_wait(barrier, len(neighbours))
    for d in near:
        x_copy(0, d).start()
    loads[0].wait()
    cot_out[...] = (
        mxu(placer_v[...], cot_v[...]).astype(jnp.bfloat16).reshape(cot_out.shape)
    )
    background = exchange(others, cot_out, arrived_ref, c_send, c_recv)
    own_cot = pltpu.make_async_copy(cot_out.at[dp], arrived_ref.at[dp], own_sem)
    for copy in background + [own_cot]:
        copy.start()

    lane = lax.broadcasted_iota(jnp.int32, (1, width), 1) // head_dim
    log_lane = lax.broadcasted_iota(jnp.int32, (1, LANES), 1)
    visible = lax.broadcasted_iota(jnp.int32, (BLOCK, BLOCK), 1) <= lax.broadcasted_iota(
        jnp.int32, (BLOCK, BLOCK), 0
    )
    scale = head_dim ** (-0.5)
    outs = ((normed_v, normed_ref), (q_v, q_ref), (k_v, k_ref), (v_v, v_ref))
    stores = [
        [
            pltpu.make_async_copy(source.at[s], target.at[s], store_sem.at[s, i])
            for i, (source, target) in enumerate(outs)
        ]
        for s in range(seqs)
    ]

    def project(s, d):
        rows = span(peer[d], shard)
        values = x_all[s, rows, :].astype(jnp.float32)
        normed, _, _ = norm_forward(values, gain1_ref[...], shift1_ref[...])
        normed = normed.astype(jnp.bfloat16)
        normed_v[s, rows, :] = normed
        q_v[s, rows, :] = mxu(normed, wq_v[...]).astype(jnp.bfloat16)
        k_v[s, rows, :] = mxu(normed, wk_v[...]).astype(jnp.bfloat16)
        v_v[s, rows, :] = mxu(normed, wv_v[...]).astype(jnp.bfloat16)

    for s in range(seqs):
        own_x[s].wait()
        if s == 0:
            for copy in loads[1:4]:
                copy.wait()
        project(s, 0)
        for d in near:
            x_copy(s, d).wait_recv()
        for copy in x_relays(s):
            copy.start()
        for d in near:
            project(s, d)
        for copy in x_relays(s):
            copy.wait_recv()
        if s + 1 < seqs:
            for d in near:
                x_copy(s + 1, d).start()
        if s:
            for d in range(1, ways):
                mixed_copy(s - 1, d).start()
        for d in far:
            project(s, d)
        for copy in stores[s]:
            copy.start()
        mixed_f[...] = jnp.zeros_like(mixed_f)
        log_s[...] = jnp.zeros_like(log_s)

        def one_head(h, carry):
            mine = (lane == h).astype(jnp.float32)
            for at in range(0, seq_len, BLOCK):
                rows = slice(at, at + BLOCK)
                query = (q_v[s, rows, :].astype(jnp.float32) * (mine * scale)).astype(
                    jnp.bfloat16
                )
                near = mxu(query, k_v[s, rows, :], ROWS_BY_ROWS)
                near = jnp.where(visible, near, -1e30)
                top = jnp.max(near, axis=1, keepdims=True)
                if at:
                    far = mxu(query, k_v[s, :at, :], ROWS_BY_ROWS)
                    top = jnp.maximum(top, jnp.max(far, axis=1, keepdims=True))
                near = jnp.exp(near - top)
                total = jnp.sum(near, axis=1, keepdims=True)
                if at:
                    far = jnp.exp(far - top)
                    total += jnp.sum(far, axis=1, keepdims=True)
                inverse = 1.0 / total
                out = mxu((near * inverse).astype(jnp.bfloat16), v_v[s, rows, :])
                if at:
                    out += mxu((far * inverse).astype(jnp.bfloat16), v_v[s, :at, :])
                mixed_f[rows, :] += out * mine
                log_s[rows, :] = jnp.where(log_lane == h, top + jnp.log(total), log_s[rows, :])
            return carry

        lax.fori_loop(0, heads, one_head, 0)
        log_ref[s] = jnp.transpose(log_s[...])[: log_ref.shape[1], :]
        mixed_h[s] = mixed_f[...].astype(jnp.bfloat16)
        mixed_tok[s, :, own_columns] = mixed_h[s, span(me, shard), :]
    for d in range(1, ways):
        mixed_copy(seqs - 1, d).start()

    loads[4].wait()
    for s in range(seqs):
        for d in range(1, ways):
            mixed_copy(s, d).wait_recv()
        rows = slice(s * shard, (s + 1) * shard)
        values = x_all[s, span(me, shard), :].astype(jnp.float32)
        values += mxu(mixed_tok[s], wo_v[...])
        residual_v[rows, :] = values
        normed, _, _ = norm_forward(values, gain2_ref[...], shift2_ref[...])
        normed2[rows, :] = normed.astype(jnp.bfloat16)
    last = [
        pltpu.make_async_copy(source, target, store_sem.at[seqs, i])
        for i, (source, target) in enumerate(
            ((mixed_tok, mixed_ref), (residual_v, residual_ref), (placer_v, placer_ref))
        )
    ]
    for copy in last:
        copy.start()
    outgoing_ref[...] = (
        mxu(placer_v[...], normed2[...]).astype(jnp.bfloat16).reshape(outgoing_ref.shape)
    )
    for s in range(seqs):
        for d in near:
            x_copy(s, d).wait_send()
        for copy in x_relays(s):
            copy.wait_send()
        for d in range(1, ways):
            mixed_copy(s, d).wait_send()
        for copy in stores[s]:
            copy.wait()
    for copy in background + [own_cot] + last:
        copy.wait()


def pair_of(sp):
    core = lax.rem(lax.axis_index("dp"), 2)
    along_x, along_y = flip(sp, 1), flip(sp, 2)
    return along_x + core * (along_y - along_x)


def shards_of(sp, ways):
    shards = [sp, flip(pair_of(sp), 3)]
    bit = 4
    while bit < ways:
        shards += [flip(shard, bit) for shard in shards]
        bit *= 2
    return shards


def run_experts(
    others,
    ways,
    outgoing_ref,
    cot_ref,
    up_ref,
    down_ref,
    back_ref,
    result_ref,
    up_own,
    up_rest,
    down_own,
    down_rest,
    received,
    arrived,
    up_v,
    down_v,
    hidden,
    slope_v,
    total,
    dn_own,
    dn_pair,
    dn_land,
    dnormed,
    out_pair,
    out_land,
    w_sem,
    o_sem,
    c_sem,
    a_send,
    a_recv,
    b_send,
    b_recv,
    f_send,
    f_recv,
    p_send,
    p_recv,
    e_send,
    e_recv,
):
    slots, width = received.shape[1:]
    rows = others * slots
    ff = up_v.shape[0]
    groups = others // 2
    me = lax.axis_index("dp")
    sp = lax.axis_index("sp")
    chip = me // 2
    pair = {"sp": pair_of(sp)}
    shards = shards_of(sp, ways)
    size = ff // len(shards)
    loads = [
        pltpu.make_async_copy(
            source.at[span(shard, size)], target.at[i * size : (i + 1) * size], w_sem.at[j, i]
        )
        for j, (source, target) in enumerate(((down_ref, down_v), (up_ref, up_v)))
        for i, shard in enumerate(shards)
    ]
    own_cot = pltpu.make_async_copy(cot_ref, arrived.at[0], c_sem.at[0])
    own_rows = pltpu.make_async_copy(outgoing_ref.at[me], received.at[me], c_sem.at[1])
    own_back = pltpu.make_async_copy(dnormed.at[me], back_ref.at[me], c_sem.at[2])
    own_rows.start()
    own_cot.start()
    for copy in loads:
        copy.start()
    greet([{"dp": flip(me, d)} for d in range(1, others)] + [pair])
    inward = exchange(others, outgoing_ref, received.at[0:others], a_send, a_recv)
    outward = exchange(others, dnormed, back_ref, b_send, b_recv)
    near = [flip(chip, group) for group in range(groups)]
    chips = [pl.ds(2 * near[group], 2) for group in range(groups)]
    forward = [
        send(
            received.at[chips[group]],
            received.at[pl.ds(others + 2 * near[group], 2)],
            f_send.at[group],
            f_recv.at[group],
            pair,
        )
        for group in range(groups)
    ]
    cot_copy = send(cot_ref, arrived.at[1], f_send.at[groups], f_recv.at[groups], pair)
    dn_copy = [
        send(
            dn_pair.at[chips[group]],
            dn_land.at[chips[group]],
            p_send.at[group],
            p_recv.at[group],
            pair,
        )
        for group in range(groups)
    ]
    out_copy = [
        send(
            out_pair.at[chips[group]],
            out_land.at[chips[group]],
            e_send.at[group],
            e_recv.at[group],
            pair,
        )
        for group in range(groups)
    ]

    early = range(groups // 2)
    middle = range(groups // 2, 3 * groups // 4)
    late = range(3 * groups // 4, groups)
    for copy in inward[: 2 * late[0] - 1]:
        copy.start()
    cot_copy.start()
    own_rows.wait()

    def slab_of(half, group):
        return pl.ds(pl.multiple_of(half * rows + near[group] * (2 * slots), 2 * slots), 2 * slots)

    def cot_half(half):
        def cot_step(i, carry):
            at = span(i, STEP)
            cot = arrived[half].reshape(rows, width)
            slope_v[half * rows : (half + 1) * rows, at] = mxu(
                cot, down_v[at, :], ROWS_BY_ROWS
            ).astype(jnp.bfloat16)
            return carry

        lax.fori_loop(0, ff // STEP, cot_step, 0)

    def up_half(half, group):
        slab = slab_of(half, group)
        total[...] = jnp.zeros_like(total)

        def up_step(i, carry):
            at = span(i, STEP)
            tokens = received[pl.ds(half * others + 2 * near[group], 2)].reshape(2 * slots, width)
            pre = mxu(tokens, up_v[at, :], ROWS_BY_ROWS)
            square = pre * pre
            inner = jnp.tanh(GELU_ROOT * pre * (1.0 + CUBIC_TERM * square))
            gate = 0.5 * (1.0 + inner)
            hidden[slab, at] = (pre * gate).astype(jnp.bfloat16)
            slope = gate + (0.5 * GELU_ROOT) * pre * (1.0 - inner * inner) * (
                1.0 + (3.0 * CUBIC_TERM) * square
            )
            dpre = (slope_v[slab, at].astype(jnp.float32) * slope).astype(jnp.bfloat16)
            slope_v[slab, at] = dpre
            total[...] += mxu(dpre, up_v[at, :])
            return carry

        lax.fori_loop(0, ff // STEP, up_step, 0)
        shaped = total[...].reshape(2, slots, width)
        if half:
            dn_pair[chips[group]] = shaped.astype(jnp.bfloat16)
            dn_copy[group].start()
        else:
            dn_own[chips[group]] = shaped

    def out_half(half, group):
        at = chips[group]
        out = mxu(hidden[slab_of(half, group), :], down_v[...]).reshape(2, slots, width)
        if half:
            out_pair[at] = out.astype(jnp.bfloat16)
            out_copy[group].start()
        else:
            out_copy[group].wait_recv()
            result_ref[at] = (out + out_land[at].astype(jnp.float32)).astype(jnp.bfloat16)

    def pass_on(group):
        for d in (2 * group, 2 * group + 1):
            if d:
                inward[d - 1].wait_recv()
        forward[group].start()

    def finish(group):
        dn_copy[group].wait_recv()
        at = chips[group]
        dnormed[at] = (dn_own[at] + dn_land[at].astype(jnp.float32)).astype(jnp.bfloat16)
        for d in (2 * group, 2 * group + 1):
            if d:
                outward[d - 1].start()
            else:
                own_back.start()

    def up_pair(group):
        forward[group].wait_recv()
        up_half(1, group)

    pass_on(0)
    own_cot.wait()
    for copy in loads[: len(shards)]:
        copy.wait()
    cot_half(0)
    for copy in loads[len(shards) :]:
        copy.wait()
    up_half(0, 0)
    for group in early[1:]:
        pass_on(group)
    for copy in inward[2 * middle[0] - 1 : 2 * late[0] - 1]:
        copy.wait_send()
    for copy in inward[2 * late[0] - 1 :]:
        copy.start()
    cot_copy.wait_recv()
    cot_half(1)
    for group in middle:
        pass_on(group)
    up_pair(0)
    for group in early[1:]:
        up_half(0, group)
        up_pair(group)
    for group in middle:
        up_half(0, group)
    for group in late:
        pass_on(group)
    for group in early:
        finish(group)
    for group in middle:
        up_pair(group)
    for group in late:
        up_half(0, group)
    for group in middle:
        finish(group)
    for group in late:
        up_pair(group)
    for group in range(groups):
        out_half(1, group)
    for group in late:
        finish(group)

    def grad(target, left, right_ref, block=0):
        def grad_step(i, carry):
            at = span(i, STEP)
            right = right_ref[...].reshape(2 * rows, width)
            out = mxu(left[:, at], right, COLS_BY_COLS).astype(jnp.bfloat16)
            if block:
                target[span(i, STEP // block)] = out.reshape(STEP // block, block, width)
            else:
                target[at, :] = out
            return carry

        lax.fori_loop(0, ff // STEP, grad_step, 0)

    grad(up_v, slope_v, received.at[0 : 2 * others])
    for copy in forward:
        copy.wait_send()
    grad(received, hidden, arrived, slots)
    first, every = size // slots, ff // slots
    stores = [
        pltpu.make_async_copy(source, target, o_sem.at[i])
        for i, (source, target) in enumerate(
            (
                (up_v.at[0:size], up_own),
                (up_v.at[size:ff], up_rest),
                (received.at[0:first], down_own),
                (received.at[first:every], down_rest),
            )
        )
    ]
    for copy in stores:
        copy.start()
    for group in range(groups):
        out_half(0, group)
    for copy in inward[: 2 * middle[0] - 1] + inward[2 * late[0] - 1 :]:
        copy.wait_send()
    for copy in [cot_copy] + dn_copy + out_copy:
        copy.wait_send()
    for copy in outward + stores + [own_back]:
        copy.wait()


class Reduction:
    def __init__(self, ways, columns, part, out, scratch):
        (
            self.core_land,
            self.core_sum,
            self.column_land,
            self.piece,
            core_send,
            core_recv,
            column_send,
            column_recv,
            spread_send,
            spread_recv,
            ring_send,
            ring_recv,
            cross_send,
            cross_recv,
            own_sem,
        ) = scratch
        me = lax.axis_index("sp")
        dp = lax.axis_index("dp")
        core = lax.rem(dp, 2)
        column = dp // 2
        twin = {"dp": dp + 1 - 2 * core}
        self.ways, self.columns, self.part = ways, columns, part
        self.core, self.column = core, column
        rows, width = self.piece.shape
        self.rows = rows

        def beside(d):
            return {"dp": 2 * lax.rem(column + d, columns) + core}

        def block(at_core, at_column, at_sp, count):
            first = pl.multiple_of((at_core * columns + at_column) * rows, rows)
            return out.at[pl.ds(first, count * rows), span(at_sp, width)]

        self.core_copy = send(
            part.at[span(1 - core, columns * rows)], self.core_land, core_send, core_recv, twin
        )
        self.column_copy = [
            send(
                self.core_sum.at[span(lax.rem(column + d, columns), rows)],
                self.column_land.at[d - 1],
                column_send.at[d],
                column_recv.at[d],
                beside(d),
            )
            for d in range(1, columns)
        ]
        spot = block(core, column, me, 1)
        self.own = pltpu.make_async_copy(self.piece, spot, own_sem)
        self.spread_copy = [
            send(self.piece, spot, spread_send.at[d], spread_recv.at[d], beside(d))
            for d in range(1, columns)
        ]
        origin = [flip(me, d) for d in range(ways)]
        half = [block(core, 0, at, columns) for at in origin]
        self.relays = []
        direct = range(1, ways)
        if ways == 4:
            direct = (1, 2)
            count = columns * rows // 2
            for i, (d, to) in enumerate(((1, 2), (2, 1))):
                first = pl.multiple_of(core * columns * rows + i * count, count)
                piece = out.at[pl.ds(first, count), span(origin[d], width)]
                self.relays.append(
                    send(piece, piece, ring_send.at[i], ring_recv.at[i], {"sp": origin[to]})
                )
            ring_send, ring_recv = ring_send.at[1:ways], ring_recv.at[1:ways]
        self.ring_copy = [
            send(half[0], half[0], ring_send.at[d], ring_recv.at[d], {"sp": origin[d]})
            for d in direct
        ]
        self.cross_copy = [
            send(half[d], half[d], cross_send.at[d], cross_recv.at[d], twin) for d in range(ways)
        ]

    def add_core(self):
        self.core_copy.wait()
        self.core_sum[...] = (
            self.part[span(self.core, self.columns * self.rows), :].astype(jnp.float32)
            + self.core_land[...].astype(jnp.float32)
        ).astype(jnp.bfloat16)
        for copy in self.column_copy:
            copy.start()

    def add_column(self):
        total = self.core_sum[span(self.column, self.rows), :].astype(jnp.float32)
        for d, copy in enumerate(self.column_copy):
            copy.wait()
            total += self.column_land[d].astype(jnp.float32)
        return total

    def spread(self):
        self.own.start()
        for copy in self.spread_copy:
            copy.start()

    def ring(self):
        self.own.wait()
        for copy in self.spread_copy:
            copy.wait()
        for copy in self.ring_copy:
            copy.start()
        self.cross_copy[0].start()

    def relay(self):
        for ring, cross in zip(self.ring_copy, self.cross_copy[1:]):
            ring.wait_recv()
            cross.start()
        for relay in self.relays:
            relay.start()

    def cross(self):
        for relay in self.relays:
            relay.wait_recv()
        if self.relays:
            self.cross_copy[3].start()

    def finish(self):
        for copy in self.ring_copy + self.relays:
            copy.wait_send()
        for copy in self.cross_copy:
            copy.wait()


def backward(
    ways,
    others,
    head_dim,
    back_ref,
    placer_ref,
    cot_ref,
    residual_ref,
    wo_ref,
    mixed_ref,
    q_ref,
    k_ref,
    v_ref,
    normed_ref,
    wq_ref,
    wk_ref,
    wv_ref,
    x_ref,
    result_ref,
    up_rest,
    down_rest,
    log_ref,
    gain1_ref,
    gain2_ref,
    counts_ref,
    out_q,
    out_k,
    out_v,
    out_o,
    up_land,
    down_land,
    block_ref,
    tokens_ref,
    small_out,
    back_v,
    placer_v,
    cot_v,
    residual_v,
    wo_v,
    mixed_v,
    q_v,
    k_v,
    v_v,
    normed_v,
    wq_v,
    wk_v,
    wv_v,
    x_v,
    returned,
    dresid,
    dattn,
    dmixed,
    dmixed_h,
    dq_f,
    dk_f,
    dv_f,
    grads_h,
    grads_tok,
    part_o,
    parts_w,
    o_land,
    small_own,
    small_land,
    small_sum,
    m_send,
    m_recv,
    g_send,
    g_recv,
    c_send,
    c_recv,
    s_send,
    s_recv,
    o_send,
    o_recv,
    small_send,
    small_recv,
    load_sem,
    *scratch,
):
    seqs, shard, model = x_v.shape
    seq_len, width = q_v.shape[1:]
    heads = width // head_dim
    columns = others // 2
    me = lax.axis_index("sp")
    dp = lax.axis_index("dp")
    core = lax.rem(dp, 2)
    peer = [lax.rem(me + d, ways) for d in range(ways)]
    barrier = pltpu.get_barrier_semaphore()
    neighbours = [{"sp": peer[d]} for d in range(1, ways)]
    neighbours += [{"dp": flip(dp, d)} for d in range(1, others)]
    for device in neighbours:
        pl.semaphore_signal(barrier, inc=1, device_id=device, device_id_type=MESH)
    sources = (
        (back_ref, back_v),
        (placer_ref, placer_v),
        (residual_ref, residual_v),
        (cot_ref, cot_v),
        (wo_ref, wo_v),
        (mixed_ref, mixed_v),
        (q_ref, q_v),
        (k_ref, k_v),
        (v_ref, v_v),
        (normed_ref, normed_v),
        (wq_ref, wq_v),
        (wk_ref, wk_v),
        (wv_ref, wv_v),
        (x_ref, x_v),
        (result_ref.at[dp], returned.at[dp]),
    )
    loads = [
        pltpu.make_async_copy(source, target, load_sem.at[i])
        for i, (source, target) in enumerate(sources)
    ]
    for copy in loads:
        copy.start()

    def dmixed_copy(s, d):
        return send(
            dmixed.at[s, :, span(peer[d], width)],
            dmixed_h.at[s, span(me, shard)],
            m_send.at[s, d],
            m_recv.at[s, d],
            {"sp": peer[d]},
        )

    def grad_copy(s, d):
        return send(
            grads_h.at[s, span(peer[d], shard)],
            grads_tok.at[s, :, span(me, 3 * width)],
            g_send.at[s, d],
            g_recv.at[s, d],
            {"sp": peer[d]},
        )

    small_own[...] = jnp.zeros_like(small_own)
    small_own[4:5, 0:LANES] = counts_ref[0:1, :]
    for s in range(seqs):
        if s == 0:
            for copy in loads[:4]:
                copy.wait()
        rows = slice(s * shard, (s + 1) * shard)
        dnormed = mxu(placer_v[:, rows], back_v[...].reshape(-1, model), COLS_BY_COLS)
        gain = gain2_ref[...]
        _, unit, rstd = norm_forward(residual_v[rows, :], gain, jnp.zeros_like(gain))
        dinput, gain_grad, shift_grad = norm_backward(dnormed, unit, rstd, gain)
        total = cot_v[rows, :].astype(jnp.float32) + dinput
        dresid[s] = total
        dattn[rows, :] = total.astype(jnp.bfloat16)
        small_own[2:3, :] += gain_grad.reshape(1, model)
        small_own[3:4, :] += shift_grad.reshape(1, model)
        if s == 0:
            loads[4].wait()
        dmixed[s] = mxu(dattn[rows, :], wo_v[...], ROWS_BY_ROWS).astype(jnp.bfloat16)
        if s == 0:
            pl.semaphore_wait(barrier, len(neighbours))
        for d in range(1, ways):
            dmixed_copy(s, d).start()
    routed_back = exchange(others, result_ref, returned, c_send, c_recv)
    for copy in routed_back[: others // 2 - 1]:
        copy.start()
    shards = shards_of(me, ways)
    scatter = []
    for j, (rest, land) in enumerate(((up_rest, up_land), (down_rest, down_land))):
        size = land.shape[1]
        scatter += [
            send(
                rest.at[(i - 1) * size : i * size],
                land.at[i - 1],
                s_send.at[j, i],
                s_recv.at[j, i],
                {"sp": shards[i]},
            )
            for i in range(1, len(shards))
        ]
    sum_o = Reduction(ways, columns, part_o, out_o, scratch[:15])
    sums_w = [
        Reduction(ways, columns, parts_w.at[i], out, scratch[15 * (i + 1) : 15 * (i + 2)])
        for i, out in enumerate((out_q, out_k, out_v))
    ]
    sum_q, sum_k, sum_v = sums_w

    loads[5].wait()

    def out_step(i, carry):
        at = span(i, BLOCK)
        left = mixed_v[:, :, at].reshape(seqs * shard, BLOCK)
        part_o[at, :] = mxu(left, dattn[...], COLS_BY_COLS).astype(jnp.bfloat16)
        return carry

    lax.fori_loop(0, model // BLOCK, out_step, 0)
    sum_o.core_copy.start()
    for copy in loads[6:9]:
        copy.wait()

    lane = lax.broadcasted_iota(jnp.int32, (1, width), 1) // head_dim
    visible = lax.broadcasted_iota(jnp.int32, (BLOCK, BLOCK), 0) <= lax.broadcasted_iota(
        jnp.int32, (BLOCK, BLOCK), 1
    )
    scale = head_dim ** (-0.5)
    for s in range(seqs):
        dmixed_h[s, span(me, shard), :] = dmixed[s, :, span(me, width)]
        for d in range(1, ways):
            dmixed_copy(s, d).wait_recv()
        if s == 0:
            sum_o.add_core()
            for copy in scatter:
                copy.start()
        dq_f[...] = jnp.zeros_like(dq_f)
        dk_f[...] = jnp.zeros_like(dk_f)
        dv_f[...] = jnp.zeros_like(dv_f)

        def one_head(h, carry):
            mine = (lane == h).astype(jnp.float32)
            for at in range(0, seq_len, BLOCK):
                rows = slice(at, at + BLOCK)
                query = (q_v[s, rows, :].astype(jnp.float32) * (mine * scale)).astype(
                    jnp.bfloat16
                )
                dout = (dmixed_h[s, rows, :].astype(jnp.float32) * mine).astype(jnp.bfloat16)
                log_row = log_ref[s, pl.ds(h, 1), rows]
                parts = [(rows, True)] + ([(slice(0, at), False)] if at else [])
                kept = []
                delta = jnp.zeros((1, BLOCK), jnp.float32)
                for keys, diagonal in parts:
                    prob = jnp.exp(mxu(k_v[s, keys, :], query, ROWS_BY_ROWS) - log_row)
                    if diagonal:
                        prob = jnp.where(visible, prob, 0.0)
                    dprob = mxu(v_v[s, keys, :], dout, ROWS_BY_ROWS)
                    delta += jnp.sum(prob * dprob, axis=0, keepdims=True)
                    kept.append((keys, prob, dprob))
                dquery = jnp.zeros((BLOCK, width), jnp.float32)
                for keys, prob, dprob in kept:
                    dv_f[keys, :] += mxu(prob.astype(jnp.bfloat16), dout)
                    dlogit = (prob * (dprob - delta)).astype(jnp.bfloat16)
                    dk_f[keys, :] += mxu(dlogit, query)
                    dquery += mxu(dlogit, k_v[s, keys, :], COLS_BY_COLS)
                dq_f[rows, :] += dquery * (mine * scale)
            return carry

        lax.fori_loop(0, heads, one_head, 0)
        for i, total in enumerate((dq_f, dk_f, dv_f)):
            grads_h[s, :, i * width : (i + 1) * width] = total[...].astype(jnp.bfloat16)
        for d in range(1, ways):
            grad_copy(s, d).start()
        grads_tok[s, :, span(me, 3 * width)] = grads_h[s, span(me, shard), :]
        if s == 0:
            for copy in routed_back[others // 2 - 1 : 3 * others // 4 - 1]:
                copy.start()

    loads[9].wait()

    def weight_step(i, carry):
        at = span(i, BLOCK)
        grad = mxu(normed_v[0, :, at], grads_h[0], COLS_BY_COLS)
        for s in range(1, seqs):
            grad += mxu(normed_v[s, :, at], grads_h[s], COLS_BY_COLS)
        for j in range(3):
            parts_w[j, at, :] = grad[:, j * width : (j + 1) * width].astype(jnp.bfloat16)
        return carry

    lax.fori_loop(0, model // BLOCK, weight_step, 0)
    for total in (sum_v, sum_k, sum_q):
        total.core_copy.start()

    o_land[0] = sum_o.add_column().astype(jnp.bfloat16)
    o_copy = [
        send(
            o_land.at[0, :, span(peer[d], width)],
            o_land.at[d, :, 0:width],
            o_send.at[d],
            o_recv.at[d],
            {"sp": peer[d]},
        )
        for d in range(1, ways)
    ]
    for copy in o_copy:
        copy.start()
    for total in (sum_v, sum_k, sum_q):
        total.add_core()
    for total in (sum_v, sum_k, sum_q):
        total.piece[...] = total.add_column().astype(jnp.bfloat16)
        total.spread()

    def norm_grad(s):
        for d in range(1, ways):
            grad_copy(s, d).wait()
        dnormed = jnp.zeros((shard, model), jnp.float32)
        for j in range(ways):
            for i, weight in enumerate((wq_v, wk_v, wv_v)):
                at = (3 * j + i) * width
                dnormed += mxu(
                    grads_tok[s, :, at : at + width],
                    weight[:, j * width : (j + 1) * width],
                    ROWS_BY_ROWS,
                )
        gain = gain1_ref[...]
        _, unit, rstd = norm_forward(x_v[s].astype(jnp.float32), gain, jnp.zeros_like(gain))
        dinput, gain_grad, shift_grad = norm_backward(dnormed, unit, rstd, gain)
        tokens_ref[s] = (dresid[s] + dinput).astype(jnp.bfloat16)
        small_own[0:1, :] += gain_grad.reshape(1, model)
        small_own[1:2, :] += shift_grad.reshape(1, model)

    for copy in loads[10:14]:
        copy.wait()
    for s in range(seqs - 1):
        norm_grad(s)
    sum_v.ring()
    total = o_land[0, :, span(me, width)].astype(jnp.float32)
    for d, copy in enumerate(o_copy):
        copy.wait()
        total += o_land[d + 1, :, 0:width].astype(jnp.float32)
    sum_o.piece[...] = total.astype(jnp.bfloat16)
    sum_o.spread()
    sum_k.ring()
    sum_q.ring()
    for copy in routed_back[3 * others // 4 - 1 :]:
        copy.start()
    sum_v.relay()
    norm_grad(seqs - 1)
    sum_o.ring()
    sum_k.relay()

    steps = [[{"dp": dp + 1 - 2 * core}]]
    steps.append([{"dp": 2 * lax.rem(dp // 2 + d, columns) + core} for d in range(1, columns)])
    steps.append([{"sp": peer[d]} for d in range(1, ways)])
    slot = 0
    source = small_own
    for number, peers in enumerate(steps):
        copies = [
            send(
                source,
                small_land.at[slot + i],
                small_send.at[slot + i],
                small_recv.at[slot + i],
                device,
            )
            for i, device in enumerate(peers)
        ]
        for copy in copies:
            copy.start()
        if number == 0:
            sum_q.relay()
        elif number == 1:
            sum_v.cross()
            sum_o.relay()
        total = source[...]
        for i, copy in enumerate(copies):
            copy.wait()
            total += small_land[slot + i]
        slot += len(peers)
        if number == len(steps) - 1:
            small_out[...] = total
        else:
            small_sum[number] = total
            source = small_sum.at[number]

    loads[14].wait()
    for copy in routed_back:
        copy.wait()
    for s in range(seqs):
        rows = slice(s * shard, (s + 1) * shard)
        out = mxu(placer_v[:, rows], returned[...].reshape(-1, model), COLS_BY_COLS)
        block_ref[s] = (residual_v[rows, :] + out).astype(jnp.bfloat16)
    sum_k.cross()
    sum_q.cross()
    sum_o.cross()
    for s in range(seqs):
        for d in range(1, ways):
            dmixed_copy(s, d).wait_send()
    for copy in scatter:
        copy.wait()
    for total in [sum_o] + sums_w:
        total.finish()


def vmem(count):
    return [pl.BlockSpec(memory_space=pltpu.VMEM)] * count


def params(collective_id):
    return pltpu.CompilerParams(
        collective_id=collective_id, has_side_effects=True, vmem_limit_bytes=VMEM_BYTES
    )


def dma(*shape):
    return pltpu.SemaphoreType.DMA(shape)


def local(
    tokens_in,
    expert_ids,
    query_weight,
    key_weight,
    value_weight,
    out_weight,
    norm1_gain,
    norm1_shift,
    norm2_gain,
    norm2_shift,
    up_weight,
    down_weight,
    out_cotangent,
    load_mean,
):
    seq_count, shard_len, model_width = tokens_in.shape
    row_count = seq_count * shard_len
    head_dim = model_width // HEADS
    dp_ways = lax.axis_size("dp")
    sp_ways = lax.axis_size("sp")
    sp_at = lax.axis_index("sp")
    seq_len = shard_len * sp_ways
    experts = load_mean.shape[0]
    slot_count = 2 * row_count // experts
    local_experts = up_weight.shape[0]
    ff_width = up_weight.shape[1]
    width = model_width // sp_ways
    bf16 = jnp.bfloat16
    f32 = jnp.float32

    def shape(*sizes, dtype=bf16):
        return jax.ShapeDtypeStruct(sizes, dtype)

    cot_b = out_cotangent.reshape(row_count, model_width)
    hbm = [pl.BlockSpec(memory_space=pl.ANY)]
    routed = shape(experts, slot_count, model_width)
    square = pltpu.VMEM((model_width, model_width), bf16)
    by_head = pltpu.VMEM((seq_count, seq_len, width), bf16)
    token_shape = (seq_count, shard_len, model_width)
    whole_tokens = pltpu.VMEM((seq_count, seq_len, model_width), bf16)
    weight_columns = pltpu.VMEM((model_width, width), bf16)
    slots = (experts * slot_count, row_count)
    flat = (row_count, model_width)
    (
        normed_all,
        query_h,
        key_h,
        value_h,
        mixed_b,
        arrived,
        placer,
        residual_stream,
        log_total,
        outgoing,
        counts,
    ) = pl.pallas_call(
        functools.partial(forward, sp_ways, dp_ways, head_dim),
        out_shape=[
            shape(seq_count, seq_len, model_width),
            shape(seq_count, seq_len, width),
            shape(seq_count, seq_len, width),
            shape(seq_count, seq_len, width),
            shape(*token_shape),
            routed,
            shape(*slots),
            shape(*flat, dtype=f32),
            shape(seq_count, 8, seq_len, dtype=f32),
            routed,
            shape(8, LANES, dtype=f32),
        ],
        in_specs=hbm * 6 + vmem(5),
        out_specs=hbm * 8 + vmem(3),
        scratch_shapes=[
            whole_tokens,
            pltpu.VMEM(flat, bf16),
            pltpu.VMEM(routed.shape, bf16),
            weight_columns,
            weight_columns,
            weight_columns,
            square,
            pltpu.VMEM(slots, bf16),
            whole_tokens,
            by_head,
            by_head,
            by_head,
            pltpu.VMEM((seq_len, width), f32),
            by_head,
            pltpu.VMEM(token_shape, bf16),
            pltpu.VMEM((seq_len, LANES), f32),
            pltpu.VMEM(flat, f32),
            pltpu.VMEM(flat, bf16),
            dma(seq_count, sp_ways),
            dma(seq_count, sp_ways),
            dma(seq_count, sp_ways),
            dma(seq_count, sp_ways),
            dma(dp_ways),
            dma(dp_ways),
            dma(5),
            dma(seq_count),
            dma(seq_count + 1, 4),
            pltpu.SemaphoreType.DMA,
        ],
        compiler_params=params(0),
    )(
        tokens_in,
        cot_b,
        query_weight,
        key_weight,
        value_weight,
        out_weight,
        expert_ids.reshape(1, row_count),
        *(
            vector.reshape(1, model_width)
            for vector in (norm1_gain, norm1_shift, norm2_gain, norm2_shift)
        ),
    )
    ff_own = ff_width // 2
    received_blocks = max(2 * experts, ff_own // slot_count)
    shard_size = ff_width // sp_ways
    rest = sp_ways // 2 - 1
    blocks = shard_size // slot_count
    dnormed_back, expert_out, up_own, up_rest, down_own, down_rest = pl.pallas_call(
        functools.partial(run_experts, dp_ways, sp_ways),
        out_shape=[
            routed,
            routed,
            shape(shard_size, model_width),
            shape(rest * shard_size, model_width),
            shape(blocks, slot_count, model_width),
            shape(rest * blocks, slot_count, model_width),
        ],
        in_specs=hbm * 4,
        out_specs=hbm + vmem(1) + hbm * 4,
        scratch_shapes=[
            pltpu.VMEM((received_blocks, slot_count, model_width), bf16),
            pltpu.VMEM((2,) + routed.shape, bf16),
            pltpu.VMEM((ff_own, model_width), bf16),
            pltpu.VMEM((ff_own, model_width), bf16),
            pltpu.VMEM((2 * experts * slot_count, ff_own), bf16),
            pltpu.VMEM((2 * experts * slot_count, ff_own), bf16),
            pltpu.VMEM((2 * slot_count, model_width), f32),
            pltpu.VMEM(routed.shape, f32),
            pltpu.VMEM(routed.shape, bf16),
            pltpu.VMEM(routed.shape, bf16),
            pltpu.VMEM(routed.shape, bf16),
            pltpu.VMEM(routed.shape, bf16),
            pltpu.VMEM(routed.shape, bf16),
            dma(2, sp_ways // 2),
            dma(4),
            dma(3),
            dma(dp_ways),
            dma(dp_ways),
            dma(dp_ways),
            dma(dp_ways),
            dma(dp_ways // 2 + 1),
            dma(dp_ways // 2 + 1),
            dma(dp_ways // 2 + 1),
            dma(dp_ways // 2 + 1),
            dma(dp_ways // 2),
            dma(dp_ways // 2),
        ],
        compiler_params=params(3),
    )(outgoing, arrived, up_weight[0], down_weight[0])
    columns = dp_ways // 2
    rows = model_width // dp_ways

    def reduction(part_width):
        return [
            pltpu.VMEM((columns * rows, part_width), bf16),
            pltpu.VMEM((columns * rows, part_width), bf16),
            pltpu.VMEM((columns - 1, rows, part_width), bf16),
            pltpu.VMEM((rows, width), bf16),
            pltpu.SemaphoreType.DMA,
            pltpu.SemaphoreType.DMA,
            dma(columns),
            dma(columns),
            dma(columns),
            dma(columns),
            dma(sp_ways),
            dma(sp_ways),
            dma(sp_ways),
            dma(sp_ways),
            pltpu.SemaphoreType.DMA,
        ]

    small_slots = 1 + (columns - 1) + (sp_ways - 1)
    whole = shape(model_width, model_width)
    tokens = pltpu.VMEM(token_shape, bf16)
    *weight_grads, up_land, down_land, block_out, tokens_grad, small_sum = pl.pallas_call(
        functools.partial(backward, sp_ways, dp_ways, head_dim),
        out_shape=[whole] * 4
        + [
            shape(rest, shard_size, model_width),
            shape(rest, blocks, slot_count, model_width),
            shape(*token_shape),
            shape(*token_shape),
            shape(8, model_width, dtype=f32),
        ],
        in_specs=hbm * 17 + vmem(4),
        out_specs=hbm * 6 + vmem(3),
        scratch_shapes=[
            pltpu.VMEM(routed.shape, bf16),
            pltpu.VMEM(placer.shape, bf16),
            pltpu.VMEM(flat, bf16),
            pltpu.VMEM(flat, f32),
            square,
            tokens,
            by_head,
            by_head,
            by_head,
            whole_tokens,
            square,
            square,
            square,
            tokens,
            pltpu.VMEM(routed.shape, bf16),
            pltpu.VMEM(token_shape, f32),
            pltpu.VMEM(flat, bf16),
            tokens,
            by_head,
            pltpu.VMEM((seq_len, width), f32),
            pltpu.VMEM((seq_len, width), f32),
            pltpu.VMEM((seq_len, width), f32),
            pltpu.VMEM((seq_count, seq_len, 3 * width), bf16),
            pltpu.VMEM((seq_count, shard_len, 3 * model_width), bf16),
            square,
            pltpu.VMEM((3, model_width, width), bf16),
            pltpu.VMEM((sp_ways, rows, model_width), bf16),
            pltpu.VMEM((8, model_width), f32),
            pltpu.VMEM((small_slots, 8, model_width), f32),
            pltpu.VMEM((2, 8, model_width), f32),
            dma(seq_count, sp_ways),
            dma(seq_count, sp_ways),
            dma(seq_count, sp_ways),
            dma(seq_count, sp_ways),
            dma(dp_ways),
            dma(dp_ways),
            dma(2, sp_ways // 2),
            dma(2, sp_ways // 2),
            dma(sp_ways),
            dma(sp_ways),
            dma(small_slots),
            dma(small_slots),
            dma(15),
        ]
        + reduction(model_width)
        + reduction(width) * 3,
        compiler_params=params(1),
    )(
        dnormed_back,
        placer,
        cot_b,
        residual_stream,
        out_weight,
        mixed_b,
        query_h,
        key_h,
        value_h,
        normed_all,
        query_weight,
        key_weight,
        value_weight,
        tokens_in,
        expert_out,
        up_rest,
        down_rest,
        log_total,
        norm1_gain.reshape(1, model_width),
        norm2_gain.reshape(1, model_width),
        counts,
    )
    shard_shape = (shard_size, model_width)
    up_grad, down_grad = (
        sum((land[i].reshape(shard_shape).astype(f32) for i in range(rest)), own.astype(f32))[None]
        for own, land in ((up_own, up_land), (down_own.reshape(shard_shape), down_land))
    )
    query_grad, key_grad, value_grad, out_grad = (grad.astype(f32) for grad in weight_grads)
    load_now = small_sum[4, :experts] * experts / (row_count * dp_ways * sp_ways)
    load_next = 0.9 * load_mean + 0.1 * load_now
    return (
        block_out,
        tokens_grad,
        query_grad,
        key_grad,
        value_grad,
        out_grad,
        small_sum[0],
        small_sum[1],
        small_sum[2],
        small_sum[3],
        up_grad,
        down_grad,
        load_next,
    )


def solution(mesh):
    return jax.shard_map(
        local,
        mesh=mesh,
        in_specs=(
            P("dp", "sp", None),
            P("dp", "sp", None, None),
            P(),
            P(),
            P(),
            P(),
            P(),
            P(),
            P(),
            P(),
            P("dp", None, None),
            P("dp", None, None),
            P("dp", "sp", None),
            P(),
        ),
        out_specs=(
            P("dp", "sp", None),
            P("dp", "sp", None),
            P(),
            P(),
            P(),
            P(),
            P(),
            P(),
            P(),
            P(),
            P("dp", "sp", None),
            P("dp", "sp", None),
            P(),
        ),
        check_vma=False,
    )
```

```python
import functools

import jax
import jax.numpy as jnp
from jax import lax
from jax.experimental import pallas as pl
from jax.experimental.pallas import tpu as pltpu
from jax.sharding import PartitionSpec as P

HEADS = 16
MESH = pl.DeviceIdType.MESH
BLOCK = 256
LANES = 128
STEP = 1024
VMEM_BYTES = 60 * 2**20

NORM_EPSILON = 1e-05
GELU_ROOT = 0.7978845608028654
CUBIC_TERM = 0.044715

ROWS_BY_COLS = (((1,), (0,)), ((), ()))
ROWS_BY_ROWS = (((1,), (1,)), ((), ()))
COLS_BY_COLS = (((0,), (0,)), ((), ()))


def smooth(values):
    return (
        0.5
        * values
        * (1.0 + jnp.tanh(GELU_ROOT * (values + CUBIC_TERM * values * values * values)))
    )


def smooth_slope(values):
    inner = jnp.tanh(GELU_ROOT * (values + CUBIC_TERM * values * values * values))
    return 0.5 * (1.0 + inner) + 0.5 * values * (1.0 - inner * inner) * GELU_ROOT * (
        1.0 + 3.0 * CUBIC_TERM * values * values
    )


def norm_forward(values, gain, shift):
    center = jnp.mean(values, axis=-1, keepdims=True)
    offset = values - center
    rstd = lax.rsqrt(jnp.mean(offset * offset, axis=-1, keepdims=True) + NORM_EPSILON)
    unit = offset * rstd
    return (unit * gain + shift, unit, rstd)


def norm_backward(grad, unit, rstd, gain):
    scaled = grad * gain
    inner = (
        scaled
        - jnp.mean(scaled, axis=-1, keepdims=True)
        - unit * jnp.mean(scaled * unit, axis=-1, keepdims=True)
    )
    return (inner * rstd, jnp.sum(grad * unit, axis=0), jnp.sum(grad, axis=0))


def mxu(left, right, dims=ROWS_BY_COLS):
    return lax.dot_general(left, right, dims, preferred_element_type=jnp.float32)


def span(index, size):
    return pl.ds(pl.multiple_of(index * size, size), size)


def greet(peers):
    barrier = pltpu.get_barrier_semaphore()
    for peer in peers:
        pl.semaphore_signal(barrier, inc=1, device_id=peer, device_id_type=MESH)
    pl.semaphore_wait(barrier, len(peers))


def send(source, target, send_sem, recv_sem, peer):
    return pltpu.make_async_remote_copy(
        src_ref=source,
        dst_ref=target,
        send_sem=send_sem,
        recv_sem=recv_sem,
        device_id=peer,
        device_id_type=MESH,
    )


def exchange(others, source, target, send_sem, recv_sem):
    me = lax.axis_index("dp")
    return [
        send(
            source.at[flip(me, d)],
            target.at[me],
            send_sem.at[d],
            recv_sem.at[d],
            {"dp": flip(me, d)},
        )
        for d in range(1, others)
    ]


def flip(index, bits):
    bit = 1
    while bit <= bits:
        if bits & bit:
            index = index + bit - 2 * bit * lax.rem(index // bit, 2)
        bit *= 2
    return index


def forward(
    ways,
    others,
    head_dim,
    x_ref,
    cot_ref,
    wq_ref,
    wk_ref,
    wv_ref,
    wo_ref,
    ids_ref,
    gain1_ref,
    shift1_ref,
    gain2_ref,
    shift2_ref,
    normed_ref,
    q_ref,
    k_ref,
    v_ref,
    mixed_ref,
    arrived_ref,
    placer_ref,
    residual_ref,
    log_ref,
    outgoing_ref,
    counts_ref,
    x_all,
    cot_v,
    cot_out,
    wq_v,
    wk_v,
    wv_v,
    wo_v,
    placer_v,
    normed_v,
    q_v,
    k_v,
    v_v,
    mixed_f,
    mixed_h,
    mixed_tok,
    log_s,
    residual_v,
    normed2,
    x_send,
    x_recv,
    m_send,
    m_recv,
    c_send,
    c_recv,
    load_sem,
    x_sem,
    store_sem,
    own_sem,
):
    seqs, seq_len, model = x_all.shape
    shard = seq_len // ways
    width = q_v.shape[2]
    heads = width // head_dim
    slots = cot_out.shape[1]
    me = lax.axis_index("sp")
    dp = lax.axis_index("dp")
    peer = [flip(me, d) for d in range(ways)]
    near = (1, 2) if ways == 4 else tuple(range(1, ways))
    far = tuple(range(1 + len(near), ways))
    barrier = pltpu.get_barrier_semaphore()
    neighbours = [{"sp": peer[d]} for d in range(1, ways)]
    neighbours += [{"dp": flip(dp, d)} for d in range(1, others)]
    for device in neighbours:
        pl.semaphore_signal(barrier, inc=1, device_id=device, device_id_type=MESH)
    own_columns = span(me, width)
    loads = [
        pltpu.make_async_copy(source, target, load_sem.at[i])
        for i, (source, target) in enumerate(
            (
                (cot_ref, cot_v),
                (wq_ref.at[:, own_columns], wq_v),
                (wk_ref.at[:, own_columns], wk_v),
                (wv_ref.at[:, own_columns], wv_v),
                (wo_ref, wo_v),
            )
        )
    ]
    own_x = [
        pltpu.make_async_copy(x_ref.at[s], x_all.at[s, span(me, shard)], x_sem.at[s])
        for s in range(seqs)
    ]
    for copy in own_x + loads:
        copy.start()

    def x_copy(s, d):
        return send(
            x_ref.at[s],
            x_all.at[s, span(me, shard)],
            x_send.at[s, d],
            x_recv.at[s, d],
            {"sp": peer[d]},
        )

    def x_relays(s):
        if not far:
            return []
        size = shard // 2
        pieces = [
            x_all.at[s, pl.ds(pl.multiple_of(peer[1] * shard, size), size)],
            x_all.at[s, pl.ds(pl.multiple_of(peer[2] * shard + size, size), size)],
        ]
        return [
            send(piece, piece, x_send.at[s, at], x_recv.at[s, at], {"sp": peer[to]})
            for piece, at, to in zip(pieces, (0, 3), (2, 1))
        ]

    def mixed_copy(s, d):
        return send(
            mixed_h.at[s, span(peer[d], shard)],
            mixed_tok.at[s, :, own_columns],
            m_send.at[s, d],
            m_recv.at[s, d],
            {"sp": peer[d]},
        )

    tokens = seqs * shard
    ids = ids_ref[...]
    named = lax.broadcasted_iota(jnp.int32, (LANES, tokens), 0) == ids
    named = jnp.where(named, 1.0, 0.0)
    upper = lax.broadcasted_iota(jnp.int32, (tokens, tokens), 0) <= lax.broadcasted_iota(
        jnp.int32, (tokens, tokens), 1
    )
    running = mxu(named.astype(jnp.bfloat16), jnp.where(upper, 1.0, 0.0).astype(jnp.bfloat16))
    slot = jnp.sum(named * (running - 1.0), axis=0, keepdims=True).astype(jnp.int32)
    places = lax.broadcasted_iota(jnp.int32, placer_v.shape, 0) == ids * slots + slot
    placer_v[...] = jnp.where(places, 1.0, 0.0).astype(jnp.bfloat16)
    ones = jnp.ones((8, tokens), jnp.float32)
    counts_ref[...] = mxu(ones, named, ROWS_BY_ROWS)
    pl.semaphore_wait(barrier, len(neighbours))
    for d in near:
        x_copy(0, d).start()
    loads[0].wait()
    cot_out[...] = (
        mxu(placer_v[...], cot_v[...]).astype(jnp.bfloat16).reshape(cot_out.shape)
    )
    background = exchange(others, cot_out, arrived_ref, c_send, c_recv)
    own_cot = pltpu.make_async_copy(cot_out.at[dp], arrived_ref.at[dp], own_sem)
    for copy in background + [own_cot]:
        copy.start()

    lane = lax.broadcasted_iota(jnp.int32, (1, width), 1) // head_dim
    log_lane = lax.broadcasted_iota(jnp.int32, (1, LANES), 1)
    visible = lax.broadcasted_iota(jnp.int32, (BLOCK, BLOCK), 1) <= lax.broadcasted_iota(
        jnp.int32, (BLOCK, BLOCK), 0
    )
    scale = head_dim ** (-0.5)
    outs = ((normed_v, normed_ref), (q_v, q_ref), (k_v, k_ref), (v_v, v_ref))
    stores = [
        [
            pltpu.make_async_copy(source.at[s], target.at[s], store_sem.at[s, i])
            for i, (source, target) in enumerate(outs)
        ]
        for s in range(seqs)
    ]

    def project(s, d):
        rows = span(peer[d], shard)
        values = x_all[s, rows, :].astype(jnp.float32)
        normed, _, _ = norm_forward(values, gain1_ref[...], shift1_ref[...])
        normed = normed.astype(jnp.bfloat16)
        normed_v[s, rows, :] = normed
        q_v[s, rows, :] = mxu(normed, wq_v[...]).astype(jnp.bfloat16)
        k_v[s, rows, :] = mxu(normed, wk_v[...]).astype(jnp.bfloat16)
        v_v[s, rows, :] = mxu(normed, wv_v[...]).astype(jnp.bfloat16)

    for s in range(seqs):
        own_x[s].wait()
        if s == 0:
            for copy in loads[1:4]:
                copy.wait()
        project(s, 0)
        for d in near:
            x_copy(s, d).wait_recv()
        for copy in x_relays(s):
            copy.start()
        for d in near:
            project(s, d)
        for copy in x_relays(s):
            copy.wait_recv()
        if s + 1 < seqs:
            for d in near:
                x_copy(s + 1, d).start()
        if s:
            for d in range(1, ways):
                mixed_copy(s - 1, d).start()
        for d in far:
            project(s, d)
        for copy in stores[s]:
            copy.start()
        mixed_f[...] = jnp.zeros_like(mixed_f)
        log_s[...] = jnp.zeros_like(log_s)

        def one_head(h, carry):
            mine = (lane == h).astype(jnp.float32)
            for at in range(0, seq_len, BLOCK):
                rows = slice(at, at + BLOCK)
                query = (q_v[s, rows, :].astype(jnp.float32) * (mine * scale)).astype(
                    jnp.bfloat16
                )
                near = mxu(query, k_v[s, rows, :], ROWS_BY_ROWS)
                near = jnp.where(visible, near, -1e30)
                top = jnp.max(near, axis=1, keepdims=True)
                if at:
                    far = mxu(query, k_v[s, :at, :], ROWS_BY_ROWS)
                    top = jnp.maximum(top, jnp.max(far, axis=1, keepdims=True))
                near = jnp.exp(near - top)
                total = jnp.sum(near, axis=1, keepdims=True)
                if at:
                    far = jnp.exp(far - top)
                    total += jnp.sum(far, axis=1, keepdims=True)
                inverse = 1.0 / total
                out = mxu((near * inverse).astype(jnp.bfloat16), v_v[s, rows, :])
                if at:
                    out += mxu((far * inverse).astype(jnp.bfloat16), v_v[s, :at, :])
                mixed_f[rows, :] += out * mine
                log_s[rows, :] = jnp.where(log_lane == h, top + jnp.log(total), log_s[rows, :])
            return carry

        lax.fori_loop(0, heads, one_head, 0)
        log_ref[s] = jnp.transpose(log_s[...])[: log_ref.shape[1], :]
        mixed_h[s] = mixed_f[...].astype(jnp.bfloat16)
        mixed_tok[s, :, own_columns] = mixed_h[s, span(me, shard), :]
    for d in range(1, ways):
        mixed_copy(seqs - 1, d).start()

    loads[4].wait()
    for s in range(seqs):
        for d in range(1, ways):
            mixed_copy(s, d).wait_recv()
        rows = slice(s * shard, (s + 1) * shard)
        values = x_all[s, span(me, shard), :].astype(jnp.float32)
        values += mxu(mixed_tok[s], wo_v[...])
        residual_v[rows, :] = values
        normed, _, _ = norm_forward(values, gain2_ref[...], shift2_ref[...])
        normed2[rows, :] = normed.astype(jnp.bfloat16)
    last = [
        pltpu.make_async_copy(source, target, store_sem.at[seqs, i])
        for i, (source, target) in enumerate(
            ((mixed_tok, mixed_ref), (residual_v, residual_ref), (placer_v, placer_ref))
        )
    ]
    for copy in last:
        copy.start()
    outgoing_ref[...] = (
        mxu(placer_v[...], normed2[...]).astype(jnp.bfloat16).reshape(outgoing_ref.shape)
    )
    for s in range(seqs):
        for d in near:
            x_copy(s, d).wait_send()
        for copy in x_relays(s):
            copy.wait_send()
        for d in range(1, ways):
            mixed_copy(s, d).wait_send()
        for copy in stores[s]:
            copy.wait()
    for copy in background + [own_cot] + last:
        copy.wait()


def pair_of(sp):
    core = lax.rem(lax.axis_index("dp"), 2)
    along_x, along_y = flip(sp, 1), flip(sp, 2)
    return along_x + core * (along_y - along_x)


def shards_of(sp, ways):
    shards = [sp, flip(pair_of(sp), 3)]
    bit = 4
    while bit < ways:
        shards += [flip(shard, bit) for shard in shards]
        bit *= 2
    return shards


def run_experts(
    others,
    ways,
    outgoing_ref,
    cot_ref,
    up_ref,
    down_ref,
    back_ref,
    result_ref,
    up_own,
    up_rest,
    down_own,
    down_rest,
    received,
    arrived,
    up_v,
    down_v,
    hidden,
    slope_v,
    total,
    dn_own,
    dn_pair,
    dn_land,
    dnormed,
    out_pair,
    out_land,
    w_sem,
    o_sem,
    c_sem,
    a_send,
    a_recv,
    b_send,
    b_recv,
    f_send,
    f_recv,
    p_send,
    p_recv,
    e_send,
    e_recv,
):
    slots, width = received.shape[1:]
    rows = others * slots
    ff = up_v.shape[0]
    groups = others // 2
    me = lax.axis_index("dp")
    sp = lax.axis_index("sp")
    chip = me // 2
    pair = {"sp": pair_of(sp)}
    shards = shards_of(sp, ways)
    size = ff // len(shards)
    loads = [
        pltpu.make_async_copy(
            source.at[span(shard, size)], target.at[i * size : (i + 1) * size], w_sem.at[j, i]
        )
        for j, (source, target) in enumerate(((down_ref, down_v), (up_ref, up_v)))
        for i, shard in enumerate(shards)
    ]
    own_cot = pltpu.make_async_copy(cot_ref, arrived.at[0], c_sem.at[0])
    own_rows = pltpu.make_async_copy(outgoing_ref.at[me], received.at[me], c_sem.at[1])
    own_back = pltpu.make_async_copy(dnormed.at[me], back_ref.at[me], c_sem.at[2])
    own_rows.start()
    own_cot.start()
    for copy in loads:
        copy.start()
    greet([{"dp": flip(me, d)} for d in range(1, others)] + [pair])
    inward = exchange(others, outgoing_ref, received.at[0:others], a_send, a_recv)
    outward = exchange(others, dnormed, back_ref, b_send, b_recv)
    near = [flip(chip, group) for group in range(groups)]
    chips = [pl.ds(2 * near[group], 2) for group in range(groups)]
    forward = [
        send(
            received.at[chips[group]],
            received.at[pl.ds(others + 2 * near[group], 2)],
            f_send.at[group],
            f_recv.at[group],
            pair,
        )
        for group in range(groups)
    ]
    cot_copy = send(cot_ref, arrived.at[1], f_send.at[groups], f_recv.at[groups], pair)
    dn_copy = [
        send(
            dn_pair.at[chips[group]],
            dn_land.at[chips[group]],
            p_send.at[group],
            p_recv.at[group],
            pair,
        )
        for group in range(groups)
    ]
    out_copy = [
        send(
            out_pair.at[chips[group]],
            out_land.at[chips[group]],
            e_send.at[group],
            e_recv.at[group],
            pair,
        )
        for group in range(groups)
    ]

    early = range(groups // 2)
    middle = range(groups // 2, 3 * groups // 4)
    late = range(3 * groups // 4, groups)
    for copy in [inward[0]] + inward[2 * middle[0] - 1 : 2 * late[0] - 1]:
        copy.start()
    for copy in inward[1 : 2 * middle[0] - 1]:
        copy.start()
    cot_copy.start()
    own_rows.wait()

    def slab_of(half, group):
        return pl.ds(pl.multiple_of(half * rows + near[group] * (2 * slots), 2 * slots), 2 * slots)

    def cot_half(half):
        def cot_step(i, carry):
            at = span(i, STEP)
            cot = arrived[half].reshape(rows, width)
            slope_v[half * rows : (half + 1) * rows, at] = mxu(
                cot, down_v[at, :], ROWS_BY_ROWS
            ).astype(jnp.bfloat16)
            return carry

        lax.fori_loop(0, ff // STEP, cot_step, 0)

    def up_half(half, group):
        slab = slab_of(half, group)
        total[...] = jnp.zeros_like(total)

        def up_step(i, carry):
            at = span(i, STEP)
            tokens = received[pl.ds(half * others + 2 * near[group], 2)].reshape(2 * slots, width)
            pre = mxu(tokens, up_v[at, :], ROWS_BY_ROWS)
            square = pre * pre
            inner = jnp.tanh(GELU_ROOT * pre * (1.0 + CUBIC_TERM * square))
            gate = 0.5 * (1.0 + inner)
            hidden[slab, at] = (pre * gate).astype(jnp.bfloat16)
            slope = gate + (0.5 * GELU_ROOT) * pre * (1.0 - inner * inner) * (
                1.0 + (3.0 * CUBIC_TERM) * square
            )
            dpre = (slope_v[slab, at].astype(jnp.float32) * slope).astype(jnp.bfloat16)
            slope_v[slab, at] = dpre
            total[...] += mxu(dpre, up_v[at, :])
            return carry

        lax.fori_loop(0, ff // STEP, up_step, 0)
        shaped = total[...].reshape(2, slots, width)
        if half:
            dn_pair[chips[group]] = shaped.astype(jnp.bfloat16)
            dn_copy[group].start()
        else:
            dn_own[chips[group]] = shaped

    def out_half(half, group):
        at = chips[group]
        out = mxu(hidden[slab_of(half, group), :], down_v[...]).reshape(2, slots, width)
        if half:
            out_pair[at] = out.astype(jnp.bfloat16)
        else:
            out_copy[group].wait_recv()
            result_ref[at] = (out + out_land[at].astype(jnp.float32)).astype(jnp.bfloat16)

    def pass_on(group):
        for d in (2 * group, 2 * group + 1):
            if d:
                inward[d - 1].wait_recv()
        forward[group].start()

    def finish(group):
        dn_copy[group].wait_recv()
        at = chips[group]
        dnormed[at] = (dn_own[at] + dn_land[at].astype(jnp.float32)).astype(jnp.bfloat16)
        for d in (2 * group, 2 * group + 1):
            if d:
                outward[d - 1].start()
            else:
                own_back.start()

    def up_pair(group):
        forward[group].wait_recv()
        up_half(1, group)

    pass_on(0)
    own_cot.wait()
    for copy in loads[: len(shards)]:
        copy.wait()
    cot_half(0)
    for copy in loads[len(shards) :]:
        copy.wait()
    up_half(0, 0)
    for group in middle:
        pass_on(group)
        up_half(0, group)
    for copy in inward[2 * middle[0] - 1 : 2 * late[0] - 1]:
        copy.wait_send()
    for copy in inward[2 * late[0] - 1 :]:
        copy.start()
    for group in early[1:]:
        pass_on(group)
    cot_copy.wait_recv()
    cot_half(1)
    for group in early[1:]:
        up_half(0, group)
    for group in middle:
        up_pair(group)
    up_pair(0)
    for group in middle:
        finish(group)
    for group in late:
        pass_on(group)
    for group in early[1:]:
        up_pair(group)
    for group in late:
        up_half(0, group)
    for group in middle:
        out_half(1, group)
    finish(0)
    for group in late:
        up_pair(group)
    for group in [*early, *late]:
        out_half(1, group)
    for group in [*early[1:], *late]:
        finish(group)
    for copy in out_copy:
        copy.start()

    def grad(target, left, right_ref, block=0):
        def grad_step(i, carry):
            at = span(i, STEP)
            right = right_ref[...].reshape(2 * rows, width)
            out = mxu(left[:, at], right, COLS_BY_COLS).astype(jnp.bfloat16)
            if block:
                target[span(i, STEP // block)] = out.reshape(STEP // block, block, width)
            else:
                target[at, :] = out
            return carry

        lax.fori_loop(0, ff // STEP, grad_step, 0)

    grad(up_v, slope_v, received.at[0 : 2 * others])
    for copy in forward:
        copy.wait_send()
    grad(received, hidden, arrived, slots)
    first, every = size // slots, ff // slots
    stores = [
        pltpu.make_async_copy(source, target, o_sem.at[i])
        for i, (source, target) in enumerate(
            (
                (up_v.at[0:size], up_own),
                (up_v.at[size:ff], up_rest),
                (received.at[0:first], down_own),
                (received.at[first:every], down_rest),
            )
        )
    ]
    for copy in stores:
        copy.start()
    for group in range(groups):
        out_half(0, group)
    for copy in inward[: 2 * middle[0] - 1] + inward[2 * late[0] - 1 :]:
        copy.wait_send()
    for copy in [cot_copy] + dn_copy + out_copy:
        copy.wait_send()
    for copy in outward + stores + [own_back]:
        copy.wait()


class Reduction:
    def __init__(self, ways, columns, part, out, across_first, scratch):
        (
            self.core_land,
            self.core_sum,
            self.column_land,
            self.piece,
            core_send,
            core_recv,
            column_send,
            column_recv,
            spread_send,
            spread_recv,
            ring_send,
            ring_recv,
            cross_send,
            cross_recv,
            own_sem,
        ) = scratch
        me = lax.axis_index("sp")
        dp = lax.axis_index("dp")
        core = lax.rem(dp, 2)
        column = dp // 2
        twin = {"dp": dp + 1 - 2 * core}
        self.ways, self.columns, self.part = ways, columns, part
        self.core = core
        rows, width = self.piece.shape
        self.rows = rows

        bits = [1 << i for i in range(columns.bit_length() - 1)]
        place = 0
        for bit in bits:
            place = 2 * place + lax.rem(column // bit, 2)
        self.place = place

        def beside(bit):
            return {"dp": 2 * flip(column, bit) + core}

        def block(first, at_sp, count):
            first = pl.multiple_of((core * columns + first) * rows, rows)
            return out.at[pl.ds(first, count * rows), span(at_sp, width)]

        self.core_copy = send(
            part.at[span(1 - core, columns * rows)], self.core_land, core_send, core_recv, twin
        )
        self.column_copy, self.kept, self.lands = [], [], []
        first, count, used = 0, columns, 0
        for i, bit in enumerate(bits):
            count //= 2
            mine = lax.rem(column // bit, 2)
            size = count * rows
            gone = pl.ds(pl.multiple_of((first + (1 - mine) * count) * rows, size), size)
            first = first + mine * count
            self.kept.append(pl.ds(pl.multiple_of(first * rows, size), size))
            land = self.column_land.at[used : used + size]
            used += size
            self.lands.append(land)
            self.column_copy.append(
                send(self.core_sum.at[gone], land, column_send.at[i], column_recv.at[i], beside(bit))
            )
        spot = block(place, me, 1)
        self.own = pltpu.make_async_copy(self.piece, spot, own_sem)
        origin = [flip(me, d) for d in range(ways)]
        across_count = 1 if across_first else columns
        across_at = place if across_first else 0
        near = (1, 2) if ways == 4 else tuple(range(1, ways))
        held = [block(across_at, at, across_count) for at in origin]
        self.ring_copy = [
            send(held[0], held[0], ring_send.at[d], ring_recv.at[d], {"sp": origin[d]})
            for d in near
        ]
        self.relays = []
        if ways == 4:
            count = across_count * rows // 2
            first = (core * columns + across_at) * rows
            for i, (d, to) in enumerate(((1, 2), (2, 1))):
                at = pl.multiple_of(first + i * count, count)
                half = out.at[pl.ds(at, count), span(origin[d], width)]
                index = (0, 3)[i]
                self.relays.append(
                    send(
                        half, half, ring_send.at[index], ring_recv.at[index], {"sp": origin[to]}
                    )
                )

        def rows_of(first, count):
            first = pl.multiple_of((core * columns + first) * rows, rows)
            return out.at[pl.ds(first, count * rows)]

        self.spread_copy, gathered = [], [rows_of(place, 1)]
        for i, bit in enumerate(reversed(bits)):
            count = 1 << i
            at = place - lax.rem(place, count)
            spot = rows_of(at, count) if across_first else block(at, me, count)
            gathered.append(rows_of(flip(at, count), count))
            self.spread_copy.append(
                send(spot, spot, spread_send.at[i], spread_recv.at[i], beside(bit))
            )
        crossing = gathered if across_first else held
        self.cross_copy = [
            send(part, part, cross_send.at[i], cross_recv.at[i], twin)
            for i, part in enumerate(crossing)
        ]
        self.phases = iter(self.across_then_along() if across_first else self.along_then_across())

    def along_then_across(self):
        self.own.start()
        self.own.wait()
        for copy in self.spread_copy:
            copy.start()
            yield
            copy.wait()
        for copy in self.ring_copy:
            copy.start()
        self.cross_copy[0].start()
        yield
        for ring, cross in zip(self.ring_copy, self.cross_copy[1:]):
            ring.wait_recv()
            cross.start()
        for copy in self.relays:
            copy.start()
        yield
        for copy in self.relays:
            copy.wait_recv()
        if self.relays:
            self.cross_copy[3].start()
        yield

    def across_then_along(self):
        self.own.start()
        self.own.wait()
        for copy in self.ring_copy:
            copy.start()
        yield
        for copy in self.ring_copy:
            copy.wait_recv()
        for copy in self.relays:
            copy.start()
        yield
        for copy in self.relays:
            copy.wait_recv()
        for spread, cross in zip(self.spread_copy, self.cross_copy):
            spread.start()
            cross.start()
            yield
            spread.wait()
        self.cross_copy[-1].start()
        yield

    def advance(self):
        next(self.phases)

    def add_core(self):
        self.core_copy.wait()
        self.core_sum[...] = (
            self.part[span(self.core, self.columns * self.rows), :].astype(jnp.float32)
            + self.core_land[...].astype(jnp.float32)
        ).astype(jnp.bfloat16)
        self.column_copy[0].start()

    def add_column(self, step):
        self.column_copy[step].wait()
        total = self.core_sum[self.kept[step], :].astype(jnp.float32)
        total += self.lands[step][...].astype(jnp.float32)
        if step + 1 < len(self.column_copy):
            self.core_sum[self.kept[step], :] = total.astype(jnp.bfloat16)
            self.column_copy[step + 1].start()
        return total

    def finish(self):
        for copy in self.ring_copy + self.relays:
            copy.wait_send()
        for copy in self.cross_copy:
            copy.wait()


def backward(
    ways,
    others,
    head_dim,
    back_ref,
    placer_ref,
    cot_ref,
    residual_ref,
    wo_ref,
    mixed_ref,
    q_ref,
    k_ref,
    v_ref,
    normed_ref,
    wq_ref,
    wk_ref,
    wv_ref,
    x_ref,
    result_ref,
    up_rest,
    down_rest,
    log_ref,
    gain1_ref,
    gain2_ref,
    counts_ref,
    out_q,
    out_k,
    out_v,
    out_o,
    up_land,
    down_land,
    block_ref,
    tokens_ref,
    small_out,
    back_v,
    placer_v,
    cot_v,
    residual_v,
    wo_v,
    mixed_v,
    q_v,
    k_v,
    v_v,
    normed_v,
    wq_v,
    wk_v,
    wv_v,
    x_v,
    returned,
    dresid,
    dattn,
    dmixed,
    dmixed_h,
    dq_f,
    dk_f,
    dv_f,
    grads_h,
    grads_tok,
    part_o,
    parts_w,
    o_land,
    small_own,
    small_land,
    small_sum,
    m_send,
    m_recv,
    g_send,
    g_recv,
    c_send,
    c_recv,
    s_send,
    s_recv,
    o_send,
    o_recv,
    small_send,
    small_recv,
    load_sem,
    *scratch,
):
    seqs, shard, model = x_v.shape
    seq_len, width = q_v.shape[1:]
    heads = width // head_dim
    columns = others // 2
    me = lax.axis_index("sp")
    dp = lax.axis_index("dp")
    core = lax.rem(dp, 2)
    peer = [lax.rem(me + d, ways) for d in range(ways)]
    barrier = pltpu.get_barrier_semaphore()
    neighbours = [{"sp": peer[d]} for d in range(1, ways)]
    neighbours += [{"dp": flip(dp, d)} for d in range(1, others)]
    for device in neighbours:
        pl.semaphore_signal(barrier, inc=1, device_id=device, device_id_type=MESH)
    sources = (
        (back_ref, back_v),
        (placer_ref, placer_v),
        (residual_ref, residual_v),
        (cot_ref, cot_v),
        (wo_ref, wo_v),
        (mixed_ref, mixed_v),
        (q_ref, q_v),
        (k_ref, k_v),
        (v_ref, v_v),
        (normed_ref, normed_v),
        (wq_ref, wq_v),
        (wk_ref, wk_v),
        (wv_ref, wv_v),
        (x_ref, x_v),
        (result_ref.at[dp], returned.at[dp]),
    )
    loads = [
        pltpu.make_async_copy(source, target, load_sem.at[i])
        for i, (source, target) in enumerate(sources)
    ]
    for copy in loads:
        copy.start()

    def dmixed_copy(s, d):
        return send(
            dmixed.at[s, :, span(peer[d], width)],
            dmixed_h.at[s, span(me, shard)],
            m_send.at[s, d],
            m_recv.at[s, d],
            {"sp": peer[d]},
        )

    def grad_copy(s, d):
        return send(
            grads_h.at[s, span(peer[d], shard)],
            grads_tok.at[s, :, span(me, 3 * width)],
            g_send.at[s, d],
            g_recv.at[s, d],
            {"sp": peer[d]},
        )

    shards = shards_of(me, ways)
    scatter = []
    for j, (rest, land) in enumerate(((up_rest, up_land), (down_rest, down_land))):
        size = land.shape[1]
        scatter += [
            send(
                rest.at[(i - 1) * size : i * size],
                land.at[i - 1],
                s_send.at[j, i],
                s_recv.at[j, i],
                {"sp": shards[i]},
            )
            for i in range(1, len(shards))
        ]
    small_own[...] = jnp.zeros_like(small_own)
    small_own[4:5, 0:LANES] = counts_ref[0:1, :]
    for s in range(seqs):
        if s == 0:
            for copy in loads[:4]:
                copy.wait()
        rows = slice(s * shard, (s + 1) * shard)
        dnormed = mxu(placer_v[:, rows], back_v[...].reshape(-1, model), COLS_BY_COLS)
        gain = gain2_ref[...]
        _, unit, rstd = norm_forward(residual_v[rows, :], gain, jnp.zeros_like(gain))
        dinput, gain_grad, shift_grad = norm_backward(dnormed, unit, rstd, gain)
        total = cot_v[rows, :].astype(jnp.float32) + dinput
        dresid[s] = total
        dattn[rows, :] = total.astype(jnp.bfloat16)
        small_own[2:3, :] += gain_grad.reshape(1, model)
        small_own[3:4, :] += shift_grad.reshape(1, model)
        if s == 0:
            loads[4].wait()
        dmixed[s] = mxu(dattn[rows, :], wo_v[...], ROWS_BY_ROWS).astype(jnp.bfloat16)
        if s == 0:
            pl.semaphore_wait(barrier, len(neighbours))
        for d in range(1, ways):
            dmixed_copy(s, d).start()
    for copy in scatter:
        copy.start()
    routed_back = exchange(others, result_ref, returned, c_send, c_recv)
    sum_o = Reduction(ways, columns, part_o, out_o, False, scratch[:15])
    sums_w = [
        Reduction(ways, columns, parts_w.at[i], out, False, scratch[15 * (i + 1) : 15 * (i + 2)])
        for i, out in enumerate((out_q, out_k, out_v))
    ]
    sum_q, sum_k, sum_v = sums_w
    steps = columns.bit_length() - 1

    loads[5].wait()

    def out_step(i, carry):
        at = span(i, BLOCK)
        left = mixed_v[:, :, at].reshape(seqs * shard, BLOCK)
        part_o[at, :] = mxu(left, dattn[...], COLS_BY_COLS).astype(jnp.bfloat16)
        return carry

    lax.fori_loop(0, model // BLOCK, out_step, 0)
    sum_o.core_copy.start()
    for copy in loads[6:9]:
        copy.wait()

    lane = lax.broadcasted_iota(jnp.int32, (1, width), 1) // head_dim
    visible = lax.broadcasted_iota(jnp.int32, (BLOCK, BLOCK), 0) <= lax.broadcasted_iota(
        jnp.int32, (BLOCK, BLOCK), 1
    )
    scale = head_dim ** (-0.5)
    for s in range(seqs):
        dmixed_h[s, span(me, shard), :] = dmixed[s, :, span(me, width)]
        for d in range(1, ways):
            dmixed_copy(s, d).wait_recv()
        if s == 0:
            sum_o.add_core()
        dq_f[...] = jnp.zeros_like(dq_f)
        dk_f[...] = jnp.zeros_like(dk_f)
        dv_f[...] = jnp.zeros_like(dv_f)

        def one_head(h, carry):
            mine = (lane == h).astype(jnp.float32)
            for at in range(0, seq_len, BLOCK):
                rows = slice(at, at + BLOCK)
                query = (q_v[s, rows, :].astype(jnp.float32) * (mine * scale)).astype(
                    jnp.bfloat16
                )
                dout = (dmixed_h[s, rows, :].astype(jnp.float32) * mine).astype(jnp.bfloat16)
                log_row = log_ref[s, pl.ds(h, 1), rows]
                parts = [(rows, True)] + ([(slice(0, at), False)] if at else [])
                kept = []
                delta = jnp.zeros((1, BLOCK), jnp.float32)
                for keys, diagonal in parts:
                    prob = jnp.exp(mxu(k_v[s, keys, :], query, ROWS_BY_ROWS) - log_row)
                    if diagonal:
                        prob = jnp.where(visible, prob, 0.0)
                    dprob = mxu(v_v[s, keys, :], dout, ROWS_BY_ROWS)
                    delta += jnp.sum(prob * dprob, axis=0, keepdims=True)
                    kept.append((keys, prob, dprob))
                dquery = jnp.zeros((BLOCK, width), jnp.float32)
                for keys, prob, dprob in kept:
                    dv_f[keys, :] += mxu(prob.astype(jnp.bfloat16), dout)
                    dlogit = (prob * (dprob - delta)).astype(jnp.bfloat16)
                    dk_f[keys, :] += mxu(dlogit, query)
                    dquery += mxu(dlogit, k_v[s, keys, :], COLS_BY_COLS)
                dq_f[rows, :] += dquery * (mine * scale)
            return carry

        lax.fori_loop(0, heads, one_head, 0)
        for i, total in enumerate((dq_f, dk_f, dv_f)):
            grads_h[s, :, i * width : (i + 1) * width] = total[...].astype(jnp.bfloat16)
        if s == 0:
            for d in range(1, ways):
                grad_copy(s, d).start()
            for step in range(steps - 1):
                sum_o.add_column(step)
            for copy in routed_back[: 3 * others // 4 - 1]:
                copy.start()
        grads_tok[s, :, span(me, 3 * width)] = grads_h[s, span(me, shard), :]

    o_land[0] = sum_o.add_column(steps - 1).astype(jnp.bfloat16)
    o_copy = [
        send(
            o_land.at[0, :, span(peer[d], width)],
            o_land.at[d, :, 0:width],
            o_send.at[d],
            o_recv.at[d],
            {"sp": peer[d]},
        )
        for d in range(1, ways)
    ]
    for copy in o_copy:
        copy.start()

    loads[9].wait()

    def weight_step(i, carry):
        at = span(i, BLOCK)
        grad = mxu(normed_v[0, :, at], grads_h[0], COLS_BY_COLS)
        for s in range(1, seqs):
            grad += mxu(normed_v[s, :, at], grads_h[s], COLS_BY_COLS)
        for j in range(3):
            parts_w[j, at, :] = grad[:, j * width : (j + 1) * width].astype(jnp.bfloat16)
        return carry

    lax.fori_loop(0, model // BLOCK, weight_step, 0)
    for total in (sum_v, sum_k, sum_q):
        total.core_copy.start()

    for total in (sum_v, sum_k, sum_q):
        total.add_core()
    for step in range(steps):
        for total in (sum_v, sum_k, sum_q):
            piece = total.add_column(step)
            if step == steps - 1:
                total.piece[...] = piece.astype(jnp.bfloat16)
                total.advance()
    for s in range(1, seqs):
        for d in range(1, ways):
            grad_copy(s, d).start()
    for copy in routed_back[3 * others // 4 - 1 :]:
        copy.start()

    def norm_grad(s):
        for d in range(1, ways):
            grad_copy(s, d).wait()
        dnormed = jnp.zeros((shard, model), jnp.float32)
        for j in range(ways):
            for i, weight in enumerate((wq_v, wk_v, wv_v)):
                at = (3 * j + i) * width
                dnormed += mxu(
                    grads_tok[s, :, at : at + width],
                    weight[:, j * width : (j + 1) * width],
                    ROWS_BY_ROWS,
                )
        gain = gain1_ref[...]
        _, unit, rstd = norm_forward(x_v[s].astype(jnp.float32), gain, jnp.zeros_like(gain))
        dinput, gain_grad, shift_grad = norm_backward(dnormed, unit, rstd, gain)
        tokens_ref[s] = (dresid[s] + dinput).astype(jnp.bfloat16)
        small_own[0:1, :] += gain_grad.reshape(1, model)
        small_own[1:2, :] += shift_grad.reshape(1, model)

    for copy in loads[10:14]:
        copy.wait()
    for _ in range(steps - 1):
        for total in (sum_v, sum_k, sum_q):
            total.advance()
    for s in range(seqs - 1):
        norm_grad(s)
    for total in (sum_v, sum_k, sum_q):
        total.advance()
    total = o_land[0, :, span(me, width)].astype(jnp.float32)
    for d, copy in enumerate(o_copy):
        copy.wait()
        total += o_land[d + 1, :, 0:width].astype(jnp.float32)
    sum_o.piece[...] = total.astype(jnp.bfloat16)
    sum_o.advance()
    norm_grad(seqs - 1)
    for _ in range(steps):
        sum_o.advance()

    stages = [[{"sp": peer[d]} for d in range(1, ways)], [{"dp": dp + 1 - 2 * core}]]
    stages.append([{"dp": 2 * lax.rem(dp // 2 + d, columns) + core} for d in range(1, columns)])
    slot = 0
    source = small_own
    for number, peers in enumerate(stages):
        copies = [
            send(
                source,
                small_land.at[slot + i],
                small_send.at[slot + i],
                small_recv.at[slot + i],
                device,
            )
            for i, device in enumerate(peers)
        ]
        for copy in copies:
            copy.start()
        if number == 0:
            sum_v.advance()
            sum_k.advance()
        elif number == 1:
            sum_q.advance()
            sum_o.advance()
        else:
            sum_v.advance()
            sum_k.advance()
        total = source[...]
        for i, copy in enumerate(copies):
            copy.wait()
            total += small_land[slot + i]
        slot += len(peers)
        if number == len(stages) - 1:
            small_out[...] = total
        else:
            small_sum[number] = total
            source = small_sum.at[number]

    loads[14].wait()
    for copy in routed_back:
        copy.wait()
    for s in range(seqs):
        rows = slice(s * shard, (s + 1) * shard)
        out = mxu(placer_v[:, rows], returned[...].reshape(-1, model), COLS_BY_COLS)
        block_ref[s] = (residual_v[rows, :] + out).astype(jnp.bfloat16)
    sum_q.advance()
    sum_o.advance()
    for s in range(seqs):
        for d in range(1, ways):
            dmixed_copy(s, d).wait_send()
    for copy in scatter:
        copy.wait()
    for total in [sum_o] + sums_w:
        total.finish()


def finish(
    experts,
    tokens,
    query_ref,
    key_ref,
    value_ref,
    out_ref,
    up_own,
    up_land,
    down_own,
    down_land,
    block_in,
    tokens_in,
    small_ref,
    load_ref,
    query_out,
    key_out,
    value_out,
    out_out,
    up_out,
    down_out,
    block_out,
    tokens_out,
    gain1_out,
    shift1_out,
    gain2_out,
    shift2_out,
    load_out,
):
    for source, target in (
        (query_ref, query_out),
        (key_ref, key_out),
        (value_ref, value_out),
        (out_ref, out_out),
    ):
        target[...] = source[...].astype(jnp.float32)
    for own, land, target in ((up_own, up_land, up_out), (down_own, down_land, down_out)):
        total = own[...].astype(jnp.float32)
        for i in range(land.shape[0]):
            total += land[i].astype(jnp.float32)
        target[...] = total
    block_out[...] = block_in[...]
    tokens_out[...] = tokens_in[...]
    for i, target in enumerate((gain1_out, shift1_out, gain2_out, shift2_out)):
        target[...] = small_ref[i : i + 1, :]
    load_now = small_ref[4:5, 0:experts] * experts / tokens
    load_out[...] = 0.9 * load_ref[...] + 0.1 * load_now


def vmem(count):
    return [pl.BlockSpec(memory_space=pltpu.VMEM)] * count


def params(collective_id):
    return pltpu.CompilerParams(
        collective_id=collective_id, has_side_effects=True, vmem_limit_bytes=VMEM_BYTES
    )


def dma(*shape):
    return pltpu.SemaphoreType.DMA(shape)


def local(
    tokens_in,
    expert_ids,
    query_weight,
    key_weight,
    value_weight,
    out_weight,
    norm1_gain,
    norm1_shift,
    norm2_gain,
    norm2_shift,
    up_weight,
    down_weight,
    out_cotangent,
    load_mean,
):
    seq_count, shard_len, model_width = tokens_in.shape
    row_count = seq_count * shard_len
    head_dim = model_width // HEADS
    dp_ways = lax.axis_size("dp")
    sp_ways = lax.axis_size("sp")
    sp_at = lax.axis_index("sp")
    seq_len = shard_len * sp_ways
    experts = load_mean.shape[0]
    slot_count = 2 * row_count // experts
    local_experts = up_weight.shape[0]
    ff_width = up_weight.shape[1]
    width = model_width // sp_ways
    bf16 = jnp.bfloat16
    f32 = jnp.float32

    def shape(*sizes, dtype=bf16):
        return jax.ShapeDtypeStruct(sizes, dtype)

    cot_b = out_cotangent.reshape(row_count, model_width)
    hbm = [pl.BlockSpec(memory_space=pl.ANY)]
    routed = shape(experts, slot_count, model_width)
    square = pltpu.VMEM((model_width, model_width), bf16)
    by_head = pltpu.VMEM((seq_count, seq_len, width), bf16)
    token_shape = (seq_count, shard_len, model_width)
    whole_tokens = pltpu.VMEM((seq_count, seq_len, model_width), bf16)
    weight_columns = pltpu.VMEM((model_width, width), bf16)
    slots = (experts * slot_count, row_count)
    flat = (row_count, model_width)
    (
        normed_all,
        query_h,
        key_h,
        value_h,
        mixed_b,
        arrived,
        placer,
        residual_stream,
        log_total,
        outgoing,
        counts,
    ) = pl.pallas_call(
        functools.partial(forward, sp_ways, dp_ways, head_dim),
        out_shape=[
            shape(seq_count, seq_len, model_width),
            shape(seq_count, seq_len, width),
            shape(seq_count, seq_len, width),
            shape(seq_count, seq_len, width),
            shape(*token_shape),
            routed,
            shape(*slots),
            shape(*flat, dtype=f32),
            shape(seq_count, 8, seq_len, dtype=f32),
            routed,
            shape(8, LANES, dtype=f32),
        ],
        in_specs=hbm * 6 + vmem(5),
        out_specs=hbm * 8 + vmem(3),
        scratch_shapes=[
            whole_tokens,
            pltpu.VMEM(flat, bf16),
            pltpu.VMEM(routed.shape, bf16),
            weight_columns,
            weight_columns,
            weight_columns,
            square,
            pltpu.VMEM(slots, bf16),
            whole_tokens,
            by_head,
            by_head,
            by_head,
            pltpu.VMEM((seq_len, width), f32),
            by_head,
            pltpu.VMEM(token_shape, bf16),
            pltpu.VMEM((seq_len, LANES), f32),
            pltpu.VMEM(flat, f32),
            pltpu.VMEM(flat, bf16),
            dma(seq_count, sp_ways),
            dma(seq_count, sp_ways),
            dma(seq_count, sp_ways),
            dma(seq_count, sp_ways),
            dma(dp_ways),
            dma(dp_ways),
            dma(5),
            dma(seq_count),
            dma(seq_count + 1, 4),
            pltpu.SemaphoreType.DMA,
        ],
        compiler_params=params(0),
    )(
        tokens_in,
        cot_b,
        query_weight,
        key_weight,
        value_weight,
        out_weight,
        expert_ids.reshape(1, row_count),
        *(
            vector.reshape(1, model_width)
            for vector in (norm1_gain, norm1_shift, norm2_gain, norm2_shift)
        ),
    )
    ff_own = ff_width // 2
    received_blocks = max(2 * experts, ff_own // slot_count)
    shard_size = ff_width // sp_ways
    rest = sp_ways // 2 - 1
    blocks = shard_size // slot_count
    dnormed_back, expert_out, up_own, up_rest, down_own, down_rest = pl.pallas_call(
        functools.partial(run_experts, dp_ways, sp_ways),
        out_shape=[
            routed,
            routed,
            shape(shard_size, model_width),
            shape(rest * shard_size, model_width),
            shape(blocks, slot_count, model_width),
            shape(rest * blocks, slot_count, model_width),
        ],
        in_specs=hbm * 4,
        out_specs=hbm + vmem(1) + hbm * 4,
        scratch_shapes=[
            pltpu.VMEM((received_blocks, slot_count, model_width), bf16),
            pltpu.VMEM((2,) + routed.shape, bf16),
            pltpu.VMEM((ff_own, model_width), bf16),
            pltpu.VMEM((ff_own, model_width), bf16),
            pltpu.VMEM((2 * experts * slot_count, ff_own), bf16),
            pltpu.VMEM((2 * experts * slot_count, ff_own), bf16),
            pltpu.VMEM((2 * slot_count, model_width), f32),
            pltpu.VMEM(routed.shape, f32),
            pltpu.VMEM(routed.shape, bf16),
            pltpu.VMEM(routed.shape, bf16),
            pltpu.VMEM(routed.shape, bf16),
            pltpu.VMEM(routed.shape, bf16),
            pltpu.VMEM(routed.shape, bf16),
            dma(2, sp_ways // 2),
            dma(4),
            dma(3),
            dma(dp_ways),
            dma(dp_ways),
            dma(dp_ways),
            dma(dp_ways),
            dma(dp_ways // 2 + 1),
            dma(dp_ways // 2 + 1),
            dma(dp_ways // 2 + 1),
            dma(dp_ways // 2 + 1),
            dma(dp_ways // 2),
            dma(dp_ways // 2),
        ],
        compiler_params=params(3),
    )(outgoing, arrived, up_weight[0], down_weight[0])
    columns = dp_ways // 2
    rows = model_width // dp_ways

    def reduction(part_width):
        return [
            pltpu.VMEM((columns * rows, part_width), bf16),
            pltpu.VMEM((columns * rows, part_width), bf16),
            pltpu.VMEM(((columns - 1) * rows, part_width), bf16),
            pltpu.VMEM((rows, width), bf16),
            pltpu.SemaphoreType.DMA,
            pltpu.SemaphoreType.DMA,
            dma(columns),
            dma(columns),
            dma(columns),
            dma(columns),
            dma(sp_ways),
            dma(sp_ways),
            dma(sp_ways),
            dma(sp_ways),
            pltpu.SemaphoreType.DMA,
        ]

    small_slots = 1 + (columns - 1) + (sp_ways - 1)
    whole = shape(model_width, model_width)
    tokens = pltpu.VMEM(token_shape, bf16)
    *weight_grads, up_land, down_land, block_out, tokens_grad, small_sum = pl.pallas_call(
        functools.partial(backward, sp_ways, dp_ways, head_dim),
        out_shape=[whole] * 4
        + [
            shape(rest, shard_size, model_width),
            shape(rest, blocks, slot_count, model_width),
            shape(*token_shape),
            shape(*token_shape),
            shape(8, model_width, dtype=f32),
        ],
        in_specs=hbm * 17 + vmem(4),
        out_specs=hbm * 6 + vmem(3),
        scratch_shapes=[
            pltpu.VMEM(routed.shape, bf16),
            pltpu.VMEM(placer.shape, bf16),
            pltpu.VMEM(flat, bf16),
            pltpu.VMEM(flat, f32),
            square,
            tokens,
            by_head,
            by_head,
            by_head,
            whole_tokens,
            square,
            square,
            square,
            tokens,
            pltpu.VMEM(routed.shape, bf16),
            pltpu.VMEM(token_shape, f32),
            pltpu.VMEM(flat, bf16),
            tokens,
            by_head,
            pltpu.VMEM((seq_len, width), f32),
            pltpu.VMEM((seq_len, width), f32),
            pltpu.VMEM((seq_len, width), f32),
            pltpu.VMEM((seq_count, seq_len, 3 * width), bf16),
            pltpu.VMEM((seq_count, shard_len, 3 * model_width), bf16),
            square,
            pltpu.VMEM((3, model_width, width), bf16),
            pltpu.VMEM((sp_ways, rows, model_width), bf16),
            pltpu.VMEM((8, model_width), f32),
            pltpu.VMEM((small_slots, 8, model_width), f32),
            pltpu.VMEM((2, 8, model_width), f32),
            dma(seq_count, sp_ways),
            dma(seq_count, sp_ways),
            dma(seq_count, sp_ways),
            dma(seq_count, sp_ways),
            dma(dp_ways),
            dma(dp_ways),
            dma(2, sp_ways // 2),
            dma(2, sp_ways // 2),
            dma(sp_ways),
            dma(sp_ways),
            dma(small_slots),
            dma(small_slots),
            dma(15),
        ]
        + reduction(model_width)
        + reduction(width) * 3,
        compiler_params=params(1),
    )(
        dnormed_back,
        placer,
        cot_b,
        residual_stream,
        out_weight,
        mixed_b,
        query_h,
        key_h,
        value_h,
        normed_all,
        query_weight,
        key_weight,
        value_weight,
        tokens_in,
        expert_out,
        up_rest,
        down_rest,
        log_total,
        norm1_gain.reshape(1, model_width),
        norm2_gain.reshape(1, model_width),
        counts,
    )
    shard_shape = (shard_size, model_width)
    parts = 8
    big = pl.BlockSpec((model_width // parts, model_width), lambda i: (i, 0))
    own = pl.BlockSpec((shard_size // parts, model_width), lambda i: (i, 0))
    land = pl.BlockSpec((rest, shard_size // parts, model_width), lambda i: (0, i, 0))
    token = pl.BlockSpec((row_count // parts, model_width), lambda i: (i, 0))
    row = pl.BlockSpec((1, model_width), lambda i: (0, 0))
    load = pl.BlockSpec((1, experts), lambda i: (0, 0))
    results = pl.pallas_call(
        functools.partial(finish, experts, row_count * dp_ways * sp_ways),
        grid=(parts,),
        out_shape=[shape(model_width, model_width, dtype=f32)] * 4
        + [shape(*shard_shape, dtype=f32)] * 2
        + [shape(*flat)] * 2
        + [shape(1, model_width, dtype=f32)] * 4
        + [shape(1, experts, dtype=f32)],
        in_specs=[big] * 4
        + [own, land, own, land, token, token]
        + [pl.BlockSpec((8, model_width), lambda i: (0, 0)), load],
        out_specs=[big] * 4 + [own, own, token, token] + [row] * 4 + [load],
        compiler_params=pltpu.CompilerParams(vmem_limit_bytes=VMEM_BYTES),
    )(
        *weight_grads,
        up_own,
        up_land,
        down_own.reshape(shard_shape),
        down_land.reshape((rest,) + shard_shape),
        block_out.reshape(flat),
        tokens_grad.reshape(flat),
        small_sum,
        load_mean.reshape(1, experts),
    )
    return (
        results[6].reshape(token_shape),
        results[7].reshape(token_shape),
        *results[:4],
        *(vector.reshape(model_width) for vector in results[8:12]),
        results[4][None],
        results[5][None],
        results[12].reshape(experts),
    )


def solution(mesh):
    return jax.shard_map(
        local,
        mesh=mesh,
        in_specs=(
            P("dp", "sp", None),
            P("dp", "sp", None, None),
            P(),
            P(),
            P(),
            P(),
            P(),
            P(),
            P(),
            P(),
            P("dp", None, None),
            P("dp", None, None),
            P("dp", "sp", None),
            P(),
        ),
        out_specs=(
            P("dp", "sp", None),
            P("dp", "sp", None),
            P(),
            P(),
            P(),
            P(),
            P(),
            P(),
            P(),
            P(),
            P("dp", "sp", None),
            P("dp", "sp", None),
            P(),
        ),
        check_vma=False,
    )
```

```python
import functools

import jax
import jax.numpy as jnp
from jax import lax
from jax.experimental import pallas as pl
from jax.experimental.pallas import tpu as pltpu
from jax.sharding import PartitionSpec as P

HEADS = 16
MESH = pl.DeviceIdType.MESH
BLOCK = 256
LANES = 128
STEP = 1024
VMEM_BYTES = 60 * 2**20

NORM_EPSILON = 1e-05
GELU_ROOT = 0.7978845608028654
CUBIC_TERM = 0.044715

ROWS_BY_COLS = (((1,), (0,)), ((), ()))
ROWS_BY_ROWS = (((1,), (1,)), ((), ()))
COLS_BY_COLS = (((0,), (0,)), ((), ()))


def smooth(values):
    return (
        0.5
        * values
        * (1.0 + jnp.tanh(GELU_ROOT * (values + CUBIC_TERM * values * values * values)))
    )


def smooth_slope(values):
    inner = jnp.tanh(GELU_ROOT * (values + CUBIC_TERM * values * values * values))
    return 0.5 * (1.0 + inner) + 0.5 * values * (1.0 - inner * inner) * GELU_ROOT * (
        1.0 + 3.0 * CUBIC_TERM * values * values
    )


def norm_forward(values, gain, shift):
    center = jnp.mean(values, axis=-1, keepdims=True)
    offset = values - center
    rstd = lax.rsqrt(jnp.mean(offset * offset, axis=-1, keepdims=True) + NORM_EPSILON)
    unit = offset * rstd
    return (unit * gain + shift, unit, rstd)


def norm_backward(grad, unit, rstd, gain):
    scaled = grad * gain
    inner = (
        scaled
        - jnp.mean(scaled, axis=-1, keepdims=True)
        - unit * jnp.mean(scaled * unit, axis=-1, keepdims=True)
    )
    return (inner * rstd, jnp.sum(grad * unit, axis=0), jnp.sum(grad, axis=0))


def mxu(left, right, dims=ROWS_BY_COLS):
    return lax.dot_general(left, right, dims, preferred_element_type=jnp.float32)


def span(index, size):
    return pl.ds(pl.multiple_of(index * size, size), size)


def greet(peers):
    barrier = pltpu.get_barrier_semaphore()
    for peer in peers:
        pl.semaphore_signal(barrier, inc=1, device_id=peer, device_id_type=MESH)
    pl.semaphore_wait(barrier, len(peers))


def send(source, target, send_sem, recv_sem, peer):
    return pltpu.make_async_remote_copy(
        src_ref=source,
        dst_ref=target,
        send_sem=send_sem,
        recv_sem=recv_sem,
        device_id=peer,
        device_id_type=MESH,
    )


def exchange(others, source, target, send_sem, recv_sem):
    me = lax.axis_index("dp")
    return [
        send(
            source.at[flip(me, d)],
            target.at[me],
            send_sem.at[d],
            recv_sem.at[d],
            {"dp": flip(me, d)},
        )
        for d in range(1, others)
    ]


def flip(index, bits):
    bit = 1
    while bit <= bits:
        if bits & bit:
            index = index + bit - 2 * bit * lax.rem(index // bit, 2)
        bit *= 2
    return index


def forward(
    ways,
    others,
    head_dim,
    x_ref,
    cot_ref,
    wq_ref,
    wk_ref,
    wv_ref,
    wo_ref,
    ids_ref,
    gain1_ref,
    shift1_ref,
    gain2_ref,
    shift2_ref,
    normed_ref,
    q_ref,
    k_ref,
    v_ref,
    mixed_ref,
    arrived_ref,
    placer_ref,
    residual_ref,
    log_ref,
    outgoing_ref,
    counts_ref,
    x_all,
    cot_v,
    cot_out,
    wq_v,
    wk_v,
    wv_v,
    wo_v,
    placer_v,
    normed_v,
    q_v,
    k_v,
    v_v,
    mixed_f,
    mixed_h,
    mixed_tok,
    log_s,
    residual_v,
    normed2,
    x_send,
    x_recv,
    m_send,
    m_recv,
    c_send,
    c_recv,
    load_sem,
    x_sem,
    store_sem,
    own_sem,
):
    seqs, seq_len, model = x_all.shape
    shard = seq_len // ways
    width = q_v.shape[2]
    heads = width // head_dim
    slots = cot_out.shape[1]
    me = lax.axis_index("sp")
    dp = lax.axis_index("dp")
    peer = [flip(me, d) for d in range(ways)]
    near = (1, 2) if ways == 4 else tuple(range(1, ways))
    far = tuple(range(1 + len(near), ways))
    barrier = pltpu.get_barrier_semaphore()
    neighbours = [{"sp": peer[d]} for d in range(1, ways)]
    neighbours += [{"dp": flip(dp, d)} for d in range(1, others)]
    for device in neighbours:
        pl.semaphore_signal(barrier, inc=1, device_id=device, device_id_type=MESH)
    own_columns = span(me, width)
    loads = [
        pltpu.make_async_copy(source, target, load_sem.at[i])
        for i, (source, target) in enumerate(
            (
                (cot_ref, cot_v),
                (wq_ref.at[:, own_columns], wq_v),
                (wk_ref.at[:, own_columns], wk_v),
                (wv_ref.at[:, own_columns], wv_v),
                (wo_ref, wo_v),
            )
        )
    ]
    own_x = [
        pltpu.make_async_copy(x_ref.at[s], x_all.at[s, span(me, shard)], x_sem.at[s])
        for s in range(seqs)
    ]
    for copy in own_x + loads:
        copy.start()

    def x_copy(s, d):
        return send(
            x_ref.at[s],
            x_all.at[s, span(me, shard)],
            x_send.at[s, d],
            x_recv.at[s, d],
            {"sp": peer[d]},
        )

    def x_relays(s):
        if not far:
            return []
        size = shard // 2
        pieces = [
            x_all.at[s, pl.ds(pl.multiple_of(peer[1] * shard, size), size)],
            x_all.at[s, pl.ds(pl.multiple_of(peer[2] * shard + size, size), size)],
        ]
        return [
            send(piece, piece, x_send.at[s, at], x_recv.at[s, at], {"sp": peer[to]})
            for piece, at, to in zip(pieces, (0, 3), (2, 1))
        ]

    cuts = max(1, width // BLOCK)
    cuts = 2 * cuts if width // (2 * cuts) % LANES == 0 else cuts
    cut = width // cuts

    def mixed_copy(s, d, c):
        return send(
            mixed_h.at[s, span(peer[d], shard), c * cut : (c + 1) * cut],
            mixed_tok.at[s, :, span(me * cuts + c, cut)],
            m_send.at[s, c, d],
            m_recv.at[s, c, d],
            {"sp": peer[d]},
        )

    tokens = seqs * shard
    ids = ids_ref[...]
    named = lax.broadcasted_iota(jnp.int32, (LANES, tokens), 0) == ids
    named = jnp.where(named, 1.0, 0.0)
    upper = lax.broadcasted_iota(jnp.int32, (tokens, tokens), 0) <= lax.broadcasted_iota(
        jnp.int32, (tokens, tokens), 1
    )
    running = mxu(named.astype(jnp.bfloat16), jnp.where(upper, 1.0, 0.0).astype(jnp.bfloat16))
    slot = jnp.sum(named * (running - 1.0), axis=0, keepdims=True).astype(jnp.int32)
    places = lax.broadcasted_iota(jnp.int32, placer_v.shape, 0) == ids * slots + slot
    placer_v[...] = jnp.where(places, 1.0, 0.0).astype(jnp.bfloat16)
    ones = jnp.ones((8, tokens), jnp.float32)
    counts_ref[...] = mxu(ones, named, ROWS_BY_ROWS)
    pl.semaphore_wait(barrier, len(neighbours))
    for d in near:
        x_copy(0, d).start()
    loads[0].wait()
    cot_out[...] = (
        mxu(placer_v[...], cot_v[...]).astype(jnp.bfloat16).reshape(cot_out.shape)
    )
    background = exchange(others, cot_out, arrived_ref, c_send, c_recv)
    own_cot = pltpu.make_async_copy(cot_out.at[dp], arrived_ref.at[dp], own_sem)
    for copy in background + [own_cot]:
        copy.start()

    lane = lax.broadcasted_iota(jnp.int32, (1, width), 1) // head_dim
    log_lane = lax.broadcasted_iota(jnp.int32, (1, LANES), 1)
    visible = lax.broadcasted_iota(jnp.int32, (BLOCK, BLOCK), 1) <= lax.broadcasted_iota(
        jnp.int32, (BLOCK, BLOCK), 0
    )
    scale = head_dim ** (-0.5)
    outs = ((normed_v, normed_ref), (q_v, q_ref), (k_v, k_ref), (v_v, v_ref))
    stores = [
        [
            pltpu.make_async_copy(source.at[s], target.at[s], store_sem.at[s, i])
            for i, (source, target) in enumerate(outs)
        ]
        for s in range(seqs)
    ]

    def project(s, d):
        rows = span(peer[d], shard)
        values = x_all[s, rows, :].astype(jnp.float32)
        normed, _, _ = norm_forward(values, gain1_ref[...], shift1_ref[...])
        normed = normed.astype(jnp.bfloat16)
        normed_v[s, rows, :] = normed
        q_v[s, rows, :] = mxu(normed, wq_v[...]).astype(jnp.bfloat16)
        k_v[s, rows, :] = mxu(normed, wk_v[...]).astype(jnp.bfloat16)
        v_v[s, rows, :] = mxu(normed, wv_v[...]).astype(jnp.bfloat16)

    for s in range(seqs):
        own_x[s].wait()
        if s == 0:
            for copy in loads[1:4]:
                copy.wait()
        project(s, 0)
        for d in near:
            x_copy(s, d).wait_recv()
        for copy in x_relays(s):
            copy.start()
        for d in near:
            project(s, d)
        for copy in x_relays(s):
            copy.wait_recv()
        if s + 1 < seqs:
            for d in near:
                x_copy(s + 1, d).start()
        if s:
            for c in range(cuts):
                for d in range(1, ways):
                    mixed_copy(s - 1, d, c).start()
        for d in far:
            project(s, d)
        for copy in stores[s]:
            copy.start()
        mixed_f[...] = jnp.zeros_like(mixed_f)
        log_s[...] = jnp.zeros_like(log_s)

        def one_head(h, carry):
            mine = (lane == h).astype(jnp.float32)
            for at in range(0, seq_len, BLOCK):
                rows = slice(at, at + BLOCK)
                query = (q_v[s, rows, :].astype(jnp.float32) * (mine * scale)).astype(
                    jnp.bfloat16
                )
                near = mxu(query, k_v[s, rows, :], ROWS_BY_ROWS)
                near = jnp.where(visible, near, -1e30)
                top = jnp.max(near, axis=1, keepdims=True)
                if at:
                    far = mxu(query, k_v[s, :at, :], ROWS_BY_ROWS)
                    top = jnp.maximum(top, jnp.max(far, axis=1, keepdims=True))
                near = jnp.exp(near - top)
                total = jnp.sum(near, axis=1, keepdims=True)
                if at:
                    far = jnp.exp(far - top)
                    total += jnp.sum(far, axis=1, keepdims=True)
                inverse = 1.0 / total
                out = mxu((near * inverse).astype(jnp.bfloat16), v_v[s, rows, :])
                if at:
                    out += mxu((far * inverse).astype(jnp.bfloat16), v_v[s, :at, :])
                mixed_f[rows, :] += out * mine
                log_s[rows, :] = jnp.where(log_lane == h, top + jnp.log(total), log_s[rows, :])
            return carry

        for c in range(cuts):
            lax.fori_loop(c * heads // cuts, (c + 1) * heads // cuts, one_head, 0)
            columns = slice(c * cut, (c + 1) * cut)
            mixed_h[s, :, columns] = mixed_f[:, columns].astype(jnp.bfloat16)
            if s == seqs - 1:
                for d in range(1, ways):
                    mixed_copy(s, d, c).start()
        log_ref[s] = jnp.transpose(log_s[...])[: log_ref.shape[1], :]
        mixed_tok[s, :, own_columns] = mixed_h[s, span(me, shard), :]

    loads[4].wait()
    for s in range(seqs):
        for c in range(cuts):
            for d in range(1, ways):
                mixed_copy(s, d, c).wait_recv()
        rows = slice(s * shard, (s + 1) * shard)
        values = x_all[s, span(me, shard), :].astype(jnp.float32)
        values += mxu(mixed_tok[s], wo_v[...])
        residual_v[rows, :] = values
        normed, _, _ = norm_forward(values, gain2_ref[...], shift2_ref[...])
        normed2[rows, :] = normed.astype(jnp.bfloat16)
    last = [
        pltpu.make_async_copy(source, target, store_sem.at[seqs, i])
        for i, (source, target) in enumerate(
            ((mixed_tok, mixed_ref), (residual_v, residual_ref), (placer_v, placer_ref))
        )
    ]
    for copy in last:
        copy.start()
    outgoing_ref[...] = (
        mxu(placer_v[...], normed2[...]).astype(jnp.bfloat16).reshape(outgoing_ref.shape)
    )
    for s in range(seqs):
        for d in near:
            x_copy(s, d).wait_send()
        for copy in x_relays(s):
            copy.wait_send()
        for c in range(cuts):
            for d in range(1, ways):
                mixed_copy(s, d, c).wait_send()
        for copy in stores[s]:
            copy.wait()
    for copy in background + [own_cot] + last:
        copy.wait()


def pair_of(sp):
    core = lax.rem(lax.axis_index("dp"), 2)
    along_x, along_y = flip(sp, 1), flip(sp, 2)
    return along_x + core * (along_y - along_x)


def shards_of(sp, ways):
    shards = [sp, flip(pair_of(sp), 3)]
    bit = 4
    while bit < ways:
        shards += [flip(shard, bit) for shard in shards]
        bit *= 2
    return shards


def run_experts(
    others,
    ways,
    outgoing_ref,
    cot_ref,
    up_ref,
    down_ref,
    back_ref,
    result_ref,
    up_own,
    up_rest,
    down_own,
    down_rest,
    received,
    arrived,
    up_v,
    down_v,
    hidden,
    slope_v,
    total,
    dn_own,
    dn_pair,
    dn_land,
    dnormed,
    out_pair,
    out_land,
    w_sem,
    o_sem,
    c_sem,
    a_send,
    a_recv,
    b_send,
    b_recv,
    f_send,
    f_recv,
    p_send,
    p_recv,
    e_send,
    e_recv,
):
    slots, width = received.shape[1:]
    rows = others * slots
    ff = up_v.shape[0]
    groups = others // 2
    me = lax.axis_index("dp")
    sp = lax.axis_index("sp")
    chip = me // 2
    pair = {"sp": pair_of(sp)}
    shards = shards_of(sp, ways)
    size = ff // len(shards)
    loads = [
        pltpu.make_async_copy(
            source.at[span(shard, size)], target.at[i * size : (i + 1) * size], w_sem.at[j, i]
        )
        for j, (source, target) in enumerate(((down_ref, down_v), (up_ref, up_v)))
        for i, shard in enumerate(shards)
    ]
    own_cot = pltpu.make_async_copy(cot_ref, arrived.at[0], c_sem.at[0])
    own_rows = pltpu.make_async_copy(outgoing_ref.at[me], received.at[me], c_sem.at[1])
    own_back = pltpu.make_async_copy(dnormed.at[me], back_ref.at[me], c_sem.at[2])
    own_rows.start()
    own_cot.start()
    for copy in loads:
        copy.start()
    greet([{"dp": flip(me, d)} for d in range(1, others)] + [pair])
    inward = exchange(others, outgoing_ref, received.at[0:others], a_send, a_recv)
    outward = exchange(others, dnormed, back_ref, b_send, b_recv)
    near = [flip(chip, group) for group in range(groups)]
    chips = [pl.ds(2 * near[group], 2) for group in range(groups)]
    forward = [
        send(
            received.at[chips[group]],
            received.at[pl.ds(others + 2 * near[group], 2)],
            f_send.at[group],
            f_recv.at[group],
            pair,
        )
        for group in range(groups)
    ]
    cot_copy = [
        send(
            cot_ref.at[i * groups : (i + 1) * groups],
            arrived.at[1, i * groups : (i + 1) * groups],
            f_send.at[groups + i],
            f_recv.at[groups + i],
            pair,
        )
        for i in range(2)
    ]
    dn_copy = [
        send(
            dn_pair.at[chips[group]],
            dn_land.at[chips[group]],
            p_send.at[group],
            p_recv.at[group],
            pair,
        )
        for group in range(groups)
    ]
    out_copy = [
        send(
            out_pair.at[chips[group]],
            out_land.at[chips[group]],
            e_send.at[group],
            e_recv.at[group],
            pair,
        )
        for group in range(groups)
    ]

    early = range(groups // 2)
    middle = range(groups // 2, 3 * groups // 4)
    late = range(3 * groups // 4, groups)
    for copy in [inward[0]] + inward[2 * middle[0] - 1 : 2 * late[0] - 1]:
        copy.start()
    for copy in inward[1 : 2 * middle[0] - 1]:
        copy.start()
    for copy in cot_copy:
        copy.start()
    own_rows.wait()

    def slab_of(half, group):
        return pl.ds(pl.multiple_of(half * rows + near[group] * (2 * slots), 2 * slots), 2 * slots)

    def cot_part(half, begin, end):
        def cot_step(i, carry):
            at = span(i, STEP)
            cot = arrived[half, begin:end].reshape((end - begin) * slots, width)
            slope_v[half * rows + begin * slots : half * rows + end * slots, at] = mxu(
                cot, down_v[at, :], ROWS_BY_ROWS
            ).astype(jnp.bfloat16)
            return carry

        lax.fori_loop(0, ff // STEP, cot_step, 0)

    def up_half(half, group):
        slab = slab_of(half, group)
        total[...] = jnp.zeros_like(total)

        def up_step(i, carry):
            at = span(i, STEP)
            tokens = received[pl.ds(half * others + 2 * near[group], 2)].reshape(2 * slots, width)
            pre = mxu(tokens, up_v[at, :], ROWS_BY_ROWS)
            square = pre * pre
            inner = jnp.tanh(GELU_ROOT * pre * (1.0 + CUBIC_TERM * square))
            gate = 0.5 * (1.0 + inner)
            hidden[slab, at] = (pre * gate).astype(jnp.bfloat16)
            slope = gate + (0.5 * GELU_ROOT) * pre * (1.0 - inner * inner) * (
                1.0 + (3.0 * CUBIC_TERM) * square
            )
            dpre = (slope_v[slab, at].astype(jnp.float32) * slope).astype(jnp.bfloat16)
            slope_v[slab, at] = dpre
            total[...] += mxu(dpre, up_v[at, :])
            return carry

        lax.fori_loop(0, ff // STEP, up_step, 0)
        shaped = total[...].reshape(2, slots, width)
        if half:
            dn_pair[chips[group]] = shaped.astype(jnp.bfloat16)
        else:
            dn_own[chips[group]] = shaped

    def out_half(half, group):
        at = chips[group]
        out = mxu(hidden[slab_of(half, group), :], down_v[...]).reshape(2, slots, width)
        if half:
            out_pair[at] = out.astype(jnp.bfloat16)
        else:
            out_copy[group].wait_recv()
            result_ref[at] = (out + out_land[at].astype(jnp.float32)).astype(jnp.bfloat16)

    def pass_on(group):
        for d in (2 * group, 2 * group + 1):
            if d:
                inward[d - 1].wait_recv()
        forward[group].start()

    def finish(group):
        dn_copy[group].wait_recv()
        at = chips[group]
        dnormed[at] = (dn_own[at] + dn_land[at].astype(jnp.float32)).astype(jnp.bfloat16)
        for d in (2 * group, 2 * group + 1):
            if d:
                outward[d - 1].start()
            else:
                own_back.start()

    def up_pair(group):
        forward[group].wait_recv()
        up_half(1, group)
        if group not in early:
            dn_copy[group].start()

    def grad(target, left, right_ref, begin, end, block=0):
        def grad_step(i, carry):
            at = span(i, STEP)
            right = right_ref[...].reshape(2 * rows, width)
            out = mxu(left[:, at], right, COLS_BY_COLS).astype(jnp.bfloat16)
            if block:
                target[span(i, STEP // block)] = out.reshape(STEP // block, block, width)
            else:
                target[at, :] = out
            return carry

        lax.fori_loop(begin, end, grad_step, 0)

    pass_on(0)
    own_cot.wait()
    for copy in loads[: len(shards)]:
        copy.wait()
    cot_part(0, 0, others)
    for copy in loads[len(shards) :]:
        copy.wait()
    up_half(0, 0)
    cot_copy[0].wait_recv()
    cot_part(1, 0, groups)
    for group in middle:
        pass_on(group)
        up_half(0, group)
    for copy in inward[2 * middle[0] - 1 : 2 * late[0] - 1]:
        copy.wait_send()
    for copy in inward[2 * late[0] - 1 :]:
        copy.start()
    for group in early[1:]:
        pass_on(group)
    cot_copy[1].wait_recv()
    cot_part(1, groups, others)
    for group in early[1:]:
        up_half(0, group)
    for group in middle:
        up_pair(group)
    for group in early:
        up_pair(group)
    for group in late:
        pass_on(group)
    dn_copy[0].start()
    for group in middle:
        finish(group)
    for group in late:
        up_half(0, group)
    for group in middle:
        out_half(1, group)
    for group in late:
        up_pair(group)
    for group in early[1:]:
        dn_copy[group].start()
    for group in middle:
        out_copy[group].start()
    for group in [*early, *late]:
        out_half(1, group)
    tokens_all = received.at[0 : 2 * others]
    grad(up_v, slope_v, tokens_all, 0, 1)
    for group in late:
        finish(group)
    for group in [*early, *late]:
        out_copy[group].start()
    grad(up_v, slope_v, tokens_all, 1, ff // STEP)
    for group in early:
        finish(group)
    for copy in forward:
        copy.wait_send()
    grad(received, hidden, arrived, 0, ff // STEP, slots)
    first, every = size // slots, ff // slots
    stores = [
        pltpu.make_async_copy(source, target, o_sem.at[i])
        for i, (source, target) in enumerate(
            (
                (up_v.at[0:size], up_own),
                (up_v.at[size:ff], up_rest),
                (received.at[0:first], down_own),
                (received.at[first:every], down_rest),
            )
        )
    ]
    for copy in stores:
        copy.start()
    for group in range(groups):
        out_half(0, group)
    for copy in inward[: 2 * middle[0] - 1] + inward[2 * late[0] - 1 :]:
        copy.wait_send()
    for copy in cot_copy + dn_copy + out_copy:
        copy.wait_send()
    for copy in outward + stores + [own_back]:
        copy.wait()


class Reduction:
    def __init__(self, ways, columns, part, out, across_first, scratch):
        (
            self.core_land,
            self.core_sum,
            self.column_land,
            self.piece,
            core_send,
            core_recv,
            column_send,
            column_recv,
            spread_send,
            spread_recv,
            ring_send,
            ring_recv,
            cross_send,
            cross_recv,
            own_sem,
        ) = scratch
        me = lax.axis_index("sp")
        dp = lax.axis_index("dp")
        core = lax.rem(dp, 2)
        column = dp // 2
        twin = {"dp": dp + 1 - 2 * core}
        self.ways, self.columns, self.part = ways, columns, part
        self.core = core
        rows, width = self.piece.shape
        self.rows = rows

        bits = [1 << i for i in range(columns.bit_length() - 1)]
        place = 0
        for bit in bits:
            place = 2 * place + lax.rem(column // bit, 2)
        self.place = place

        def beside(bit):
            return {"dp": 2 * flip(column, bit) + core}

        def block(first, at_sp, count):
            first = pl.multiple_of((core * columns + first) * rows, rows)
            return out.at[pl.ds(first, count * rows), span(at_sp, width)]

        self.core_copy = send(
            part.at[span(1 - core, columns * rows)], self.core_land, core_send, core_recv, twin
        )
        self.column_copy, self.kept, self.lands = [], [], []
        first, count, used = 0, columns, 0
        for i, bit in enumerate(bits):
            count //= 2
            mine = lax.rem(column // bit, 2)
            size = count * rows
            gone = pl.ds(pl.multiple_of((first + (1 - mine) * count) * rows, size), size)
            first = first + mine * count
            self.kept.append(pl.ds(pl.multiple_of(first * rows, size), size))
            land = self.column_land.at[used : used + size]
            used += size
            self.lands.append(land)
            self.column_copy.append(
                send(self.core_sum.at[gone], land, column_send.at[i], column_recv.at[i], beside(bit))
            )
        spot = block(place, me, 1)
        self.own = pltpu.make_async_copy(self.piece, spot, own_sem)
        origin = [flip(me, d) for d in range(ways)]
        across_count = 1 if across_first else columns
        across_at = place if across_first else 0
        near = (1, 2) if ways == 4 else tuple(range(1, ways))
        held = [block(across_at, at, across_count) for at in origin]
        self.ring_copy = [
            send(held[0], held[0], ring_send.at[d], ring_recv.at[d], {"sp": origin[d]})
            for d in near
        ]
        self.relays = []
        if ways == 4:
            count = across_count * rows // 2
            first = (core * columns + across_at) * rows
            for i, (d, to) in enumerate(((1, 2), (2, 1))):
                at = pl.multiple_of(first + i * count, count)
                half = out.at[pl.ds(at, count), span(origin[d], width)]
                index = (0, 3)[i]
                self.relays.append(
                    send(
                        half, half, ring_send.at[index], ring_recv.at[index], {"sp": origin[to]}
                    )
                )

        def rows_of(first, count):
            first = pl.multiple_of((core * columns + first) * rows, rows)
            return out.at[pl.ds(first, count * rows)]

        self.spread_copy, gathered = [], [rows_of(place, 1)]
        for i, bit in enumerate(reversed(bits)):
            count = 1 << i
            at = place - lax.rem(place, count)
            spot = rows_of(at, count) if across_first else block(at, me, count)
            gathered.append(rows_of(flip(at, count), count))
            self.spread_copy.append(
                send(spot, spot, spread_send.at[i], spread_recv.at[i], beside(bit))
            )
        crossing = gathered if across_first else held
        self.cross_copy = [
            send(part, part, cross_send.at[i], cross_recv.at[i], twin)
            for i, part in enumerate(crossing)
        ]
        self.phases = iter(self.across_then_along() if across_first else self.along_then_across())

    def along_then_across(self):
        self.own.start()
        self.own.wait()
        for copy in self.spread_copy:
            copy.start()
            yield
            copy.wait()
        for copy in self.ring_copy:
            copy.start()
        self.cross_copy[0].start()
        yield
        for ring, cross in zip(self.ring_copy, self.cross_copy[1:]):
            ring.wait_recv()
            cross.start()
        for copy in self.relays:
            copy.start()
        yield
        for copy in self.relays:
            copy.wait_recv()
        if self.relays:
            self.cross_copy[3].start()
        yield

    def across_then_along(self):
        self.own.start()
        self.own.wait()
        for copy in self.ring_copy:
            copy.start()
        yield
        for copy in self.ring_copy:
            copy.wait_recv()
        for copy in self.relays:
            copy.start()
        yield
        for copy in self.relays:
            copy.wait_recv()
        for spread, cross in zip(self.spread_copy, self.cross_copy):
            spread.start()
            cross.start()
            yield
            spread.wait()
        self.cross_copy[-1].start()
        yield

    def advance(self):
        next(self.phases)

    def add_core(self):
        self.core_copy.wait()
        self.core_sum[...] = (
            self.part[span(self.core, self.columns * self.rows), :].astype(jnp.float32)
            + self.core_land[...].astype(jnp.float32)
        ).astype(jnp.bfloat16)
        self.column_copy[0].start()

    def add_column(self, step):
        self.column_copy[step].wait()
        total = self.core_sum[self.kept[step], :].astype(jnp.float32)
        total += self.lands[step][...].astype(jnp.float32)
        if step + 1 < len(self.column_copy):
            self.core_sum[self.kept[step], :] = total.astype(jnp.bfloat16)
            self.column_copy[step + 1].start()
        return total

    def finish(self):
        for copy in self.ring_copy + self.relays:
            copy.wait_send()
        for copy in self.cross_copy:
            copy.wait()


def backward(
    ways,
    others,
    head_dim,
    back_ref,
    placer_ref,
    cot_ref,
    residual_ref,
    wo_ref,
    mixed_ref,
    q_ref,
    k_ref,
    v_ref,
    normed_ref,
    wq_ref,
    wk_ref,
    wv_ref,
    x_ref,
    result_ref,
    up_rest,
    down_rest,
    log_ref,
    gain1_ref,
    gain2_ref,
    counts_ref,
    out_q,
    out_k,
    out_v,
    out_o,
    up_land,
    down_land,
    block_ref,
    tokens_ref,
    small_out,
    back_v,
    placer_v,
    cot_v,
    residual_v,
    wo_v,
    mixed_v,
    q_v,
    k_v,
    v_v,
    normed_v,
    wq_v,
    wk_v,
    wv_v,
    x_v,
    returned,
    dresid,
    dattn,
    dmixed,
    dmixed_h,
    dq_f,
    dk_f,
    dv_f,
    grads_h,
    grads_tok,
    part_o,
    parts_w,
    o_land,
    small_own,
    small_land,
    small_sum,
    m_send,
    m_recv,
    g_send,
    g_recv,
    c_send,
    c_recv,
    s_send,
    s_recv,
    o_send,
    o_recv,
    small_send,
    small_recv,
    load_sem,
    *scratch,
):
    seqs, shard, model = x_v.shape
    seq_len, width = q_v.shape[1:]
    heads = width // head_dim
    columns = others // 2
    me = lax.axis_index("sp")
    dp = lax.axis_index("dp")
    core = lax.rem(dp, 2)
    peer = [lax.rem(me + d, ways) for d in range(ways)]
    barrier = pltpu.get_barrier_semaphore()
    neighbours = [{"sp": peer[d]} for d in range(1, ways)]
    neighbours += [{"dp": flip(dp, d)} for d in range(1, others)]
    for device in neighbours:
        pl.semaphore_signal(barrier, inc=1, device_id=device, device_id_type=MESH)
    sources = (
        (back_ref, back_v),
        (placer_ref, placer_v),
        (residual_ref, residual_v),
        (cot_ref, cot_v),
        (wo_ref, wo_v),
        (mixed_ref, mixed_v),
        (q_ref, q_v),
        (k_ref, k_v),
        (v_ref, v_v),
        (normed_ref, normed_v),
        (wq_ref, wq_v),
        (wk_ref, wk_v),
        (wv_ref, wv_v),
        (x_ref, x_v),
        (result_ref.at[dp], returned.at[dp]),
    )
    loads = [
        pltpu.make_async_copy(source, target, load_sem.at[i])
        for i, (source, target) in enumerate(sources)
    ]
    for copy in loads:
        copy.start()

    def dmixed_copy(s, d):
        return send(
            dmixed.at[s, :, span(peer[d], width)],
            dmixed_h.at[s, span(me, shard)],
            m_send.at[s, d],
            m_recv.at[s, d],
            {"sp": peer[d]},
        )

    def grad_copy(s, d):
        return send(
            grads_h.at[s, span(peer[d], shard)],
            grads_tok.at[s, :, span(me, 3 * width)],
            g_send.at[s, d],
            g_recv.at[s, d],
            {"sp": peer[d]},
        )

    shards = shards_of(me, ways)
    scatter = []
    for j, (rest, land) in enumerate(((up_rest, up_land), (down_rest, down_land))):
        size = land.shape[1]
        first = size // 4
        for part, (begin, end) in enumerate(((0, first), (first, size))):
            scatter += [
                send(
                    rest.at[(i - 1) * size + begin : (i - 1) * size + end],
                    land.at[i - 1, begin:end],
                    s_send.at[j, part, i],
                    s_recv.at[j, part, i],
                    {"sp": shards[i]},
                )
                for i in range(1, len(shards))
            ]
    routed_back = exchange(others, result_ref, returned, c_send, c_recv)
    pl.semaphore_wait(barrier, len(neighbours))
    for copy in scatter[: len(shards) - 1]:
        copy.start()
    for copy in routed_back:
        copy.start()

    small_own[...] = jnp.zeros_like(small_own)
    small_own[4:5, 0:LANES] = counts_ref[0:1, :]
    for s in range(seqs):
        if s == 0:
            for copy in loads[:4]:
                copy.wait()
        rows = slice(s * shard, (s + 1) * shard)
        dnormed = mxu(placer_v[:, rows], back_v[...].reshape(-1, model), COLS_BY_COLS)
        gain = gain2_ref[...]
        _, unit, rstd = norm_forward(residual_v[rows, :], gain, jnp.zeros_like(gain))
        dinput, gain_grad, shift_grad = norm_backward(dnormed, unit, rstd, gain)
        total = cot_v[rows, :].astype(jnp.float32) + dinput
        dresid[s] = total
        dattn[rows, :] = total.astype(jnp.bfloat16)
        small_own[2:3, :] += gain_grad.reshape(1, model)
        small_own[3:4, :] += shift_grad.reshape(1, model)
        if s == 0:
            loads[4].wait()
        dmixed[s] = mxu(dattn[rows, :], wo_v[...], ROWS_BY_ROWS).astype(jnp.bfloat16)
        for d in range(1, ways):
            dmixed_copy(s, d).start()
    for copy in scatter[len(shards) - 1 :]:
        copy.start()
    sum_o = Reduction(ways, columns, part_o, out_o, False, scratch[:15])
    sums_w = [
        Reduction(ways, columns, parts_w.at[i], out, i == 0, scratch[15 * (i + 1) : 15 * (i + 2)])
        for i, out in enumerate((out_q, out_k, out_v))
    ]
    sum_q, sum_k, sum_v = sums_w
    steps = columns.bit_length() - 1

    loads[5].wait()

    def out_step(i, carry):
        at = span(i, BLOCK)
        left = mixed_v[:, :, at].reshape(seqs * shard, BLOCK)
        part_o[at, :] = mxu(left, dattn[...], COLS_BY_COLS).astype(jnp.bfloat16)
        return carry

    lax.fori_loop(0, model // BLOCK, out_step, 0)
    sum_o.core_copy.start()
    for copy in loads[6:9]:
        copy.wait()

    lane = lax.broadcasted_iota(jnp.int32, (1, width), 1) // head_dim
    visible = lax.broadcasted_iota(jnp.int32, (BLOCK, BLOCK), 0) <= lax.broadcasted_iota(
        jnp.int32, (BLOCK, BLOCK), 1
    )
    scale = head_dim ** (-0.5)
    for s in range(seqs):
        dmixed_h[s, span(me, shard), :] = dmixed[s, :, span(me, width)]
        for d in range(1, ways):
            dmixed_copy(s, d).wait_recv()
        if s == 0:
            sum_o.add_core()
        dq_f[...] = jnp.zeros_like(dq_f)
        dk_f[...] = jnp.zeros_like(dk_f)
        dv_f[...] = jnp.zeros_like(dv_f)

        def one_head(h, carry):
            mine = (lane == h).astype(jnp.float32)
            for at in range(0, seq_len, BLOCK):
                rows = slice(at, at + BLOCK)
                query = (q_v[s, rows, :].astype(jnp.float32) * (mine * scale)).astype(
                    jnp.bfloat16
                )
                dout = (dmixed_h[s, rows, :].astype(jnp.float32) * mine).astype(jnp.bfloat16)
                log_row = log_ref[s, pl.ds(h, 1), rows]
                parts = [(rows, True)] + ([(slice(0, at), False)] if at else [])
                kept = []
                delta = jnp.zeros((1, BLOCK), jnp.float32)
                for keys, diagonal in parts:
                    prob = jnp.exp(mxu(k_v[s, keys, :], query, ROWS_BY_ROWS) - log_row)
                    if diagonal:
                        prob = jnp.where(visible, prob, 0.0)
                    dprob = mxu(v_v[s, keys, :], dout, ROWS_BY_ROWS)
                    delta += jnp.sum(prob * dprob, axis=0, keepdims=True)
                    kept.append((keys, prob, dprob))
                dquery = jnp.zeros((BLOCK, width), jnp.float32)
                for keys, prob, dprob in kept:
                    dv_f[keys, :] += mxu(prob.astype(jnp.bfloat16), dout)
                    dlogit = (prob * (dprob - delta)).astype(jnp.bfloat16)
                    dk_f[keys, :] += mxu(dlogit, query)
                    dquery += mxu(dlogit, k_v[s, keys, :], COLS_BY_COLS)
                dq_f[rows, :] += dquery * (mine * scale)
            return carry

        lax.fori_loop(0, heads, one_head, 0)
        for i, total in enumerate((dq_f, dk_f, dv_f)):
            grads_h[s, :, i * width : (i + 1) * width] = total[...].astype(jnp.bfloat16)
        if s == 0:
            for d in range(1, ways):
                grad_copy(s, d).start()
        grads_tok[s, :, span(me, 3 * width)] = grads_h[s, span(me, shard), :]

    loads[9].wait()

    def weight_step(i, carry):
        at = span(i, BLOCK)
        grad = mxu(normed_v[0, :, at], grads_h[0], COLS_BY_COLS)
        for s in range(1, seqs):
            grad += mxu(normed_v[s, :, at], grads_h[s], COLS_BY_COLS)
        for j in range(3):
            parts_w[j, at, :] = grad[:, j * width : (j + 1) * width].astype(jnp.bfloat16)
        return carry

    lax.fori_loop(0, model // BLOCK, weight_step, 0)
    for total in (sum_v, sum_k, sum_q):
        total.core_copy.start()

    along, across = (sum_v, sum_k), (sum_q,)
    for total in (*across, *along):
        total.add_core()
    for step in range(steps - 1):
        sum_o.add_column(step)
    for step in range(steps):
        for total in (*across, *along):
            piece = total.add_column(step)
            if step == steps - 1:
                total.piece[...] = piece.astype(jnp.bfloat16)
                total.advance()

    o_land[0] = sum_o.add_column(steps - 1).astype(jnp.bfloat16)
    o_copy = [
        send(
            o_land.at[0, :, span(peer[d], width)],
            o_land.at[d, :, 0:width],
            o_send.at[d],
            o_recv.at[d],
            {"sp": peer[d]},
        )
        for d in range(1, ways)
    ]
    for copy in o_copy:
        copy.start()

    def norm_grad(s):
        for d in range(1, ways):
            grad_copy(s, d).wait()
        dnormed = jnp.zeros((shard, model), jnp.float32)
        for j in range(ways):
            for i, weight in enumerate((wq_v, wk_v, wv_v)):
                at = (3 * j + i) * width
                dnormed += mxu(
                    grads_tok[s, :, at : at + width],
                    weight[:, j * width : (j + 1) * width],
                    ROWS_BY_ROWS,
                )
        gain = gain1_ref[...]
        _, unit, rstd = norm_forward(x_v[s].astype(jnp.float32), gain, jnp.zeros_like(gain))
        dinput, gain_grad, shift_grad = norm_backward(dnormed, unit, rstd, gain)
        tokens_ref[s] = (dresid[s] + dinput).astype(jnp.bfloat16)
        small_own[0:1, :] += gain_grad.reshape(1, model)
        small_own[1:2, :] += shift_grad.reshape(1, model)

    for copy in loads[10:14]:
        copy.wait()
    for total in across:
        total.advance()
    for s in range(1, seqs):
        for d in range(1, ways):
            grad_copy(s, d).start()
    total = o_land[0, :, span(me, width)].astype(jnp.float32)
    for d, copy in enumerate(o_copy):
        copy.wait()
        total += o_land[d + 1, :, 0:width].astype(jnp.float32)
    sum_o.piece[...] = total.astype(jnp.bfloat16)
    sum_o.advance()
    for _ in range(steps - 1):
        for total in along:
            total.advance()
    for total in across:
        total.advance()
    for _ in range(steps - 1):
        sum_o.advance()
    for s in range(seqs - 1):
        norm_grad(s)
    along[0].advance()
    norm_grad(seqs - 1)

    stages = [[{"sp": peer[d]} for d in range(1, ways)], [{"dp": dp + 1 - 2 * core}]]
    stages.append([{"dp": 2 * lax.rem(dp // 2 + d, columns) + core} for d in range(1, columns)])
    slot = 0
    source = small_own
    for number, peers in enumerate(stages):
        copies = [
            send(
                source,
                small_land.at[slot + i],
                small_send.at[slot + i],
                small_recv.at[slot + i],
                device,
            )
            for i, device in enumerate(peers)
        ]
        for copy in copies:
            copy.start()
        if number == 0:
            for total in (*along[1:], sum_o):
                total.advance()
            for _ in range(steps - 1):
                for total in across:
                    total.advance()
            along[0].advance()
        elif number == 1:
            for total in along[1:]:
                total.advance()
        else:
            sum_o.advance()
        total = source[...]
        for i, copy in enumerate(copies):
            copy.wait()
            total += small_land[slot + i]
        slot += len(peers)
        if number == len(stages) - 1:
            small_out[...] = total
        else:
            small_sum[number] = total
            source = small_sum.at[number]

    loads[14].wait()
    for copy in routed_back:
        copy.wait()
    for s in range(seqs):
        rows = slice(s * shard, (s + 1) * shard)
        out = mxu(placer_v[:, rows], returned[...].reshape(-1, model), COLS_BY_COLS)
        block_ref[s] = (residual_v[rows, :] + out).astype(jnp.bfloat16)
    for total in [*across, *along, sum_o]:
        total.advance()
    for s in range(seqs):
        for d in range(1, ways):
            dmixed_copy(s, d).wait_send()
    for copy in scatter:
        copy.wait()
    for total in [sum_o] + sums_w:
        total.finish()


def finish(
    experts,
    tokens,
    query_ref,
    key_ref,
    value_ref,
    out_ref,
    up_own,
    up_land,
    down_own,
    down_land,
    block_in,
    tokens_in,
    small_ref,
    load_ref,
    query_out,
    key_out,
    value_out,
    out_out,
    up_out,
    down_out,
    block_out,
    tokens_out,
    gain1_out,
    shift1_out,
    gain2_out,
    shift2_out,
    load_out,
):
    for source, target in (
        (query_ref, query_out),
        (key_ref, key_out),
        (value_ref, value_out),
        (out_ref, out_out),
    ):
        target[...] = source[...].astype(jnp.float32)
    for own, land, target in ((up_own, up_land, up_out), (down_own, down_land, down_out)):
        total = own[...].astype(jnp.float32)
        for i in range(land.shape[0]):
            total += land[i].astype(jnp.float32)
        target[...] = total
    block_out[...] = block_in[...]
    tokens_out[...] = tokens_in[...]
    for i, target in enumerate((gain1_out, shift1_out, gain2_out, shift2_out)):
        target[...] = small_ref[i : i + 1, :]
    load_now = small_ref[4:5, 0:experts] * experts / tokens
    load_out[...] = 0.9 * load_ref[...] + 0.1 * load_now


def vmem(count):
    return [pl.BlockSpec(memory_space=pltpu.VMEM)] * count


def params(collective_id):
    return pltpu.CompilerParams(
        collective_id=collective_id, has_side_effects=True, vmem_limit_bytes=VMEM_BYTES
    )


def dma(*shape):
    return pltpu.SemaphoreType.DMA(shape)


def local(
    tokens_in,
    expert_ids,
    query_weight,
    key_weight,
    value_weight,
    out_weight,
    norm1_gain,
    norm1_shift,
    norm2_gain,
    norm2_shift,
    up_weight,
    down_weight,
    out_cotangent,
    load_mean,
):
    seq_count, shard_len, model_width = tokens_in.shape
    row_count = seq_count * shard_len
    head_dim = model_width // HEADS
    dp_ways = lax.axis_size("dp")
    sp_ways = lax.axis_size("sp")
    sp_at = lax.axis_index("sp")
    seq_len = shard_len * sp_ways
    experts = load_mean.shape[0]
    slot_count = 2 * row_count // experts
    local_experts = up_weight.shape[0]
    ff_width = up_weight.shape[1]
    width = model_width // sp_ways
    bf16 = jnp.bfloat16
    f32 = jnp.float32

    def shape(*sizes, dtype=bf16):
        return jax.ShapeDtypeStruct(sizes, dtype)

    cot_b = out_cotangent.reshape(row_count, model_width)
    hbm = [pl.BlockSpec(memory_space=pl.ANY)]
    routed = shape(experts, slot_count, model_width)
    square = pltpu.VMEM((model_width, model_width), bf16)
    by_head = pltpu.VMEM((seq_count, seq_len, width), bf16)
    token_shape = (seq_count, shard_len, model_width)
    whole_tokens = pltpu.VMEM((seq_count, seq_len, model_width), bf16)
    weight_columns = pltpu.VMEM((model_width, width), bf16)
    slots = (experts * slot_count, row_count)
    flat = (row_count, model_width)
    (
        normed_all,
        query_h,
        key_h,
        value_h,
        mixed_b,
        arrived,
        placer,
        residual_stream,
        log_total,
        outgoing,
        counts,
    ) = pl.pallas_call(
        functools.partial(forward, sp_ways, dp_ways, head_dim),
        out_shape=[
            shape(seq_count, seq_len, model_width),
            shape(seq_count, seq_len, width),
            shape(seq_count, seq_len, width),
            shape(seq_count, seq_len, width),
            shape(*token_shape),
            routed,
            shape(*slots),
            shape(*flat, dtype=f32),
            shape(seq_count, 8, seq_len, dtype=f32),
            routed,
            shape(8, LANES, dtype=f32),
        ],
        in_specs=hbm * 6 + vmem(5),
        out_specs=hbm * 8 + vmem(3),
        scratch_shapes=[
            whole_tokens,
            pltpu.VMEM(flat, bf16),
            pltpu.VMEM(routed.shape, bf16),
            weight_columns,
            weight_columns,
            weight_columns,
            square,
            pltpu.VMEM(slots, bf16),
            whole_tokens,
            by_head,
            by_head,
            by_head,
            pltpu.VMEM((seq_len, width), f32),
            by_head,
            pltpu.VMEM(token_shape, bf16),
            pltpu.VMEM((seq_len, LANES), f32),
            pltpu.VMEM(flat, f32),
            pltpu.VMEM(flat, bf16),
            dma(seq_count, sp_ways),
            dma(seq_count, sp_ways),
            dma(seq_count, 2, sp_ways),
            dma(seq_count, 2, sp_ways),
            dma(dp_ways),
            dma(dp_ways),
            dma(5),
            dma(seq_count),
            dma(seq_count + 1, 4),
            pltpu.SemaphoreType.DMA,
        ],
        compiler_params=params(0),
    )(
        tokens_in,
        cot_b,
        query_weight,
        key_weight,
        value_weight,
        out_weight,
        expert_ids.reshape(1, row_count),
        *(
            vector.reshape(1, model_width)
            for vector in (norm1_gain, norm1_shift, norm2_gain, norm2_shift)
        ),
    )
    ff_own = ff_width // 2
    received_blocks = max(2 * experts, ff_own // slot_count)
    shard_size = ff_width // sp_ways
    rest = sp_ways // 2 - 1
    blocks = shard_size // slot_count
    dnormed_back, expert_out, up_own, up_rest, down_own, down_rest = pl.pallas_call(
        functools.partial(run_experts, dp_ways, sp_ways),
        out_shape=[
            routed,
            routed,
            shape(shard_size, model_width),
            shape(rest * shard_size, model_width),
            shape(blocks, slot_count, model_width),
            shape(rest * blocks, slot_count, model_width),
        ],
        in_specs=hbm * 4,
        out_specs=hbm + vmem(1) + hbm * 4,
        scratch_shapes=[
            pltpu.VMEM((received_blocks, slot_count, model_width), bf16),
            pltpu.VMEM((2,) + routed.shape, bf16),
            pltpu.VMEM((ff_own, model_width), bf16),
            pltpu.VMEM((ff_own, model_width), bf16),
            pltpu.VMEM((2 * experts * slot_count, ff_own), bf16),
            pltpu.VMEM((2 * experts * slot_count, ff_own), bf16),
            pltpu.VMEM((2 * slot_count, model_width), f32),
            pltpu.VMEM(routed.shape, f32),
            pltpu.VMEM(routed.shape, bf16),
            pltpu.VMEM(routed.shape, bf16),
            pltpu.VMEM(routed.shape, bf16),
            pltpu.VMEM(routed.shape, bf16),
            pltpu.VMEM(routed.shape, bf16),
            dma(2, sp_ways // 2),
            dma(4),
            dma(3),
            dma(dp_ways),
            dma(dp_ways),
            dma(dp_ways),
            dma(dp_ways),
            dma(dp_ways // 2 + 2),
            dma(dp_ways // 2 + 2),
            dma(dp_ways // 2),
            dma(dp_ways // 2),
            dma(dp_ways // 2),
            dma(dp_ways // 2),
        ],
        compiler_params=params(3),
    )(outgoing, arrived, up_weight[0], down_weight[0])
    columns = dp_ways // 2
    rows = model_width // dp_ways

    def reduction(part_width):
        return [
            pltpu.VMEM((columns * rows, part_width), bf16),
            pltpu.VMEM((columns * rows, part_width), bf16),
            pltpu.VMEM(((columns - 1) * rows, part_width), bf16),
            pltpu.VMEM((rows, width), bf16),
            pltpu.SemaphoreType.DMA,
            pltpu.SemaphoreType.DMA,
            dma(columns),
            dma(columns),
            dma(columns),
            dma(columns),
            dma(sp_ways),
            dma(sp_ways),
            dma(sp_ways),
            dma(sp_ways),
            pltpu.SemaphoreType.DMA,
        ]

    small_slots = 1 + (columns - 1) + (sp_ways - 1)
    whole = shape(model_width, model_width)
    tokens = pltpu.VMEM(token_shape, bf16)
    *weight_grads, up_land, down_land, block_out, tokens_grad, small_sum = pl.pallas_call(
        functools.partial(backward, sp_ways, dp_ways, head_dim),
        out_shape=[whole] * 4
        + [
            shape(rest, shard_size, model_width),
            shape(rest, blocks, slot_count, model_width),
            shape(*token_shape),
            shape(*token_shape),
            shape(8, model_width, dtype=f32),
        ],
        in_specs=hbm * 17 + vmem(4),
        out_specs=hbm * 6 + vmem(3),
        scratch_shapes=[
            pltpu.VMEM(routed.shape, bf16),
            pltpu.VMEM(placer.shape, bf16),
            pltpu.VMEM(flat, bf16),
            pltpu.VMEM(flat, f32),
            square,
            tokens,
            by_head,
            by_head,
            by_head,
            whole_tokens,
            square,
            square,
            square,
            tokens,
            pltpu.VMEM(routed.shape, bf16),
            pltpu.VMEM(token_shape, f32),
            pltpu.VMEM(flat, bf16),
            tokens,
            by_head,
            pltpu.VMEM((seq_len, width), f32),
            pltpu.VMEM((seq_len, width), f32),
            pltpu.VMEM((seq_len, width), f32),
            pltpu.VMEM((seq_count, seq_len, 3 * width), bf16),
            pltpu.VMEM((seq_count, shard_len, 3 * model_width), bf16),
            square,
            pltpu.VMEM((3, model_width, width), bf16),
            pltpu.VMEM((sp_ways, rows, model_width), bf16),
            pltpu.VMEM((8, model_width), f32),
            pltpu.VMEM((small_slots, 8, model_width), f32),
            pltpu.VMEM((2, 8, model_width), f32),
            dma(seq_count, sp_ways),
            dma(seq_count, sp_ways),
            dma(seq_count, sp_ways),
            dma(seq_count, sp_ways),
            dma(dp_ways),
            dma(dp_ways),
            dma(2, 2, sp_ways // 2),
            dma(2, 2, sp_ways // 2),
            dma(sp_ways),
            dma(sp_ways),
            dma(small_slots),
            dma(small_slots),
            dma(15),
        ]
        + reduction(model_width)
        + reduction(width) * 3,
        compiler_params=params(1),
    )(
        dnormed_back,
        placer,
        cot_b,
        residual_stream,
        out_weight,
        mixed_b,
        query_h,
        key_h,
        value_h,
        normed_all,
        query_weight,
        key_weight,
        value_weight,
        tokens_in,
        expert_out,
        up_rest,
        down_rest,
        log_total,
        norm1_gain.reshape(1, model_width),
        norm2_gain.reshape(1, model_width),
        counts,
    )
    shard_shape = (shard_size, model_width)
    parts = 8
    big = pl.BlockSpec((model_width // parts, model_width), lambda i: (i, 0))
    own = pl.BlockSpec((shard_size // parts, model_width), lambda i: (i, 0))
    land = pl.BlockSpec((rest, shard_size // parts, model_width), lambda i: (0, i, 0))
    token = pl.BlockSpec((row_count // parts, model_width), lambda i: (i, 0))
    row = pl.BlockSpec((1, model_width), lambda i: (0, 0))
    load = pl.BlockSpec((1, experts), lambda i: (0, 0))
    results = pl.pallas_call(
        functools.partial(finish, experts, row_count * dp_ways * sp_ways),
        grid=(parts,),
        out_shape=[shape(model_width, model_width, dtype=f32)] * 4
        + [shape(*shard_shape, dtype=f32)] * 2
        + [shape(*flat)] * 2
        + [shape(1, model_width, dtype=f32)] * 4
        + [shape(1, experts, dtype=f32)],
        in_specs=[big] * 4
        + [own, land, own, land, token, token]
        + [pl.BlockSpec((8, model_width), lambda i: (0, 0)), load],
        out_specs=[big] * 4 + [own, own, token, token] + [row] * 4 + [load],
        compiler_params=pltpu.CompilerParams(vmem_limit_bytes=VMEM_BYTES),
    )(
        *weight_grads,
        up_own,
        up_land,
        down_own.reshape(shard_shape),
        down_land.reshape((rest,) + shard_shape),
        block_out.reshape(flat),
        tokens_grad.reshape(flat),
        small_sum,
        load_mean.reshape(1, experts),
    )
    return (
        results[6].reshape(token_shape),
        results[7].reshape(token_shape),
        *results[:4],
        *(vector.reshape(model_width) for vector in results[8:12]),
        results[4][None],
        results[5][None],
        results[12].reshape(experts),
    )


def solution(mesh):
    return jax.shard_map(
        local,
        mesh=mesh,
        in_specs=(
            P("dp", "sp", None),
            P("dp", "sp", None, None),
            P(),
            P(),
            P(),
            P(),
            P(),
            P(),
            P(),
            P(),
            P("dp", None, None),
            P("dp", None, None),
            P("dp", "sp", None),
            P(),
        ),
        out_specs=(
            P("dp", "sp", None),
            P("dp", "sp", None),
            P(),
            P(),
            P(),
            P(),
            P(),
            P(),
            P(),
            P(),
            P("dp", "sp", None),
            P("dp", "sp", None),
            P(),
        ),
        check_vma=False,
    )
```

```python
import functools

import jax
import jax.numpy as jnp
from jax import lax
from jax.experimental import pallas as pl
from jax.experimental.pallas import tpu as pltpu
from jax.sharding import PartitionSpec as P

HEADS = 16
MESH = pl.DeviceIdType.MESH
BLOCK = 256
LANES = 128
STEP = 1024
VMEM_BYTES = 60 * 2**20

NORM_EPSILON = 1e-05
GELU_ROOT = 0.7978845608028654
CUBIC_TERM = 0.044715

ROWS_BY_COLS = (((1,), (0,)), ((), ()))
ROWS_BY_ROWS = (((1,), (1,)), ((), ()))
COLS_BY_COLS = (((0,), (0,)), ((), ()))


def smooth(values):
    return (
        0.5
        * values
        * (1.0 + jnp.tanh(GELU_ROOT * (values + CUBIC_TERM * values * values * values)))
    )


def smooth_slope(values):
    inner = jnp.tanh(GELU_ROOT * (values + CUBIC_TERM * values * values * values))
    return 0.5 * (1.0 + inner) + 0.5 * values * (1.0 - inner * inner) * GELU_ROOT * (
        1.0 + 3.0 * CUBIC_TERM * values * values
    )


def norm_forward(values, gain, shift):
    center = jnp.mean(values, axis=-1, keepdims=True)
    offset = values - center
    rstd = lax.rsqrt(jnp.mean(offset * offset, axis=-1, keepdims=True) + NORM_EPSILON)
    unit = offset * rstd
    return (unit * gain + shift, unit, rstd)


def norm_backward(grad, unit, rstd, gain):
    scaled = grad * gain
    inner = (
        scaled
        - jnp.mean(scaled, axis=-1, keepdims=True)
        - unit * jnp.mean(scaled * unit, axis=-1, keepdims=True)
    )
    return (inner * rstd, jnp.sum(grad * unit, axis=0), jnp.sum(grad, axis=0))


def mxu(left, right, dims=ROWS_BY_COLS):
    return lax.dot_general(left, right, dims, preferred_element_type=jnp.float32)


def span(index, size):
    return pl.ds(pl.multiple_of(index * size, size), size)


def greet(peers):
    barrier = pltpu.get_barrier_semaphore()
    for peer in peers:
        pl.semaphore_signal(barrier, inc=1, device_id=peer, device_id_type=MESH)
    pl.semaphore_wait(barrier, len(peers))


def send(source, target, send_sem, recv_sem, peer):
    return pltpu.make_async_remote_copy(
        src_ref=source,
        dst_ref=target,
        send_sem=send_sem,
        recv_sem=recv_sem,
        device_id=peer,
        device_id_type=MESH,
    )


def exchange(others, source, target, send_sem, recv_sem):
    me = lax.axis_index("dp")
    return [
        send(
            source.at[flip(me, d)],
            target.at[me],
            send_sem.at[d],
            recv_sem.at[d],
            {"dp": flip(me, d)},
        )
        for d in range(1, others)
    ]


def flip(index, bits):
    bit = 1
    while bit <= bits:
        if bits & bit:
            index = index + bit - 2 * bit * lax.rem(index // bit, 2)
        bit *= 2
    return index


def forward(
    ways,
    others,
    head_dim,
    x_ref,
    cot_ref,
    wq_ref,
    wk_ref,
    wv_ref,
    wo_ref,
    ids_ref,
    gain1_ref,
    shift1_ref,
    gain2_ref,
    shift2_ref,
    normed_ref,
    q_ref,
    k_ref,
    v_ref,
    mixed_ref,
    arrived_ref,
    placer_ref,
    residual_ref,
    outgoing_ref,
    log_ref,
    counts_ref,
    x_all,
    cot_v,
    cot_out,
    wq_v,
    wk_v,
    wv_v,
    wo_v,
    placer_v,
    normed_v,
    q_v,
    k_v,
    v_v,
    mixed_f,
    mixed_h,
    mixed_tok,
    log_s,
    residual_v,
    normed2,
    outgoing_v,
    x_send,
    x_recv,
    m_send,
    m_recv,
    c_send,
    c_recv,
    load_sem,
    x_sem,
    store_sem,
    own_sem,
):
    seqs, seq_len, model = x_all.shape
    shard = seq_len // ways
    width = q_v.shape[2]
    heads = width // head_dim
    slots = cot_out.shape[1]
    me = lax.axis_index("sp")
    dp = lax.axis_index("dp")
    peer = [flip(me, d) for d in range(ways)]
    near = (1, 2) if ways == 4 else tuple(range(1, ways))
    far = tuple(range(1 + len(near), ways))
    barrier = pltpu.get_barrier_semaphore()
    neighbours = [{"sp": peer[d]} for d in range(1, ways)]
    neighbours += [{"dp": flip(dp, d)} for d in range(1, others)]
    for device in neighbours:
        pl.semaphore_signal(barrier, inc=1, device_id=device, device_id_type=MESH)
    own_columns = span(me, width)
    loads = [
        pltpu.make_async_copy(source, target, load_sem.at[i])
        for i, (source, target) in enumerate(
            (
                (cot_ref, cot_v),
                (wq_ref.at[:, own_columns], wq_v),
                (wk_ref.at[:, own_columns], wk_v),
                (wv_ref.at[:, own_columns], wv_v),
                (wo_ref, wo_v),
            )
        )
    ]
    own_x = [
        pltpu.make_async_copy(x_ref.at[s], x_all.at[s, span(me, shard)], x_sem.at[s])
        for s in range(seqs)
    ]
    for copy in own_x + loads:
        copy.start()

    def x_copy(s, d):
        return send(
            x_ref.at[s],
            x_all.at[s, span(me, shard)],
            x_send.at[s, d],
            x_recv.at[s, d],
            {"sp": peer[d]},
        )

    def x_relays(s):
        if not far:
            return []
        size = shard // 2
        pieces = [
            x_all.at[s, pl.ds(pl.multiple_of(peer[1] * shard, size), size)],
            x_all.at[s, pl.ds(pl.multiple_of(peer[2] * shard + size, size), size)],
        ]
        return [
            send(piece, piece, x_send.at[s, at], x_recv.at[s, at], {"sp": peer[to]})
            for piece, at, to in zip(pieces, (0, 3), (2, 1))
        ]

    cuts = max(1, width // BLOCK)
    cuts = 2 * cuts if width // (2 * cuts) % LANES == 0 else cuts
    cut = width // cuts

    def mixed_copy(s, d, c):
        return send(
            mixed_h.at[s, span(peer[d], shard), c * cut : (c + 1) * cut],
            mixed_tok.at[s, :, span(me * cuts + c, cut)],
            m_send.at[s, c, d],
            m_recv.at[s, c, d],
            {"sp": peer[d]},
        )

    pl.semaphore_wait(barrier, len(neighbours))
    for d in near:
        x_copy(0, d).start()

    tokens = seqs * shard
    ids = ids_ref[...]
    named = lax.broadcasted_iota(jnp.int32, (LANES, tokens), 0) == ids
    named = jnp.where(named, 1.0, 0.0)
    upper = lax.broadcasted_iota(jnp.int32, (tokens, tokens), 0) <= lax.broadcasted_iota(
        jnp.int32, (tokens, tokens), 1
    )
    running = mxu(named.astype(jnp.bfloat16), jnp.where(upper, 1.0, 0.0).astype(jnp.bfloat16))
    slot = jnp.sum(named * (running - 1.0), axis=0, keepdims=True).astype(jnp.int32)
    places = lax.broadcasted_iota(jnp.int32, placer_v.shape, 0) == ids * slots + slot
    placer_v[...] = jnp.where(places, 1.0, 0.0).astype(jnp.bfloat16)
    ones = jnp.ones((8, tokens), jnp.float32)
    counts_ref[...] = mxu(ones, named, ROWS_BY_ROWS)
    loads[0].wait()
    cot_out[...] = (
        mxu(placer_v[...], cot_v[...]).astype(jnp.bfloat16).reshape(cot_out.shape)
    )
    background = exchange(others, cot_out, arrived_ref, c_send, c_recv)
    own_cot = pltpu.make_async_copy(cot_out.at[dp], arrived_ref.at[dp], own_sem)
    for copy in background + [own_cot]:
        copy.start()

    lane = lax.broadcasted_iota(jnp.int32, (1, width), 1) // head_dim
    log_lane = lax.broadcasted_iota(jnp.int32, (1, LANES), 1)
    visible = lax.broadcasted_iota(jnp.int32, (BLOCK, BLOCK), 1) <= lax.broadcasted_iota(
        jnp.int32, (BLOCK, BLOCK), 0
    )
    scale = head_dim ** (-0.5)
    outs = ((normed_v, normed_ref), (q_v, q_ref), (k_v, k_ref), (v_v, v_ref))
    stores = [
        [
            pltpu.make_async_copy(source.at[s], target.at[s], store_sem.at[s, i])
            for i, (source, target) in enumerate(outs)
        ]
        for s in range(seqs)
    ]

    def project(s, d):
        rows = span(peer[d], shard)
        values = x_all[s, rows, :].astype(jnp.float32)
        normed, _, _ = norm_forward(values, gain1_ref[...], shift1_ref[...])
        normed = normed.astype(jnp.bfloat16)
        normed_v[s, rows, :] = normed
        q_v[s, rows, :] = mxu(normed, wq_v[...]).astype(jnp.bfloat16)
        k_v[s, rows, :] = mxu(normed, wk_v[...]).astype(jnp.bfloat16)
        v_v[s, rows, :] = mxu(normed, wv_v[...]).astype(jnp.bfloat16)

    for s in range(seqs):
        own_x[s].wait()
        if s == 0:
            for copy in loads[1:4]:
                copy.wait()
        project(s, 0)
        for d in near:
            x_copy(s, d).wait_recv()
        for copy in x_relays(s):
            copy.start()
        if s + 1 < seqs:
            for d in near:
                x_copy(s + 1, d).start()
        for d in near:
            project(s, d)
        for copy in x_relays(s):
            copy.wait_recv()
        if s:
            for c in range(cuts):
                for d in range(1, ways):
                    mixed_copy(s - 1, d, c).start()
        for d in far:
            project(s, d)
        for copy in stores[s]:
            copy.start()
        mixed_f[...] = jnp.zeros_like(mixed_f)
        log_s[...] = jnp.zeros_like(log_s)

        def one_head(h, carry):
            mine = (lane == h).astype(jnp.float32)
            for at in range(0, seq_len, BLOCK):
                rows = slice(at, at + BLOCK)
                query = (q_v[s, rows, :].astype(jnp.float32) * (mine * scale)).astype(
                    jnp.bfloat16
                )
                near = mxu(query, k_v[s, rows, :], ROWS_BY_ROWS)
                near = jnp.where(visible, near, -1e30)
                top = jnp.max(near, axis=1, keepdims=True)
                if at:
                    far = mxu(query, k_v[s, :at, :], ROWS_BY_ROWS)
                    top = jnp.maximum(top, jnp.max(far, axis=1, keepdims=True))
                near = jnp.exp(near - top)
                total = jnp.sum(near, axis=1, keepdims=True)
                if at:
                    far = jnp.exp(far - top)
                    total += jnp.sum(far, axis=1, keepdims=True)
                inverse = 1.0 / total
                out = mxu((near * inverse).astype(jnp.bfloat16), v_v[s, rows, :])
                if at:
                    out += mxu((far * inverse).astype(jnp.bfloat16), v_v[s, :at, :])
                mixed_f[rows, :] += out * mine
                log_s[rows, :] = jnp.where(log_lane == h, top + jnp.log(total), log_s[rows, :])
            return carry

        for c in range(cuts):
            lax.fori_loop(c * heads // cuts, (c + 1) * heads // cuts, one_head, 0)
            columns = slice(c * cut, (c + 1) * cut)
            mixed_h[s, :, columns] = mixed_f[:, columns].astype(jnp.bfloat16)
            if s == seqs - 1:
                for d in range(1, ways):
                    mixed_copy(s, d, c).start()
        log_ref[s] = jnp.transpose(log_s[...])[: log_ref.shape[1], :]
        mixed_tok[s, :, own_columns] = mixed_h[s, span(me, shard), :]

    loads[4].wait()
    for s in range(seqs):
        for c in range(cuts):
            for d in range(1, ways):
                mixed_copy(s, d, c).wait_recv()
        rows = slice(s * shard, (s + 1) * shard)
        values = x_all[s, span(me, shard), :].astype(jnp.float32)
        values += mxu(mixed_tok[s], wo_v[...])
        residual_v[rows, :] = values
        normed, _, _ = norm_forward(values, gain2_ref[...], shift2_ref[...])
        normed2[rows, :] = normed.astype(jnp.bfloat16)
    last = [
        pltpu.make_async_copy(source, target, store_sem.at[seqs, i])
        for i, (source, target) in enumerate(
            ((mixed_tok, mixed_ref), (residual_v, residual_ref), (placer_v, placer_ref))
        )
    ]
    for copy in last:
        copy.start()
    for i in range(2):
        part = slots * others // 2
        rows = slice(i * part, (i + 1) * part)
        blocks = pl.ds(i * others // 2, others // 2)
        outgoing_v[blocks] = (
            mxu(placer_v[rows, :], normed2[...])
            .astype(jnp.bfloat16)
            .reshape(others // 2, slots, model)
        )
        copy = pltpu.make_async_copy(
            outgoing_v.at[blocks], outgoing_ref.at[blocks], store_sem.at[seqs + 1, i]
        )
        copy.start()
        last.append(copy)
    for s in range(seqs):
        for d in near:
            x_copy(s, d).wait_send()
        for copy in x_relays(s):
            copy.wait_send()
        for c in range(cuts):
            for d in range(1, ways):
                mixed_copy(s, d, c).wait_send()
        for copy in stores[s]:
            copy.wait()
    for copy in background + [own_cot] + last:
        copy.wait()


def pair_of(sp):
    core = lax.rem(lax.axis_index("dp"), 2)
    along_x, along_y = flip(sp, 1), flip(sp, 2)
    return along_x + core * (along_y - along_x)


def shards_of(sp, ways):
    shards = [sp, flip(pair_of(sp), 3)]
    bit = 4
    while bit < ways:
        shards += [flip(shard, bit) for shard in shards]
        bit *= 2
    return shards


def run_experts(
    others,
    ways,
    outgoing_ref,
    cot_ref,
    up_ref,
    down_ref,
    back_ref,
    result_ref,
    up_own,
    up_rest,
    down_own,
    down_rest,
    received,
    arrived,
    up_v,
    down_v,
    hidden,
    slope_v,
    total,
    dn_own,
    dn_pair,
    dn_land,
    dnormed,
    out_pair,
    out_land,
    w_sem,
    o_sem,
    c_sem,
    a_send,
    a_recv,
    b_send,
    b_recv,
    f_send,
    f_recv,
    p_send,
    p_recv,
    e_send,
    e_recv,
):
    slots, width = received.shape[1:]
    rows = others * slots
    ff = up_v.shape[0]
    groups = others // 2
    me = lax.axis_index("dp")
    sp = lax.axis_index("sp")
    chip = me // 2
    pair = {"sp": pair_of(sp)}
    shards = shards_of(sp, ways)
    size = ff // len(shards)
    loads = [
        pltpu.make_async_copy(
            source.at[span(shard, size)], target.at[i * size : (i + 1) * size], w_sem.at[j, i]
        )
        for j, (source, target) in enumerate(((down_ref, down_v), (up_ref, up_v)))
        for i, shard in enumerate(shards)
    ]
    own_cot = pltpu.make_async_copy(cot_ref, arrived.at[0], c_sem.at[0])
    own_rows = pltpu.make_async_copy(outgoing_ref.at[me], received.at[me], c_sem.at[1])
    own_back = pltpu.make_async_copy(dnormed.at[me], back_ref.at[me], c_sem.at[2])
    own_rows.start()
    own_cot.start()
    for copy in loads:
        copy.start()
    greet([{"dp": flip(me, d)} for d in range(1, others)] + [pair])
    inward = exchange(others, outgoing_ref, received.at[0:others], a_send, a_recv)
    outward = exchange(others, dnormed, back_ref, b_send, b_recv)
    near = [flip(chip, group) for group in range(groups)]
    chips = [pl.ds(2 * near[group], 2) for group in range(groups)]
    forward = [
        send(
            received.at[chips[group]],
            received.at[pl.ds(others + 2 * near[group], 2)],
            f_send.at[group],
            f_recv.at[group],
            pair,
        )
        for group in range(groups)
    ]
    cot_copy = [
        send(
            cot_ref.at[i * groups : (i + 1) * groups],
            arrived.at[1, i * groups : (i + 1) * groups],
            f_send.at[groups + i],
            f_recv.at[groups + i],
            pair,
        )
        for i in range(2)
    ]
    dn_copy = [
        send(
            dn_pair.at[chips[group]],
            dn_land.at[chips[group]],
            p_send.at[group],
            p_recv.at[group],
            pair,
        )
        for group in range(groups)
    ]
    out_copy = [
        send(
            out_pair.at[chips[group]],
            out_land.at[chips[group]],
            e_send.at[group],
            e_recv.at[group],
            pair,
        )
        for group in range(groups)
    ]

    early = range(groups // 2)
    middle = range(groups // 2, 3 * groups // 4)
    late = range(3 * groups // 4, groups)
    for copy in [inward[0]] + inward[2 * middle[0] - 1 : 2 * late[0] - 1]:
        copy.start()
    for copy in inward[1 : 2 * middle[0] - 1]:
        copy.start()
    for copy in cot_copy:
        copy.start()
    own_rows.wait()

    def slab_of(half, group):
        return pl.ds(pl.multiple_of(half * rows + near[group] * (2 * slots), 2 * slots), 2 * slots)

    def cot_part(half, begin, end):
        def cot_step(i, carry):
            at = span(i, STEP)
            cot = arrived[half, begin:end].reshape((end - begin) * slots, width)
            slope_v[half * rows + begin * slots : half * rows + end * slots, at] = mxu(
                cot, down_v[at, :], ROWS_BY_ROWS
            ).astype(jnp.bfloat16)
            return carry

        lax.fori_loop(0, ff // STEP, cot_step, 0)

    def up_half(half, group):
        slab = slab_of(half, group)
        total[...] = jnp.zeros_like(total)

        def up_step(i, carry):
            at = span(i, STEP)
            tokens = received[pl.ds(half * others + 2 * near[group], 2)].reshape(2 * slots, width)
            pre = mxu(tokens, up_v[at, :], ROWS_BY_ROWS)
            square = pre * pre
            inner = jnp.tanh(GELU_ROOT * pre * (1.0 + CUBIC_TERM * square))
            gate = 0.5 * (1.0 + inner)
            hidden[slab, at] = (pre * gate).astype(jnp.bfloat16)
            slope = gate + (0.5 * GELU_ROOT) * pre * (1.0 - inner * inner) * (
                1.0 + (3.0 * CUBIC_TERM) * square
            )
            dpre = (slope_v[slab, at].astype(jnp.float32) * slope).astype(jnp.bfloat16)
            slope_v[slab, at] = dpre
            total[...] += mxu(dpre, up_v[at, :])
            return carry

        lax.fori_loop(0, ff // STEP, up_step, 0)
        shaped = total[...].reshape(2, slots, width)
        if half:
            dn_pair[chips[group]] = shaped.astype(jnp.bfloat16)
        else:
            dn_own[chips[group]] = shaped

    def out_half(half, group):
        at = chips[group]
        out = mxu(hidden[slab_of(half, group), :], down_v[...]).reshape(2, slots, width)
        if half:
            out_pair[at] = out.astype(jnp.bfloat16)
        else:
            out_copy[group].wait_recv()
            result_ref[at] = (out + out_land[at].astype(jnp.float32)).astype(jnp.bfloat16)

    def pass_on(group):
        for d in (2 * group, 2 * group + 1):
            if d:
                inward[d - 1].wait_recv()
        forward[group].start()

    def finish(group):
        dn_copy[group].wait_recv()
        at = chips[group]
        dnormed[at] = (dn_own[at] + dn_land[at].astype(jnp.float32)).astype(jnp.bfloat16)
        for d in (2 * group, 2 * group + 1):
            if d:
                outward[d - 1].start()
            else:
                own_back.start()

    def up_pair(group):
        forward[group].wait_recv()
        up_half(1, group)
        if group not in early:
            dn_copy[group].start()

    def grad(target, left, right_ref, begin, end, block=0):
        def grad_step(i, carry):
            at = span(i, STEP)
            right = right_ref[...].reshape(2 * rows, width)
            out = mxu(left[:, at], right, COLS_BY_COLS).astype(jnp.bfloat16)
            if block:
                target[span(i, STEP // block)] = out.reshape(STEP // block, block, width)
            else:
                target[at, :] = out
            return carry

        lax.fori_loop(begin, end, grad_step, 0)

    pass_on(0)
    own_cot.wait()
    for copy in loads[: len(shards)]:
        copy.wait()
    cot_part(0, 0, others)
    for copy in loads[len(shards) :]:
        copy.wait()
    up_half(0, 0)
    cot_copy[0].wait_recv()
    cot_part(1, 0, groups)
    for group in middle:
        pass_on(group)
        up_half(0, group)
    for copy in inward[2 * middle[0] - 1 : 2 * late[0] - 1]:
        copy.wait_send()
    for copy in inward[2 * late[0] - 1 :]:
        copy.start()
    for group in early[1:]:
        pass_on(group)
    cot_copy[1].wait_recv()
    cot_part(1, groups, others)
    for group in early[1:]:
        up_half(0, group)
    for group in middle:
        up_pair(group)
    for group in early:
        up_pair(group)
    for group in late:
        pass_on(group)
    dn_copy[0].start()
    for group in middle:
        finish(group)
    for group in late:
        up_half(0, group)
    for group in middle:
        out_half(1, group)
    for group in late:
        up_pair(group)
    for group in early[1:]:
        dn_copy[group].start()
    for group in middle:
        out_copy[group].start()
    for group in [*early, *late]:
        out_half(1, group)
    tokens_all = received.at[0 : 2 * others]
    grad(up_v, slope_v, tokens_all, 0, 1)
    for group in late:
        finish(group)
    for group in [*early, *late]:
        out_copy[group].start()
    grad(up_v, slope_v, tokens_all, 1, ff // STEP)
    for group in early:
        finish(group)
    for copy in forward:
        copy.wait_send()
    grad(received, hidden, arrived, 0, ff // STEP, slots)
    first, every = size // slots, ff // slots
    stores = [
        pltpu.make_async_copy(source, target, o_sem.at[i])
        for i, (source, target) in enumerate(
            (
                (up_v.at[0:size], up_own),
                (up_v.at[size:ff], up_rest),
                (received.at[0:first], down_own),
                (received.at[first:every], down_rest),
            )
        )
    ]
    for copy in stores:
        copy.start()
    for group in range(groups):
        out_half(0, group)
    for copy in inward[: 2 * middle[0] - 1] + inward[2 * late[0] - 1 :]:
        copy.wait_send()
    for copy in cot_copy + dn_copy + out_copy:
        copy.wait_send()
    for copy in outward + stores + [own_back]:
        copy.wait()


class Reduction:
    def __init__(self, ways, columns, part, out, across_first, scratch):
        (
            self.core_land,
            self.core_sum,
            self.column_land,
            self.piece,
            core_send,
            core_recv,
            column_send,
            column_recv,
            spread_send,
            spread_recv,
            ring_send,
            ring_recv,
            cross_send,
            cross_recv,
            own_sem,
        ) = scratch
        me = lax.axis_index("sp")
        dp = lax.axis_index("dp")
        core = lax.rem(dp, 2)
        column = dp // 2
        twin = {"dp": dp + 1 - 2 * core}
        self.ways, self.columns, self.part = ways, columns, part
        self.core = core
        rows, width = self.piece.shape
        self.rows = rows

        bits = [1 << i for i in range(columns.bit_length() - 1)]
        place = 0
        for bit in bits:
            place = 2 * place + lax.rem(column // bit, 2)
        self.place = place

        def beside(bit):
            return {"dp": 2 * flip(column, bit) + core}

        def block(first, at_sp, count):
            first = pl.multiple_of((core * columns + first) * rows, rows)
            return out.at[pl.ds(first, count * rows), span(at_sp, width)]

        self.core_copy = send(
            part.at[span(1 - core, columns * rows)], self.core_land, core_send, core_recv, twin
        )
        self.column_copy, self.kept, self.lands = [], [], []
        first, count, used = 0, columns, 0
        for i, bit in enumerate(bits):
            count //= 2
            mine = lax.rem(column // bit, 2)
            size = count * rows
            gone = pl.ds(pl.multiple_of((first + (1 - mine) * count) * rows, size), size)
            first = first + mine * count
            self.kept.append(pl.ds(pl.multiple_of(first * rows, size), size))
            land = self.column_land.at[used : used + size]
            used += size
            self.lands.append(land)
            self.column_copy.append(
                send(self.core_sum.at[gone], land, column_send.at[i], column_recv.at[i], beside(bit))
            )
        spot = block(place, me, 1)
        self.own = pltpu.make_async_copy(self.piece, spot, own_sem)
        origin = [flip(me, d) for d in range(ways)]
        across_count = 1 if across_first else columns
        across_at = place if across_first else 0
        near = (1, 2) if ways == 4 else tuple(range(1, ways))
        held = [block(across_at, at, across_count) for at in origin]
        self.ring_copy = [
            send(held[0], held[0], ring_send.at[d], ring_recv.at[d], {"sp": origin[d]})
            for d in near
        ]
        self.relays = []
        if ways == 4:
            count = across_count * rows // 2
            first = (core * columns + across_at) * rows
            for i, (d, to) in enumerate(((1, 2), (2, 1))):
                at = pl.multiple_of(first + i * count, count)
                half = out.at[pl.ds(at, count), span(origin[d], width)]
                index = (0, 3)[i]
                self.relays.append(
                    send(
                        half, half, ring_send.at[index], ring_recv.at[index], {"sp": origin[to]}
                    )
                )

        def rows_of(first, count):
            first = pl.multiple_of((core * columns + first) * rows, rows)
            return out.at[pl.ds(first, count * rows)]

        self.spread_copy, gathered = [], [rows_of(place, 1)]
        for i, bit in enumerate(reversed(bits)):
            count = 1 << i
            at = place - lax.rem(place, count)
            spot = rows_of(at, count) if across_first else block(at, me, count)
            gathered.append(rows_of(flip(at, count), count))
            self.spread_copy.append(
                send(spot, spot, spread_send.at[i], spread_recv.at[i], beside(bit))
            )
        crossing = gathered if across_first else held
        self.cross_copy = [
            send(part, part, cross_send.at[i], cross_recv.at[i], twin)
            for i, part in enumerate(crossing)
        ]
        self.phases = iter(self.across_then_along() if across_first else self.along_then_across())

    def along_then_across(self):
        self.own.start()
        self.own.wait()
        for copy in self.spread_copy:
            copy.start()
            yield
            copy.wait()
        for copy in self.ring_copy:
            copy.start()
        self.cross_copy[0].start()
        yield
        for ring, cross in zip(self.ring_copy, self.cross_copy[1:]):
            ring.wait_recv()
            cross.start()
        for copy in self.relays:
            copy.start()
        yield
        for copy in self.relays:
            copy.wait_recv()
        if self.relays:
            self.cross_copy[3].start()
        yield

    def across_then_along(self):
        self.own.start()
        self.own.wait()
        for copy in self.ring_copy:
            copy.start()
        yield
        for copy in self.ring_copy:
            copy.wait_recv()
        for copy in self.relays:
            copy.start()
        yield
        for copy in self.relays:
            copy.wait_recv()
        for spread, cross in zip(self.spread_copy, self.cross_copy):
            spread.start()
            cross.start()
            yield
            spread.wait()
        self.cross_copy[-1].start()
        yield

    def advance(self):
        next(self.phases)

    def add_core(self):
        self.core_copy.wait()
        self.core_sum[...] = (
            self.part[span(self.core, self.columns * self.rows), :].astype(jnp.float32)
            + self.core_land[...].astype(jnp.float32)
        ).astype(jnp.bfloat16)
        self.column_copy[0].start()

    def add_column(self, step):
        self.column_copy[step].wait()
        total = self.core_sum[self.kept[step], :].astype(jnp.float32)
        total += self.lands[step][...].astype(jnp.float32)
        if step + 1 < len(self.column_copy):
            self.core_sum[self.kept[step], :] = total.astype(jnp.bfloat16)
            self.column_copy[step + 1].start()
        return total

    def finish(self):
        for copy in self.ring_copy + self.relays:
            copy.wait_send()
        for copy in self.cross_copy:
            copy.wait()


def backward(
    ways,
    others,
    head_dim,
    back_ref,
    placer_ref,
    cot_ref,
    residual_ref,
    wo_ref,
    mixed_ref,
    q_ref,
    k_ref,
    v_ref,
    normed_ref,
    wq_ref,
    wk_ref,
    wv_ref,
    x_ref,
    result_ref,
    up_rest,
    down_rest,
    log_ref,
    gain1_ref,
    gain2_ref,
    counts_ref,
    out_q,
    out_k,
    out_v,
    out_o,
    up_land,
    down_land,
    block_ref,
    tokens_ref,
    small_out,
    block_v,
    tokens_v,
    back_v,
    placer_v,
    cot_v,
    residual_v,
    wo_v,
    mixed_v,
    q_v,
    k_v,
    v_v,
    normed_v,
    wq_v,
    wk_v,
    wv_v,
    x_v,
    returned,
    dresid,
    dattn,
    dmixed,
    dmixed_h,
    dq_f,
    dk_f,
    dv_f,
    grads_h,
    grads_tok,
    part_o,
    parts_w,
    o_land,
    small_own,
    small_land,
    small_sum,
    m_send,
    m_recv,
    g_send,
    g_recv,
    c_send,
    c_recv,
    s_send,
    s_recv,
    o_send,
    o_recv,
    small_send,
    small_recv,
    load_sem,
    out_sem,
    *scratch,
):
    seqs, shard, model = x_v.shape
    seq_len, width = q_v.shape[1:]
    heads = width // head_dim
    columns = others // 2
    me = lax.axis_index("sp")
    dp = lax.axis_index("dp")
    core = lax.rem(dp, 2)
    peer = [lax.rem(me + d, ways) for d in range(ways)]
    barrier = pltpu.get_barrier_semaphore()
    neighbours = [{"sp": peer[d]} for d in range(1, ways)]
    neighbours += [{"dp": flip(dp, d)} for d in range(1, others)]
    for device in neighbours:
        pl.semaphore_signal(barrier, inc=1, device_id=device, device_id_type=MESH)
    results = [
        pltpu.make_async_copy(source.at[s], target.at[s], out_sem.at[i, s])
        for i, (source, target) in enumerate(((tokens_v, tokens_ref), (block_v, block_ref)))
        for s in range(seqs)
    ]
    sources = (
        (back_ref, back_v),
        (placer_ref, placer_v),
        (residual_ref, residual_v),
        (cot_ref, cot_v),
        (wo_ref, wo_v),
        (mixed_ref, mixed_v),
        (q_ref, q_v),
        (k_ref, k_v),
        (v_ref, v_v),
        (normed_ref, normed_v),
        (wq_ref, wq_v),
        (wk_ref, wk_v),
        (wv_ref, wv_v),
        (x_ref, x_v),
        (result_ref.at[dp], returned.at[dp]),
    )
    loads = [
        pltpu.make_async_copy(source, target, load_sem.at[i])
        for i, (source, target) in enumerate(sources)
    ]
    for copy in loads:
        copy.start()

    def dmixed_copy(s, d):
        return send(
            dmixed.at[s, :, span(peer[d], width)],
            dmixed_h.at[s, span(me, shard)],
            m_send.at[s, d],
            m_recv.at[s, d],
            {"sp": peer[d]},
        )

    def grad_copy(s, d):
        return send(
            grads_h.at[s, span(peer[d], shard)],
            grads_tok.at[s, :, span(me, 3 * width)],
            g_send.at[s, d],
            g_recv.at[s, d],
            {"sp": peer[d]},
        )

    shards = shards_of(me, ways)
    scatter = []
    for j, (rest, land) in enumerate(((up_rest, up_land), (down_rest, down_land))):
        size = land.shape[1]
        first = size // 4
        for part, (begin, end) in enumerate(((0, first), (first, size))):
            scatter += [
                send(
                    rest.at[(i - 1) * size + begin : (i - 1) * size + end],
                    land.at[i - 1, begin:end],
                    s_send.at[j, part, i],
                    s_recv.at[j, part, i],
                    {"sp": shards[i]},
                )
                for i in range(1, len(shards))
            ]
    routed_back = exchange(others, result_ref, returned, c_send, c_recv)
    pl.semaphore_wait(barrier, len(neighbours))
    for copy in scatter[: len(shards) - 1]:
        copy.start()
    for copy in routed_back:
        copy.start()

    small_own[...] = jnp.zeros_like(small_own)
    small_own[4:5, 0:LANES] = counts_ref[0:1, :]
    for s in range(seqs):
        if s == 0:
            for copy in loads[:4]:
                copy.wait()
        rows = slice(s * shard, (s + 1) * shard)
        dnormed = mxu(placer_v[:, rows], back_v[...].reshape(-1, model), COLS_BY_COLS)
        gain = gain2_ref[...]
        _, unit, rstd = norm_forward(residual_v[rows, :], gain, jnp.zeros_like(gain))
        dinput, gain_grad, shift_grad = norm_backward(dnormed, unit, rstd, gain)
        total = cot_v[rows, :].astype(jnp.float32) + dinput
        dresid[s] = total
        dattn[rows, :] = total.astype(jnp.bfloat16)
        small_own[2:3, :] += gain_grad.reshape(1, model)
        small_own[3:4, :] += shift_grad.reshape(1, model)
        if s == 0:
            loads[4].wait()
        dmixed[s] = mxu(dattn[rows, :], wo_v[...], ROWS_BY_ROWS).astype(jnp.bfloat16)
        for d in range(1, ways):
            dmixed_copy(s, d).start()
    for copy in scatter[len(shards) - 1 :]:
        copy.start()
    sum_o = Reduction(ways, columns, part_o, out_o, False, scratch[:15])
    sums_w = [
        Reduction(ways, columns, parts_w.at[i], out, i == 0, scratch[15 * (i + 1) : 15 * (i + 2)])
        for i, out in enumerate((out_q, out_k, out_v))
    ]
    sum_q, sum_k, sum_v = sums_w
    steps = columns.bit_length() - 1

    loads[5].wait()

    def out_step(i, carry):
        at = span(i, BLOCK)
        left = mixed_v[:, :, at].reshape(seqs * shard, BLOCK)
        part_o[at, :] = mxu(left, dattn[...], COLS_BY_COLS).astype(jnp.bfloat16)
        return carry

    lax.fori_loop(0, model // BLOCK, out_step, 0)
    sum_o.core_copy.start()
    for copy in loads[6:9]:
        copy.wait()

    lane = lax.broadcasted_iota(jnp.int32, (1, width), 1) // head_dim
    visible = lax.broadcasted_iota(jnp.int32, (BLOCK, BLOCK), 0) <= lax.broadcasted_iota(
        jnp.int32, (BLOCK, BLOCK), 1
    )
    scale = head_dim ** (-0.5)
    for s in range(seqs):
        dmixed_h[s, span(me, shard), :] = dmixed[s, :, span(me, width)]
        for d in range(1, ways):
            dmixed_copy(s, d).wait_recv()
        if s == 0:
            sum_o.add_core()
        dq_f[...] = jnp.zeros_like(dq_f)
        dk_f[...] = jnp.zeros_like(dk_f)
        dv_f[...] = jnp.zeros_like(dv_f)

        def one_head(h, carry):
            mine = (lane == h).astype(jnp.float32)
            for at in range(0, seq_len, BLOCK):
                rows = slice(at, at + BLOCK)
                query = (q_v[s, rows, :].astype(jnp.float32) * (mine * scale)).astype(
                    jnp.bfloat16
                )
                dout = (dmixed_h[s, rows, :].astype(jnp.float32) * mine).astype(jnp.bfloat16)
                log_row = log_ref[s, pl.ds(h, 1), rows]
                parts = [(rows, True)] + ([(slice(0, at), False)] if at else [])
                kept = []
                delta = jnp.zeros((1, BLOCK), jnp.float32)
                for keys, diagonal in parts:
                    prob = jnp.exp(mxu(k_v[s, keys, :], query, ROWS_BY_ROWS) - log_row)
                    if diagonal:
                        prob = jnp.where(visible, prob, 0.0)
                    dprob = mxu(v_v[s, keys, :], dout, ROWS_BY_ROWS)
                    delta += jnp.sum(prob * dprob, axis=0, keepdims=True)
                    kept.append((keys, prob, dprob))
                dquery = jnp.zeros((BLOCK, width), jnp.float32)
                for keys, prob, dprob in kept:
                    dv_f[keys, :] += mxu(prob.astype(jnp.bfloat16), dout)
                    dlogit = (prob * (dprob - delta)).astype(jnp.bfloat16)
                    dk_f[keys, :] += mxu(dlogit, query)
                    dquery += mxu(dlogit, k_v[s, keys, :], COLS_BY_COLS)
                dq_f[rows, :] += dquery * (mine * scale)
            return carry

        lax.fori_loop(0, heads, one_head, 0)
        for i, total in enumerate((dq_f, dk_f, dv_f)):
            grads_h[s, :, i * width : (i + 1) * width] = total[...].astype(jnp.bfloat16)
        if s == 0:
            for d in range(1, ways):
                grad_copy(s, d).start()
        grads_tok[s, :, span(me, 3 * width)] = grads_h[s, span(me, shard), :]

    loads[9].wait()

    def weight_step(i, carry):
        at = span(i, BLOCK)
        grad = mxu(normed_v[0, :, at], grads_h[0], COLS_BY_COLS)
        for s in range(1, seqs):
            grad += mxu(normed_v[s, :, at], grads_h[s], COLS_BY_COLS)
        for j in range(3):
            parts_w[j, at, :] = grad[:, j * width : (j + 1) * width].astype(jnp.bfloat16)
        return carry

    lax.fori_loop(0, model // BLOCK, weight_step, 0)
    for total in (sum_v, sum_k, sum_q):
        total.core_copy.start()

    along, across = (sum_v, sum_k), (sum_q,)
    for total in (*across, *along):
        total.add_core()
    for step in range(steps - 1):
        sum_o.add_column(step)
    for step in range(steps):
        for total in (*across, *along):
            piece = total.add_column(step)
            if step == steps - 1:
                total.piece[...] = piece.astype(jnp.bfloat16)
                total.advance()

    o_land[0] = sum_o.add_column(steps - 1).astype(jnp.bfloat16)
    o_copy = [
        send(
            o_land.at[0, :, span(peer[d], width)],
            o_land.at[d, :, 0:width],
            o_send.at[d],
            o_recv.at[d],
            {"sp": peer[d]},
        )
        for d in range(1, ways)
    ]
    for copy in o_copy:
        copy.start()

    def norm_grad(s):
        for d in range(1, ways):
            grad_copy(s, d).wait()
        dnormed = jnp.zeros((shard, model), jnp.float32)
        for j in range(ways):
            for i, weight in enumerate((wq_v, wk_v, wv_v)):
                at = (3 * j + i) * width
                dnormed += mxu(
                    grads_tok[s, :, at : at + width],
                    weight[:, j * width : (j + 1) * width],
                    ROWS_BY_ROWS,
                )
        gain = gain1_ref[...]
        _, unit, rstd = norm_forward(x_v[s].astype(jnp.float32), gain, jnp.zeros_like(gain))
        dinput, gain_grad, shift_grad = norm_backward(dnormed, unit, rstd, gain)
        tokens_v[s] = (dresid[s] + dinput).astype(jnp.bfloat16)
        results[s].start()
        small_own[0:1, :] += gain_grad.reshape(1, model)
        small_own[1:2, :] += shift_grad.reshape(1, model)

    for copy in loads[10:14]:
        copy.wait()
    for total in across:
        total.advance()
    for s in range(1, seqs):
        for d in range(1, ways):
            grad_copy(s, d).start()
    total = o_land[0, :, span(me, width)].astype(jnp.float32)
    for d, copy in enumerate(o_copy):
        copy.wait()
        total += o_land[d + 1, :, 0:width].astype(jnp.float32)
    sum_o.piece[...] = total.astype(jnp.bfloat16)
    sum_o.advance()
    for _ in range(steps - 1):
        for total in along:
            total.advance()
    for total in across:
        total.advance()
    for _ in range(steps - 1):
        sum_o.advance()
    for s in range(seqs - 1):
        norm_grad(s)
    along[0].advance()
    norm_grad(seqs - 1)

    stages = [[{"sp": peer[d]} for d in range(1, ways)], [{"dp": dp + 1 - 2 * core}]]
    stages.append([{"dp": 2 * lax.rem(dp // 2 + d, columns) + core} for d in range(1, columns)])
    slot = 0
    source = small_own
    for number, peers in enumerate(stages):
        copies = [
            send(
                source,
                small_land.at[slot + i],
                small_send.at[slot + i],
                small_recv.at[slot + i],
                device,
            )
            for i, device in enumerate(peers)
        ]
        for copy in copies:
            copy.start()
        if number == 0:
            for total in (*along[1:], sum_o):
                total.advance()
            for _ in range(steps - 1):
                for total in across:
                    total.advance()
            along[0].advance()
        elif number == 1:
            for total in along[1:]:
                total.advance()
        else:
            sum_o.advance()
        total = source[...]
        for i, copy in enumerate(copies):
            copy.wait()
            total += small_land[slot + i]
        slot += len(peers)
        if number == len(stages) - 1:
            small_out[...] = total
        else:
            small_sum[number] = total
            source = small_sum.at[number]

    loads[14].wait()
    for copy in routed_back:
        copy.wait()
    for s in range(seqs):
        rows = slice(s * shard, (s + 1) * shard)
        out = mxu(placer_v[:, rows], returned[...].reshape(-1, model), COLS_BY_COLS)
        block_v[s] = (residual_v[rows, :] + out).astype(jnp.bfloat16)
        results[seqs + s].start()
    for total in [*across, *along, sum_o]:
        total.advance()
    for s in range(seqs):
        for d in range(1, ways):
            dmixed_copy(s, d).wait_send()
    for copy in scatter + results:
        copy.wait()
    for total in [sum_o] + sums_w:
        total.finish()


def finish(
    experts,
    tokens,
    query_ref,
    key_ref,
    value_ref,
    out_ref,
    up_own,
    up_land,
    down_own,
    down_land,
    block_in,
    tokens_in,
    small_ref,
    load_ref,
    query_out,
    key_out,
    value_out,
    out_out,
    up_out,
    down_out,
    block_out,
    tokens_out,
    gain1_out,
    shift1_out,
    gain2_out,
    shift2_out,
    load_out,
):
    for source, target in (
        (query_ref, query_out),
        (key_ref, key_out),
        (value_ref, value_out),
        (out_ref, out_out),
    ):
        target[...] = source[...].astype(jnp.float32)
    for own, land, target in ((up_own, up_land, up_out), (down_own, down_land, down_out)):
        total = own[...].astype(jnp.float32)
        for i in range(land.shape[0]):
            total += land[i].astype(jnp.float32)
        target[...] = total
    block_out[...] = block_in[...]
    tokens_out[...] = tokens_in[...]
    for i, target in enumerate((gain1_out, shift1_out, gain2_out, shift2_out)):
        target[...] = small_ref[i : i + 1, :]
    load_now = small_ref[4:5, 0:experts] * experts / tokens
    load_out[...] = 0.9 * load_ref[...] + 0.1 * load_now


def vmem(count):
    return [pl.BlockSpec(memory_space=pltpu.VMEM)] * count


def params(collective_id):
    return pltpu.CompilerParams(
        collective_id=collective_id, has_side_effects=True, vmem_limit_bytes=VMEM_BYTES
    )


def dma(*shape):
    return pltpu.SemaphoreType.DMA(shape)


def local(
    tokens_in,
    expert_ids,
    query_weight,
    key_weight,
    value_weight,
    out_weight,
    norm1_gain,
    norm1_shift,
    norm2_gain,
    norm2_shift,
    up_weight,
    down_weight,
    out_cotangent,
    load_mean,
):
    seq_count, shard_len, model_width = tokens_in.shape
    row_count = seq_count * shard_len
    head_dim = model_width // HEADS
    dp_ways = lax.axis_size("dp")
    sp_ways = lax.axis_size("sp")
    sp_at = lax.axis_index("sp")
    seq_len = shard_len * sp_ways
    experts = load_mean.shape[0]
    slot_count = 2 * row_count // experts
    local_experts = up_weight.shape[0]
    ff_width = up_weight.shape[1]
    width = model_width // sp_ways
    bf16 = jnp.bfloat16
    f32 = jnp.float32

    def shape(*sizes, dtype=bf16):
        return jax.ShapeDtypeStruct(sizes, dtype)

    cot_b = out_cotangent.reshape(row_count, model_width)
    hbm = [pl.BlockSpec(memory_space=pl.ANY)]
    routed = shape(experts, slot_count, model_width)
    square = pltpu.VMEM((model_width, model_width), bf16)
    by_head = pltpu.VMEM((seq_count, seq_len, width), bf16)
    token_shape = (seq_count, shard_len, model_width)
    whole_tokens = pltpu.VMEM((seq_count, seq_len, model_width), bf16)
    weight_columns = pltpu.VMEM((model_width, width), bf16)
    slots = (experts * slot_count, row_count)
    flat = (row_count, model_width)
    (
        normed_all,
        query_h,
        key_h,
        value_h,
        mixed_b,
        arrived,
        placer,
        residual_stream,
        outgoing,
        log_total,
        counts,
    ) = pl.pallas_call(
        functools.partial(forward, sp_ways, dp_ways, head_dim),
        out_shape=[
            shape(seq_count, seq_len, model_width),
            shape(seq_count, seq_len, width),
            shape(seq_count, seq_len, width),
            shape(seq_count, seq_len, width),
            shape(*token_shape),
            routed,
            shape(*slots),
            shape(*flat, dtype=f32),
            routed,
            shape(seq_count, 8, seq_len, dtype=f32),
            shape(8, LANES, dtype=f32),
        ],
        in_specs=hbm * 6 + vmem(5),
        out_specs=hbm * 9 + vmem(2),
        scratch_shapes=[
            whole_tokens,
            pltpu.VMEM(flat, bf16),
            pltpu.VMEM(routed.shape, bf16),
            weight_columns,
            weight_columns,
            weight_columns,
            square,
            pltpu.VMEM(slots, bf16),
            whole_tokens,
            by_head,
            by_head,
            by_head,
            pltpu.VMEM((seq_len, width), f32),
            by_head,
            pltpu.VMEM(token_shape, bf16),
            pltpu.VMEM((seq_len, LANES), f32),
            pltpu.VMEM(flat, f32),
            pltpu.VMEM(flat, bf16),
            pltpu.VMEM(routed.shape, bf16),
            dma(seq_count, sp_ways),
            dma(seq_count, sp_ways),
            dma(seq_count, 2, sp_ways),
            dma(seq_count, 2, sp_ways),
            dma(dp_ways),
            dma(dp_ways),
            dma(5),
            dma(seq_count),
            dma(seq_count + 2, 4),
            pltpu.SemaphoreType.DMA,
        ],
        compiler_params=params(0),
    )(
        tokens_in,
        cot_b,
        query_weight,
        key_weight,
        value_weight,
        out_weight,
        expert_ids.reshape(1, row_count),
        *(
            vector.reshape(1, model_width)
            for vector in (norm1_gain, norm1_shift, norm2_gain, norm2_shift)
        ),
    )
    ff_own = ff_width // 2
    received_blocks = max(2 * experts, ff_own // slot_count)
    shard_size = ff_width // sp_ways
    rest = sp_ways // 2 - 1
    blocks = shard_size // slot_count
    dnormed_back, expert_out, up_own, up_rest, down_own, down_rest = pl.pallas_call(
        functools.partial(run_experts, dp_ways, sp_ways),
        out_shape=[
            routed,
            routed,
            shape(shard_size, model_width),
            shape(rest * shard_size, model_width),
            shape(blocks, slot_count, model_width),
            shape(rest * blocks, slot_count, model_width),
        ],
        in_specs=hbm * 4,
        out_specs=hbm + vmem(1) + hbm * 4,
        scratch_shapes=[
            pltpu.VMEM((received_blocks, slot_count, model_width), bf16),
            pltpu.VMEM((2,) + routed.shape, bf16),
            pltpu.VMEM((ff_own, model_width), bf16),
            pltpu.VMEM((ff_own, model_width), bf16),
            pltpu.VMEM((2 * experts * slot_count, ff_own), bf16),
            pltpu.VMEM((2 * experts * slot_count, ff_own), bf16),
            pltpu.VMEM((2 * slot_count, model_width), f32),
            pltpu.VMEM(routed.shape, f32),
            pltpu.VMEM(routed.shape, bf16),
            pltpu.VMEM(routed.shape, bf16),
            pltpu.VMEM(routed.shape, bf16),
            pltpu.VMEM(routed.shape, bf16),
            pltpu.VMEM(routed.shape, bf16),
            dma(2, sp_ways // 2),
            dma(4),
            dma(3),
            dma(dp_ways),
            dma(dp_ways),
            dma(dp_ways),
            dma(dp_ways),
            dma(dp_ways // 2 + 2),
            dma(dp_ways // 2 + 2),
            dma(dp_ways // 2),
            dma(dp_ways // 2),
            dma(dp_ways // 2),
            dma(dp_ways // 2),
        ],
        compiler_params=params(3),
    )(outgoing, arrived, up_weight[0], down_weight[0])
    columns = dp_ways // 2
    rows = model_width // dp_ways

    def reduction(part_width):
        return [
            pltpu.VMEM((columns * rows, part_width), bf16),
            pltpu.VMEM((columns * rows, part_width), bf16),
            pltpu.VMEM(((columns - 1) * rows, part_width), bf16),
            pltpu.VMEM((rows, width), bf16),
            pltpu.SemaphoreType.DMA,
            pltpu.SemaphoreType.DMA,
            dma(columns),
            dma(columns),
            dma(columns),
            dma(columns),
            dma(sp_ways),
            dma(sp_ways),
            dma(sp_ways),
            dma(sp_ways),
            pltpu.SemaphoreType.DMA,
        ]

    small_slots = 1 + (columns - 1) + (sp_ways - 1)
    whole = shape(model_width, model_width)
    tokens = pltpu.VMEM(token_shape, bf16)
    *weight_grads, up_land, down_land, block_out, tokens_grad, small_sum = pl.pallas_call(
        functools.partial(backward, sp_ways, dp_ways, head_dim),
        out_shape=[whole] * 4
        + [
            shape(rest, shard_size, model_width),
            shape(rest, blocks, slot_count, model_width),
            shape(*token_shape),
            shape(*token_shape),
            shape(8, model_width, dtype=f32),
        ],
        in_specs=hbm * 17 + vmem(4),
        out_specs=hbm * 8 + vmem(1),
        scratch_shapes=[
            tokens,
            tokens,
            pltpu.VMEM(routed.shape, bf16),
            pltpu.VMEM(placer.shape, bf16),
            pltpu.VMEM(flat, bf16),
            pltpu.VMEM(flat, f32),
            square,
            tokens,
            by_head,
            by_head,
            by_head,
            whole_tokens,
            square,
            square,
            square,
            tokens,
            pltpu.VMEM(routed.shape, bf16),
            pltpu.VMEM(token_shape, f32),
            pltpu.VMEM(flat, bf16),
            tokens,
            by_head,
            pltpu.VMEM((seq_len, width), f32),
            pltpu.VMEM((seq_len, width), f32),
            pltpu.VMEM((seq_len, width), f32),
            pltpu.VMEM((seq_count, seq_len, 3 * width), bf16),
            pltpu.VMEM((seq_count, shard_len, 3 * model_width), bf16),
            square,
            pltpu.VMEM((3, model_width, width), bf16),
            pltpu.VMEM((sp_ways, rows, model_width), bf16),
            pltpu.VMEM((8, model_width), f32),
            pltpu.VMEM((small_slots, 8, model_width), f32),
            pltpu.VMEM((2, 8, model_width), f32),
            dma(seq_count, sp_ways),
            dma(seq_count, sp_ways),
            dma(seq_count, sp_ways),
            dma(seq_count, sp_ways),
            dma(dp_ways),
            dma(dp_ways),
            dma(2, 2, sp_ways // 2),
            dma(2, 2, sp_ways // 2),
            dma(sp_ways),
            dma(sp_ways),
            dma(small_slots),
            dma(small_slots),
            dma(15),
            dma(2, seq_count),
        ]
        + reduction(model_width)
        + reduction(width) * 3,
        compiler_params=params(1),
    )(
        dnormed_back,
        placer,
        cot_b,
        residual_stream,
        out_weight,
        mixed_b,
        query_h,
        key_h,
        value_h,
        normed_all,
        query_weight,
        key_weight,
        value_weight,
        tokens_in,
        expert_out,
        up_rest,
        down_rest,
        log_total,
        norm1_gain.reshape(1, model_width),
        norm2_gain.reshape(1, model_width),
        counts,
    )
    shard_shape = (shard_size, model_width)
    parts = 8
    big = pl.BlockSpec((model_width // parts, model_width), lambda i: (i, 0))
    own = pl.BlockSpec((shard_size // parts, model_width), lambda i: (i, 0))
    land = pl.BlockSpec((rest, shard_size // parts, model_width), lambda i: (0, i, 0))
    token = pl.BlockSpec((row_count // parts, model_width), lambda i: (i, 0))
    row = pl.BlockSpec((1, model_width), lambda i: (0, 0))
    load = pl.BlockSpec((1, experts), lambda i: (0, 0))
    results = pl.pallas_call(
        functools.partial(finish, experts, row_count * dp_ways * sp_ways),
        grid=(parts,),
        out_shape=[shape(model_width, model_width, dtype=f32)] * 4
        + [shape(*shard_shape, dtype=f32)] * 2
        + [shape(*flat)] * 2
        + [shape(1, model_width, dtype=f32)] * 4
        + [shape(1, experts, dtype=f32)],
        in_specs=[big] * 4
        + [own, land, own, land, token, token]
        + [pl.BlockSpec((8, model_width), lambda i: (0, 0)), load],
        out_specs=[big] * 4 + [own, own, token, token] + [row] * 4 + [load],
        compiler_params=pltpu.CompilerParams(vmem_limit_bytes=VMEM_BYTES),
    )(
        *weight_grads,
        up_own,
        up_land,
        down_own.reshape(shard_shape),
        down_land.reshape((rest,) + shard_shape),
        block_out.reshape(flat),
        tokens_grad.reshape(flat),
        small_sum,
        load_mean.reshape(1, experts),
    )
    return (
        results[6].reshape(token_shape),
        results[7].reshape(token_shape),
        *results[:4],
        *(vector.reshape(model_width) for vector in results[8:12]),
        results[4][None],
        results[5][None],
        results[12].reshape(experts),
    )


def solution(mesh):
    return jax.shard_map(
        local,
        mesh=mesh,
        in_specs=(
            P("dp", "sp", None),
            P("dp", "sp", None, None),
            P(),
            P(),
            P(),
            P(),
            P(),
            P(),
            P(),
            P(),
            P("dp", None, None),
            P("dp", None, None),
            P("dp", "sp", None),
            P(),
        ),
        out_specs=(
            P("dp", "sp", None),
            P("dp", "sp", None),
            P(),
            P(),
            P(),
            P(),
            P(),
            P(),
            P(),
            P(),
            P("dp", "sp", None),
            P("dp", "sp", None),
            P(),
        ),
        check_vma=False,
    )
```

```python
import functools

import jax
import jax.numpy as jnp
from jax import lax
from jax.experimental import pallas as pl
from jax.experimental.pallas import tpu as pltpu
from jax.sharding import PartitionSpec as P

HEADS = 16
MESH = pl.DeviceIdType.MESH
BLOCK = 256
LANES = 128
STEP = 1024
VMEM_BYTES = 60 * 2**20

NORM_EPSILON = 1e-05
GELU_ROOT = 0.7978845608028654
CUBIC_TERM = 0.044715

ROWS_BY_COLS = (((1,), (0,)), ((), ()))
ROWS_BY_ROWS = (((1,), (1,)), ((), ()))
COLS_BY_COLS = (((0,), (0,)), ((), ()))


def smooth(values):
    return (
        0.5
        * values
        * (1.0 + jnp.tanh(GELU_ROOT * (values + CUBIC_TERM * values * values * values)))
    )


def smooth_slope(values):
    inner = jnp.tanh(GELU_ROOT * (values + CUBIC_TERM * values * values * values))
    return 0.5 * (1.0 + inner) + 0.5 * values * (1.0 - inner * inner) * GELU_ROOT * (
        1.0 + 3.0 * CUBIC_TERM * values * values
    )


def norm_forward(values, gain, shift):
    center = jnp.mean(values, axis=-1, keepdims=True)
    offset = values - center
    rstd = lax.rsqrt(jnp.mean(offset * offset, axis=-1, keepdims=True) + NORM_EPSILON)
    unit = offset * rstd
    return (unit * gain + shift, unit, rstd)


def norm_backward(grad, unit, rstd, gain):
    scaled = grad * gain
    inner = (
        scaled
        - jnp.mean(scaled, axis=-1, keepdims=True)
        - unit * jnp.mean(scaled * unit, axis=-1, keepdims=True)
    )
    return (inner * rstd, jnp.sum(grad * unit, axis=0), jnp.sum(grad, axis=0))


def mxu(left, right, dims=ROWS_BY_COLS):
    return lax.dot_general(left, right, dims, preferred_element_type=jnp.float32)


def span(index, size):
    return pl.ds(pl.multiple_of(index * size, size), size)


def greet(peers):
    barrier = pltpu.get_barrier_semaphore()
    for peer in peers:
        pl.semaphore_signal(barrier, inc=1, device_id=peer, device_id_type=MESH)
    pl.semaphore_wait(barrier, len(peers))


def send(source, target, send_sem, recv_sem, peer):
    return pltpu.make_async_remote_copy(
        src_ref=source,
        dst_ref=target,
        send_sem=send_sem,
        recv_sem=recv_sem,
        device_id=peer,
        device_id_type=MESH,
    )


def exchange(others, source, target, send_sem, recv_sem):
    me = lax.axis_index("dp")
    return [
        send(
            source.at[flip(me, d)],
            target.at[me],
            send_sem.at[d],
            recv_sem.at[d],
            {"dp": flip(me, d)},
        )
        for d in range(1, others)
    ]


def flip(index, bits):
    bit = 1
    while bit <= bits:
        if bits & bit:
            index = index + bit - 2 * bit * lax.rem(index // bit, 2)
        bit *= 2
    return index


def forward(
    ways,
    others,
    head_dim,
    x_ref,
    cot_ref,
    wq_ref,
    wk_ref,
    wv_ref,
    wo_ref,
    ids_ref,
    gain1_ref,
    shift1_ref,
    gain2_ref,
    shift2_ref,
    normed_ref,
    q_ref,
    k_ref,
    v_ref,
    mixed_ref,
    arrived_ref,
    placer_ref,
    residual_ref,
    outgoing_ref,
    log_ref,
    counts_ref,
    x_all,
    cot_v,
    cot_out,
    wq_v,
    wk_v,
    wv_v,
    wo_v,
    placer_v,
    normed_v,
    q_v,
    k_v,
    v_v,
    mixed_f,
    mixed_h,
    mixed_tok,
    log_s,
    residual_v,
    normed2,
    outgoing_v,
    x_send,
    x_recv,
    m_send,
    m_recv,
    c_send,
    c_recv,
    load_sem,
    x_sem,
    store_sem,
    own_sem,
):
    seqs, seq_len, model = x_all.shape
    shard = seq_len // ways
    width = q_v.shape[2]
    heads = width // head_dim
    slots = cot_out.shape[1]
    me = lax.axis_index("sp")
    dp = lax.axis_index("dp")
    peer = [flip(me, d) for d in range(ways)]
    near = (1, 2) if ways == 4 else tuple(range(1, ways))
    far = tuple(range(1 + len(near), ways))
    barrier = pltpu.get_barrier_semaphore()
    neighbours = [{"sp": peer[d]} for d in range(1, ways)]
    neighbours += [{"dp": flip(dp, d)} for d in range(1, others)]
    for device in neighbours:
        pl.semaphore_signal(barrier, inc=1, device_id=device, device_id_type=MESH)
    own_columns = span(me, width)
    loads = [
        pltpu.make_async_copy(source, target, load_sem.at[i])
        for i, (source, target) in enumerate(
            (
                (cot_ref, cot_v),
                (wq_ref.at[:, own_columns], wq_v),
                (wk_ref.at[:, own_columns], wk_v),
                (wv_ref.at[:, own_columns], wv_v),
                (wo_ref, wo_v),
            )
        )
    ]
    own_x = [
        pltpu.make_async_copy(x_ref.at[s], x_all.at[s, span(me, shard)], x_sem.at[s])
        for s in range(seqs)
    ]
    for copy in own_x + loads:
        copy.start()

    def x_copy(s, d):
        return send(
            x_ref.at[s],
            x_all.at[s, span(me, shard)],
            x_send.at[s, d],
            x_recv.at[s, d],
            {"sp": peer[d]},
        )

    def x_relays(s):
        if not far:
            return []
        size = shard // 2
        pieces = [
            x_all.at[s, pl.ds(pl.multiple_of(peer[1] * shard, size), size)],
            x_all.at[s, pl.ds(pl.multiple_of(peer[2] * shard + size, size), size)],
        ]
        return [
            send(piece, piece, x_send.at[s, at], x_recv.at[s, at], {"sp": peer[to]})
            for piece, at, to in zip(pieces, (0, 3), (2, 1))
        ]

    cuts = max(1, width // BLOCK)
    cuts = 2 * cuts if width // (2 * cuts) % LANES == 0 else cuts
    cut = width // cuts

    def mixed_copy(s, d, c):
        return send(
            mixed_h.at[s, span(peer[d], shard), c * cut : (c + 1) * cut],
            mixed_tok.at[s, :, span(me * cuts + c, cut)],
            m_send.at[s, c, d],
            m_recv.at[s, c, d],
            {"sp": peer[d]},
        )

    pl.semaphore_wait(barrier, len(neighbours))
    for d in near:
        x_copy(0, d).start()

    tokens = seqs * shard
    ids = ids_ref[...]
    named = lax.broadcasted_iota(jnp.int32, (LANES, tokens), 0) == ids
    named = jnp.where(named, 1.0, 0.0)
    upper = lax.broadcasted_iota(jnp.int32, (tokens, tokens), 0) <= lax.broadcasted_iota(
        jnp.int32, (tokens, tokens), 1
    )
    running = mxu(named.astype(jnp.bfloat16), jnp.where(upper, 1.0, 0.0).astype(jnp.bfloat16))
    slot = jnp.sum(named * (running - 1.0), axis=0, keepdims=True).astype(jnp.int32)
    places = lax.broadcasted_iota(jnp.int32, placer_v.shape, 0) == ids * slots + slot
    placer_v[...] = jnp.where(places, 1.0, 0.0).astype(jnp.bfloat16)
    ones = jnp.ones((8, tokens), jnp.float32)
    counts_ref[...] = mxu(ones, named, ROWS_BY_ROWS)
    loads[0].wait()
    cot_out[...] = (
        mxu(placer_v[...], cot_v[...]).astype(jnp.bfloat16).reshape(cot_out.shape)
    )
    background = exchange(others, cot_out, arrived_ref, c_send, c_recv)
    own_cot = pltpu.make_async_copy(cot_out.at[dp], arrived_ref.at[dp], own_sem)
    for copy in background + [own_cot]:
        copy.start()

    lane = lax.broadcasted_iota(jnp.int32, (1, width), 1) // head_dim
    log_lane = lax.broadcasted_iota(jnp.int32, (1, LANES), 1)
    visible = lax.broadcasted_iota(jnp.int32, (BLOCK, BLOCK), 1) <= lax.broadcasted_iota(
        jnp.int32, (BLOCK, BLOCK), 0
    )
    scale = head_dim ** (-0.5)
    outs = ((normed_v, normed_ref), (q_v, q_ref), (k_v, k_ref), (v_v, v_ref))
    stores = [
        [
            pltpu.make_async_copy(source.at[s], target.at[s], store_sem.at[s, i])
            for i, (source, target) in enumerate(outs)
        ]
        for s in range(seqs)
    ]

    def project(s, d):
        rows = span(peer[d], shard)
        values = x_all[s, rows, :].astype(jnp.float32)
        normed, _, _ = norm_forward(values, gain1_ref[...], shift1_ref[...])
        normed = normed.astype(jnp.bfloat16)
        normed_v[s, rows, :] = normed
        q_v[s, rows, :] = mxu(normed, wq_v[...]).astype(jnp.bfloat16)
        k_v[s, rows, :] = mxu(normed, wk_v[...]).astype(jnp.bfloat16)
        v_v[s, rows, :] = mxu(normed, wv_v[...]).astype(jnp.bfloat16)

    for s in range(seqs):
        own_x[s].wait()
        if s == 0:
            for copy in loads[1:4]:
                copy.wait()
        project(s, 0)
        for d in near:
            x_copy(s, d).wait_recv()
        for copy in x_relays(s):
            copy.start()
        if s + 1 < seqs:
            for d in near:
                x_copy(s + 1, d).start()
        for d in near:
            project(s, d)
        for copy in x_relays(s):
            copy.wait_recv()
        if s:
            for c in range(cuts):
                for d in range(1, ways):
                    mixed_copy(s - 1, d, c).start()
        for d in far:
            project(s, d)
        for copy in stores[s]:
            copy.start()
        mixed_f[...] = jnp.zeros_like(mixed_f)
        log_s[...] = jnp.zeros_like(log_s)

        def one_head(h, carry):
            mine = (lane == h).astype(jnp.float32)
            for at in range(0, seq_len, BLOCK):
                rows = slice(at, at + BLOCK)
                query = (q_v[s, rows, :].astype(jnp.float32) * (mine * scale)).astype(
                    jnp.bfloat16
                )
                near = mxu(query, k_v[s, rows, :], ROWS_BY_ROWS)
                near = jnp.where(visible, near, -1e30)
                top = jnp.max(near, axis=1, keepdims=True)
                if at:
                    far = mxu(query, k_v[s, :at, :], ROWS_BY_ROWS)
                    top = jnp.maximum(top, jnp.max(far, axis=1, keepdims=True))
                near = jnp.exp(near - top)
                total = jnp.sum(near, axis=1, keepdims=True)
                if at:
                    far = jnp.exp(far - top)
                    total += jnp.sum(far, axis=1, keepdims=True)
                inverse = 1.0 / total
                out = mxu((near * inverse).astype(jnp.bfloat16), v_v[s, rows, :])
                if at:
                    out += mxu((far * inverse).astype(jnp.bfloat16), v_v[s, :at, :])
                mixed_f[rows, :] += out * mine
                log_s[rows, :] = jnp.where(log_lane == h, top + jnp.log(total), log_s[rows, :])
            return carry

        for c in range(cuts):
            lax.fori_loop(c * heads // cuts, (c + 1) * heads // cuts, one_head, 0)
            columns = slice(c * cut, (c + 1) * cut)
            mixed_h[s, :, columns] = mixed_f[:, columns].astype(jnp.bfloat16)
            if s == seqs - 1:
                for d in range(1, ways):
                    mixed_copy(s, d, c).start()
        log_ref[s] = jnp.transpose(log_s[...])[: log_ref.shape[1], :]
        mixed_tok[s, :, own_columns] = mixed_h[s, span(me, shard), :]

    loads[4].wait()
    for s in range(seqs):
        for c in range(cuts):
            for d in range(1, ways):
                mixed_copy(s, d, c).wait_recv()
        rows = slice(s * shard, (s + 1) * shard)
        values = x_all[s, span(me, shard), :].astype(jnp.float32)
        values += mxu(mixed_tok[s], wo_v[...])
        residual_v[rows, :] = values
        normed, _, _ = norm_forward(values, gain2_ref[...], shift2_ref[...])
        normed2[rows, :] = normed.astype(jnp.bfloat16)
    last = [
        pltpu.make_async_copy(source, target, store_sem.at[seqs, i])
        for i, (source, target) in enumerate(
            ((mixed_tok, mixed_ref), (residual_v, residual_ref), (placer_v, placer_ref))
        )
    ]
    for copy in last:
        copy.start()
    for i in range(2):
        part = slots * others // 2
        rows = slice(i * part, (i + 1) * part)
        blocks = pl.ds(i * others // 2, others // 2)
        outgoing_v[blocks] = (
            mxu(placer_v[rows, :], normed2[...])
            .astype(jnp.bfloat16)
            .reshape(others // 2, slots, model)
        )
        copy = pltpu.make_async_copy(
            outgoing_v.at[blocks], outgoing_ref.at[blocks], store_sem.at[seqs + 1, i]
        )
        copy.start()
        last.append(copy)
    for s in range(seqs):
        for d in near:
            x_copy(s, d).wait_send()
        for copy in x_relays(s):
            copy.wait_send()
        for c in range(cuts):
            for d in range(1, ways):
                mixed_copy(s, d, c).wait_send()
        for copy in stores[s]:
            copy.wait()
    for copy in background + [own_cot] + last:
        copy.wait()


def pair_of(sp):
    core = lax.rem(lax.axis_index("dp"), 2)
    along_x, along_y = flip(sp, 1), flip(sp, 2)
    return along_x + core * (along_y - along_x)


def shards_of(sp, ways):
    shards = [sp, flip(pair_of(sp), 3)]
    bit = 4
    while bit < ways:
        shards += [flip(shard, bit) for shard in shards]
        bit *= 2
    return shards


def run_experts(
    others,
    ways,
    outgoing_ref,
    cot_ref,
    up_ref,
    down_ref,
    back_ref,
    result_ref,
    up_own,
    up_rest,
    down_own,
    down_rest,
    received,
    arrived,
    up_v,
    down_v,
    hidden,
    slope_v,
    total,
    dn_own,
    dn_pair,
    dn_land,
    dnormed,
    out_pair,
    out_land,
    w_sem,
    o_sem,
    c_sem,
    a_send,
    a_recv,
    b_send,
    b_recv,
    f_send,
    f_recv,
    p_send,
    p_recv,
    e_send,
    e_recv,
):
    slots, width = received.shape[1:]
    rows = others * slots
    ff = up_v.shape[0]
    groups = others // 2
    me = lax.axis_index("dp")
    sp = lax.axis_index("sp")
    chip = me // 2
    pair = {"sp": pair_of(sp)}
    shards = shards_of(sp, ways)
    size = ff // len(shards)
    loads = [
        pltpu.make_async_copy(
            source.at[span(shard, size)], target.at[i * size : (i + 1) * size], w_sem.at[j, i]
        )
        for j, (source, target) in enumerate(((down_ref, down_v), (up_ref, up_v)))
        for i, shard in enumerate(shards)
    ]
    own_cot = pltpu.make_async_copy(cot_ref, arrived.at[0], c_sem.at[0])
    own_rows = pltpu.make_async_copy(outgoing_ref.at[me], received.at[me], c_sem.at[1])
    own_back = pltpu.make_async_copy(dnormed.at[me], back_ref.at[me], c_sem.at[2])
    own_rows.start()
    own_cot.start()
    for copy in loads:
        copy.start()
    greet([{"dp": flip(me, d)} for d in range(1, others)] + [pair])
    inward = exchange(others, outgoing_ref, received.at[0:others], a_send, a_recv)
    outward = exchange(others, dnormed, back_ref, b_send, b_recv)
    near = [flip(chip, group) for group in range(groups)]
    chips = [pl.ds(2 * near[group], 2) for group in range(groups)]
    forward = [
        send(
            received.at[chips[group]],
            received.at[pl.ds(others + 2 * near[group], 2)],
            f_send.at[group],
            f_recv.at[group],
            pair,
        )
        for group in range(groups)
    ]
    cot_copy = [
        send(
            cot_ref.at[i * groups : (i + 1) * groups],
            arrived.at[1, i * groups : (i + 1) * groups],
            f_send.at[groups + i],
            f_recv.at[groups + i],
            pair,
        )
        for i in range(2)
    ]
    dn_copy = [
        send(
            dn_pair.at[chips[group]],
            dn_land.at[chips[group]],
            p_send.at[group],
            p_recv.at[group],
            pair,
        )
        for group in range(groups)
    ]
    out_copy = [
        send(
            out_pair.at[chips[group]],
            out_land.at[chips[group]],
            e_send.at[group],
            e_recv.at[group],
            pair,
        )
        for group in range(groups)
    ]

    early = range(groups // 2)
    middle = range(groups // 2, 3 * groups // 4)
    late = range(3 * groups // 4, groups)
    for copy in [inward[0]] + inward[2 * middle[0] - 1 : 2 * late[0] - 1]:
        copy.start()
    for copy in inward[1 : 2 * middle[0] - 1]:
        copy.start()
    for copy in cot_copy:
        copy.start()
    own_rows.wait()

    def slab_of(half, group):
        return pl.ds(pl.multiple_of(half * rows + near[group] * (2 * slots), 2 * slots), 2 * slots)

    def cot_part(half, begin, end):
        def cot_step(i, carry):
            at = span(i, STEP)
            cot = arrived[half, begin:end].reshape((end - begin) * slots, width)
            slope_v[half * rows + begin * slots : half * rows + end * slots, at] = mxu(
                cot, down_v[at, :], ROWS_BY_ROWS
            ).astype(jnp.bfloat16)
            return carry

        lax.fori_loop(0, ff // STEP, cot_step, 0)

    def up_half(half, group):
        slab = slab_of(half, group)
        total[...] = jnp.zeros_like(total)

        def up_step(i, carry):
            at = span(i, STEP)
            tokens = received[pl.ds(half * others + 2 * near[group], 2)].reshape(2 * slots, width)
            pre = mxu(tokens, up_v[at, :], ROWS_BY_ROWS)
            square = pre * pre
            inner = jnp.tanh(GELU_ROOT * pre * (1.0 + CUBIC_TERM * square))
            gate = 0.5 * (1.0 + inner)
            hidden[slab, at] = (pre * gate).astype(jnp.bfloat16)
            slope = gate + (0.5 * GELU_ROOT) * pre * (1.0 - inner * inner) * (
                1.0 + (3.0 * CUBIC_TERM) * square
            )
            dpre = (slope_v[slab, at].astype(jnp.float32) * slope).astype(jnp.bfloat16)
            slope_v[slab, at] = dpre
            total[...] += mxu(dpre, up_v[at, :])
            return carry

        lax.fori_loop(0, ff // STEP, up_step, 0)
        shaped = total[...].reshape(2, slots, width)
        if half:
            dn_pair[chips[group]] = shaped.astype(jnp.bfloat16)
        else:
            dn_own[chips[group]] = shaped

    def out_half(half, group):
        at = chips[group]
        out = mxu(hidden[slab_of(half, group), :], down_v[...]).reshape(2, slots, width)
        if half:
            out_pair[at] = out.astype(jnp.bfloat16)
        else:
            out_copy[group].wait_recv()
            result_ref[at] = (out + out_land[at].astype(jnp.float32)).astype(jnp.bfloat16)

    def pass_on(group):
        for d in (2 * group, 2 * group + 1):
            if d:
                inward[d - 1].wait_recv()
        forward[group].start()

    def finish(group):
        dn_copy[group].wait_recv()
        at = chips[group]
        dnormed[at] = (dn_own[at] + dn_land[at].astype(jnp.float32)).astype(jnp.bfloat16)
        for d in (2 * group, 2 * group + 1):
            if d:
                outward[d - 1].start()
            else:
                own_back.start()

    def up_pair(group):
        forward[group].wait_recv()
        up_half(1, group)
        if group not in early:
            dn_copy[group].start()

    def grad(target, left, right_ref, begin, end, block=0):
        def grad_step(i, carry):
            at = span(i, STEP)
            right = right_ref[...].reshape(2 * rows, width)
            out = mxu(left[:, at], right, COLS_BY_COLS).astype(jnp.bfloat16)
            if block:
                target[span(i, STEP // block)] = out.reshape(STEP // block, block, width)
            else:
                target[at, :] = out
            return carry

        lax.fori_loop(begin, end, grad_step, 0)

    pass_on(0)
    own_cot.wait()
    for copy in loads[: len(shards)]:
        copy.wait()
    cot_part(0, 0, others)
    for copy in loads[len(shards) :]:
        copy.wait()
    up_half(0, 0)
    cot_copy[0].wait_recv()
    cot_part(1, 0, groups)
    for group in middle:
        pass_on(group)
        up_half(0, group)
    for copy in inward[2 * middle[0] - 1 : 2 * late[0] - 1]:
        copy.wait_send()
    for copy in inward[2 * late[0] - 1 :]:
        copy.start()
    for group in early[1:]:
        pass_on(group)
    cot_copy[1].wait_recv()
    cot_part(1, groups, others)
    for group in early[1:]:
        up_half(0, group)
    for group in middle:
        up_pair(group)
    for group in early:
        up_pair(group)
    for group in late:
        pass_on(group)
    dn_copy[0].start()
    for group in middle:
        finish(group)
    for group in late:
        up_half(0, group)
    for group in middle:
        out_half(1, group)
    for group in late:
        up_pair(group)
    for group in early[1:]:
        dn_copy[group].start()
    for group in middle:
        out_copy[group].start()
    for group in [*early, *late]:
        out_half(1, group)
    tokens_all = received.at[0 : 2 * others]
    grad(up_v, slope_v, tokens_all, 0, 1)
    for group in late:
        finish(group)
    for group in [*early, *late]:
        out_copy[group].start()
    grad(up_v, slope_v, tokens_all, 1, ff // STEP)
    for group in early:
        finish(group)
    for copy in forward:
        copy.wait_send()
    grad(received, hidden, arrived, 0, ff // STEP, slots)
    first, every = size // slots, ff // slots
    stores = [
        pltpu.make_async_copy(source, target, o_sem.at[i])
        for i, (source, target) in enumerate(
            (
                (up_v.at[0:size], up_own),
                (up_v.at[size:ff], up_rest),
                (received.at[0:first], down_own),
                (received.at[first:every], down_rest),
            )
        )
    ]
    for copy in stores:
        copy.start()
    for group in range(groups):
        out_half(0, group)
    for copy in inward[: 2 * middle[0] - 1] + inward[2 * late[0] - 1 :]:
        copy.wait_send()
    for copy in cot_copy + dn_copy + out_copy:
        copy.wait_send()
    for copy in outward + stores + [own_back]:
        copy.wait()


class Reduction:
    def __init__(self, ways, columns, part, out, across_first, scratch):
        (
            self.core_land,
            self.core_sum,
            self.column_land,
            self.piece,
            core_send,
            core_recv,
            column_send,
            column_recv,
            spread_send,
            spread_recv,
            ring_send,
            ring_recv,
            cross_send,
            cross_recv,
            own_sem,
        ) = scratch
        me = lax.axis_index("sp")
        dp = lax.axis_index("dp")
        core = lax.rem(dp, 2)
        column = dp // 2
        twin = {"dp": dp + 1 - 2 * core}
        self.ways, self.columns, self.part = ways, columns, part
        self.core = core
        rows, width = self.piece.shape
        self.rows = rows

        bits = [1 << i for i in range(columns.bit_length() - 1)]
        place = 0
        for bit in bits:
            place = 2 * place + lax.rem(column // bit, 2)
        self.place = place

        def beside(bit):
            return {"dp": 2 * flip(column, bit) + core}

        def block(first, at_sp, count):
            first = pl.multiple_of((core * columns + first) * rows, rows)
            return out.at[pl.ds(first, count * rows), span(at_sp, width)]

        self.core_copy = send(
            part.at[span(1 - core, columns * rows)], self.core_land, core_send, core_recv, twin
        )
        self.column_copy, self.kept, self.lands = [], [], []
        first, count, used = 0, columns, 0
        for i, bit in enumerate(bits):
            count //= 2
            mine = lax.rem(column // bit, 2)
            size = count * rows
            gone = pl.ds(pl.multiple_of((first + (1 - mine) * count) * rows, size), size)
            first = first + mine * count
            self.kept.append(pl.ds(pl.multiple_of(first * rows, size), size))
            land = self.column_land.at[used : used + size]
            used += size
            self.lands.append(land)
            self.column_copy.append(
                send(self.core_sum.at[gone], land, column_send.at[i], column_recv.at[i], beside(bit))
            )
        spot = block(place, me, 1)
        self.own = pltpu.make_async_copy(self.piece, spot, own_sem)
        origin = [flip(me, d) for d in range(ways)]
        across_count = 1 if across_first else columns
        across_at = place if across_first else 0
        near = (1, 2) if ways == 4 else tuple(range(1, ways))
        held = [block(across_at, at, across_count) for at in origin]
        self.ring_copy = [
            send(held[0], held[0], ring_send.at[d], ring_recv.at[d], {"sp": origin[d]})
            for d in near
        ]
        self.relays = []
        if ways == 4:
            count = across_count * rows // 2
            first = (core * columns + across_at) * rows
            for i, (d, to) in enumerate(((1, 2), (2, 1))):
                at = pl.multiple_of(first + i * count, count)
                half = out.at[pl.ds(at, count), span(origin[d], width)]
                index = (0, 3)[i]
                self.relays.append(
                    send(
                        half, half, ring_send.at[index], ring_recv.at[index], {"sp": origin[to]}
                    )
                )

        def rows_of(first, count):
            first = pl.multiple_of((core * columns + first) * rows, rows)
            return out.at[pl.ds(first, count * rows)]

        self.spread_copy, gathered = [], [rows_of(place, 1)]
        for i, bit in enumerate(reversed(bits)):
            count = 1 << i
            at = place - lax.rem(place, count)
            spot = rows_of(at, count) if across_first else block(at, me, count)
            gathered.append(rows_of(flip(at, count), count))
            self.spread_copy.append(
                send(spot, spot, spread_send.at[i], spread_recv.at[i], beside(bit))
            )
        crossing = gathered if across_first else held
        self.cross_copy = [
            send(part, part, cross_send.at[i], cross_recv.at[i], twin)
            for i, part in enumerate(crossing)
        ]
        self.phases = iter(self.across_then_along() if across_first else self.along_then_across())

    def along_then_across(self):
        self.own.start()
        self.own.wait()
        for copy in self.spread_copy:
            copy.start()
            yield
            copy.wait()
        for copy in self.ring_copy:
            copy.start()
        self.cross_copy[0].start()
        yield
        for ring, cross in zip(self.ring_copy, self.cross_copy[1:]):
            ring.wait_recv()
            cross.start()
        for copy in self.relays:
            copy.start()
        yield
        for copy in self.relays:
            copy.wait_recv()
        if self.relays:
            self.cross_copy[3].start()
        yield

    def across_then_along(self):
        self.own.start()
        self.own.wait()
        for copy in self.ring_copy:
            copy.start()
        yield
        for copy in self.ring_copy:
            copy.wait_recv()
        for copy in self.relays:
            copy.start()
        yield
        for copy in self.relays:
            copy.wait_recv()
        for spread, cross in zip(self.spread_copy, self.cross_copy):
            spread.start()
            cross.start()
            yield
            spread.wait()
        self.cross_copy[-1].start()
        yield

    def advance(self):
        next(self.phases)

    def add_core(self):
        self.core_copy.wait()
        self.core_sum[...] = (
            self.part[span(self.core, self.columns * self.rows), :].astype(jnp.float32)
            + self.core_land[...].astype(jnp.float32)
        ).astype(jnp.bfloat16)
        self.column_copy[0].start()

    def add_column(self, step):
        self.column_copy[step].wait()
        total = self.core_sum[self.kept[step], :].astype(jnp.float32)
        total += self.lands[step][...].astype(jnp.float32)
        if step + 1 < len(self.column_copy):
            self.core_sum[self.kept[step], :] = total.astype(jnp.bfloat16)
            self.column_copy[step + 1].start()
        return total

    def finish(self):
        for copy in self.ring_copy + self.relays:
            copy.wait_send()
        for copy in self.cross_copy:
            copy.wait()


def backward(
    ways,
    others,
    head_dim,
    back_ref,
    placer_ref,
    cot_ref,
    residual_ref,
    wo_ref,
    mixed_ref,
    q_ref,
    k_ref,
    v_ref,
    normed_ref,
    wq_ref,
    wk_ref,
    wv_ref,
    x_ref,
    result_ref,
    up_rest,
    down_rest,
    log_ref,
    gain1_ref,
    gain2_ref,
    counts_ref,
    out_q,
    out_k,
    out_v,
    out_o,
    up_land,
    down_land,
    block_ref,
    tokens_ref,
    small_out,
    block_v,
    tokens_v,
    back_v,
    placer_v,
    cot_v,
    residual_v,
    wo_v,
    mixed_v,
    q_v,
    k_v,
    v_v,
    normed_v,
    wq_v,
    wk_v,
    wv_v,
    x_v,
    returned,
    dresid,
    dattn,
    dmixed,
    dmixed_h,
    dq_f,
    dk_f,
    dv_f,
    grads_h,
    grads_tok,
    part_o,
    parts_w,
    o_land,
    small_own,
    small_land,
    small_sum,
    m_send,
    m_recv,
    g_send,
    g_recv,
    c_send,
    c_recv,
    s_send,
    s_recv,
    o_send,
    o_recv,
    small_send,
    small_recv,
    load_sem,
    out_sem,
    *scratch,
):
    seqs, shard, model = x_v.shape
    seq_len, width = q_v.shape[1:]
    heads = width // head_dim
    columns = others // 2
    me = lax.axis_index("sp")
    dp = lax.axis_index("dp")
    core = lax.rem(dp, 2)
    peer = [lax.rem(me + d, ways) for d in range(ways)]
    barrier = pltpu.get_barrier_semaphore()
    neighbours = [{"sp": peer[d]} for d in range(1, ways)]
    neighbours += [{"dp": flip(dp, d)} for d in range(1, others)]
    for device in neighbours:
        pl.semaphore_signal(barrier, inc=1, device_id=device, device_id_type=MESH)
    results = [
        pltpu.make_async_copy(source.at[s], target.at[s], out_sem.at[i, s])
        for i, (source, target) in enumerate(((tokens_v, tokens_ref), (block_v, block_ref)))
        for s in range(seqs)
    ]
    sources = (
        (back_ref, back_v),
        (placer_ref, placer_v),
        (residual_ref, residual_v),
        (cot_ref, cot_v),
        (wo_ref, wo_v),
        (mixed_ref, mixed_v),
        (q_ref, q_v),
        (k_ref, k_v),
        (v_ref, v_v),
        (normed_ref, normed_v),
        (wq_ref, wq_v),
        (wk_ref, wk_v),
        (wv_ref, wv_v),
        (x_ref, x_v),
        (result_ref.at[dp], returned.at[dp]),
    )
    loads = [
        pltpu.make_async_copy(source, target, load_sem.at[i])
        for i, (source, target) in enumerate(sources)
    ]
    for copy in loads:
        copy.start()

    def dmixed_copy(s, d):
        return send(
            dmixed.at[s, :, span(peer[d], width)],
            dmixed_h.at[s, span(me, shard)],
            m_send.at[s, d],
            m_recv.at[s, d],
            {"sp": peer[d]},
        )

    def grad_copy(s, d):
        return send(
            grads_h.at[s, span(peer[d], shard)],
            grads_tok.at[s, :, span(me, 3 * width)],
            g_send.at[s, d],
            g_recv.at[s, d],
            {"sp": peer[d]},
        )

    shards = shards_of(me, ways)
    scatter = []
    for j, (rest, land) in enumerate(((up_rest, up_land), (down_rest, down_land))):
        size = land.shape[1]
        first = size // 4
        for part, (begin, end) in enumerate(((0, first), (first, size))):
            scatter += [
                send(
                    rest.at[(i - 1) * size + begin : (i - 1) * size + end],
                    land.at[i - 1, begin:end],
                    s_send.at[j, part, i],
                    s_recv.at[j, part, i],
                    {"sp": shards[i]},
                )
                for i in range(1, len(shards))
            ]
    routed_back = exchange(others, result_ref, returned, c_send, c_recv)
    pl.semaphore_wait(barrier, len(neighbours))
    for copy in scatter[: len(shards) - 1]:
        copy.start()
    for copy in routed_back:
        copy.start()

    small_own[...] = jnp.zeros_like(small_own)
    small_own[4:5, 0:LANES] = counts_ref[0:1, :]
    for s in range(seqs):
        if s == 0:
            for copy in loads[:4]:
                copy.wait()
        rows = slice(s * shard, (s + 1) * shard)
        dnormed = mxu(placer_v[:, rows], back_v[...].reshape(-1, model), COLS_BY_COLS)
        gain = gain2_ref[...]
        _, unit, rstd = norm_forward(residual_v[rows, :], gain, jnp.zeros_like(gain))
        dinput, gain_grad, shift_grad = norm_backward(dnormed, unit, rstd, gain)
        total = cot_v[rows, :].astype(jnp.float32) + dinput
        dresid[s] = total
        dattn[rows, :] = total.astype(jnp.bfloat16)
        small_own[2:3, :] += gain_grad.reshape(1, model)
        small_own[3:4, :] += shift_grad.reshape(1, model)
        if s == 0:
            loads[4].wait()
        dmixed[s] = mxu(dattn[rows, :], wo_v[...], ROWS_BY_ROWS).astype(jnp.bfloat16)
        for d in range(1, ways):
            dmixed_copy(s, d).start()
    for copy in scatter[len(shards) - 1 :]:
        copy.start()
    sum_o = Reduction(ways, columns, part_o, out_o, False, scratch[:15])
    sums_w = [
        Reduction(ways, columns, parts_w.at[i], out, i == 0, scratch[15 * (i + 1) : 15 * (i + 2)])
        for i, out in enumerate((out_q, out_k, out_v))
    ]
    sum_q, sum_k, sum_v = sums_w
    steps = columns.bit_length() - 1

    loads[5].wait()

    def out_step(i, carry):
        at = span(i, BLOCK)
        left = mixed_v[:, :, at].reshape(seqs * shard, BLOCK)
        part_o[at, :] = mxu(left, dattn[...], COLS_BY_COLS).astype(jnp.bfloat16)
        return carry

    lax.fori_loop(0, model // BLOCK, out_step, 0)
    sum_o.core_copy.start()
    for copy in loads[6:9]:
        copy.wait()

    lane = lax.broadcasted_iota(jnp.int32, (1, width), 1) // head_dim
    visible = lax.broadcasted_iota(jnp.int32, (BLOCK, BLOCK), 0) <= lax.broadcasted_iota(
        jnp.int32, (BLOCK, BLOCK), 1
    )
    scale = head_dim ** (-0.5)
    for s in range(seqs):
        dmixed_h[s, span(me, shard), :] = dmixed[s, :, span(me, width)]
        for d in range(1, ways):
            dmixed_copy(s, d).wait_recv()
        if s == 0:
            sum_o.add_core()
        dq_f[...] = jnp.zeros_like(dq_f)
        dk_f[...] = jnp.zeros_like(dk_f)
        dv_f[...] = jnp.zeros_like(dv_f)

        def one_head(h, carry):
            mine = (lane == h).astype(jnp.float32)
            for at in range(0, seq_len, BLOCK):
                rows = slice(at, at + BLOCK)
                query = (q_v[s, rows, :].astype(jnp.float32) * (mine * scale)).astype(
                    jnp.bfloat16
                )
                dout = (dmixed_h[s, rows, :].astype(jnp.float32) * mine).astype(jnp.bfloat16)
                log_row = log_ref[s, pl.ds(h, 1), rows]
                parts = [(rows, True)] + ([(slice(0, at), False)] if at else [])
                kept = []
                delta = jnp.zeros((1, BLOCK), jnp.float32)
                for keys, diagonal in parts:
                    prob = jnp.exp(mxu(k_v[s, keys, :], query, ROWS_BY_ROWS) - log_row)
                    if diagonal:
                        prob = jnp.where(visible, prob, 0.0)
                    dprob = mxu(v_v[s, keys, :], dout, ROWS_BY_ROWS)
                    delta += jnp.sum(prob * dprob, axis=0, keepdims=True)
                    kept.append((keys, prob, dprob))
                dquery = jnp.zeros((BLOCK, width), jnp.float32)
                for keys, prob, dprob in kept:
                    dv_f[keys, :] += mxu(prob.astype(jnp.bfloat16), dout)
                    dlogit = (prob * (dprob - delta)).astype(jnp.bfloat16)
                    dk_f[keys, :] += mxu(dlogit, query)
                    dquery += mxu(dlogit, k_v[s, keys, :], COLS_BY_COLS)
                dq_f[rows, :] += dquery * (mine * scale)
            return carry

        lax.fori_loop(0, heads, one_head, 0)
        for i, total in enumerate((dq_f, dk_f, dv_f)):
            grads_h[s, :, i * width : (i + 1) * width] = total[...].astype(jnp.bfloat16)
        if s == 0:
            for d in range(1, ways):
                grad_copy(s, d).start()
        grads_tok[s, :, span(me, 3 * width)] = grads_h[s, span(me, shard), :]

    loads[9].wait()

    def weight_step(i, carry):
        at = span(i, BLOCK)
        grad = mxu(normed_v[0, :, at], grads_h[0], COLS_BY_COLS)
        for s in range(1, seqs):
            grad += mxu(normed_v[s, :, at], grads_h[s], COLS_BY_COLS)
        for j in range(3):
            parts_w[j, at, :] = grad[:, j * width : (j + 1) * width].astype(jnp.bfloat16)
        return carry

    lax.fori_loop(0, model // BLOCK, weight_step, 0)
    for total in (sum_v, sum_k, sum_q):
        total.core_copy.start()

    along, across = (sum_v, sum_k), (sum_q,)
    for total in (*across, *along):
        total.add_core()
    for step in range(steps - 1):
        sum_o.add_column(step)
    for step in range(steps):
        for total in (*across, *along):
            piece = total.add_column(step)
            if step == steps - 1:
                total.piece[...] = piece.astype(jnp.bfloat16)
                total.advance()

    o_land[0] = sum_o.add_column(steps - 1).astype(jnp.bfloat16)
    o_copy = [
        send(
            o_land.at[0, :, span(peer[d], width)],
            o_land.at[d, :, 0:width],
            o_send.at[d],
            o_recv.at[d],
            {"sp": peer[d]},
        )
        for d in range(1, ways)
    ]
    for copy in o_copy:
        copy.start()

    def norm_grad(s):
        for d in range(1, ways):
            grad_copy(s, d).wait()
        dnormed = jnp.zeros((shard, model), jnp.float32)
        for j in range(ways):
            for i, weight in enumerate((wq_v, wk_v, wv_v)):
                at = (3 * j + i) * width
                dnormed += mxu(
                    grads_tok[s, :, at : at + width],
                    weight[:, j * width : (j + 1) * width],
                    ROWS_BY_ROWS,
                )
        gain = gain1_ref[...]
        _, unit, rstd = norm_forward(x_v[s].astype(jnp.float32), gain, jnp.zeros_like(gain))
        dinput, gain_grad, shift_grad = norm_backward(dnormed, unit, rstd, gain)
        tokens_v[s] = (dresid[s] + dinput).astype(jnp.bfloat16)
        results[s].start()
        small_own[0:1, :] += gain_grad.reshape(1, model)
        small_own[1:2, :] += shift_grad.reshape(1, model)

    for copy in loads[10:14]:
        copy.wait()
    for s in range(1, seqs):
        grad_copy(s, 1).start()
    for total in across:
        total.advance()
    for s in range(1, seqs):
        for d in range(2, ways):
            grad_copy(s, d).start()
    total = o_land[0, :, span(me, width)].astype(jnp.float32)
    for d, copy in enumerate(o_copy):
        copy.wait()
        total += o_land[d + 1, :, 0:width].astype(jnp.float32)
    sum_o.piece[...] = total.astype(jnp.bfloat16)
    sum_o.advance()
    for _ in range(steps - 1):
        for total in along:
            total.advance()
    for total in across:
        total.advance()
    for _ in range(steps - 1):
        sum_o.advance()
    for s in range(seqs - 1):
        norm_grad(s)
    along[0].advance()
    norm_grad(seqs - 1)

    stages = [[{"sp": peer[d]} for d in range(1, ways)], [{"dp": dp + 1 - 2 * core}]]
    stages.append([{"dp": 2 * lax.rem(dp // 2 + d, columns) + core} for d in range(1, columns)])
    slot = 0
    source = small_own
    for number, peers in enumerate(stages):
        copies = [
            send(
                source,
                small_land.at[slot + i],
                small_send.at[slot + i],
                small_recv.at[slot + i],
                device,
            )
            for i, device in enumerate(peers)
        ]
        for copy in copies:
            copy.start()
        if number == 0:
            for total in (*along[1:], sum_o):
                total.advance()
            for _ in range(steps - 1):
                for total in across:
                    total.advance()
            along[0].advance()
        elif number == 1:
            for total in along[1:]:
                total.advance()
        else:
            sum_o.advance()
        total = source[...]
        for i, copy in enumerate(copies):
            copy.wait()
            total += small_land[slot + i]
        slot += len(peers)
        if number == len(stages) - 1:
            small_out[...] = total
        else:
            small_sum[number] = total
            source = small_sum.at[number]

    loads[14].wait()
    for copy in routed_back:
        copy.wait()
    for s in range(seqs):
        rows = slice(s * shard, (s + 1) * shard)
        out = mxu(placer_v[:, rows], returned[...].reshape(-1, model), COLS_BY_COLS)
        block_v[s] = (residual_v[rows, :] + out).astype(jnp.bfloat16)
        results[seqs + s].start()
    for total in [*across, *along, sum_o]:
        total.advance()
    for s in range(seqs):
        for d in range(1, ways):
            dmixed_copy(s, d).wait_send()
    for copy in scatter + results:
        copy.wait()
    for total in [sum_o] + sums_w:
        total.finish()


def finish(
    experts,
    tokens,
    query_ref,
    key_ref,
    value_ref,
    out_ref,
    up_own,
    up_land,
    down_own,
    down_land,
    block_in,
    tokens_in,
    small_ref,
    load_ref,
    query_out,
    key_out,
    value_out,
    out_out,
    up_out,
    down_out,
    block_out,
    tokens_out,
    gain1_out,
    shift1_out,
    gain2_out,
    shift2_out,
    load_out,
):
    for source, target in (
        (query_ref, query_out),
        (key_ref, key_out),
        (value_ref, value_out),
        (out_ref, out_out),
    ):
        target[...] = source[...].astype(jnp.float32)
    for own, land, target in ((up_own, up_land, up_out), (down_own, down_land, down_out)):
        total = own[...].astype(jnp.float32)
        for i in range(land.shape[0]):
            total += land[i].astype(jnp.float32)
        target[...] = total
    block_out[...] = block_in[...]
    tokens_out[...] = tokens_in[...]
    for i, target in enumerate((gain1_out, shift1_out, gain2_out, shift2_out)):
        target[...] = small_ref[i : i + 1, :]
    load_now = small_ref[4:5, 0:experts] * experts / tokens
    load_out[...] = 0.9 * load_ref[...] + 0.1 * load_now


def vmem(count):
    return [pl.BlockSpec(memory_space=pltpu.VMEM)] * count


def params(collective_id):
    return pltpu.CompilerParams(
        collective_id=collective_id, has_side_effects=True, vmem_limit_bytes=VMEM_BYTES
    )


def dma(*shape):
    return pltpu.SemaphoreType.DMA(shape)


def local(
    tokens_in,
    expert_ids,
    query_weight,
    key_weight,
    value_weight,
    out_weight,
    norm1_gain,
    norm1_shift,
    norm2_gain,
    norm2_shift,
    up_weight,
    down_weight,
    out_cotangent,
    load_mean,
):
    seq_count, shard_len, model_width = tokens_in.shape
    row_count = seq_count * shard_len
    head_dim = model_width // HEADS
    dp_ways = lax.axis_size("dp")
    sp_ways = lax.axis_size("sp")
    sp_at = lax.axis_index("sp")
    seq_len = shard_len * sp_ways
    experts = load_mean.shape[0]
    slot_count = 2 * row_count // experts
    local_experts = up_weight.shape[0]
    ff_width = up_weight.shape[1]
    width = model_width // sp_ways
    bf16 = jnp.bfloat16
    f32 = jnp.float32

    def shape(*sizes, dtype=bf16):
        return jax.ShapeDtypeStruct(sizes, dtype)

    cot_b = out_cotangent.reshape(row_count, model_width)
    hbm = [pl.BlockSpec(memory_space=pl.ANY)]
    routed = shape(experts, slot_count, model_width)
    square = pltpu.VMEM((model_width, model_width), bf16)
    by_head = pltpu.VMEM((seq_count, seq_len, width), bf16)
    token_shape = (seq_count, shard_len, model_width)
    whole_tokens = pltpu.VMEM((seq_count, seq_len, model_width), bf16)
    weight_columns = pltpu.VMEM((model_width, width), bf16)
    slots = (experts * slot_count, row_count)
    flat = (row_count, model_width)
    (
        normed_all,
        query_h,
        key_h,
        value_h,
        mixed_b,
        arrived,
        placer,
        residual_stream,
        outgoing,
        log_total,
        counts,
    ) = pl.pallas_call(
        functools.partial(forward, sp_ways, dp_ways, head_dim),
        out_shape=[
            shape(seq_count, seq_len, model_width),
            shape(seq_count, seq_len, width),
            shape(seq_count, seq_len, width),
            shape(seq_count, seq_len, width),
            shape(*token_shape),
            routed,
            shape(*slots),
            shape(*flat, dtype=f32),
            routed,
            shape(seq_count, 8, seq_len, dtype=f32),
            shape(8, LANES, dtype=f32),
        ],
        in_specs=hbm * 6 + vmem(5),
        out_specs=hbm * 9 + vmem(2),
        scratch_shapes=[
            whole_tokens,
            pltpu.VMEM(flat, bf16),
            pltpu.VMEM(routed.shape, bf16),
            weight_columns,
            weight_columns,
            weight_columns,
            square,
            pltpu.VMEM(slots, bf16),
            whole_tokens,
            by_head,
            by_head,
            by_head,
            pltpu.VMEM((seq_len, width), f32),
            by_head,
            pltpu.VMEM(token_shape, bf16),
            pltpu.VMEM((seq_len, LANES), f32),
            pltpu.VMEM(flat, f32),
            pltpu.VMEM(flat, bf16),
            pltpu.VMEM(routed.shape, bf16),
            dma(seq_count, sp_ways),
            dma(seq_count, sp_ways),
            dma(seq_count, 2, sp_ways),
            dma(seq_count, 2, sp_ways),
            dma(dp_ways),
            dma(dp_ways),
            dma(5),
            dma(seq_count),
            dma(seq_count + 2, 4),
            pltpu.SemaphoreType.DMA,
        ],
        compiler_params=params(0),
    )(
        tokens_in,
        cot_b,
        query_weight,
        key_weight,
        value_weight,
        out_weight,
        expert_ids.reshape(1, row_count),
        *(
            vector.reshape(1, model_width)
            for vector in (norm1_gain, norm1_shift, norm2_gain, norm2_shift)
        ),
    )
    ff_own = ff_width // 2
    received_blocks = max(2 * experts, ff_own // slot_count)
    shard_size = ff_width // sp_ways
    rest = sp_ways // 2 - 1
    blocks = shard_size // slot_count
    dnormed_back, expert_out, up_own, up_rest, down_own, down_rest = pl.pallas_call(
        functools.partial(run_experts, dp_ways, sp_ways),
        out_shape=[
            routed,
            routed,
            shape(shard_size, model_width),
            shape(rest * shard_size, model_width),
            shape(blocks, slot_count, model_width),
            shape(rest * blocks, slot_count, model_width),
        ],
        in_specs=hbm * 4,
        out_specs=hbm + vmem(1) + hbm * 4,
        scratch_shapes=[
            pltpu.VMEM((received_blocks, slot_count, model_width), bf16),
            pltpu.VMEM((2,) + routed.shape, bf16),
            pltpu.VMEM((ff_own, model_width), bf16),
            pltpu.VMEM((ff_own, model_width), bf16),
            pltpu.VMEM((2 * experts * slot_count, ff_own), bf16),
            pltpu.VMEM((2 * experts * slot_count, ff_own), bf16),
            pltpu.VMEM((2 * slot_count, model_width), f32),
            pltpu.VMEM(routed.shape, f32),
            pltpu.VMEM(routed.shape, bf16),
            pltpu.VMEM(routed.shape, bf16),
            pltpu.VMEM(routed.shape, bf16),
            pltpu.VMEM(routed.shape, bf16),
            pltpu.VMEM(routed.shape, bf16),
            dma(2, sp_ways // 2),
            dma(4),
            dma(3),
            dma(dp_ways),
            dma(dp_ways),
            dma(dp_ways),
            dma(dp_ways),
            dma(dp_ways // 2 + 2),
            dma(dp_ways // 2 + 2),
            dma(dp_ways // 2),
            dma(dp_ways // 2),
            dma(dp_ways // 2),
            dma(dp_ways // 2),
        ],
        compiler_params=params(3),
    )(outgoing, arrived, up_weight[0], down_weight[0])
    columns = dp_ways // 2
    rows = model_width // dp_ways

    def reduction(part_width):
        return [
            pltpu.VMEM((columns * rows, part_width), bf16),
            pltpu.VMEM((columns * rows, part_width), bf16),
            pltpu.VMEM(((columns - 1) * rows, part_width), bf16),
            pltpu.VMEM((rows, width), bf16),
            pltpu.SemaphoreType.DMA,
            pltpu.SemaphoreType.DMA,
            dma(columns),
            dma(columns),
            dma(columns),
            dma(columns),
            dma(sp_ways),
            dma(sp_ways),
            dma(sp_ways),
            dma(sp_ways),
            pltpu.SemaphoreType.DMA,
        ]

    small_slots = 1 + (columns - 1) + (sp_ways - 1)
    whole = shape(model_width, model_width)
    tokens = pltpu.VMEM(token_shape, bf16)
    *weight_grads, up_land, down_land, block_out, tokens_grad, small_sum = pl.pallas_call(
        functools.partial(backward, sp_ways, dp_ways, head_dim),
        out_shape=[whole] * 4
        + [
            shape(rest, shard_size, model_width),
            shape(rest, blocks, slot_count, model_width),
            shape(*token_shape),
            shape(*token_shape),
            shape(8, model_width, dtype=f32),
        ],
        in_specs=hbm * 17 + vmem(4),
        out_specs=hbm * 8 + vmem(1),
        scratch_shapes=[
            tokens,
            tokens,
            pltpu.VMEM(routed.shape, bf16),
            pltpu.VMEM(placer.shape, bf16),
            pltpu.VMEM(flat, bf16),
            pltpu.VMEM(flat, f32),
            square,
            tokens,
            by_head,
            by_head,
            by_head,
            whole_tokens,
            square,
            square,
            square,
            tokens,
            pltpu.VMEM(routed.shape, bf16),
            pltpu.VMEM(token_shape, f32),
            pltpu.VMEM(flat, bf16),
            tokens,
            by_head,
            pltpu.VMEM((seq_len, width), f32),
            pltpu.VMEM((seq_len, width), f32),
            pltpu.VMEM((seq_len, width), f32),
            pltpu.VMEM((seq_count, seq_len, 3 * width), bf16),
            pltpu.VMEM((seq_count, shard_len, 3 * model_width), bf16),
            square,
            pltpu.VMEM((3, model_width, width), bf16),
            pltpu.VMEM((sp_ways, rows, model_width), bf16),
            pltpu.VMEM((8, model_width), f32),
            pltpu.VMEM((small_slots, 8, model_width), f32),
            pltpu.VMEM((2, 8, model_width), f32),
            dma(seq_count, sp_ways),
            dma(seq_count, sp_ways),
            dma(seq_count, sp_ways),
            dma(seq_count, sp_ways),
            dma(dp_ways),
            dma(dp_ways),
            dma(2, 2, sp_ways // 2),
            dma(2, 2, sp_ways // 2),
            dma(sp_ways),
            dma(sp_ways),
            dma(small_slots),
            dma(small_slots),
            dma(15),
            dma(2, seq_count),
        ]
        + reduction(model_width)
        + reduction(width) * 3,
        compiler_params=params(1),
    )(
        dnormed_back,
        placer,
        cot_b,
        residual_stream,
        out_weight,
        mixed_b,
        query_h,
        key_h,
        value_h,
        normed_all,
        query_weight,
        key_weight,
        value_weight,
        tokens_in,
        expert_out,
        up_rest,
        down_rest,
        log_total,
        norm1_gain.reshape(1, model_width),
        norm2_gain.reshape(1, model_width),
        counts,
    )
    shard_shape = (shard_size, model_width)
    parts = 8
    big = pl.BlockSpec((model_width // parts, model_width), lambda i: (i, 0))
    own = pl.BlockSpec((shard_size // parts, model_width), lambda i: (i, 0))
    land = pl.BlockSpec((rest, shard_size // parts, model_width), lambda i: (0, i, 0))
    token = pl.BlockSpec((row_count // parts, model_width), lambda i: (i, 0))
    row = pl.BlockSpec((1, model_width), lambda i: (0, 0))
    load = pl.BlockSpec((1, experts), lambda i: (0, 0))
    results = pl.pallas_call(
        functools.partial(finish, experts, row_count * dp_ways * sp_ways),
        grid=(parts,),
        out_shape=[shape(model_width, model_width, dtype=f32)] * 4
        + [shape(*shard_shape, dtype=f32)] * 2
        + [shape(*flat)] * 2
        + [shape(1, model_width, dtype=f32)] * 4
        + [shape(1, experts, dtype=f32)],
        in_specs=[big] * 4
        + [own, land, own, land, token, token]
        + [pl.BlockSpec((8, model_width), lambda i: (0, 0)), load],
        out_specs=[big] * 4 + [own, own, token, token] + [row] * 4 + [load],
        compiler_params=pltpu.CompilerParams(vmem_limit_bytes=VMEM_BYTES),
    )(
        *weight_grads,
        up_own,
        up_land,
        down_own.reshape(shard_shape),
        down_land.reshape((rest,) + shard_shape),
        block_out.reshape(flat),
        tokens_grad.reshape(flat),
        small_sum,
        load_mean.reshape(1, experts),
    )
    return (
        results[6].reshape(token_shape),
        results[7].reshape(token_shape),
        *results[:4],
        *(vector.reshape(model_width) for vector in results[8:12]),
        results[4][None],
        results[5][None],
        results[12].reshape(experts),
    )


def solution(mesh):
    return jax.shard_map(
        local,
        mesh=mesh,
        in_specs=(
            P("dp", "sp", None),
            P("dp", "sp", None, None),
            P(),
            P(),
            P(),
            P(),
            P(),
            P(),
            P(),
            P(),
            P("dp", None, None),
            P("dp", None, None),
            P("dp", "sp", None),
            P(),
        ),
        out_specs=(
            P("dp", "sp", None),
            P("dp", "sp", None),
            P(),
            P(),
            P(),
            P(),
            P(),
            P(),
            P(),
            P(),
            P("dp", "sp", None),
            P("dp", "sp", None),
            P(),
        ),
        check_vma=False,
    )
```
